32 devices in a mesh: heads: 2 (over x), pages: 16 (over z, y, core).
Axes of the slice: x: 2, y: 2, z: 4, core: 2. Of those that a mesh axis runs over, the one named last changes fastest.
Arguments:
- queries: bfloat16 [4608, 16, 128], P('pages', 'heads'), may hold values from -60 to 60
- keys: bfloat16 [4608, 16, 128], P('pages', 'heads'), may hold values from -6 to 6
- values: bfloat16 [4608, 16, 128], P('pages', 'heads'), may hold values from -6 to 6
- key_cache: bfloat16 [192, 128, 16, 128], P('pages', None, 'heads'), may hold values from -6 to 6
- value_cache: bfloat16 [192, 128, 16, 128], P('pages', None, 'heads'), may hold values from -6 to 6
- cache_len: int32 [6], replicated, may hold values from 0 to 3328, as said below
- page_table: int32 [6, 26], replicated, may hold values from 0 to 191, as said below
- append_slots: int32 [6, 6], replicated, may hold values from 0 to 191
- out_weight: bfloat16 [2048, 4096], P('heads', 'pages'), may hold values from -0.125 to 0.125
- out_bias: float32 [4096], P('heads'), may hold values from -3 to 3
Outputs:
- hidden: bfloat16 [4608, 4096], P('pages', 'heads')
- key_cache_out: bfloat16 [192, 128, 16, 128], P('pages', None, 'heads')
- value_cache_out: bfloat16 [192, 128, 16, 128], P('pages', None, 'heads')
The draws below stay inside these ranges and needn't reach their ends.
Inputs may be any that keep to these rules, and one draw needn't show every extreme that they name: Every entry of page_table and append_slots together is a different slot. `cache_len`: A multiple of 128; some request has exactly 3328.
All inputs are finite; a program needn't handle non-finite values.
Results may differ from the reference program's by a relative error of at most 0.018.
Values may be sent and summed in bfloat16 or wider, within the bound.
No kernel may reach another device: no remote copies, remote signals or barrier semaphores. Data moves between devices by JAX's collectives and lax.ppermute only.
A program may use at most 128 MiB of HBM per device.

```python
import math
import jax
import jax.numpy as jnp
from jax import lax

D = 4096
HEADS = 16
HD = 128
ROT = 32
PAGE = 128
REQS = 6
SPAN = 768
TOKENS = 4608
NEWP = 6
SLOTS = 192
MAXP = 26


def shared_order(key):
    return jax.random.permutation(jax.random.fold_in(key, 7), SLOTS)


def draw_page_table(key, part):
    slot_order = shared_order(key)
    return slot_order[:REQS * MAXP].reshape(REQS, MAXP).astype(jnp.int32)


def draw_append_slots(key, part):
    slot_order = shared_order(key)
    return slot_order[REQS * MAXP:REQS * (MAXP + NEWP)].reshape(REQS, NEWP).astype(jnp.int32)


def draw_cache_len(key, part):
    page_count = jax.random.randint(jax.random.fold_in(key, 1), (REQS,), 0, MAXP + 1)
    longest = jax.random.randint(jax.random.fold_in(key, 2), (), 0, REQS)
    page_count = jnp.where(jnp.arange(REQS) == longest, MAXP, page_count)
    return (page_count * PAGE).astype(jnp.int32)


def draw_queries(key, part):
    scaled = jax.random.normal(jax.random.fold_in(key, 3), (TOKENS, HEADS, HD), jnp.float32) * 2.5
    return jnp.clip(scaled, -60.0, 60.0).astype(jnp.bfloat16)


def level_of(stream_key, shape, split, smallest, top_value):
    def one(axis_at, shards_of):
        draws = jax.random.uniform(jax.random.fold_in(jax.random.fold_in(stream_key, 6), axis_at), (shards_of,), jnp.float32, smallest / len(split), top_value / len(split))
        return jnp.repeat(jnp.exp(draws), shape[axis_at] // shards_of).reshape((-1,) + (1,) * (len(shape) - axis_at - 1))

    factor_of = one(*split[0])
    for cut in split[1:]:
        factor_of = factor_of * one(*cut)
    return factor_of


def bell_draw(own_key, dims, scale, limit, cuts=(), kind=jnp.bfloat16):
    loudness = level_of(own_key, dims, cuts, -0.22, 0.18) if cuts else 1.0
    drawn = jax.random.normal(own_key, dims, jnp.float32) * scale * loudness
    return jnp.minimum(jnp.maximum(drawn, -limit), limit).astype(kind)


def setup_inputs(seed: int = 0) -> dict:
    seeds = jax.random.split(jax.random.key(seed), 11)
    queries = draw_queries(jax.random.fold_in(seeds[10], 71), 0)
    keys = bell_draw(seeds[1], (TOKENS, HEADS, HD), 1.0, 6.0, ((0, 16), (1, 2)))
    values = bell_draw(seeds[2], (TOKENS, HEADS, HD), 1.0, 6.0, ((0, 16), (1, 2)))
    key_cache = bell_draw(seeds[3], (SLOTS, PAGE, HEADS, HD), 1.0, 6.0, ((0, 16), (2, 2)))
    value_cache = bell_draw(seeds[4], (SLOTS, PAGE, HEADS, HD), 1.0, 6.0, ((0, 16), (2, 2)))
    cache_len = draw_cache_len(jax.random.fold_in(seeds[10], 71), 0)
    page_table = draw_page_table(jax.random.fold_in(seeds[10], 71), 0)
    append_slots = draw_append_slots(jax.random.fold_in(seeds[10], 71), 0)
    out_weight = bell_draw(seeds[8], (HEADS * HD, D), (HEADS * HD) ** -0.5, 0.125, ((0, 2), (1, 16)))
    out_bias = bell_draw(seeds[9], (D,), 0.5, 3.0, ((0, 2),), jnp.float32)
    return dict(queries=queries, keys=keys, values=values, key_cache=key_cache, value_cache=value_cache, cache_len=cache_len, page_table=page_table, append_slots=append_slots, out_weight=out_weight, out_bias=out_bias)


low_score = -1e+30

def rotate(vectors, positions):
    half_rot = ROT // 2
    inv_freq = 10000.0 ** (-2.0 * jnp.arange(half_rot, dtype=jnp.float32) / ROT)
    angles = positions[:, None] * inv_freq[None, :]
    cosine = jnp.cos(angles)[:, None, :]
    sine = jnp.sin(angles)[:, None, :]
    first_half = vectors[..., :half_rot]
    second_half = vectors[..., half_rot:ROT]
    return jnp.concatenate([first_half * cosine - second_half * sine, second_half * cosine + first_half * sine, vectors[..., ROT:]], axis=-1)

def reference(queries, keys, values, key_cache, value_cache, cache_len, page_table, append_slots, out_weight, out_bias):
    token_ids = jnp.arange(TOKENS, dtype=jnp.int32)
    request_ids = token_ids // SPAN
    starts = jnp.take(cache_len, request_ids)
    positions = (starts + token_ids % SPAN).astype(jnp.float32)
    rotated_q = rotate(queries.astype(jnp.float32), positions).astype(jnp.bfloat16)
    rotated_k = rotate(keys.astype(jnp.float32), positions).astype(jnp.bfloat16)
    fresh_slots = append_slots.reshape(-1)
    key_out = key_cache.at[fresh_slots].set(rotated_k.reshape(REQS * NEWP, PAGE, HEADS, HD))
    value_out = value_cache.at[fresh_slots].set(values.reshape(REQS * NEWP, PAGE, HEADS, HD))
    score_scale = 1.0 / math.sqrt(HD)
    offsets = jnp.arange(PAGE * (MAXP + NEWP), dtype=jnp.int32)
    query_offsets = jnp.arange(SPAN, dtype=jnp.int32)

    def one_request(request):
        length = cache_len[request]
        slot_list = jnp.concatenate([page_table[request], append_slots[request]]).astype(jnp.int32)
        req_keys = jnp.take(key_out, slot_list, axis=0).reshape(-1, HEADS, HD).astype(jnp.float32)
        req_values = jnp.take(value_out, slot_list, axis=0).reshape(-1, HEADS, HD).astype(jnp.float32)
        query_pos = length + query_offsets
        cached_part = offsets < PAGE * MAXP
        key_pos = jnp.where(cached_part, offsets, length + offsets - PAGE * MAXP)
        allowed = jnp.where(cached_part[None, :], (key_pos < length)[None, :], key_pos[None, :] <= query_pos[:, None])
        block = lax.dynamic_slice_in_dim(rotated_q, (request * SPAN).astype(jnp.int32), SPAN, 0).astype(jnp.float32)

        def one_head(head):
            head_q = lax.dynamic_index_in_dim(block, head, 1, keepdims=False)
            head_k = lax.dynamic_index_in_dim(req_keys, head, 1, keepdims=False)
            head_v = lax.dynamic_index_in_dim(req_values, head, 1, keepdims=False)
            scores = jnp.dot(head_q, head_k.T, precision=lax.Precision.HIGHEST) * score_scale
            scores = jnp.where(allowed, scores, low_score)
            peak = lax.optimization_barrier(jnp.max(scores, axis=1, keepdims=True))
            weights = jnp.where(allowed, jnp.exp(scores - peak), 0.0)
            totals = lax.optimization_barrier(jnp.sum(weights, axis=1, keepdims=True))
            rounded = lax.optimization_barrier(weights.astype(jnp.bfloat16))
            weighted = jnp.dot(rounded.astype(jnp.float32), head_v, precision=lax.Precision.HIGHEST)
            return (weighted / totals).astype(jnp.bfloat16)
        return lax.map(one_head, jnp.arange(HEADS, dtype=jnp.int32))
    attended = lax.map(one_request, jnp.arange(REQS, dtype=jnp.int32))
    attended = jnp.transpose(attended, (0, 2, 1, 3)).reshape(TOKENS, HEADS * HD)
    hidden = (jnp.dot(attended, out_weight, preferred_element_type=jnp.float32) + out_bias[None, :]).astype(jnp.bfloat16)
    return (hidden, key_out, value_out)
```

```python
import math

import jax
import jax.numpy as jnp
from jax import lax
from jax.experimental import pallas as pl
from jax.experimental.pallas import tpu as pltpu
from jax.sharding import PartitionSpec as P

ROT = 32
PAGE = 128
QTILE = 256

low_score = -(2.0**99)


def rotate(vectors, positions):
    half_rot = ROT // 2
    inv_freq = 10000.0 ** (-2.0 * jnp.arange(half_rot, dtype=jnp.float32) / ROT)
    angles = positions[:, None] * inv_freq[None, :]
    cosine = jnp.cos(angles)[:, None, :]
    sine = jnp.sin(angles)[:, None, :]
    first_half = vectors[..., :half_rot]
    second_half = vectors[..., half_rot:ROT]
    return jnp.concatenate(
        [
            first_half * cosine - second_half * sine,
            second_half * cosine + first_half * sine,
            vectors[..., ROT:],
        ],
        axis=-1,
    )


def cached_kernel(unit, span, scale2, order_ref, start_ref, count_ref, q_ref, k_ref, v_ref,
                  o_ref, m_ref, l_ref, q_scr, acc_scr):
    requests = m_ref.shape[1]
    per_part = q_ref.shape[2] // unit
    per_request = span // unit

    def place(request, index):
        at = request * per_request + index
        return at // per_part, pl.multiple_of((at % per_part) * unit, unit)

    def one_request(request, _):
        for index in range(per_request):
            part, row = place(request, index)
            q_scr[index * unit : (index + 1) * unit, :] = q_ref[part, 0, pl.ds(row, unit), :]
        first = start_ref[request]
        count = count_ref[request]
        m_ref[0, request] = jnp.full((1, span), low_score, jnp.float32)
        l_ref[0, request] = jnp.zeros((1, span), jnp.float32)
        acc_scr[...] = jnp.zeros(acc_scr.shape, jnp.float32)

        def pages(slots):
            k = jnp.concatenate([k_ref[0, s] for s in slots], axis=0)
            v = jnp.concatenate([v_ref[0, s] for s in slots], axis=1)
            for c in range(0, span, QTILE):
                cols = slice(c, c + QTILE)
                scores = lax.dot_general(
                    k, q_scr[cols, :], (((1,), (1,)), ((), ())),
                    preferred_element_type=jnp.float32,
                )
                before = m_ref[0, request, :, cols]
                peak = jnp.maximum(before, jnp.max(scores, axis=0, keepdims=True))
                weights = jnp.exp2((scores - peak) * scale2)
                fade = jnp.exp2((before - peak) * scale2)
                m_ref[0, request, :, cols] = peak
                l_ref[0, request, :, cols] = (
                    l_ref[0, request, :, cols] * fade + jnp.sum(weights, axis=0, keepdims=True)
                )
                acc_scr[:, cols] = acc_scr[:, cols] * fade + jnp.dot(
                    v, weights.astype(jnp.bfloat16), preferred_element_type=jnp.float32
                )

        def pair(index, _):
            at = first + 2 * index
            pages([order_ref[at], order_ref[at + 1]])
            return 0

        lax.fori_loop(0, count // 2, pair, 0)

        @pl.when(count % 2 == 1)
        def _():
            pages([order_ref[first + count - 1]])

        out = acc_scr[...].T.astype(jnp.bfloat16)
        for index in range(per_request):
            part, row = place(request, index)
            o_ref[part, 0, pl.ds(row, unit), :] = out[index * unit : (index + 1) * unit, :]
        return 0

    lax.fori_loop(0, requests, one_request, 0)


def cached_attention(q_parts, k_heads, v_heads, order, starts, counts, span, scale2):
    parts, heads, part_len, head_dim = q_parts.shape
    slots = k_heads.shape[1]
    requests = counts.shape[0]
    unit = math.gcd(span, part_len)
    head_block = lambda h, *_: (0, h, 0, 0)
    own_block = lambda h, *_: (h, 0, 0, 0)
    return pl.pallas_call(
        lambda *refs: cached_kernel(unit, span, scale2, *refs),
        grid_spec=pltpu.PrefetchScalarGridSpec(
            num_scalar_prefetch=3,
            grid=(heads,),
            in_specs=[
                pl.BlockSpec((parts, 1, part_len, head_dim), head_block),
                pl.BlockSpec((1, slots, PAGE, head_dim), own_block),
                pl.BlockSpec((1, slots, head_dim, PAGE), own_block),
            ],
            out_specs=[
                pl.BlockSpec((parts, 1, part_len, head_dim), head_block),
                pl.BlockSpec((1, requests, 1, span), own_block),
                pl.BlockSpec((1, requests, 1, span), own_block),
            ],
            scratch_shapes=[
                pltpu.VMEM((span, head_dim), jnp.bfloat16),
                pltpu.VMEM((head_dim, span), jnp.float32),
            ],
        ),
        out_shape=[
            jax.ShapeDtypeStruct((parts, heads, part_len, head_dim), jnp.bfloat16),
            jax.ShapeDtypeStruct((heads, requests, 1, span), jnp.float32),
            jax.ShapeDtypeStruct((heads, requests, 1, span), jnp.float32),
        ],
        compiler_params=pltpu.CompilerParams(vmem_limit_bytes=40 * 2**20),
        name="cached_attention",
    )(order, starts, counts, q_parts, k_heads, v_heads)


def fresh_kernel(scale2, q_ref, k_ref, v_ref, tok_ref, key_ref, o_ref, m_ref, l_ref):
    scores = lax.dot_general(
        k_ref[0], q_ref[0], (((1,), (1,)), ((), ())), preferred_element_type=jnp.float32
    )
    token = tok_ref[0:1, :]
    first = tok_ref[1:2, :]
    key = key_ref[:, 0:1]
    visible = (key <= token) & (key >= first)
    scores = jnp.where(visible, scores, low_score)
    peak = jnp.max(scores, axis=0, keepdims=True)
    weights = jnp.where(visible, jnp.exp2((scores - peak) * scale2), 0.0)
    m_ref[0] = peak
    l_ref[0] = jnp.sum(weights, axis=0, keepdims=True)
    o_ref[0] = jnp.dot(
        v_ref[0], weights.astype(jnp.bfloat16), preferred_element_type=jnp.float32
    )


def fresh_attention(q_own, k_window, v_window, token_rows, key_cols, scale2):
    heads, tok_dev, head_dim = q_own.shape
    window = k_window.shape[1]
    own = lambda h: (h, 0, 0)
    fixed = lambda h: (0, 0)
    return pl.pallas_call(
        lambda *refs: fresh_kernel(scale2, *refs),
        grid=(heads,),
        in_specs=[
            pl.BlockSpec((1, tok_dev, head_dim), own),
            pl.BlockSpec((1, window, head_dim), own),
            pl.BlockSpec((1, head_dim, window), own),
            pl.BlockSpec(token_rows.shape, fixed),
            pl.BlockSpec(key_cols.shape, fixed),
        ],
        out_specs=[
            pl.BlockSpec((1, head_dim, tok_dev), own),
            pl.BlockSpec((1, 1, tok_dev), own),
            pl.BlockSpec((1, 1, tok_dev), own),
        ],
        out_shape=[
            jax.ShapeDtypeStruct((heads, head_dim, tok_dev), jnp.float32),
            jax.ShapeDtypeStruct((heads, 1, tok_dev), jnp.float32),
            jax.ShapeDtypeStruct((heads, 1, tok_dev), jnp.float32),
        ],
        compiler_params=pltpu.CompilerParams(vmem_limit_bytes=40 * 2**20),
        name="fresh_attention",
    )(q_own, k_window, v_window, token_rows, key_cols)


def per_device(
    queries,
    keys,
    values,
    key_cache,
    value_cache,
    cache_len,
    page_table,
    append_slots,
    out_weight,
    out_bias,
):
    tok_dev, head_count, head_dim = queries.shape
    requests = cache_len.shape[0]
    max_pages = page_table.shape[1]
    new_pages = append_slots.shape[1]
    span_len = new_pages * PAGE
    slot_count = key_cache.shape[0]
    tokens = requests * span_len
    page_devs = tokens // tok_dev
    scale2 = math.log2(math.e) / math.sqrt(head_dim)
    device_at = lax.axis_index("pages")
    token_ids = device_at * tok_dev + jnp.arange(tok_dev, dtype=jnp.int32)
    request_ids = token_ids // span_len
    request_grid = jnp.arange(requests, dtype=jnp.int32)
    starts = jnp.sum(
        jnp.where(request_ids[:, None] == request_grid[None, :], cache_len[None, :], 0), axis=1
    )
    positions = (starts + token_ids % span_len).astype(jnp.float32)
    rotated_q = rotate(queries.astype(jnp.float32), positions).astype(jnp.bfloat16)
    rotated_k = rotate(keys.astype(jnp.float32), positions).astype(jnp.bfloat16)
    q_own = jnp.transpose(rotated_q, (1, 0, 2))
    q_parts = lax.all_gather(q_own, "pages", axis=0, tiled=False)
    if math.gcd(span_len, tok_dev) % 16:
        q_all = jnp.transpose(q_parts, (1, 0, 2, 3)).reshape(1, head_count, tokens, head_dim)
    else:
        q_all = q_parts
    all_k = lax.all_gather(rotated_k, "pages", axis=0, tiled=True)
    all_v = lax.all_gather(values, "pages", axis=0, tiled=True)
    weight = lax.all_gather(out_weight, "pages", axis=1, tiled=True)

    my_slots = device_at * slot_count + jnp.arange(slot_count, dtype=jnp.int32)
    cached_hit = page_table.reshape(-1)[None, :] == my_slots[:, None]
    fresh_hit = append_slots.reshape(-1)[None, :] == my_slots[:, None]
    table_at = jnp.arange(requests * max_pages, dtype=jnp.int32)
    shown = (table_at % max_pages) * PAGE < jnp.repeat(cache_len, max_pages)
    is_fresh = jnp.any(fresh_hit, axis=1)
    fresh_index = jnp.sum(
        jnp.where(fresh_hit, jnp.arange(requests * new_pages, dtype=jnp.int32)[None, :], 0), axis=1
    )
    slot_key = requests - jnp.sum(
        jnp.where(cached_hit & shown[None, :], requests - (table_at // max_pages)[None, :], 0),
        axis=1,
    )
    slot_at = jnp.arange(slot_count, dtype=jnp.int32)
    earlier = (slot_key[None, :] < slot_key[:, None]) | (
        (slot_key[None, :] == slot_key[:, None]) & (slot_at[None, :] < slot_at[:, None])
    )
    rank = jnp.sum(earlier.astype(jnp.int32), axis=1)
    order = jnp.sum(jnp.where(rank[None, :] == slot_at[:, None], slot_at[None, :], 0), axis=1)
    slot_starts = jnp.sum((slot_key[None, :] < request_grid[:, None]).astype(jnp.int32), axis=1)
    slot_counts = jnp.sum((slot_key[None, :] == request_grid[:, None]).astype(jnp.int32), axis=1)

    k_heads = jnp.transpose(key_cache, (2, 0, 1, 3))
    v_heads = jnp.transpose(value_cache, (2, 0, 3, 1))
    weighted, peaks, totals = cached_attention(
        q_all, k_heads, v_heads, order, slot_starts, slot_counts, span_len, scale2
    )
    peaks = peaks.reshape(head_count, tokens)
    totals = totals.reshape(head_count, tokens)
    top = lax.pmax(peaks.astype(jnp.bfloat16), "pages").astype(jnp.float32)
    fade = jnp.exp2((peaks - top) * scale2)

    def by_owner(rows):
        return jnp.transpose(rows.reshape(head_count, page_devs, tok_dev), (1, 0, 2))

    if q_all.shape[0] == 1:
        weighted = jnp.transpose(
            weighted.reshape(head_count, page_devs, tok_dev, head_dim), (1, 0, 2, 3)
        )
    scaled = (weighted.astype(jnp.float32) * by_owner(fade)[..., None]).astype(jnp.bfloat16)
    sums = by_owner(totals * fade).astype(jnp.bfloat16).reshape(page_devs, -1)
    sum_rows = -(-sums.shape[1] // (16 * head_dim)) * 16
    sums = jnp.pad(sums, ((0, 0), (0, sum_rows * head_dim - sums.shape[1])))
    packed = jnp.concatenate(
        [
            scaled.reshape(page_devs, head_count * tok_dev, head_dim),
            sums.reshape(page_devs, sum_rows, head_dim),
        ],
        axis=1,
    )
    packed = lax.psum_scatter(packed, "pages", scatter_dimension=0, tiled=True)[0]
    packed = packed.astype(jnp.float32)
    cached_sum = packed[: head_count * tok_dev].reshape(head_count, tok_dev, head_dim)
    cached_total = packed[head_count * tok_dev :].reshape(-1)[: head_count * tok_dev]
    cached_total = cached_total.reshape(head_count, tok_dev)
    cached_top = lax.dynamic_slice_in_dim(top, device_at * tok_dev, tok_dev, 1)

    window_at = jnp.minimum(request_ids[0], requests - 2) * span_len
    k_window = lax.dynamic_slice_in_dim(all_k, window_at, 2 * span_len, 0)
    v_window = lax.dynamic_slice_in_dim(all_v, window_at, 2 * span_len, 0)
    token_rows = jnp.stack([token_ids, request_ids * span_len])
    key_cols = (window_at + jnp.arange(2 * span_len, dtype=jnp.int32))[:, None]
    fresh_sum, fresh_top, fresh_total = fresh_attention(
        q_own,
        jnp.transpose(k_window, (1, 0, 2)),
        jnp.transpose(v_window, (1, 2, 0)),
        token_rows,
        key_cols,
        scale2,
    )
    fresh_sum = jnp.transpose(fresh_sum, (0, 2, 1))
    fresh_top = fresh_top[:, 0]
    fresh_total = fresh_total[:, 0]
    best = jnp.maximum(cached_top, fresh_top)
    cached_part = jnp.exp2((cached_top - best) * scale2)
    fresh_part = jnp.exp2((fresh_top - best) * scale2)
    total = cached_total * cached_part + fresh_total * fresh_part
    attended = (
        cached_sum * (cached_part / total)[..., None] + fresh_sum * (fresh_part / total)[..., None]
    ).astype(jnp.bfloat16)
    attended = jnp.transpose(attended, (1, 0, 2)).reshape(tok_dev, head_count * head_dim)

    projected = jnp.dot(attended, weight, preferred_element_type=jnp.float32)
    summed = lax.psum_scatter(
        projected.astype(jnp.bfloat16), "heads", scatter_dimension=1, tiled=True
    ).astype(jnp.float32)
    hidden = (summed + out_bias[None, :]).astype(jnp.bfloat16)

    page_shape = (requests * new_pages, PAGE, head_count, head_dim)
    key_out = jnp.where(
        is_fresh[:, None, None, None],
        jnp.take(all_k.reshape(page_shape), fresh_index, axis=0),
        key_cache,
    )
    value_out = jnp.where(
        is_fresh[:, None, None, None],
        jnp.take(all_v.reshape(page_shape), fresh_index, axis=0),
        value_cache,
    )
    return (hidden, key_out, value_out)


def solution(mesh):
    placed = (
        P("pages", "heads", None),
        P("pages", "heads", None),
        P("pages", "heads", None),
        P("pages", None, "heads", None),
        P("pages", None, "heads", None),
        P(),
        P(),
        P(),
        P("heads", "pages"),
        P("heads"),
    )
    return jax.shard_map(
        per_device,
        mesh=mesh,
        in_specs=placed,
        out_specs=(
            P("pages", "heads"),
            P("pages", None, "heads", None),
            P("pages", None, "heads", None),
        ),
        check_vma=False,
    )
```

```python
import math

import jax
import jax.numpy as jnp
from jax import lax
from jax.experimental import pallas as pl
from jax.experimental.pallas import tpu as pltpu
from jax.sharding import PartitionSpec as P

ROT = 32
PAGE = 128
QTILE = 256

low_score = -(2.0**99)


def rotate(vectors, positions):
    half_rot = ROT // 2
    inv_freq = 10000.0 ** (-2.0 * jnp.arange(half_rot, dtype=jnp.float32) / ROT)
    angles = positions[:, None] * inv_freq[None, :]
    cosine = jnp.cos(angles)[:, None, :]
    sine = jnp.sin(angles)[:, None, :]
    first_half = vectors[..., :half_rot]
    second_half = vectors[..., half_rot:ROT]
    return jnp.concatenate(
        [
            first_half * cosine - second_half * sine,
            second_half * cosine + first_half * sine,
            vectors[..., ROT:],
        ],
        axis=-1,
    )


def cached_kernel(unit, span, scale2, sides, side_ref, order_ref, start_ref, count_ref, *refs):
    q_refs, (k_ref, v_ref), refs = refs[:sides], refs[sides : sides + 2], refs[sides + 2 :]
    o_refs, (m_ref, l_ref, q_scr, acc_scr) = refs[:sides], refs[sides:]
    requests = m_ref.shape[1]
    per_part = q_refs[0].shape[2] // unit
    per_request = span // unit

    def on_side(request, index, action):
        at = request * per_request + index
        part = at // per_part
        row = pl.ds(pl.multiple_of((at % per_part) * unit, unit), unit)
        if sides == 1:
            action(0, part, row)
            return
        same = part % 2 == side_ref[0]

        @pl.when(same)
        def _():
            action(0, part // 2, row)

        @pl.when(jnp.logical_not(same))
        def _():
            action(1, part // 2, row)

    def one_request(request, _):
        for index in range(per_request):

            def load(side, part, row, index=index):
                q_scr[index * unit : (index + 1) * unit, :] = q_refs[side][part, 0, row, :]

            on_side(request, index, load)
        first = start_ref[request]
        count = count_ref[request]
        m_ref[0, request] = jnp.full((1, span), low_score, jnp.float32)
        l_ref[0, request] = jnp.zeros((1, span), jnp.float32)
        acc_scr[...] = jnp.zeros(acc_scr.shape, jnp.float32)

        def pages(slots):
            k = jnp.concatenate([k_ref[0, s] for s in slots], axis=0)
            v = jnp.concatenate([v_ref[0, s] for s in slots], axis=1)
            for c in range(0, span, QTILE):
                cols = slice(c, c + QTILE)
                scores = lax.dot_general(
                    k, q_scr[cols, :], (((1,), (1,)), ((), ())),
                    preferred_element_type=jnp.float32,
                )
                before = m_ref[0, request, :, cols]
                peak = jnp.maximum(before, jnp.max(scores, axis=0, keepdims=True))
                weights = jnp.exp2((scores - peak) * scale2)
                fade = jnp.exp2((before - peak) * scale2)
                m_ref[0, request, :, cols] = peak
                l_ref[0, request, :, cols] = (
                    l_ref[0, request, :, cols] * fade + jnp.sum(weights, axis=0, keepdims=True)
                )
                acc_scr[:, cols] = acc_scr[:, cols] * fade + jnp.dot(
                    v, weights.astype(jnp.bfloat16), preferred_element_type=jnp.float32
                )

        def pair(index, _):
            at = first + 2 * index
            pages([order_ref[at], order_ref[at + 1]])
            return 0

        lax.fori_loop(0, count // 2, pair, 0)

        @pl.when(count % 2 == 1)
        def _():
            pages([order_ref[first + count - 1]])

        out = acc_scr[...].T.astype(jnp.bfloat16)
        for index in range(per_request):

            def store(side, part, row, index=index):
                o_refs[side][part, 0, row, :] = out[index * unit : (index + 1) * unit, :]

            on_side(request, index, store)
        return 0

    lax.fori_loop(0, requests, one_request, 0)


def cached_attention(q_sides, k_heads, v_heads, side, order, starts, counts, span, scale2):
    sides = len(q_sides)
    parts, heads, part_len, head_dim = q_sides[0].shape
    slots = k_heads.shape[1]
    requests = counts.shape[0]
    unit = math.gcd(span, part_len)
    head_block = pl.BlockSpec((parts, 1, part_len, head_dim), lambda h, *_: (0, h, 0, 0))
    own_block = lambda *dims: pl.BlockSpec((1,) + dims, lambda h, *_: (h, 0, 0, 0))
    outs = pl.pallas_call(
        lambda *refs: cached_kernel(unit, span, scale2, sides, *refs),
        grid_spec=pltpu.PrefetchScalarGridSpec(
            num_scalar_prefetch=4,
            grid=(heads,),
            in_specs=[head_block] * sides
            + [own_block(slots, PAGE, head_dim), own_block(slots, head_dim, PAGE)],
            out_specs=[head_block] * sides
            + [own_block(requests, 1, span), own_block(requests, 1, span)],
            scratch_shapes=[
                pltpu.VMEM((span, head_dim), jnp.bfloat16),
                pltpu.VMEM((head_dim, span), jnp.float32),
            ],
        ),
        out_shape=[jax.ShapeDtypeStruct((parts, heads, part_len, head_dim), jnp.bfloat16)] * sides
        + [jax.ShapeDtypeStruct((heads, requests, 1, span), jnp.float32)] * 2,
        compiler_params=pltpu.CompilerParams(vmem_limit_bytes=40 * 2**20),
        name="cached_attention",
    )(side, order, starts, counts, *q_sides, k_heads, v_heads)
    return outs[:sides], outs[sides], outs[sides + 1]


def page_kernel(fresh_ref, index_ref, kc_ref, vc_ref, kn_ref, vn_ref, ko_ref, vo_ref):
    fresh = fresh_ref[pl.program_id(0)] > 0

    @pl.when(fresh)
    def _():
        ko_ref[...] = kn_ref[...]
        vo_ref[...] = vn_ref[...]

    @pl.when(jnp.logical_not(fresh))
    def _():
        ko_ref[...] = kc_ref[...]
        vo_ref[...] = vc_ref[...]


def write_pages(key_cache, value_cache, new_keys, new_values, is_fresh, fresh_index):
    block = (1,) + key_cache.shape[1:]
    own = pl.BlockSpec(block, lambda s, fresh, index: (s, 0, 0, 0))
    new = pl.BlockSpec(block, lambda s, fresh, index: (index[s], 0, 0, 0))
    return pl.pallas_call(
        page_kernel,
        grid_spec=pltpu.PrefetchScalarGridSpec(
            num_scalar_prefetch=2,
            grid=(key_cache.shape[0],),
            in_specs=[own, own, new, new],
            out_specs=[own, own],
        ),
        out_shape=[jax.ShapeDtypeStruct(key_cache.shape, key_cache.dtype)] * 2,
        compiler_params=pltpu.CompilerParams(vmem_limit_bytes=40 * 2**20),
        name="write_pages",
    )(is_fresh.astype(jnp.int32), fresh_index, key_cache, value_cache, new_keys, new_values)


def swap(x, bit):
    devs = lax.axis_size("pages")
    return lax.ppermute(x, "pages", [(p, p ^ bit) for p in range(devs)])


def gather_lines(x):
    devs = lax.axis_size("pages")
    device_at = lax.axis_index("pages")
    step = devs // 4
    lines = [[g + step * i for i in range(4)] for g in range(step)]
    held = lax.all_gather(x, "pages", axis=0, tiled=False, axis_index_groups=lines)[None]
    bit = step // 2
    while bit:
        mine = (device_at // bit) % 2
        got = swap(held, bit)
        held = jnp.concatenate(
            [jnp.where(mine == 0, held, got), jnp.where(mine == 0, got, held)], axis=0
        )
        bit //= 2
    bits = step.bit_length() - 1
    held = held.reshape((2,) * bits + (4,) + x.shape)
    order = (bits,) + tuple(range(bits - 1, -1, -1)) + tuple(range(bits + 1, held.ndim))
    return jnp.transpose(held, order).reshape((devs * x.shape[0],) + x.shape[1:])


def fresh_kernel(scale2, q_ref, k_ref, v_ref, tok_ref, key_ref, o_ref, m_ref, l_ref):
    scores = lax.dot_general(
        k_ref[0], q_ref[0], (((1,), (1,)), ((), ())), preferred_element_type=jnp.float32
    )
    token = tok_ref[0:1, :]
    first = tok_ref[1:2, :]
    key = key_ref[:, 0:1]
    visible = (key <= token) & (key >= first)
    scores = jnp.where(visible, scores, low_score)
    peak = jnp.max(scores, axis=0, keepdims=True)
    weights = jnp.where(visible, jnp.exp2((scores - peak) * scale2), 0.0)
    m_ref[0] = peak
    l_ref[0] = jnp.sum(weights, axis=0, keepdims=True)
    o_ref[0] = jnp.dot(
        v_ref[0], weights.astype(jnp.bfloat16), preferred_element_type=jnp.float32
    )


def fresh_attention(q_own, k_window, v_window, token_rows, key_cols, scale2):
    heads, tok_dev, head_dim = q_own.shape
    window = k_window.shape[1]
    own = lambda h: (h, 0, 0)
    fixed = lambda h: (0, 0)
    return pl.pallas_call(
        lambda *refs: fresh_kernel(scale2, *refs),
        grid=(heads,),
        in_specs=[
            pl.BlockSpec((1, tok_dev, head_dim), own),
            pl.BlockSpec((1, window, head_dim), own),
            pl.BlockSpec((1, head_dim, window), own),
            pl.BlockSpec(token_rows.shape, fixed),
            pl.BlockSpec(key_cols.shape, fixed),
        ],
        out_specs=[
            pl.BlockSpec((1, head_dim, tok_dev), own),
            pl.BlockSpec((1, 1, tok_dev), own),
            pl.BlockSpec((1, 1, tok_dev), own),
        ],
        out_shape=[
            jax.ShapeDtypeStruct((heads, head_dim, tok_dev), jnp.float32),
            jax.ShapeDtypeStruct((heads, 1, tok_dev), jnp.float32),
            jax.ShapeDtypeStruct((heads, 1, tok_dev), jnp.float32),
        ],
        compiler_params=pltpu.CompilerParams(vmem_limit_bytes=40 * 2**20),
        name="fresh_attention",
    )(q_own, k_window, v_window, token_rows, key_cols)


def per_device(
    queries,
    keys,
    values,
    key_cache,
    value_cache,
    cache_len,
    page_table,
    append_slots,
    out_weight,
    out_bias,
):
    tok_dev, head_count, head_dim = queries.shape
    requests = cache_len.shape[0]
    max_pages = page_table.shape[1]
    new_pages = append_slots.shape[1]
    span_len = new_pages * PAGE
    slot_count = key_cache.shape[0]
    tokens = requests * span_len
    page_devs = tokens // tok_dev
    scale2 = math.log2(math.e) / math.sqrt(head_dim)
    device_at = lax.axis_index("pages")
    token_ids = device_at * tok_dev + jnp.arange(tok_dev, dtype=jnp.int32)
    request_ids = token_ids // span_len
    request_grid = jnp.arange(requests, dtype=jnp.int32)
    starts = jnp.sum(
        jnp.where(request_ids[:, None] == request_grid[None, :], cache_len[None, :], 0), axis=1
    )
    positions = (starts + token_ids % span_len).astype(jnp.float32)
    rotated_q = rotate(queries.astype(jnp.float32), positions).astype(jnp.bfloat16)
    rotated_k = rotate(keys.astype(jnp.float32), positions).astype(jnp.bfloat16)
    q_own = jnp.transpose(rotated_q, (1, 0, 2))
    core = device_at % 2
    by_core = [[p for p in range(page_devs) if p % 2 == c] for c in range(2)]
    q_same = lax.all_gather(q_own, "pages", axis=0, tiled=False, axis_index_groups=by_core)
    q_other = swap(q_same, 1)
    one_side = math.gcd(span_len, tok_dev) % 16 != 0
    if one_side:
        q_all = jnp.stack(
            [jnp.where(core == 0, q_same, q_other), jnp.where(core == 0, q_other, q_same)], axis=1
        ).reshape(page_devs, head_count, tok_dev, head_dim)
        q_sides = [jnp.transpose(q_all, (1, 0, 2, 3)).reshape(1, head_count, tokens, head_dim)]
    else:
        q_sides = [q_same, q_other]
    all_k = lax.all_gather(rotated_k, "pages", axis=0, tiled=True)
    all_v = gather_lines(values)
    weight = lax.all_gather(out_weight, "pages", axis=1, tiled=True)

    my_slots = device_at * slot_count + jnp.arange(slot_count, dtype=jnp.int32)
    cached_hit = page_table.reshape(-1)[None, :] == my_slots[:, None]
    fresh_hit = append_slots.reshape(-1)[None, :] == my_slots[:, None]
    table_at = jnp.arange(requests * max_pages, dtype=jnp.int32)
    shown = (table_at % max_pages) * PAGE < jnp.repeat(cache_len, max_pages)
    is_fresh = jnp.any(fresh_hit, axis=1)
    fresh_index = jnp.sum(
        jnp.where(fresh_hit, jnp.arange(requests * new_pages, dtype=jnp.int32)[None, :], 0), axis=1
    )
    slot_key = requests - jnp.sum(
        jnp.where(cached_hit & shown[None, :], requests - (table_at // max_pages)[None, :], 0),
        axis=1,
    )
    slot_at = jnp.arange(slot_count, dtype=jnp.int32)
    earlier = (slot_key[None, :] < slot_key[:, None]) | (
        (slot_key[None, :] == slot_key[:, None]) & (slot_at[None, :] < slot_at[:, None])
    )
    rank = jnp.sum(earlier.astype(jnp.int32), axis=1)
    order = jnp.sum(jnp.where(rank[None, :] == slot_at[:, None], slot_at[None, :], 0), axis=1)
    slot_starts = jnp.sum((slot_key[None, :] < request_grid[:, None]).astype(jnp.int32), axis=1)
    slot_counts = jnp.sum((slot_key[None, :] == request_grid[:, None]).astype(jnp.int32), axis=1)

    k_heads = jnp.transpose(key_cache, (2, 0, 1, 3))
    v_heads = jnp.transpose(value_cache, (2, 0, 3, 1))
    weighted, peaks, totals = cached_attention(
        q_sides, k_heads, v_heads, core[None], order, slot_starts, slot_counts, span_len, scale2
    )
    peaks = peaks.reshape(head_count, tokens)
    totals = totals.reshape(head_count, tokens)
    top = lax.all_gather(peaks.astype(jnp.bfloat16), "pages", axis=0, tiled=False)
    top = jnp.max(top, axis=0).astype(jnp.float32)
    fade = jnp.exp2((peaks - top) * scale2)

    def by_side(rows):
        rows = rows.reshape((head_count, page_devs // 2, 2, tok_dev) + rows.shape[2:])
        rows = jnp.moveaxis(rows, 2, 0)
        same = jnp.where(core == 0, rows[0], rows[1])
        other = jnp.where(core == 0, rows[1], rows[0])
        return jnp.moveaxis(same, 1, 0), jnp.moveaxis(other, 1, 0)

    if one_side:
        weighted = by_side(weighted[0][0])
    chunk_rows = head_count * tok_dev
    sum_rows = -(-chunk_rows // (16 * head_dim)) * 16

    def pack(part, fade_part, total_part):
        scaled = (part.astype(jnp.float32) * fade_part[..., None]).astype(jnp.bfloat16)
        sums = (total_part * fade_part).astype(jnp.bfloat16).reshape(page_devs // 2, -1)
        sums = jnp.pad(sums, ((0, 0), (0, sum_rows * head_dim - sums.shape[1])))
        return jnp.concatenate(
            [
                scaled.reshape(page_devs // 2, chunk_rows, head_dim),
                sums.reshape(page_devs // 2, sum_rows, head_dim),
            ],
            axis=1,
        )

    packed_same, packed_other = [
        pack(*parts) for parts in zip(weighted, by_side(fade), by_side(totals))
    ]
    packed = packed_same.astype(jnp.float32) + swap(packed_other, 1).astype(jnp.float32)
    packed = lax.psum_scatter(
        packed.astype(jnp.bfloat16),
        "pages",
        scatter_dimension=0,
        axis_index_groups=by_core,
        tiled=True,
    )[0].astype(jnp.float32)
    cached_sum = packed[: head_count * tok_dev].reshape(head_count, tok_dev, head_dim)
    cached_total = packed[head_count * tok_dev :].reshape(-1)[: head_count * tok_dev]
    cached_total = cached_total.reshape(head_count, tok_dev)
    cached_top = lax.dynamic_slice_in_dim(top, device_at * tok_dev, tok_dev, 1)

    window_at = jnp.minimum(request_ids[0], requests - 2) * span_len
    k_window = lax.dynamic_slice_in_dim(all_k, window_at, 2 * span_len, 0)
    v_window = lax.dynamic_slice_in_dim(all_v, window_at, 2 * span_len, 0)
    token_rows = jnp.stack([token_ids, request_ids * span_len])
    key_cols = (window_at + jnp.arange(2 * span_len, dtype=jnp.int32))[:, None]
    fresh_sum, fresh_top, fresh_total = fresh_attention(
        q_own,
        jnp.transpose(k_window, (1, 0, 2)),
        jnp.transpose(v_window, (1, 2, 0)),
        token_rows,
        key_cols,
        scale2,
    )
    fresh_sum = jnp.transpose(fresh_sum, (0, 2, 1))
    fresh_top = fresh_top[:, 0]
    fresh_total = fresh_total[:, 0]
    best = jnp.maximum(cached_top, fresh_top)
    cached_part = jnp.exp2((cached_top - best) * scale2)
    fresh_part = jnp.exp2((fresh_top - best) * scale2)
    total = cached_total * cached_part + fresh_total * fresh_part
    attended = (
        cached_sum * (cached_part / total)[..., None] + fresh_sum * (fresh_part / total)[..., None]
    ).astype(jnp.bfloat16)
    attended = jnp.transpose(attended, (1, 0, 2)).reshape(tok_dev, head_count * head_dim)

    projected = jnp.dot(attended, weight, preferred_element_type=jnp.float32)
    summed = lax.psum_scatter(
        projected.astype(jnp.bfloat16), "heads", scatter_dimension=1, tiled=True
    ).astype(jnp.float32)
    hidden = (summed + out_bias[None, :]).astype(jnp.bfloat16)

    page_shape = (requests * new_pages, PAGE, head_count, head_dim)
    key_out, value_out = write_pages(
        key_cache,
        value_cache,
        all_k.reshape(page_shape),
        all_v.reshape(page_shape),
        is_fresh,
        fresh_index,
    )
    return (hidden, key_out, value_out)


def solution(mesh):
    placed = (
        P("pages", "heads", None),
        P("pages", "heads", None),
        P("pages", "heads", None),
        P("pages", None, "heads", None),
        P("pages", None, "heads", None),
        P(),
        P(),
        P(),
        P("heads", "pages"),
        P("heads"),
    )
    return jax.shard_map(
        per_device,
        mesh=mesh,
        in_specs=placed,
        out_specs=(
            P("pages", "heads"),
            P("pages", None, "heads", None),
            P("pages", None, "heads", None),
        ),
        check_vma=False,
    )
```

```python
import functools
import math

import jax
import jax.numpy as jnp
from jax import lax
from jax.experimental import pallas as pl
from jax.experimental.layout import Layout, with_layout_constraint
from jax.experimental.pallas import tpu as pltpu
from jax.sharding import PartitionSpec as P

ROT = 32
PAGE = 128
QTILE = 256

low_score = -(2.0**99)


def rotate(vectors, positions):
    half_rot = ROT // 2
    inv_freq = 10000.0 ** (-2.0 * jnp.arange(half_rot, dtype=jnp.float32) / ROT)
    angles = positions[:, None] * inv_freq[None, :]
    cosine = jnp.cos(angles)[:, None, :]
    sine = jnp.sin(angles)[:, None, :]
    first_half = vectors[..., :half_rot]
    second_half = vectors[..., half_rot:ROT]
    return jnp.concatenate(
        [
            first_half * cosine - second_half * sine,
            second_half * cosine + first_half * sine,
            vectors[..., ROT:],
        ],
        axis=-1,
    )


def stat_rows_of(part_len, unit):
    per_unit = -(-unit // 128)
    units = part_len // unit
    return per_unit, units, -(-3 * units * per_unit // 16) * 16


def stat_rows(row):
    unit = row.shape[1]
    full = -(-unit // 128) * 128
    if full > unit:
        row = jnp.concatenate([row, jnp.zeros((1, full - unit), row.dtype)], axis=1)
    return [row[:, at : at + 128] for at in range(0, full, 128)]


def stat_block(kinds, pad_to):
    rows = [piece for kind in kinds for row in kind for piece in stat_rows(row)]
    rows.append(jnp.zeros((pad_to - len(rows), 128), jnp.float32))
    return jnp.concatenate(rows, axis=0).astype(jnp.bfloat16)


def cached_kernel(unit, span, scale2, places, at_ref, ok_ref, order_ref, start_ref, count_ref,
                  *refs):
    q_refs, (k_ref, v_ref), refs = refs[:places], refs[places : places + 2], refs[places + 2 :]
    o_refs, (q_all, o_all, s_all, q_scr, m_scr, l_scr, acc_scr) = refs[:-7], refs[-7:]
    requests = count_ref.shape[0]
    chips, part_len, _ = q_all.shape
    per_part = part_len // unit
    per_request = span // unit
    per_unit, _, pad_to = stat_rows_of(part_len, unit)

    for index in range(places):

        @pl.when(ok_ref[index] > 0)
        def _(index=index):
            q_all[at_ref[index]] = q_refs[index][0]

    def place(request, index):
        at = request * per_request + index
        return at // per_part, at % per_part

    def one_request(request, _):
        for index in range(per_request):
            part, piece = place(request, index)
            row = pl.ds(pl.multiple_of(piece * unit, unit), unit)
            q_scr[index * unit : (index + 1) * unit, :] = q_all[part, row, :]
        first = start_ref[request]
        count = count_ref[request]
        m_scr[...] = jnp.full((1, span), low_score, jnp.float32)
        l_scr[...] = jnp.zeros((1, span), jnp.float32)
        acc_scr[...] = jnp.zeros(acc_scr.shape, jnp.float32)

        def pages(slots):
            k = jnp.concatenate([k_ref[0, s] for s in slots], axis=0)
            v = jnp.concatenate([v_ref[0, s] for s in slots], axis=1)
            for c in range(0, span, QTILE):
                cols = slice(c, c + QTILE)
                scores = lax.dot_general(
                    k, q_scr[cols, :], (((1,), (1,)), ((), ())),
                    preferred_element_type=jnp.float32,
                )
                before = m_scr[:, cols]
                peak = jnp.maximum(before, jnp.max(scores, axis=0, keepdims=True))
                weights = jnp.exp2((scores - peak) * scale2)
                fade = jnp.exp2((before - peak) * scale2)
                m_scr[:, cols] = peak
                l_scr[:, cols] = l_scr[:, cols] * fade + jnp.sum(weights, axis=0, keepdims=True)
                acc_scr[:, cols] = acc_scr[:, cols] * fade + jnp.dot(
                    v, weights.astype(jnp.bfloat16), preferred_element_type=jnp.float32
                )

        def pair(index, _):
            at = first + 2 * index
            pages([order_ref[at], order_ref[at + 1]])
            return 0

        lax.fori_loop(0, count // 2, pair, 0)

        @pl.when(count % 2 == 1)
        def _():
            pages([order_ref[first + count - 1]])

        totals = l_scr[...]
        peaks = m_scr[...]
        out = (acc_scr[...] / jnp.maximum(totals, 1e-30)).T.astype(jnp.bfloat16)
        sent = peaks.astype(jnp.bfloat16).astype(jnp.float32)
        totals = totals * jnp.exp2((peaks - sent) * scale2)
        high = totals.astype(jnp.bfloat16).astype(jnp.float32)
        kinds = [sent, high, totals - high]
        for index in range(per_request):
            part, piece = place(request, index)
            cols = slice(index * unit, (index + 1) * unit)
            row = pl.ds(pl.multiple_of(piece * unit, unit), unit)
            o_all[part, row, :] = out[cols, :]
            for kind, values in enumerate(kinds):
                for r, line in enumerate(stat_rows(values[:, cols])):
                    at = (kind * per_part + piece) * per_unit + r
                    s_all[part, pl.ds(at, 1), :] = line
        return 0

    lax.fori_loop(0, requests, one_request, 0)
    for index in range(chips):
        part = at_ref[places + index]
        o_refs[index][0, :part_len, :] = o_all[part]
        o_refs[index][0, part_len:, :] = s_all[part].astype(jnp.bfloat16)


def cached_attention(q_places, at, ok, out_at, k_heads, v_heads, order, starts, counts, span,
                     scale2):
    places = len(q_places)
    chips = len(out_at)
    heads, part_len, head_dim = q_places[0].shape
    slots = k_heads.shape[1]
    unit = math.gcd(span, part_len)
    _, _, pad_to = stat_rows_of(part_len, unit)
    own_block = lambda *dims: pl.BlockSpec(
        (1,) + dims, lambda h, *_: (h,) + (0,) * len(dims)
    )
    return pl.pallas_call(
        lambda *refs: cached_kernel(unit, span, scale2, places, *refs),
        grid_spec=pltpu.PrefetchScalarGridSpec(
            num_scalar_prefetch=5,
            grid=(heads,),
            in_specs=[own_block(part_len, head_dim)] * places
            + [own_block(slots, PAGE, head_dim), own_block(slots, head_dim, PAGE)],
            out_specs=[own_block(part_len + pad_to, head_dim)] * chips,
            scratch_shapes=[
                pltpu.VMEM((chips, part_len, head_dim), jnp.bfloat16),
                pltpu.VMEM((chips, part_len, head_dim), jnp.bfloat16),
                pltpu.VMEM((chips, pad_to, 128), jnp.float32),
                pltpu.VMEM((span, head_dim), jnp.bfloat16),
                pltpu.VMEM((1, span), jnp.float32),
                pltpu.VMEM((1, span), jnp.float32),
                pltpu.VMEM((head_dim, span), jnp.float32),
            ],
        ),
        out_shape=[
            jax.ShapeDtypeStruct((heads, part_len + pad_to, head_dim), jnp.bfloat16)
        ] * chips,
        compiler_params=pltpu.CompilerParams(vmem_limit_bytes=40 * 2**20),
        name="cached_attention",
    )(jnp.stack(at + out_at), jnp.stack(ok), order, starts, counts, *q_places, k_heads, v_heads)


def merge_kernel(unit, part_len, scale2, ok_ref, *refs):
    in_refs, out_ref = refs[:-1], refs[-1]
    head_dim = out_ref.shape[2]
    per_unit, units, pad_to = stat_rows_of(part_len, unit)
    stats = [ref[0, part_len:, :].astype(jnp.float32) for ref in in_refs]
    kinds = [[], [], []]
    for u in range(units):

        def line(stat, kind):
            at = (kind * units + u) * per_unit
            pieces = [stat[at + r : at + r + 1, :] for r in range(per_unit)]
            return jnp.concatenate(pieces, axis=1)

        peaks, totals = [], []
        for index, stat in enumerate(stats):
            ok = ok_ref[index] > 0
            peaks.append(jnp.where(ok, line(stat, 0), low_score))
            totals.append(jnp.where(ok, line(stat, 1) + line(stat, 2), 0.0))
        top = functools.reduce(jnp.maximum, peaks)
        shares = [t * jnp.exp2((p - top) * scale2) for t, p in zip(totals, peaks)]
        total = functools.reduce(jnp.add, shares)
        inverse = 1.0 / jnp.maximum(total, 1e-30)
        rows = slice(u * unit, (u + 1) * unit)
        merged = None
        for ref, share in zip(in_refs, shares):
            part = jnp.broadcast_to(share * inverse, (head_dim, share.shape[1])).T[:unit]
            part = part * ref[0, rows, :].astype(jnp.float32)
            merged = part if merged is None else merged + part
        out_ref[0, rows, :] = merged.astype(jnp.bfloat16)
        high = total.astype(jnp.bfloat16).astype(jnp.float32)
        for kind, value in zip(kinds, (top, high, total - high)):
            kind.append(value)
    out_ref[0, part_len:, :] = stat_block(kinds, pad_to)


def merge(parts, ok, part_len, unit, scale2):
    block = pl.BlockSpec((1,) + parts[0].shape[1:], lambda h, *_: (h, 0, 0))
    return pl.pallas_call(
        lambda *refs: merge_kernel(unit, part_len, scale2, *refs),
        grid_spec=pltpu.PrefetchScalarGridSpec(
            num_scalar_prefetch=1,
            grid=(parts[0].shape[0],),
            in_specs=[block] * len(parts),
            out_specs=block,
        ),
        out_shape=jax.ShapeDtypeStruct(parts[0].shape, jnp.bfloat16),
        name="merge",
    )(jnp.stack(ok).astype(jnp.int32), *parts)


def page_kernel(fresh_ref, index_ref, kc_ref, vc_ref, kn_ref, vn_ref, ko_ref, vo_ref):
    fresh = fresh_ref[pl.program_id(0)] > 0

    @pl.when(fresh)
    def _():
        ko_ref[...] = kn_ref[...]
        vo_ref[...] = vn_ref[...]

    @pl.when(jnp.logical_not(fresh))
    def _():
        ko_ref[...] = kc_ref[...]
        vo_ref[...] = vc_ref[...]


def write_pages(key_cache, value_cache, new_keys, new_values, is_fresh, fresh_index):
    block = (1,) + key_cache.shape[1:]
    own = pl.BlockSpec(block, lambda s, fresh, index: (s, 0, 0, 0))
    new = pl.BlockSpec(block, lambda s, fresh, index: (index[s], 0, 0, 0))
    return pl.pallas_call(
        page_kernel,
        grid_spec=pltpu.PrefetchScalarGridSpec(
            num_scalar_prefetch=2,
            grid=(key_cache.shape[0],),
            in_specs=[own, own, new, new],
            out_specs=[own, own],
        ),
        out_shape=[jax.ShapeDtypeStruct(key_cache.shape, key_cache.dtype)] * 2,
        compiler_params=pltpu.CompilerParams(vmem_limit_bytes=40 * 2**20),
        name="write_pages",
    )(is_fresh.astype(jnp.int32), fresh_index, key_cache, value_cache, new_keys, new_values)


def swap(x, bit):
    devs = lax.axis_size("pages")
    return lax.ppermute(x, "pages", [(p, p ^ bit) for p in range(devs)])


def shift(x, hop, senders):
    devs = lax.axis_size("pages")
    moves = [(p, p + 4 * hop) for p in range(devs) if p // 4 in senders]
    return lax.ppermute(x, "pages", moves)


def gather_lines(x):
    line = lax.axis_size("pages") // 4
    device_at = lax.axis_index("pages")
    at, across = device_at // 4, (device_at // 2) % 2
    always = jnp.int32(1)
    held = [(x, at, across, always), (swap(x, 2), at, 1 - across, always)]
    up = down = x
    for t in range(1, line):
        up = shift(up, 1, range(t - 1, line - 1))
        down = shift(down, -1, range(1, line - t + 1))
        has_up = (at >= t).astype(jnp.int32)
        has_down = (at + t < line).astype(jnp.int32)
        devs = lax.axis_size("pages")
        cross_up = [(p, p ^ 2) for p in range(devs) if p // 4 >= t]
        cross_down = [(p, p ^ 2) for p in range(devs) if p // 4 + t < line]
        held += [
            (up, at - t, across, has_up),
            (lax.ppermute(up, "pages", cross_up), at - t, 1 - across, has_up),
            (down, at + t, across, has_down),
            (lax.ppermute(down, "pages", cross_down), at + t, 1 - across, has_down),
        ]
    return held


def merge_lines(parts, merged):
    line = lax.axis_size("pages") // 4
    at = lax.axis_index("pages") // 4
    turns = []
    for t in range(1, line):
        turns += [k for k in (line - t, t) if k not in turns]
    yes = jnp.int32(1)
    crossed = {k: swap(parts[k][1], 2) for k in turns + [0]}
    shares = {}

    def share(k):
        if k not in shares:
            shares[k] = merged([parts[k][0], crossed[k]], [yes, yes])
        return shares[k]

    up = down = None
    for t in range(1, line):
        up_out, down_out = share(line - t), share(t)
        if up is not None:
            up_out = merged([up_out, up], [yes, (at >= 1) & (at <= t - 1)])
            down_out = merged([down_out, down], [yes, (at <= line - 2) & (at >= line - t)])
        up = shift(up_out, 1, range(0, t))
        down = shift(down_out, -1, range(line - t, line))
    return merged([share(0), up, down], [yes, at >= 1, at <= line - 2])


def fresh_kernel(scale2, q_ref, k_ref, v_ref, tok_ref, key_ref, o_ref, m_ref, l_ref):
    scores = lax.dot_general(
        k_ref[0], q_ref[0], (((1,), (1,)), ((), ())), preferred_element_type=jnp.float32
    )
    token = tok_ref[0:1, :]
    first = tok_ref[1:2, :]
    key = key_ref[:, 0:1]
    visible = (key <= token) & (key >= first)
    scores = jnp.where(visible, scores, low_score)
    peak = jnp.max(scores, axis=0, keepdims=True)
    weights = jnp.where(visible, jnp.exp2((scores - peak) * scale2), 0.0)
    m_ref[0] = peak
    l_ref[0] = jnp.sum(weights, axis=0, keepdims=True)
    o_ref[0] = jnp.dot(
        v_ref[0], weights.astype(jnp.bfloat16), preferred_element_type=jnp.float32
    )


def fresh_attention(q_own, k_window, v_window, token_rows, key_cols, scale2):
    heads, tok_dev, head_dim = q_own.shape
    window = k_window.shape[1]
    own = lambda h: (h, 0, 0)
    fixed = lambda h: (0, 0)
    return pl.pallas_call(
        lambda *refs: fresh_kernel(scale2, *refs),
        grid=(heads,),
        in_specs=[
            pl.BlockSpec((1, tok_dev, head_dim), own),
            pl.BlockSpec((1, window, head_dim), own),
            pl.BlockSpec((1, head_dim, window), own),
            pl.BlockSpec(token_rows.shape, fixed),
            pl.BlockSpec(key_cols.shape, fixed),
        ],
        out_specs=[
            pl.BlockSpec((1, head_dim, tok_dev), own),
            pl.BlockSpec((1, 1, tok_dev), own),
            pl.BlockSpec((1, 1, tok_dev), own),
        ],
        out_shape=[
            jax.ShapeDtypeStruct((heads, head_dim, tok_dev), jnp.float32),
            jax.ShapeDtypeStruct((heads, 1, tok_dev), jnp.float32),
            jax.ShapeDtypeStruct((heads, 1, tok_dev), jnp.float32),
        ],
        compiler_params=pltpu.CompilerParams(vmem_limit_bytes=40 * 2**20),
        name="fresh_attention",
    )(q_own, k_window, v_window, token_rows, key_cols)


def per_device(
    queries,
    keys,
    values,
    key_cache,
    value_cache,
    cache_len,
    page_table,
    append_slots,
    out_weight,
    out_bias,
):
    tok_dev, head_count, head_dim = queries.shape
    requests = cache_len.shape[0]
    max_pages = page_table.shape[1]
    new_pages = append_slots.shape[1]
    span_len = new_pages * PAGE
    slot_count = key_cache.shape[0]
    tokens = requests * span_len
    page_devs = tokens // tok_dev
    scale2 = math.log2(math.e) / math.sqrt(head_dim)
    device_at = lax.axis_index("pages")
    token_ids = device_at * tok_dev + jnp.arange(tok_dev, dtype=jnp.int32)
    request_ids = token_ids // span_len
    request_grid = jnp.arange(requests, dtype=jnp.int32)
    starts = jnp.sum(
        jnp.where(request_ids[:, None] == request_grid[None, :], cache_len[None, :], 0), axis=1
    )
    positions = (starts + token_ids % span_len).astype(jnp.float32)
    rotated_q = rotate(queries.astype(jnp.float32), positions).astype(jnp.bfloat16)
    rotated_k = rotate(keys.astype(jnp.float32), positions).astype(jnp.bfloat16)
    core = device_at % 2
    half = head_count // 2
    chip_len = 2 * tok_dev

    def halves(x):
        return (
            lax.dynamic_slice_in_dim(x, core * half, half, 0),
            lax.dynamic_slice_in_dim(x, (1 - core) * half, half, 0),
        )

    def in_order(mine, got, axis):
        return jnp.where(
            core == 0,
            jnp.concatenate([mine, got], axis=axis),
            jnp.concatenate([got, mine], axis=axis),
        )

    q_own = jnp.transpose(rotated_q, (1, 0, 2))
    q_mine, q_other = halves(q_own)
    q_places = gather_lines(in_order(q_mine, swap(q_other, 1), 1))
    all_k = lax.all_gather(rotated_k, "pages", axis=0, tiled=True)
    all_v = lax.all_gather(values, "pages", axis=0, tiled=True)
    natural = Layout((0, 1, 2))
    all_k = with_layout_constraint(all_k, natural)
    all_v = with_layout_constraint(all_v, natural)
    weight = lax.all_gather(out_weight, "pages", axis=1, tiled=True)

    my_slots = device_at * slot_count + jnp.arange(slot_count, dtype=jnp.int32)
    chip_slots = jnp.concatenate(
        [my_slots, (device_at ^ 1) * slot_count + jnp.arange(slot_count, dtype=jnp.int32)]
    )
    cached_hit = page_table.reshape(-1)[None, :] == chip_slots[:, None]
    fresh_hit = append_slots.reshape(-1)[None, :] == my_slots[:, None]
    table_at = jnp.arange(requests * max_pages, dtype=jnp.int32)
    shown = (table_at % max_pages) * PAGE < jnp.repeat(cache_len, max_pages)
    is_fresh = jnp.any(fresh_hit, axis=1)
    fresh_index = jnp.sum(
        jnp.where(fresh_hit, jnp.arange(requests * new_pages, dtype=jnp.int32)[None, :], 0), axis=1
    )
    slot_key = requests - jnp.sum(
        jnp.where(cached_hit & shown[None, :], requests - (table_at // max_pages)[None, :], 0),
        axis=1,
    )
    slot_at = jnp.arange(2 * slot_count, dtype=jnp.int32)
    earlier = (slot_key[None, :] < slot_key[:, None]) | (
        (slot_key[None, :] == slot_key[:, None]) & (slot_at[None, :] < slot_at[:, None])
    )
    rank = jnp.sum(earlier.astype(jnp.int32), axis=1)
    order = jnp.sum(jnp.where(rank[None, :] == slot_at[:, None], slot_at[None, :], 0), axis=1)
    slot_starts = jnp.sum((slot_key[None, :] < request_grid[:, None]).astype(jnp.int32), axis=1)
    slot_counts = jnp.sum((slot_key[None, :] == request_grid[:, None]).astype(jnp.int32), axis=1)

    k_mine, k_other = halves(jnp.transpose(key_cache, (2, 0, 1, 3)))
    v_mine, v_other = halves(jnp.transpose(value_cache, (2, 0, 3, 1)))
    k_heads = jnp.concatenate([k_mine, swap(k_other, 1)], axis=1)
    v_heads = jnp.concatenate([v_mine, swap(v_other, 1)], axis=1)

    line = page_devs // 4
    line_at, across = device_at // 4, (device_at // 2) % 2
    outs = cached_attention(
        [q for q, _, _, _ in q_places],
        [jnp.clip(at, 0, line - 1) * 2 + side for _, at, side, _ in q_places],
        [ok for _, _, _, ok in q_places],
        [((line_at + k) % line) * 2 + (across ^ d) for k in range(line) for d in range(2)],
        k_heads,
        v_heads,
        order,
        slot_starts,
        slot_counts,
        span_len,
        scale2,
    )
    unit = math.gcd(span_len, chip_len)
    merged = lambda parts, ok: merge(parts, ok, chip_len, unit, scale2)
    chip_part = merge_lines([outs[2 * k : 2 * k + 2] for k in range(line)], merged)
    other_part = swap(chip_part, 1)
    per_unit, units, _ = stat_rows_of(chip_len, unit)

    def own_tokens(part):
        rows = lax.dynamic_slice_in_dim(part[:, :chip_len], core * tok_dev, tok_dev, 1)
        stats = part[:, chip_len : chip_len + 3 * units * per_unit].astype(jnp.float32)
        stats = stats.reshape(half, 3, units, per_unit * 128)[..., :unit]
        stats = stats.reshape(half, 3, chip_len)
        stats = lax.dynamic_slice_in_dim(stats, core * tok_dev, tok_dev, 2)
        return rows.astype(jnp.float32), stats[:, 0], stats[:, 1] + stats[:, 2]

    cached_mean, cached_top, cached_total = [
        in_order(mine, got, 0)
        for mine, got in zip(own_tokens(chip_part), own_tokens(other_part))
    ]

    window_at = jnp.minimum(request_ids[0], requests - 2) * span_len
    k_window = lax.dynamic_slice_in_dim(all_k, window_at, 2 * span_len, 0)
    v_window = lax.dynamic_slice_in_dim(all_v, window_at, 2 * span_len, 0)
    token_rows = jnp.stack([token_ids, request_ids * span_len])
    key_cols = (window_at + jnp.arange(2 * span_len, dtype=jnp.int32))[:, None]
    fresh_sum, fresh_top, fresh_total = fresh_attention(
        q_own,
        jnp.transpose(k_window, (1, 0, 2)),
        jnp.transpose(v_window, (1, 2, 0)),
        token_rows,
        key_cols,
        scale2,
    )
    fresh_sum = jnp.transpose(fresh_sum, (0, 2, 1))
    fresh_top = fresh_top[:, 0]
    fresh_total = fresh_total[:, 0]
    best = jnp.maximum(cached_top, fresh_top)
    cached_part = cached_total * jnp.exp2((cached_top - best) * scale2)
    fresh_part = jnp.exp2((fresh_top - best) * scale2)
    total = cached_part + fresh_total * fresh_part
    attended = (
        cached_mean * (cached_part / total)[..., None] + fresh_sum * (fresh_part / total)[..., None]
    ).astype(jnp.bfloat16)
    attended = jnp.transpose(attended, (1, 0, 2)).reshape(tok_dev, head_count * head_dim)

    projected = jnp.dot(attended, weight, preferred_element_type=jnp.float32)
    summed = lax.psum_scatter(
        projected.astype(jnp.bfloat16), "heads", scatter_dimension=1, tiled=True
    ).astype(jnp.float32)
    hidden = (summed + out_bias[None, :]).astype(jnp.bfloat16)

    page_shape = (requests * new_pages, PAGE, head_count, head_dim)
    key_out, value_out = write_pages(
        key_cache,
        value_cache,
        all_k.reshape(page_shape),
        all_v.reshape(page_shape),
        is_fresh,
        fresh_index,
    )
    return (hidden, key_out, value_out)


def solution(mesh):
    placed = (
        P("pages", "heads", None),
        P("pages", "heads", None),
        P("pages", "heads", None),
        P("pages", None, "heads", None),
        P("pages", None, "heads", None),
        P(),
        P(),
        P(),
        P("heads", "pages"),
        P("heads"),
    )
    return jax.shard_map(
        per_device,
        mesh=mesh,
        in_specs=placed,
        out_specs=(
            P("pages", "heads"),
            P("pages", None, "heads", None),
            P("pages", None, "heads", None),
        ),
        check_vma=False,
    )
```

```python
import functools
import math

import jax
import jax.numpy as jnp
from jax import lax
from jax.experimental import pallas as pl
from jax.experimental.pallas import tpu as pltpu
from jax.sharding import PartitionSpec as P

ROT = 32
PAGE = 128
QTILE = 256

low_score = -(2.0**99)


def rotate(vectors, positions):
    half_rot = ROT // 2
    inv_freq = 10000.0 ** (-2.0 * jnp.arange(half_rot, dtype=jnp.float32) / ROT)
    angles = positions[:, None] * inv_freq[None, :]
    cosine = jnp.cos(angles)[:, None, :]
    sine = jnp.sin(angles)[:, None, :]
    first_half = vectors[..., :half_rot]
    second_half = vectors[..., half_rot:ROT]
    return jnp.concatenate(
        [
            first_half * cosine - second_half * sine,
            second_half * cosine + first_half * sine,
            vectors[..., ROT:],
        ],
        axis=-1,
    )


def stat_rows_of(part_len, unit):
    per_unit = -(-unit // 128)
    units = part_len // unit
    return per_unit, units, -(-3 * units * per_unit // 16) * 16


def stat_rows(row):
    unit = row.shape[1]
    full = -(-unit // 128) * 128
    if full > unit:
        row = jnp.concatenate([row, jnp.zeros((1, full - unit), row.dtype)], axis=1)
    return [row[:, at : at + 128] for at in range(0, full, 128)]


def stat_block(kinds, pad_to):
    rows = [piece for kind in kinds for row in kind for piece in stat_rows(row)]
    rows.append(jnp.zeros((pad_to - len(rows), 128), jnp.float32))
    return jnp.concatenate(rows, axis=0).astype(jnp.bfloat16)


def cached_kernel(unit, stat_unit, span, scale2, places, at_ref, ok_ref, order_ref, start_ref, count_ref,
                  *refs):
    q_refs, (k_ref, v_ref), refs = refs[:places], refs[places : places + 2], refs[places + 2 :]
    o_refs, (q_all, o_all, s_all, q_scr, m_scr, l_scr, acc_scr) = refs[:-7], refs[-7:]
    requests = count_ref.shape[0]
    chips, part_len, _ = q_all.shape
    per_part = part_len // unit
    per_request = span // unit
    per_unit, units, pad_to = stat_rows_of(part_len, stat_unit)

    for index in range(places):

        @pl.when(ok_ref[index] > 0)
        def _(index=index):
            q_all[at_ref[index]] = q_refs[index][0]

    def place(at, per_part):
        return at // per_part, at % per_part

    def one_request(request, _):
        for index in range(per_request):
            part, piece = place(request * per_request + index, per_part)
            row = pl.ds(pl.multiple_of(piece * unit, unit), unit)
            q_scr[index * unit : (index + 1) * unit, :] = q_all[part, row, :]
        first = start_ref[request]
        count = count_ref[request]
        m_scr[...] = jnp.full((1, span), low_score, jnp.float32)
        l_scr[...] = jnp.zeros((1, span), jnp.float32)
        acc_scr[...] = jnp.zeros(acc_scr.shape, jnp.float32)

        def pages(slots):
            k = jnp.concatenate([k_ref[0, s] for s in slots], axis=0)
            v = jnp.concatenate([v_ref[0, s] for s in slots], axis=1)
            for c in range(0, span, QTILE):
                cols = slice(c, c + QTILE)
                scores = lax.dot_general(
                    k, q_scr[cols, :], (((1,), (1,)), ((), ())),
                    preferred_element_type=jnp.float32,
                )
                before = m_scr[:, cols]
                peak = jnp.maximum(before, jnp.max(scores, axis=0, keepdims=True))
                weights = jnp.exp2((scores - peak) * scale2)
                fade = jnp.exp2((before - peak) * scale2)
                m_scr[:, cols] = peak
                l_scr[:, cols] = l_scr[:, cols] * fade + jnp.sum(weights, axis=0, keepdims=True)
                acc_scr[:, cols] = acc_scr[:, cols] * fade + jnp.dot(
                    v, weights.astype(jnp.bfloat16), preferred_element_type=jnp.float32
                )

        def pair(index, _):
            at = first + 2 * index
            pages([order_ref[at], order_ref[at + 1]])
            return 0

        lax.fori_loop(0, count // 2, pair, 0)

        @pl.when(count % 2 == 1)
        def _():
            pages([order_ref[first + count - 1]])

        totals = l_scr[...]
        peaks = m_scr[...]
        out = (acc_scr[...] / jnp.maximum(totals, 1e-30)).T.astype(jnp.bfloat16)
        sent = peaks.astype(jnp.bfloat16).astype(jnp.float32)
        totals = totals * jnp.exp2((peaks - sent) * scale2)
        high = totals.astype(jnp.bfloat16).astype(jnp.float32)
        kinds = [sent, high, totals - high]
        for index in range(per_request):
            part, piece = place(request * per_request + index, per_part)
            row = pl.ds(pl.multiple_of(piece * unit, unit), unit)
            o_all[part, row, :] = out[index * unit : (index + 1) * unit, :]
        for index in range(span // stat_unit):
            part, piece = place(request * (span // stat_unit) + index, units)
            cols = slice(index * stat_unit, (index + 1) * stat_unit)
            for kind, values in enumerate(kinds):
                for r, line in enumerate(stat_rows(values[:, cols])):
                    at = (kind * units + piece) * per_unit + r
                    s_all[part, pl.ds(at, 1), :] = line
        return 0

    lax.fori_loop(0, requests, one_request, 0)
    for index in range(chips):
        part = at_ref[places + index]
        o_refs[index][0, :part_len, :] = o_all[part]
        o_refs[index][0, part_len:, :] = s_all[part].astype(jnp.bfloat16)


def cached_attention(q_places, at, ok, out_at, k_heads, v_heads, order, starts, counts, span,
                     stat_unit, scale2):
    places = len(q_places)
    chips = len(out_at)
    heads, part_len, head_dim = q_places[0].shape
    slots = k_heads.shape[1]
    unit = math.gcd(span, part_len)
    _, _, pad_to = stat_rows_of(part_len, stat_unit)
    own_block = lambda *dims: pl.BlockSpec(
        (1,) + dims, lambda h, *_: (h,) + (0,) * len(dims)
    )
    return pl.pallas_call(
        lambda *refs: cached_kernel(unit, stat_unit, span, scale2, places, *refs),
        grid_spec=pltpu.PrefetchScalarGridSpec(
            num_scalar_prefetch=5,
            grid=(heads,),
            in_specs=[own_block(part_len, head_dim)] * places
            + [own_block(slots, PAGE, head_dim), own_block(slots, head_dim, PAGE)],
            out_specs=[own_block(part_len + pad_to, head_dim)] * chips,
            scratch_shapes=[
                pltpu.VMEM((chips, part_len, head_dim), jnp.bfloat16),
                pltpu.VMEM((chips, part_len, head_dim), jnp.bfloat16),
                pltpu.VMEM((chips, pad_to, 128), jnp.float32),
                pltpu.VMEM((span, head_dim), jnp.bfloat16),
                pltpu.VMEM((1, span), jnp.float32),
                pltpu.VMEM((1, span), jnp.float32),
                pltpu.VMEM((head_dim, span), jnp.float32),
            ],
        ),
        out_shape=[
            jax.ShapeDtypeStruct((heads, part_len + pad_to, head_dim), jnp.bfloat16)
        ] * chips,
        compiler_params=pltpu.CompilerParams(vmem_limit_bytes=40 * 2**20),
        name="cached_attention",
    )(jnp.stack(at + out_at), jnp.stack(ok), order, starts, counts, *q_places, k_heads, v_heads)


def spread(row, width, unit):
    return jnp.broadcast_to(row, (width, row.shape[1])).T[:unit]


def merge_kernel(unit, part_len, scale2, ok_ref, *refs):
    in_refs, out_ref = refs[:-1], refs[-1]
    head_dim = out_ref.shape[2]
    per_unit, units, pad_to = stat_rows_of(part_len, unit)
    stats = [ref[0, part_len:, :].astype(jnp.float32) for ref in in_refs]
    rows = [ref[0, :part_len, :].astype(jnp.float32) for ref in in_refs]
    outs = []
    kinds = [[], [], []]
    for u in range(units):

        def line(stat, kind):
            at = (kind * units + u) * per_unit
            pieces = [stat[at + r : at + r + 1, :] for r in range(per_unit)]
            return jnp.concatenate(pieces, axis=1)

        peaks, totals = [], []
        for index, stat in enumerate(stats):
            ok = ok_ref[index] > 0
            peaks.append(jnp.where(ok, line(stat, 0), low_score))
            totals.append(jnp.where(ok, line(stat, 1) + line(stat, 2), 0.0))
        top = functools.reduce(jnp.maximum, peaks)
        shares = [t * jnp.exp2((p - top) * scale2) for t, p in zip(totals, peaks)]
        total = functools.reduce(jnp.add, shares)
        inverse = 1.0 / jnp.maximum(total, 1e-30)
        merged = None
        for values, share in zip(rows, shares):
            part = spread(share * inverse, head_dim, unit) * values[u * unit : (u + 1) * unit]
            merged = part if merged is None else merged + part
        outs.append(merged)
        high = total.astype(jnp.bfloat16).astype(jnp.float32)
        for kind, value in zip(kinds, (top, high, total - high)):
            kind.append(value)
    out_ref[0, :part_len, :] = jnp.concatenate(outs, axis=0).astype(jnp.bfloat16)
    out_ref[0, part_len:, :] = stat_block(kinds, pad_to)


def merge(parts, ok, part_len, unit, scale2):
    block = pl.BlockSpec((1,) + parts[0].shape[1:], lambda h, *_: (h, 0, 0))
    return pl.pallas_call(
        lambda *refs: merge_kernel(unit, part_len, scale2, *refs),
        grid_spec=pltpu.PrefetchScalarGridSpec(
            num_scalar_prefetch=1,
            grid=(parts[0].shape[0],),
            in_specs=[block] * len(parts),
            out_specs=block,
        ),
        out_shape=jax.ShapeDtypeStruct(parts[0].shape, jnp.bfloat16),
        name="merge",
    )(jnp.stack(ok).astype(jnp.int32), *parts)


def page_kernel(fresh_ref, index_ref, kc_ref, vc_ref, kn_ref, vn_ref, ko_ref, vo_ref):
    fresh = fresh_ref[pl.program_id(0)] > 0

    @pl.when(fresh)
    def _():
        ko_ref[...] = kn_ref[...]
        vo_ref[...] = vn_ref[...]

    @pl.when(jnp.logical_not(fresh))
    def _():
        ko_ref[...] = kc_ref[...]
        vo_ref[...] = vc_ref[...]


def write_pages(key_cache, value_cache, new_keys, new_values, is_fresh, fresh_index):
    block = (1,) + key_cache.shape[1:]
    own = pl.BlockSpec(block, lambda s, fresh, index: (s, 0, 0, 0))
    new = pl.BlockSpec(block, lambda s, fresh, index: (index[s], 0, 0, 0))
    return pl.pallas_call(
        page_kernel,
        grid_spec=pltpu.PrefetchScalarGridSpec(
            num_scalar_prefetch=2,
            grid=(key_cache.shape[0],),
            in_specs=[own, own, new, new],
            out_specs=[own, own],
        ),
        out_shape=[jax.ShapeDtypeStruct(key_cache.shape, key_cache.dtype)] * 2,
        compiler_params=pltpu.CompilerParams(vmem_limit_bytes=40 * 2**20),
        name="write_pages",
    )(is_fresh.astype(jnp.int32), fresh_index, key_cache, value_cache, new_keys, new_values)


def swap(x, bit):
    devs = lax.axis_size("pages")
    return lax.ppermute(x, "pages", [(p, p ^ bit) for p in range(devs)])


def shift(x, hop, senders):
    devs = lax.axis_size("pages")
    moves = [(p, p + 4 * hop) for p in range(devs) if p // 4 in senders]
    return lax.ppermute(x, "pages", moves)


def gather_line(x):
    line = lax.axis_size("pages") // 4
    groups = [[g + 4 * i for i in range(line)] for g in range(4)]
    return lax.all_gather(x, "pages", axis=0, tiled=False, axis_index_groups=groups)


def spread_across(here):
    across = swap(here, 2)
    return [here, swap(here, 1), across, swap(across, 1)]


def gather_lines(x):
    line = lax.axis_size("pages") // 4
    device_at = lax.axis_index("pages")
    at, across = device_at // 4, (device_at // 2) % 2
    always = jnp.int32(1)
    held = [(x, at, across, always), (swap(x, 2), at, 1 - across, always)]
    up = down = x
    for t in range(1, line):
        up = shift(up, 1, range(t - 1, line - 1))
        down = shift(down, -1, range(1, line - t + 1))
        has_up = (at >= t).astype(jnp.int32)
        has_down = (at + t < line).astype(jnp.int32)
        devs = lax.axis_size("pages")
        cross_up = [(p, p ^ 2) for p in range(devs) if p // 4 >= t]
        cross_down = [(p, p ^ 2) for p in range(devs) if p // 4 + t < line]
        held += [
            (up, at - t, across, has_up),
            (lax.ppermute(up, "pages", cross_up), at - t, 1 - across, has_up),
            (down, at + t, across, has_down),
            (lax.ppermute(down, "pages", cross_down), at + t, 1 - across, has_down),
        ]
    return held


def merge_lines(parts, merged):
    line = lax.axis_size("pages") // 4
    at = lax.axis_index("pages") // 4
    turns = []
    for t in range(1, line):
        turns += [k for k in (line - t, t) if k not in turns]
    yes = jnp.int32(1)
    crossed = {k: swap(parts[k][1], 2) for k in turns + [0]}
    shares = {}

    def share(k):
        if k not in shares:
            shares[k] = merged([parts[k][0], crossed[k]], [yes, yes])
        return shares[k]

    up = down = None
    for t in range(1, line):
        up_out, down_out = share(line - t), share(t)
        if up is not None:
            up_out = merged([up_out, up], [yes, (at >= 1) & (at <= t - 1)])
            down_out = merged([down_out, down], [yes, (at <= line - 2) & (at >= line - t)])
        up = shift(up_out, 1, range(0, t))
        down = shift(down_out, -1, range(line - t, line))
    return merged([share(0), up, down], [yes, at >= 1, at <= line - 2])


def fresh_kernel(unit, scale2, q_ref, k_ref, v_ref, tok_ref, key_ref, o_ref, s_ref):
    scores = lax.dot_general(
        k_ref[0], q_ref[0], (((1,), (1,)), ((), ())), preferred_element_type=jnp.float32
    )
    token = tok_ref[0:1, :]
    first = tok_ref[1:2, :]
    key = key_ref[:, 0:1]
    visible = (key <= token) & (key >= first)
    scores = jnp.where(visible, scores, low_score)
    peak = jnp.max(scores, axis=0, keepdims=True)
    weights = jnp.where(visible, jnp.exp2((scores - peak) * scale2), 0.0)
    out = jnp.dot(v_ref[0], weights.astype(jnp.bfloat16), preferred_element_type=jnp.float32)
    tok_dev = out.shape[1]
    pad = -tok_dev % 128
    out = jnp.concatenate([out, jnp.zeros((out.shape[0], pad), jnp.float32)], axis=1)
    o_ref[0] = out.T[:tok_dev]
    totals = jnp.sum(weights, axis=0, keepdims=True)
    lines = []
    for values in (peak, totals):
        for at in range(0, tok_dev, unit):
            lines += stat_rows(values[:, at : at + unit])
    lines.append(jnp.zeros((s_ref.shape[1] - len(lines), 128), jnp.float32))
    s_ref[0] = jnp.concatenate(lines, axis=0)


def fresh_attention(q_own, k_window, v_window, token_rows, key_cols, unit, scale2):
    heads, tok_dev, head_dim = q_own.shape
    window = k_window.shape[1]
    lines = -(-2 * (tok_dev // unit) * -(-unit // 128) // 8) * 8
    own = lambda h: (h, 0, 0)
    fixed = lambda h: (0, 0)
    return pl.pallas_call(
        lambda *refs: fresh_kernel(unit, scale2, *refs),
        grid=(heads,),
        in_specs=[
            pl.BlockSpec((1, tok_dev, head_dim), own),
            pl.BlockSpec((1, window, head_dim), own),
            pl.BlockSpec((1, head_dim, window), own),
            pl.BlockSpec(token_rows.shape, fixed),
            pl.BlockSpec(key_cols.shape, fixed),
        ],
        out_specs=[
            pl.BlockSpec((1, tok_dev, head_dim), own),
            pl.BlockSpec((1, lines, 128), own),
        ],
        out_shape=[
            jax.ShapeDtypeStruct((heads, tok_dev, head_dim), jnp.float32),
            jax.ShapeDtypeStruct((heads, lines, 128), jnp.float32),
        ],
        compiler_params=pltpu.CompilerParams(vmem_limit_bytes=40 * 2**20),
        name="fresh_attention",
    )(q_own, k_window, v_window, token_rows, key_cols)


def finish_kernel(unit, half, scale2, core_ref, mine_ref, other_ref, fo_ref, fs_ref, out_ref):
    core = core_ref[0]
    tok_dev, head_dim = out_ref.shape
    per_unit, units, _ = stat_rows_of(2 * tok_dev, unit)
    here = pl.program_id(0) // half == core
    part = jnp.where(
        here, mine_ref[0].astype(jnp.float32), other_ref[0].astype(jnp.float32)
    )
    rows = jnp.where(core == 0, part[:tok_dev], part[tok_dev : 2 * tok_dev])
    stats = part[2 * tok_dev :]
    fresh_stats = fs_ref[0]

    def line(block, at):
        pieces = [block[at + r : at + r + 1, :] for r in range(per_unit)]
        return jnp.concatenate(pieces, axis=1)

    def cached_line(kind, u):
        first = line(stats, (kind * units + u) * per_unit)
        return jnp.where(core == 0, first, line(stats, (kind * units + units // 2 + u) * per_unit))

    outs = []
    for u in range(units // 2):
        cached_top = cached_line(0, u)
        cached_total = cached_line(1, u) + cached_line(2, u)
        fresh_top = line(fresh_stats, u * per_unit)
        fresh_total = line(fresh_stats, (units // 2 + u) * per_unit)
        best = jnp.maximum(cached_top, fresh_top)
        cached_share = cached_total * jnp.exp2((cached_top - best) * scale2)
        fresh_share = jnp.exp2((fresh_top - best) * scale2)
        inverse = 1.0 / jnp.maximum(cached_share + fresh_total * fresh_share, 1e-30)
        at = slice(u * unit, (u + 1) * unit)
        outs.append(
            rows[at] * spread(cached_share * inverse, head_dim, unit)
            + fo_ref[0, at, :] * spread(fresh_share * inverse, head_dim, unit)
        )
    out_ref[...] = jnp.concatenate(outs, axis=0).astype(jnp.bfloat16)


def finish(core, mine, other, fresh_sum, fresh_stats, unit, scale2):
    half = mine.shape[0]
    heads, tok_dev, head_dim = fresh_sum.shape
    part = pl.BlockSpec((1,) + mine.shape[1:], lambda h, *_: (h % half, 0, 0))
    own = lambda x: pl.BlockSpec((1,) + x.shape[1:], lambda h, *_: (h, 0, 0))
    return pl.pallas_call(
        lambda *refs: finish_kernel(unit, half, scale2, *refs),
        grid_spec=pltpu.PrefetchScalarGridSpec(
            num_scalar_prefetch=1,
            grid=(heads,),
            in_specs=[part, part, own(fresh_sum), own(fresh_stats)],
            out_specs=pl.BlockSpec((tok_dev, head_dim), lambda h, *_: (0, h)),
        ),
        out_shape=jax.ShapeDtypeStruct((tok_dev, heads * head_dim), jnp.bfloat16),
        name="finish",
    )(core[None], mine, other, fresh_sum, fresh_stats)


def compose_kernel(at_ref, *refs):
    out_ref = refs[-1]
    for k, ref in enumerate(refs[:-1]):

        @pl.when(pl.program_id(1) == k)
        def _(ref=ref):
            out_ref[...] = ref[...]


def compose(arrays, side):
    line = arrays[0].shape[0]
    block = (1,) + arrays[0].shape[1:]
    zeros = (0,) * (len(block) - 1)
    out = pl.pallas_call(
        compose_kernel,
        grid_spec=pltpu.PrefetchScalarGridSpec(
            num_scalar_prefetch=1,
            grid=(line, 4),
            in_specs=[pl.BlockSpec(block, lambda z, k, at: (z,) + zeros)] * 4,
            out_specs=pl.BlockSpec(block, lambda z, k, at: (z * 4 + (k ^ at[0]),) + zeros),
        ),
        out_shape=jax.ShapeDtypeStruct((line * 4,) + block[1:], arrays[0].dtype),
        compiler_params=pltpu.CompilerParams(vmem_limit_bytes=40 * 2**20),
        name="compose",
    )(side[None], *arrays)
    return out.reshape((-1,) + block[2:])


def project_kernel(groups, at_ref, *refs):
    att_refs, w_refs, (bias_ref, out_ref) = refs[:groups], refs[groups:-2], refs[-2:]
    for k in range(4):

        @pl.when(pl.program_id(1) == k)
        def _(k=k):
            total = bias_ref[...].reshape(1, -1)
            for s in range(groups):
                total = total + jnp.dot(
                    att_refs[s][...],
                    w_refs[k * groups + s][0],
                    preferred_element_type=jnp.float32,
                )
            out_ref[...] = total.astype(jnp.bfloat16).reshape(out_ref.shape)


def project(attended, weights, bias, side, group_at):
    groups = len(attended)
    tok_dev = attended[0].shape[0]
    line, feats, cols = weights[0].shape
    share = line // groups
    blocks = share * 4
    wide = cols % 128 == 0
    place = lambda j, k, at: j * 4 + (k ^ at[0])

    def weight_spec(s):
        return pl.BlockSpec(
            (1, feats, cols),
            lambda j, k, at: (lax.rem(at[1] + groups - s, groups) * share + j, 0, 0),
        )

    if wide:
        out_spec = pl.BlockSpec((tok_dev, cols), lambda j, k, at: (0, place(j, k, at)))
        out_shape = (tok_dev, blocks * cols)
    else:
        out_spec = pl.BlockSpec((1, tok_dev, cols), lambda j, k, at: (place(j, k, at), 0, 0))
        out_shape = (blocks, tok_dev, cols)
    out = pl.pallas_call(
        lambda *refs: project_kernel(groups, *refs),
        grid_spec=pltpu.PrefetchScalarGridSpec(
            num_scalar_prefetch=1,
            grid=(share, 4),
            in_specs=[pl.BlockSpec(x.shape, lambda j, k, at: (0, 0)) for x in attended]
            + [weight_spec(s) for _ in range(4) for s in range(groups)]
            + [pl.BlockSpec((1, 1, cols), lambda j, k, at: (place(j, k, at), 0, 0))],
            out_specs=out_spec,
        ),
        out_shape=jax.ShapeDtypeStruct(out_shape, jnp.bfloat16),
        compiler_params=pltpu.CompilerParams(vmem_limit_bytes=40 * 2**20),
        name="project",
    )(
        jnp.stack([side, group_at]),
        *attended,
        *[w for w in weights for _ in range(groups)],
        bias.reshape(blocks, 1, cols),
    )
    return out if wide else jnp.transpose(out, (1, 0, 2)).reshape(tok_dev, blocks * cols)


def per_device(
    queries,
    keys,
    values,
    key_cache,
    value_cache,
    cache_len,
    page_table,
    append_slots,
    out_weight,
    out_bias,
):
    tok_dev, head_count, head_dim = queries.shape
    requests = cache_len.shape[0]
    max_pages = page_table.shape[1]
    new_pages = append_slots.shape[1]
    span_len = new_pages * PAGE
    slot_count = key_cache.shape[0]
    tokens = requests * span_len
    page_devs = tokens // tok_dev
    scale2 = math.log2(math.e) / math.sqrt(head_dim)
    device_at = lax.axis_index("pages")
    token_ids = device_at * tok_dev + jnp.arange(tok_dev, dtype=jnp.int32)
    request_ids = token_ids // span_len
    request_grid = jnp.arange(requests, dtype=jnp.int32)
    starts = jnp.sum(
        jnp.where(request_ids[:, None] == request_grid[None, :], cache_len[None, :], 0), axis=1
    )
    positions = (starts + token_ids % span_len).astype(jnp.float32)
    rotated_q = rotate(queries.astype(jnp.float32), positions).astype(jnp.bfloat16)
    rotated_k = rotate(keys.astype(jnp.float32), positions).astype(jnp.bfloat16)
    core = device_at % 2
    half = head_count // 2
    chip_len = 2 * tok_dev

    def halves(x):
        return (
            lax.dynamic_slice_in_dim(x, core * half, half, 0),
            lax.dynamic_slice_in_dim(x, (1 - core) * half, half, 0),
        )

    def in_order(mine, got, axis):
        return jnp.where(
            core == 0,
            jnp.concatenate([mine, got], axis=axis),
            jnp.concatenate([got, mine], axis=axis),
        )

    q_own = jnp.transpose(rotated_q, (1, 0, 2))
    q_mine, q_other = halves(q_own)
    q_places = gather_lines(in_order(q_mine, swap(q_other, 1), 1))
    groups = lax.axis_size("heads")
    group_at = lax.axis_index("heads")
    share = page_devs // groups
    moves = [
        (i * page_devs + h * share + j, h * page_devs + i * share + j)
        for i in range(groups)
        for h in range(groups)
        for j in range(share)
    ]
    weight_block = lax.ppermute(out_weight, ("heads", "pages"), moves)
    side = device_at % 4
    line_k, line_v, line_w = gather_line(rotated_k), gather_line(values), gather_line(weight_block)
    q_blocks, line_k = lax.optimization_barrier(([q for q, _, _, _ in q_places], line_k))
    all_k = compose(spread_across(line_k), side)
    all_v = compose(spread_across(line_v), side)
    weights = spread_across(line_w)

    my_slots = device_at * slot_count + jnp.arange(slot_count, dtype=jnp.int32)
    chip_slots = jnp.concatenate(
        [my_slots, (device_at ^ 1) * slot_count + jnp.arange(slot_count, dtype=jnp.int32)]
    )
    cached_hit = page_table.reshape(-1)[None, :] == chip_slots[:, None]
    fresh_hit = append_slots.reshape(-1)[None, :] == my_slots[:, None]
    table_at = jnp.arange(requests * max_pages, dtype=jnp.int32)
    shown = (table_at % max_pages) * PAGE < jnp.repeat(cache_len, max_pages)
    is_fresh = jnp.any(fresh_hit, axis=1)
    fresh_index = jnp.sum(
        jnp.where(fresh_hit, jnp.arange(requests * new_pages, dtype=jnp.int32)[None, :], 0), axis=1
    )
    slot_key = requests - jnp.sum(
        jnp.where(cached_hit & shown[None, :], requests - (table_at // max_pages)[None, :], 0),
        axis=1,
    )
    slot_at = jnp.arange(2 * slot_count, dtype=jnp.int32)
    earlier = (slot_key[None, :] < slot_key[:, None]) | (
        (slot_key[None, :] == slot_key[:, None]) & (slot_at[None, :] < slot_at[:, None])
    )
    rank = jnp.sum(earlier.astype(jnp.int32), axis=1)
    order = jnp.sum(jnp.where(rank[None, :] == slot_at[:, None], slot_at[None, :], 0), axis=1)
    slot_starts = jnp.sum((slot_key[None, :] < request_grid[:, None]).astype(jnp.int32), axis=1)
    slot_counts = jnp.sum((slot_key[None, :] == request_grid[:, None]).astype(jnp.int32), axis=1)

    k_mine, k_other = halves(jnp.transpose(key_cache, (2, 0, 1, 3)))
    v_mine, v_other = halves(jnp.transpose(value_cache, (2, 0, 3, 1)))
    k_heads = jnp.concatenate([k_mine, swap(k_other, 1)], axis=1)
    v_heads = jnp.concatenate([v_mine, swap(v_other, 1)], axis=1)

    unit = math.gcd(span_len, tok_dev)
    line = page_devs // 4
    line_at, across = device_at // 4, (device_at // 2) % 2
    outs = cached_attention(
        q_blocks,
        [jnp.clip(at, 0, line - 1) * 2 + side for _, at, side, _ in q_places],
        [ok for _, _, _, ok in q_places],
        [((line_at + k) % line) * 2 + (across ^ d) for k in range(line) for d in range(2)],
        k_heads,
        v_heads,
        order,
        slot_starts,
        slot_counts,
        span_len,
        unit,
        scale2,
    )
    merged = lambda parts, ok: merge(parts, ok, chip_len, unit, scale2)
    chip_part = merge_lines([outs[2 * k : 2 * k + 2] for k in range(line)], merged)
    other_part = swap(chip_part, 1)
    window_at = jnp.minimum(request_ids[0], requests - 2) * span_len
    k_window = lax.dynamic_slice_in_dim(all_k, window_at, 2 * span_len, 0)
    v_window = lax.dynamic_slice_in_dim(all_v, window_at, 2 * span_len, 0)
    token_rows = jnp.stack([token_ids, request_ids * span_len])
    key_cols = (window_at + jnp.arange(2 * span_len, dtype=jnp.int32))[:, None]
    fresh_sum, fresh_stats = fresh_attention(
        q_own,
        jnp.transpose(k_window, (1, 0, 2)),
        jnp.transpose(v_window, (1, 2, 0)),
        token_rows,
        key_cols,
        unit,
        scale2,
    )
    attended = finish(core, chip_part, other_part, fresh_sum, fresh_stats, unit, scale2)
    attended = [attended] + [
        lax.ppermute(attended, "heads", [(h, (h + s) % groups) for h in range(groups)])
        for s in range(1, groups)
    ]
    hidden = project(attended, weights, out_bias, side, group_at)

    page_shape = (requests * new_pages, PAGE, head_count, head_dim)
    key_out, value_out = write_pages(
        key_cache,
        value_cache,
        all_k.reshape(page_shape),
        all_v.reshape(page_shape),
        is_fresh,
        fresh_index,
    )
    return (hidden, key_out, value_out)


def solution(mesh):
    placed = (
        P("pages", "heads", None),
        P("pages", "heads", None),
        P("pages", "heads", None),
        P("pages", None, "heads", None),
        P("pages", None, "heads", None),
        P(),
        P(),
        P(),
        P("heads", "pages"),
        P("heads"),
    )
    return jax.shard_map(
        per_device,
        mesh=mesh,
        in_specs=placed,
        out_specs=(
            P("pages", "heads"),
            P("pages", None, "heads", None),
            P("pages", None, "heads", None),
        ),
        check_vma=False,
    )
```

```python
import functools
import math

import jax
import jax.numpy as jnp
from jax import lax
from jax.experimental import pallas as pl
from jax.experimental.pallas import tpu as pltpu
from jax.sharding import PartitionSpec as P

ROT = 32
PAGE = 128
QTILE = 256

low_score = -(2.0**99)


def rotate(vectors, positions):
    half_rot = ROT // 2
    inv_freq = 10000.0 ** (-2.0 * jnp.arange(half_rot, dtype=jnp.float32) / ROT)
    angles = positions[:, None] * inv_freq[None, :]
    cosine = jnp.cos(angles)[:, None, :]
    sine = jnp.sin(angles)[:, None, :]
    first_half = vectors[..., :half_rot]
    second_half = vectors[..., half_rot:ROT]
    return jnp.concatenate(
        [
            first_half * cosine - second_half * sine,
            second_half * cosine + first_half * sine,
            vectors[..., ROT:],
        ],
        axis=-1,
    )


def stat_rows_of(part_len, unit):
    per_unit = -(-unit // 128)
    units = part_len // unit
    return per_unit, units, -(-3 * units * per_unit // 16) * 16


def stat_rows(row):
    unit = row.shape[1]
    full = -(-unit // 128) * 128
    if full > unit:
        row = jnp.concatenate([row, jnp.zeros((1, full - unit), row.dtype)], axis=1)
    return [row[:, at : at + 128] for at in range(0, full, 128)]


def stat_block(kinds, pad_to):
    rows = [piece for kind in kinds for row in kind for piece in stat_rows(row)]
    rows.append(jnp.zeros((pad_to - len(rows), 128), jnp.float32))
    return jnp.concatenate(rows, axis=0).astype(jnp.bfloat16)


def cached_kernel(unit, stat_unit, span, scale2, places, at_ref, ok_ref, order_ref, start_ref, count_ref,
                  *refs):
    q_refs, (k_ref, v_ref), refs = refs[:places], refs[places : places + 2], refs[places + 2 :]
    o_refs, (q_all, o_all, s_all, q_scr, m_scr, l_scr, acc_scr) = refs[:-7], refs[-7:]
    requests = count_ref.shape[0]
    chips, part_len, _ = q_all.shape
    per_part = part_len // unit
    per_request = span // unit
    per_unit, units, pad_to = stat_rows_of(part_len, stat_unit)

    for index in range(places):

        @pl.when(ok_ref[index] > 0)
        def _(index=index):
            q_all[at_ref[index]] = q_refs[index][0]

    def place(at, per_part):
        return at // per_part, at % per_part

    def one_request(request, _):
        for index in range(per_request):
            part, piece = place(request * per_request + index, per_part)
            row = pl.ds(pl.multiple_of(piece * unit, unit), unit)
            q_scr[index * unit : (index + 1) * unit, :] = q_all[part, row, :]
        first = start_ref[request]
        count = count_ref[request]
        m_scr[...] = jnp.full((1, span), low_score, jnp.float32)
        l_scr[...] = jnp.zeros((1, span), jnp.float32)
        acc_scr[...] = jnp.zeros(acc_scr.shape, jnp.float32)

        def pages(slots):
            k = jnp.concatenate([k_ref[0, s] for s in slots], axis=0)
            v = jnp.concatenate([v_ref[0, s] for s in slots], axis=1)
            for c in range(0, span, QTILE):
                cols = slice(c, c + QTILE)
                scores = lax.dot_general(
                    k, q_scr[cols, :], (((1,), (1,)), ((), ())),
                    preferred_element_type=jnp.float32,
                )
                before = m_scr[:, cols]
                peak = jnp.maximum(before, jnp.max(scores, axis=0, keepdims=True))
                weights = jnp.exp2((scores - peak) * scale2)
                fade = jnp.exp2((before - peak) * scale2)
                m_scr[:, cols] = peak
                l_scr[:, cols] = l_scr[:, cols] * fade + jnp.sum(weights, axis=0, keepdims=True)
                acc_scr[:, cols] = acc_scr[:, cols] * fade + jnp.dot(
                    v, weights.astype(jnp.bfloat16), preferred_element_type=jnp.float32
                )

        def pair(index, _):
            at = first + 2 * index
            pages([order_ref[at], order_ref[at + 1]])
            return 0

        lax.fori_loop(0, count // 2, pair, 0)

        @pl.when(count % 2 == 1)
        def _():
            pages([order_ref[first + count - 1]])

        totals = l_scr[...]
        peaks = m_scr[...]
        out = (acc_scr[...] / jnp.maximum(totals, 1e-30)).T.astype(jnp.bfloat16)
        sent = peaks.astype(jnp.bfloat16).astype(jnp.float32)
        totals = totals * jnp.exp2((peaks - sent) * scale2)
        high = totals.astype(jnp.bfloat16).astype(jnp.float32)
        kinds = [sent, high, totals - high]
        for index in range(per_request):
            part, piece = place(request * per_request + index, per_part)
            row = pl.ds(pl.multiple_of(piece * unit, unit), unit)
            o_all[part, row, :] = out[index * unit : (index + 1) * unit, :]
        for index in range(span // stat_unit):
            part, piece = place(request * (span // stat_unit) + index, units)
            cols = slice(index * stat_unit, (index + 1) * stat_unit)
            for kind, values in enumerate(kinds):
                for r, line in enumerate(stat_rows(values[:, cols])):
                    at = (kind * units + piece) * per_unit + r
                    s_all[part, pl.ds(at, 1), :] = line
        return 0

    lax.fori_loop(0, requests, one_request, 0)
    for index in range(chips):
        part = at_ref[places + index]
        o_refs[index][0, :part_len, :] = o_all[part]
        o_refs[index][0, part_len:, :] = s_all[part].astype(jnp.bfloat16)


def cached_attention(q_places, at, ok, out_at, k_heads, v_heads, order, starts, counts, span,
                     stat_unit, scale2):
    places = len(q_places)
    chips = len(out_at)
    heads, part_len, head_dim = q_places[0].shape
    slots = k_heads.shape[1]
    unit = math.gcd(span, part_len)
    _, _, pad_to = stat_rows_of(part_len, stat_unit)
    own_block = lambda *dims: pl.BlockSpec(
        (1,) + dims, lambda h, *_: (h,) + (0,) * len(dims)
    )
    return pl.pallas_call(
        lambda *refs: cached_kernel(unit, stat_unit, span, scale2, places, *refs),
        grid_spec=pltpu.PrefetchScalarGridSpec(
            num_scalar_prefetch=5,
            grid=(heads,),
            in_specs=[own_block(part_len, head_dim)] * places
            + [own_block(slots, PAGE, head_dim), own_block(slots, head_dim, PAGE)],
            out_specs=[own_block(part_len + pad_to, head_dim)] * chips,
            scratch_shapes=[
                pltpu.VMEM((chips, part_len, head_dim), jnp.bfloat16),
                pltpu.VMEM((chips, part_len, head_dim), jnp.bfloat16),
                pltpu.VMEM((chips, pad_to, 128), jnp.float32),
                pltpu.VMEM((span, head_dim), jnp.bfloat16),
                pltpu.VMEM((1, span), jnp.float32),
                pltpu.VMEM((1, span), jnp.float32),
                pltpu.VMEM((head_dim, span), jnp.float32),
            ],
        ),
        out_shape=[
            jax.ShapeDtypeStruct((heads, part_len + pad_to, head_dim), jnp.bfloat16)
        ] * chips,
        compiler_params=pltpu.CompilerParams(vmem_limit_bytes=40 * 2**20),
        cost_estimate=pl.CostEstimate(
            flops=40 * 10**9, bytes_accessed=20 * 2**20, transcendentals=10**7
        ),
        name="cached_attention",
    )(jnp.stack(at + out_at), jnp.stack(ok), order, starts, counts, *q_places, k_heads, v_heads)


def spread(row, width, unit):
    return jnp.broadcast_to(row, (width, row.shape[1])).T[:unit]


def merge_kernel(unit, part_len, scale2, ok_ref, *refs):
    in_refs, out_ref = refs[:-1], refs[-1]
    head_dim = out_ref.shape[2]
    per_unit, units, pad_to = stat_rows_of(part_len, unit)
    stats = [ref[0, part_len:, :].astype(jnp.float32) for ref in in_refs]
    rows = [ref[0, :part_len, :].astype(jnp.float32) for ref in in_refs]
    outs = []
    kinds = [[], [], []]
    for u in range(units):

        def line(stat, kind):
            at = (kind * units + u) * per_unit
            pieces = [stat[at + r : at + r + 1, :] for r in range(per_unit)]
            return jnp.concatenate(pieces, axis=1)

        peaks, totals = [], []
        for index, stat in enumerate(stats):
            ok = ok_ref[index] > 0
            peaks.append(jnp.where(ok, line(stat, 0), low_score))
            totals.append(jnp.where(ok, line(stat, 1) + line(stat, 2), 0.0))
        top = functools.reduce(jnp.maximum, peaks)
        shares = [t * jnp.exp2((p - top) * scale2) for t, p in zip(totals, peaks)]
        total = functools.reduce(jnp.add, shares)
        inverse = 1.0 / jnp.maximum(total, 1e-30)
        merged = None
        for values, share in zip(rows, shares):
            part = spread(share * inverse, head_dim, unit) * values[u * unit : (u + 1) * unit]
            merged = part if merged is None else merged + part
        outs.append(merged)
        high = total.astype(jnp.bfloat16).astype(jnp.float32)
        for kind, value in zip(kinds, (top, high, total - high)):
            kind.append(value)
    out_ref[0, :part_len, :] = jnp.concatenate(outs, axis=0).astype(jnp.bfloat16)
    out_ref[0, part_len:, :] = stat_block(kinds, pad_to)


def merge(parts, ok, part_len, unit, scale2):
    block = pl.BlockSpec((1,) + parts[0].shape[1:], lambda h, *_: (h, 0, 0))
    return pl.pallas_call(
        lambda *refs: merge_kernel(unit, part_len, scale2, *refs),
        grid_spec=pltpu.PrefetchScalarGridSpec(
            num_scalar_prefetch=1,
            grid=(parts[0].shape[0],),
            in_specs=[block] * len(parts),
            out_specs=block,
        ),
        out_shape=jax.ShapeDtypeStruct(parts[0].shape, jnp.bfloat16),
        name="merge",
    )(jnp.stack(ok).astype(jnp.int32), *parts)


def page_kernel(seg, blocks_per_line, at_ref, *refs):
    caches, (k_new, v_new), outs, sem = refs[:2], (refs[2:6], refs[6:10]), refs[10:12], refs[12]
    slots, page = caches[0].shape[:2]
    pieces = page // seg
    per_block = k_new[0].shape[1] // seg

    def one_slot(slot, _):
        page_at = at_ref[slot]

        @pl.when(page_at < 0)
        def _():
            for cache, out in zip(caches, outs):
                pltpu.make_async_copy(cache.at[slot], out.at[slot], sem).start()

        @pl.when(page_at >= 0)
        def _():
            for piece in range(pieces):
                at = page_at * pieces + piece
                device = at // per_block
                rows = pl.ds((at % per_block) * seg, seg)
                for k in range(4):

                    @pl.when(device % 4 == (k ^ at_ref[slots]))
                    def _(k=k, piece=piece, device=device, rows=rows):
                        for new, out in zip((k_new[k], v_new[k]), outs):
                            pltpu.make_async_copy(
                                new.at[device // 4, rows],
                                out.at[slot, pl.ds(piece * seg, seg)],
                                sem,
                            ).start()

        return 0

    lax.fori_loop(0, slots, one_slot, 0)
    for cache, out in zip(caches, outs):
        pltpu.make_async_copy(cache, out, sem).wait()


def write_pages(key_cache, value_cache, new_keys, new_values, page_at, side):
    seg = math.gcd(PAGE, new_keys[0].shape[1])
    anywhere = pl.BlockSpec(memory_space=pl.ANY)
    return pl.pallas_call(
        lambda *refs: page_kernel(seg, new_keys[0].shape[0], *refs),
        grid_spec=pltpu.PrefetchScalarGridSpec(
            num_scalar_prefetch=1,
            grid=(1,),
            in_specs=[anywhere] * 10,
            out_specs=[anywhere] * 2,
            scratch_shapes=[pltpu.SemaphoreType.DMA],
        ),
        out_shape=[jax.ShapeDtypeStruct(key_cache.shape, key_cache.dtype)] * 2,
        name="write_pages",
    )(jnp.concatenate([page_at, side[None]]), key_cache, value_cache, *new_keys, *new_values)


def swap(x, bit):
    devs = lax.axis_size("pages")
    return lax.ppermute(x, "pages", [(p, p ^ bit) for p in range(devs)])


def shift(x, hop, senders):
    devs = lax.axis_size("pages")
    moves = [(p, p + 4 * hop) for p in range(devs) if p // 4 in senders]
    return lax.ppermute(x, "pages", moves)


def gather_line(x):
    line = lax.axis_size("pages") // 4
    groups = [[g + 4 * i for i in range(line)] for g in range(4)]
    return lax.all_gather(x, "pages", axis=0, tiled=False, axis_index_groups=groups)


def gather_lines(x):
    line = lax.axis_size("pages") // 4
    device_at = lax.axis_index("pages")
    at, across = device_at // 4, (device_at // 2) % 2
    always = jnp.int32(1)
    held = [(x, at, across, always), (swap(x, 2), at, 1 - across, always)]
    up = down = x
    for t in range(1, line):
        up = shift(up, 1, range(t - 1, line - 1))
        down = shift(down, -1, range(1, line - t + 1))
        has_up = (at >= t).astype(jnp.int32)
        has_down = (at + t < line).astype(jnp.int32)
        devs = lax.axis_size("pages")
        cross_up = [(p, p ^ 2) for p in range(devs) if p // 4 >= t]
        cross_down = [(p, p ^ 2) for p in range(devs) if p // 4 + t < line]
        held += [
            (up, at - t, across, has_up),
            (lax.ppermute(up, "pages", cross_up), at - t, 1 - across, has_up),
            (down, at + t, across, has_down),
            (lax.ppermute(down, "pages", cross_down), at + t, 1 - across, has_down),
        ]
    return held


def merge_lines(parts, merged, beside, last):
    line = lax.axis_size("pages") // 4
    at = lax.axis_index("pages") // 4
    turns = []
    for t in range(1, line):
        turns += [k for k in (line - t, t) if k not in turns]
    yes = jnp.int32(1)
    crossed = {k: swap(parts[k][1], 2) for k in turns + [0]}
    shares = {}

    def share(k):
        if k not in shares:
            shares[k] = merged([parts[k][0], crossed[k]], [yes, yes])
        return shares[k]

    up = down = None
    for t in range(1, line):
        up_out, down_out = share(line - t), share(t)
        if up is not None:
            up_out = merged([up_out, up], [yes, (at >= 1) & (at <= t - 1)])
            down_out = merged([down_out, down], [yes, (at <= line - 2) & (at >= line - t)])
        up_out, down_out = beside(t, (up_out, down_out))
        up = shift(up_out, 1, range(0, t))
        down = shift(down_out, -1, range(line - t, line))
    return merged([share(0), up, down, last()], [yes, at >= 1, at <= line - 2, yes])


def fresh_kernel(unit, scale2, q_ref, *refs):
    k_refs, v_refs = refs[:-3:2], refs[1:-3:2]
    tok_ref, key_ref, o_ref = refs[-3:]
    k = jnp.concatenate([ref[0] for ref in k_refs], axis=0)
    v = jnp.concatenate([ref[0] for ref in v_refs], axis=0)
    token, first, key = tok_ref[0:1, :], tok_ref[1:2, :], key_ref[:, 0:1]
    scores = lax.dot_general(
        k, q_ref[0], (((1,), (1,)), ((), ())), preferred_element_type=jnp.float32
    )
    visible = (key <= token) & (key >= first)
    scores = jnp.where(visible, scores, low_score)
    peak = jnp.max(scores, axis=0, keepdims=True)
    weights = jnp.where(visible, jnp.exp2((scores - peak) * scale2), 0.0)
    totals = jnp.sum(weights, axis=0, keepdims=True)
    out = lax.dot_general(
        v, weights.astype(jnp.bfloat16), (((0,), (0,)), ((), ())),
        preferred_element_type=jnp.float32,
    )
    out = out / totals
    part_len = out.shape[1]
    pad = -part_len % 128
    out = jnp.concatenate([out, jnp.zeros((out.shape[0], pad), jnp.float32)], axis=1)
    o_ref[0, :part_len, :] = out.T[:part_len].astype(jnp.bfloat16)
    sent = peak.astype(jnp.bfloat16).astype(jnp.float32)
    totals = totals * jnp.exp2((peak - sent) * scale2)
    high = totals.astype(jnp.bfloat16).astype(jnp.float32)
    kinds = [
        [values[:, at : at + unit] for at in range(0, part_len, unit)]
        for values in (sent, high, totals - high)
    ]
    o_ref[0, part_len:, :] = stat_block(kinds, o_ref.shape[1] - part_len)


def fresh_attention(q_chip, k_blocks, v_blocks, token_rows, key_cols, unit, scale2):
    heads, part_len, head_dim = q_chip.shape
    _, _, pad_to = stat_rows_of(part_len, unit)
    own = lambda x: pl.BlockSpec((1,) + x.shape[1:], lambda h: (h, 0, 0))
    fixed = lambda x: pl.BlockSpec(x.shape, lambda h: (0, 0))
    blocks = [x for pair in zip(k_blocks, v_blocks) for x in pair]
    return pl.pallas_call(
        lambda *refs: fresh_kernel(unit, scale2, *refs),
        grid=(heads,),
        in_specs=[own(q_chip)]
        + [own(x) for x in blocks]
        + [fixed(token_rows), fixed(key_cols)],
        out_specs=pl.BlockSpec((1, part_len + pad_to, head_dim), lambda h: (h, 0, 0)),
        out_shape=jax.ShapeDtypeStruct((heads, part_len + pad_to, head_dim), jnp.bfloat16),
        compiler_params=pltpu.CompilerParams(vmem_limit_bytes=40 * 2**20),
        name="fresh_attention",
    )(q_chip, *blocks, token_rows, key_cols)


def project_kernel(groups, at_ref, *refs):
    att_refs, w_refs = refs[: 2 * groups], refs[2 * groups : -3]
    bias_ref, out_ref, rows_ref = refs[-3:]
    core = lax.rem(at_ref[0], 2)
    wide = rows_ref.shape[2]

    @pl.when((pl.program_id(0) == 0) & (pl.program_id(1) == 0))
    def _():
        for index, ref in enumerate(att_refs):
            rows_ref[index] = jnp.concatenate([ref[h] for h in range(ref.shape[0])], axis=1)

    for k in range(4):

        @pl.when(pl.program_id(1) == k)
        def _(k=k):
            total = bias_ref[...].reshape(1, -1)
            for s in range(groups):
                for d in range(2):
                    feats = pl.ds(pl.multiple_of((core ^ d) * wide, wide), wide)
                    total = total + jnp.dot(
                        rows_ref[2 * s + d],
                        w_refs[k * groups + s][0, feats, :],
                        preferred_element_type=jnp.float32,
                    )
            out_ref[...] = total.astype(jnp.bfloat16).reshape(out_ref.shape)


def project(pieces, weights, bias, side, group_at):
    groups = len(pieces) // 2
    half, tok_dev, head_dim = pieces[0].shape
    line, feats, cols = weights[0].shape
    share = line // groups
    blocks = share * 4
    wide = cols % 128 == 0
    place = lambda j, k, at: j * 4 + (k ^ at[0])

    def weight_spec(s):
        return pl.BlockSpec(
            (1, feats, cols),
            lambda j, k, at: (lax.rem(at[1] + groups - s, groups) * share + j, 0, 0),
        )

    if wide:
        out_spec = pl.BlockSpec((tok_dev, cols), lambda j, k, at: (0, place(j, k, at)))
        out_shape = (tok_dev, blocks * cols)
    else:
        out_spec = pl.BlockSpec((1, tok_dev, cols), lambda j, k, at: (place(j, k, at), 0, 0))
        out_shape = (blocks, tok_dev, cols)
    out = pl.pallas_call(
        lambda *refs: project_kernel(groups, *refs),
        grid_spec=pltpu.PrefetchScalarGridSpec(
            num_scalar_prefetch=1,
            grid=(share, 4),
            in_specs=[pl.BlockSpec(x.shape, lambda j, k, at: (0, 0, 0)) for x in pieces]
            + [weight_spec(s) for _ in range(4) for s in range(groups)]
            + [pl.BlockSpec((1, 1, cols), lambda j, k, at: (place(j, k, at), 0, 0))],
            out_specs=out_spec,
            scratch_shapes=[pltpu.VMEM((2 * groups, tok_dev, half * head_dim), jnp.bfloat16)],
        ),
        out_shape=jax.ShapeDtypeStruct(out_shape, jnp.bfloat16),
        compiler_params=pltpu.CompilerParams(vmem_limit_bytes=40 * 2**20),
        name="project",
    )(
        jnp.stack([side, group_at]),
        *pieces,
        *[w for w in weights for _ in range(groups)],
        bias.reshape(blocks, 1, cols),
    )
    return out if wide else jnp.transpose(out, (1, 0, 2)).reshape(tok_dev, blocks * cols)


def per_device(
    queries,
    keys,
    values,
    key_cache,
    value_cache,
    cache_len,
    page_table,
    append_slots,
    out_weight,
    out_bias,
):
    tok_dev, head_count, head_dim = queries.shape
    requests = cache_len.shape[0]
    max_pages = page_table.shape[1]
    new_pages = append_slots.shape[1]
    span_len = new_pages * PAGE
    slot_count = key_cache.shape[0]
    tokens = requests * span_len
    page_devs = tokens // tok_dev
    scale2 = math.log2(math.e) / math.sqrt(head_dim)
    device_at = lax.axis_index("pages")
    token_ids = device_at * tok_dev + jnp.arange(tok_dev, dtype=jnp.int32)
    request_ids = token_ids // span_len
    request_grid = jnp.arange(requests, dtype=jnp.int32)
    starts = jnp.sum(
        jnp.where(request_ids[:, None] == request_grid[None, :], cache_len[None, :], 0), axis=1
    )
    positions = (starts + token_ids % span_len).astype(jnp.float32)
    rotated_q = rotate(queries.astype(jnp.float32), positions).astype(jnp.bfloat16)
    rotated_k = rotate(keys.astype(jnp.float32), positions).astype(jnp.bfloat16)
    core = device_at % 2
    half = head_count // 2
    chip_len = 2 * tok_dev

    def halves(x):
        return (
            lax.dynamic_slice_in_dim(x, core * half, half, 0),
            lax.dynamic_slice_in_dim(x, (1 - core) * half, half, 0),
        )

    def in_order(mine, got, axis):
        return jnp.where(
            core == 0,
            jnp.concatenate([mine, got], axis=axis),
            jnp.concatenate([got, mine], axis=axis),
        )

    q_own = jnp.transpose(rotated_q, (1, 0, 2))
    q_mine, q_other = halves(q_own)
    q_chip = in_order(q_mine, swap(q_other, 1), 1)
    q_places = gather_lines(q_chip)
    groups = lax.axis_size("heads")
    group_at = lax.axis_index("heads")
    share = page_devs // groups
    moves = [
        (i * page_devs + h * share + j, h * page_devs + i * share + j)
        for i in range(groups)
        for h in range(groups)
        for j in range(share)
    ]
    weight_block = lax.ppermute(out_weight, ("heads", "pages"), moves)
    side = device_at % 4
    barrier = lax.optimization_barrier
    line_k = gather_line(rotated_k)
    line_k, values = barrier((line_k, values))
    line_v = gather_line(values)
    line_v, weight_block = barrier((line_v, weight_block))
    line_w = gather_line(weight_block)
    q_blocks, line_k = barrier(([q for q, _, _, _ in q_places], line_k))
    across_k = swap(line_k, 2)

    my_slots = device_at * slot_count + jnp.arange(slot_count, dtype=jnp.int32)
    chip_slots = jnp.concatenate(
        [my_slots, (device_at ^ 1) * slot_count + jnp.arange(slot_count, dtype=jnp.int32)]
    )
    cached_hit = page_table.reshape(-1)[None, :] == chip_slots[:, None]
    fresh_hit = append_slots.reshape(-1)[None, :] == my_slots[:, None]
    table_at = jnp.arange(requests * max_pages, dtype=jnp.int32)
    shown = (table_at % max_pages) * PAGE < jnp.repeat(cache_len, max_pages)
    is_fresh = jnp.any(fresh_hit, axis=1)
    fresh_index = jnp.sum(
        jnp.where(fresh_hit, jnp.arange(requests * new_pages, dtype=jnp.int32)[None, :], 0), axis=1
    )
    slot_key = requests - jnp.sum(
        jnp.where(cached_hit & shown[None, :], requests - (table_at // max_pages)[None, :], 0),
        axis=1,
    )
    slot_at = jnp.arange(2 * slot_count, dtype=jnp.int32)
    earlier = (slot_key[None, :] < slot_key[:, None]) | (
        (slot_key[None, :] == slot_key[:, None]) & (slot_at[None, :] < slot_at[:, None])
    )
    rank = jnp.sum(earlier.astype(jnp.int32), axis=1)
    order = jnp.sum(jnp.where(rank[None, :] == slot_at[:, None], slot_at[None, :], 0), axis=1)
    slot_starts = jnp.sum((slot_key[None, :] < request_grid[:, None]).astype(jnp.int32), axis=1)
    slot_counts = jnp.sum((slot_key[None, :] == request_grid[:, None]).astype(jnp.int32), axis=1)

    k_mine, k_other = halves(jnp.transpose(key_cache, (2, 0, 1, 3)))
    v_mine, v_other = halves(jnp.transpose(value_cache, (2, 0, 3, 1)))
    k_heads = jnp.concatenate([k_mine, swap(k_other, 1)], axis=1)
    v_heads = jnp.concatenate([v_mine, swap(v_other, 1)], axis=1)

    unit = math.gcd(span_len, tok_dev)
    line = page_devs // 4
    line_at, across = device_at // 4, (device_at // 2) % 2
    outs = cached_attention(
        q_blocks,
        [jnp.clip(at, 0, line - 1) * 2 + side for _, at, side, _ in q_places],
        [ok for _, _, _, ok in q_places],
        [((line_at + k) % line) * 2 + (across ^ d) for k in range(line) for d in range(2)],
        k_heads,
        v_heads,
        order,
        slot_starts,
        slot_counts,
        span_len,
        unit,
        scale2,
    )
    outs, across_k = barrier((outs, across_k))
    merged = lambda parts, ok: merge(parts, ok, chip_len, unit, scale2)
    later = {}

    def beside(t, sent):
        if t == 2:
            sent, later["v"] = barrier((sent, line_v))
        return sent

    def fresh_part():
        all_k = [line_k, swap(line_k, 1), across_k, swap(across_k, 1)]
        across_v = swap(later["v"], 2)
        all_v = [later["v"], swap(later["v"], 1), across_v, swap(across_v, 1)]
        later["k"], later["v"] = all_k, all_v
        chip_at = device_at // 2
        back = -(-(span_len - math.gcd(span_len, chip_len)) // chip_len)
        blocks, places = [[], []], []
        for step in range(back, -1, -1):
            chip = chip_at - step
            far = (chip % 2) != across
            for d in range(2):
                places.append(jnp.where(chip < 0, tokens, chip * chip_len) + (core ^ d) * tok_dev)
                for found, arrays in zip(blocks, (all_k, all_v)):
                    at = jnp.maximum(chip, 0) // 2
                    if step == 0:
                        block = lax.dynamic_index_in_dim(arrays[d], at, 0, keepdims=False)
                    else:
                        block = jnp.where(
                            far,
                            lax.dynamic_index_in_dim(arrays[2 + d], at, 0, keepdims=False),
                            lax.dynamic_index_in_dim(arrays[d], at, 0, keepdims=False),
                        )
                    block = lax.dynamic_slice_in_dim(block, core * half, half, 1)
                    found.append(jnp.transpose(block, (1, 0, 2)))
        chip_tokens = chip_at * chip_len + jnp.arange(chip_len, dtype=jnp.int32)
        token_rows = jnp.stack([chip_tokens, chip_tokens // span_len * span_len])
        row = jnp.arange(tok_dev, dtype=jnp.int32)
        key_cols = jnp.concatenate([place + row for place in places])[:, None]
        return fresh_attention(q_chip, *blocks, token_rows, key_cols, unit, scale2)

    chip_part = merge_lines(
        [outs[2 * k : 2 * k + 2] for k in range(line)], merged, beside, fresh_part
    )
    rows_of = lambda c: lax.dynamic_slice_in_dim(chip_part[:, :chip_len], c * tok_dev, tok_dev, 1)
    own_rows, other_rows = rows_of(core), rows_of(1 - core)
    pieces = []
    for s in range(groups):
        for d, rows in ((0, own_rows), (1, other_rows)):
            if s or d:
                rows = lax.ppermute(
                    rows,
                    ("heads", "pages"),
                    [
                        (h * page_devs + p, (h + s) % groups * page_devs + (p ^ d))
                        for h in range(groups)
                        for p in range(page_devs)
                    ],
                )
            pieces.append(rows)
    across_w = swap(line_w, 2)
    weights = [line_w, swap(line_w, 1), across_w, swap(across_w, 1)]
    hidden = project(pieces, weights, out_bias, side, group_at)
    page_at = jnp.where(is_fresh, fresh_index, -1)
    key_out, value_out = write_pages(
        key_cache, value_cache, later["k"], later["v"], page_at, side
    )
    return (hidden, key_out, value_out)


def solution(mesh):
    placed = (
        P("pages", "heads", None),
        P("pages", "heads", None),
        P("pages", "heads", None),
        P("pages", None, "heads", None),
        P("pages", None, "heads", None),
        P(),
        P(),
        P(),
        P("heads", "pages"),
        P("heads"),
    )
    return jax.shard_map(
        per_device,
        mesh=mesh,
        in_specs=placed,
        out_specs=(
            P("pages", "heads"),
            P("pages", None, "heads", None),
            P("pages", None, "heads", None),
        ),
        check_vma=False,
    )
```

```python
import functools
import math

import jax
import jax.numpy as jnp
from jax import lax
from jax.experimental import pallas as pl
from jax.experimental.layout import Layout, with_layout_constraint
from jax.experimental.pallas import tpu as pltpu
from jax.sharding import PartitionSpec as P

ROT = 32
PAGE = 128
QTILE = 256

low_score = -(2.0**99)


def rotate(vectors, positions):
    half_rot = ROT // 2
    inv_freq = 10000.0 ** (-2.0 * jnp.arange(half_rot, dtype=jnp.float32) / ROT)
    angles = positions[:, None] * inv_freq[None, :]
    cosine = jnp.cos(angles)[:, None, :]
    sine = jnp.sin(angles)[:, None, :]
    first_half = vectors[..., :half_rot]
    second_half = vectors[..., half_rot:ROT]
    return jnp.concatenate(
        [
            first_half * cosine - second_half * sine,
            second_half * cosine + first_half * sine,
            vectors[..., ROT:],
        ],
        axis=-1,
    )


def stat_rows_of(part_len, unit):
    per_unit = -(-unit // 128)
    units = part_len // unit
    return per_unit, units, -(-3 * units * per_unit // 16) * 16


def stat_rows(row):
    unit = row.shape[1]
    full = -(-unit // 128) * 128
    if full > unit:
        row = jnp.concatenate([row, jnp.zeros((1, full - unit), row.dtype)], axis=1)
    return [row[:, at : at + 128] for at in range(0, full, 128)]


def stat_block(kinds, pad_to):
    rows = [piece for kind in kinds for row in kind for piece in stat_rows(row)]
    rows.append(jnp.zeros((pad_to - len(rows), 128), jnp.float32))
    return jnp.concatenate(rows, axis=0).astype(jnp.bfloat16)


def cached_kernel(unit, stat_unit, span, scale2, places, at_ref, ok_ref, order_ref, start_ref, count_ref,
                  *refs):
    q_refs, (k_ref, v_ref), refs = refs[:places], refs[places : places + 2], refs[places + 2 :]
    o_refs, (q_all, o_all, s_all, q_scr, m_scr, l_scr, acc_scr) = refs[:-7], refs[-7:]
    requests = count_ref.shape[0]
    chips, part_len, _ = q_all.shape
    per_part = part_len // unit
    per_request = span // unit
    per_unit, units, pad_to = stat_rows_of(part_len, stat_unit)

    for index in range(places):

        @pl.when(ok_ref[index] > 0)
        def _(index=index):
            q_all[at_ref[index]] = q_refs[index][0]

    def place(at, per_part):
        return at // per_part, at % per_part

    def one_request(request, _):
        for index in range(per_request):
            part, piece = place(request * per_request + index, per_part)
            row = pl.ds(pl.multiple_of(piece * unit, unit), unit)
            q_scr[index * unit : (index + 1) * unit, :] = q_all[part, row, :]
        first = start_ref[request]
        count = count_ref[request]
        m_scr[...] = jnp.full((1, span), low_score, jnp.float32)
        l_scr[...] = jnp.zeros((1, span), jnp.float32)
        acc_scr[...] = jnp.zeros(acc_scr.shape, jnp.float32)

        def pages(slots):
            k = jnp.concatenate([k_ref[0, s] for s in slots], axis=0)
            v = jnp.concatenate([v_ref[0, s] for s in slots], axis=1)
            for c in range(0, span, QTILE):
                cols = slice(c, c + QTILE)
                scores = lax.dot_general(
                    k, q_scr[cols, :], (((1,), (1,)), ((), ())),
                    preferred_element_type=jnp.float32,
                )
                before = m_scr[:, cols]
                peak = jnp.maximum(before, jnp.max(scores, axis=0, keepdims=True))
                weights = jnp.exp2((scores - peak) * scale2)
                fade = jnp.exp2((before - peak) * scale2)
                m_scr[:, cols] = peak
                l_scr[:, cols] = l_scr[:, cols] * fade + jnp.sum(weights, axis=0, keepdims=True)
                acc_scr[:, cols] = acc_scr[:, cols] * fade + jnp.dot(
                    v, weights.astype(jnp.bfloat16), preferred_element_type=jnp.float32
                )

        def pair(index, _):
            at = first + 2 * index
            pages([order_ref[at], order_ref[at + 1]])
            return 0

        lax.fori_loop(0, count // 2, pair, 0)

        @pl.when(count % 2 == 1)
        def _():
            pages([order_ref[first + count - 1]])

        totals = l_scr[...]
        peaks = m_scr[...]
        out = (acc_scr[...] / jnp.maximum(totals, 1e-30)).T.astype(jnp.bfloat16)
        sent = peaks.astype(jnp.bfloat16).astype(jnp.float32)
        totals = totals * jnp.exp2((peaks - sent) * scale2)
        high = totals.astype(jnp.bfloat16).astype(jnp.float32)
        kinds = [sent, high, totals - high]
        for index in range(per_request):
            part, piece = place(request * per_request + index, per_part)
            row = pl.ds(pl.multiple_of(piece * unit, unit), unit)
            o_all[part, row, :] = out[index * unit : (index + 1) * unit, :]
        for index in range(span // stat_unit):
            part, piece = place(request * (span // stat_unit) + index, units)
            cols = slice(index * stat_unit, (index + 1) * stat_unit)
            for kind, values in enumerate(kinds):
                for r, line in enumerate(stat_rows(values[:, cols])):
                    at = (kind * units + piece) * per_unit + r
                    s_all[part, pl.ds(at, 1), :] = line
        return 0

    lax.fori_loop(0, requests, one_request, 0)
    for index in range(chips):
        part = at_ref[places + index]
        o_refs[index][0, :part_len, :] = o_all[part]
        o_refs[index][0, part_len:, :] = s_all[part].astype(jnp.bfloat16)


def cached_attention(q_places, at, ok, out_at, k_heads, v_heads, order, starts, counts, span,
                     stat_unit, scale2):
    places = len(q_places)
    chips = len(out_at)
    heads, part_len, head_dim = q_places[0].shape
    slots = k_heads.shape[1]
    unit = math.gcd(span, part_len)
    _, _, pad_to = stat_rows_of(part_len, stat_unit)
    own_block = lambda *dims: pl.BlockSpec(
        (1,) + dims, lambda h, *_: (h,) + (0,) * len(dims)
    )
    return pl.pallas_call(
        lambda *refs: cached_kernel(unit, stat_unit, span, scale2, places, *refs),
        grid_spec=pltpu.PrefetchScalarGridSpec(
            num_scalar_prefetch=5,
            grid=(heads,),
            in_specs=[own_block(part_len, head_dim)] * places
            + [own_block(slots, PAGE, head_dim), own_block(slots, head_dim, PAGE)],
            out_specs=[own_block(part_len + pad_to, head_dim)] * chips,
            scratch_shapes=[
                pltpu.VMEM((chips, part_len, head_dim), jnp.bfloat16),
                pltpu.VMEM((chips, part_len, head_dim), jnp.bfloat16),
                pltpu.VMEM((chips, pad_to, 128), jnp.float32),
                pltpu.VMEM((span, head_dim), jnp.bfloat16),
                pltpu.VMEM((1, span), jnp.float32),
                pltpu.VMEM((1, span), jnp.float32),
                pltpu.VMEM((head_dim, span), jnp.float32),
            ],
        ),
        out_shape=[
            jax.ShapeDtypeStruct((heads, part_len + pad_to, head_dim), jnp.bfloat16)
        ] * chips,
        compiler_params=pltpu.CompilerParams(vmem_limit_bytes=40 * 2**20),
        cost_estimate=pl.CostEstimate(
            flops=40 * 10**9, bytes_accessed=20 * 2**20, transcendentals=10**7
        ),
        name="cached_attention",
    )(jnp.stack(at + out_at), jnp.stack(ok), order, starts, counts, *q_places, k_heads, v_heads)


def spread(row, width, unit):
    return jnp.broadcast_to(row, (width, row.shape[1])).T[:unit]


def merge_kernel(unit, part_len, scale2, ok_ref, *refs):
    in_refs, out_ref = refs[:-1], refs[-1]
    head_dim = out_ref.shape[2]
    per_unit, units, pad_to = stat_rows_of(part_len, unit)
    stats = [ref[0, part_len:, :].astype(jnp.float32) for ref in in_refs]
    rows = [ref[0, :part_len, :].astype(jnp.float32) for ref in in_refs]
    outs = []
    kinds = [[], [], []]
    for u in range(units):

        def line(stat, kind):
            at = (kind * units + u) * per_unit
            pieces = [stat[at + r : at + r + 1, :] for r in range(per_unit)]
            return jnp.concatenate(pieces, axis=1)

        peaks, totals = [], []
        for index, stat in enumerate(stats):
            ok = ok_ref[index] > 0
            peaks.append(jnp.where(ok, line(stat, 0), low_score))
            totals.append(jnp.where(ok, line(stat, 1) + line(stat, 2), 0.0))
        top = functools.reduce(jnp.maximum, peaks)
        shares = [t * jnp.exp2((p - top) * scale2) for t, p in zip(totals, peaks)]
        total = functools.reduce(jnp.add, shares)
        inverse = 1.0 / jnp.maximum(total, 1e-30)
        merged = None
        for values, share in zip(rows, shares):
            part = spread(share * inverse, head_dim, unit) * values[u * unit : (u + 1) * unit]
            merged = part if merged is None else merged + part
        outs.append(merged)
        high = total.astype(jnp.bfloat16).astype(jnp.float32)
        for kind, value in zip(kinds, (top, high, total - high)):
            kind.append(value)
    out_ref[0, :part_len, :] = jnp.concatenate(outs, axis=0).astype(jnp.bfloat16)
    out_ref[0, part_len:, :] = stat_block(kinds, pad_to)


def merge(parts, ok, part_len, unit, scale2):
    block = pl.BlockSpec((1,) + parts[0].shape[1:], lambda h, *_: (h, 0, 0))
    return pl.pallas_call(
        lambda *refs: merge_kernel(unit, part_len, scale2, *refs),
        grid_spec=pltpu.PrefetchScalarGridSpec(
            num_scalar_prefetch=1,
            grid=(parts[0].shape[0],),
            in_specs=[block] * len(parts),
            out_specs=block,
        ),
        out_shape=jax.ShapeDtypeStruct(parts[0].shape, jnp.bfloat16),
        name="merge",
    )(jnp.stack(ok).astype(jnp.int32), *parts)


def page_kernel(fresh_ref, index_ref, kc_ref, vc_ref, kn_ref, vn_ref, ko_ref, vo_ref):
    fresh = fresh_ref[pl.program_id(0)] > 0

    @pl.when(fresh)
    def _():
        ko_ref[...] = kn_ref[...]
        vo_ref[...] = vn_ref[...]

    @pl.when(jnp.logical_not(fresh))
    def _():
        ko_ref[...] = kc_ref[...]
        vo_ref[...] = vc_ref[...]


def write_pages(key_cache, value_cache, new_keys, new_values, is_fresh, fresh_index):
    block = (1,) + key_cache.shape[1:]
    own = pl.BlockSpec(block, lambda s, fresh, index: (s, 0, 0, 0))
    new = pl.BlockSpec(block, lambda s, fresh, index: (index[s], 0, 0, 0))
    return pl.pallas_call(
        page_kernel,
        grid_spec=pltpu.PrefetchScalarGridSpec(
            num_scalar_prefetch=2,
            grid=(key_cache.shape[0],),
            in_specs=[own, own, new, new],
            out_specs=[own, own],
        ),
        out_shape=[jax.ShapeDtypeStruct(key_cache.shape, key_cache.dtype)] * 2,
        compiler_params=pltpu.CompilerParams(vmem_limit_bytes=40 * 2**20),
        name="write_pages",
    )(is_fresh.astype(jnp.int32), fresh_index, key_cache, value_cache, new_keys, new_values)


def swap(x, bit):
    devs = lax.axis_size("pages")
    return lax.ppermute(x, "pages", [(p, p ^ bit) for p in range(devs)])


def shift(x, hop, senders):
    devs = lax.axis_size("pages")
    moves = [(p, p + 4 * hop) for p in range(devs) if p // 4 in senders]
    return lax.ppermute(x, "pages", moves)


def gather_lines(x):
    line = lax.axis_size("pages") // 4
    device_at = lax.axis_index("pages")
    at, across = device_at // 4, (device_at // 2) % 2
    always = jnp.int32(1)
    held = [(x, at, across, always), (swap(x, 2), at, 1 - across, always)]
    up = down = x
    for t in range(1, line):
        up = shift(up, 1, range(t - 1, line - 1))
        down = shift(down, -1, range(1, line - t + 1))
        has_up = (at >= t).astype(jnp.int32)
        has_down = (at + t < line).astype(jnp.int32)
        devs = lax.axis_size("pages")
        cross_up = [(p, p ^ 2) for p in range(devs) if p // 4 >= t]
        cross_down = [(p, p ^ 2) for p in range(devs) if p // 4 + t < line]
        held += [
            (up, at - t, across, has_up),
            (lax.ppermute(up, "pages", cross_up), at - t, 1 - across, has_up),
            (down, at + t, across, has_down),
            (lax.ppermute(down, "pages", cross_down), at + t, 1 - across, has_down),
        ]
    return held


def merge_lines(parts, merged, last):
    line = lax.axis_size("pages") // 4
    at = lax.axis_index("pages") // 4
    turns = []
    for t in range(1, line):
        turns += [k for k in (line - t, t) if k not in turns]
    yes = jnp.int32(1)
    crossed = {k: swap(parts[k][1], 2) for k in turns + [0]}
    shares = {}

    def share(k):
        if k not in shares:
            shares[k] = merged([parts[k][0], crossed[k]], [yes, yes])
        return shares[k]

    up = down = None
    for t in range(1, line):
        up_out, down_out = share(line - t), share(t)
        if up is not None:
            up_out = merged([up_out, up], [yes, (at >= 1) & (at <= t - 1)])
            down_out = merged([down_out, down], [yes, (at <= line - 2) & (at >= line - t)])
        up = shift(up_out, 1, range(0, t))
        down = shift(down_out, -1, range(line - t, line))
    return merged([share(0), up, down, last()], [yes, at >= 1, at <= line - 2, yes])


def fresh_kernel(unit, scale2, q_ref, k_ref, v_ref, tok_ref, key_ref, o_ref):
    token, first, key = tok_ref[0:1, :], tok_ref[1:2, :], key_ref[:, 0:1]
    scores = lax.dot_general(
        k_ref[0], q_ref[0], (((1,), (1,)), ((), ())), preferred_element_type=jnp.float32
    )
    visible = (key <= token) & (key >= first)
    scores = jnp.where(visible, scores, low_score)
    peak = jnp.max(scores, axis=0, keepdims=True)
    weights = jnp.where(visible, jnp.exp2((scores - peak) * scale2), 0.0)
    totals = jnp.sum(weights, axis=0, keepdims=True)
    out = lax.dot_general(
        v_ref[0], weights.astype(jnp.bfloat16), (((0,), (0,)), ((), ())),
        preferred_element_type=jnp.float32,
    )
    out = out / totals
    part_len = out.shape[1]
    pad = -part_len % 128
    out = jnp.concatenate([out, jnp.zeros((out.shape[0], pad), jnp.float32)], axis=1)
    o_ref[0, :part_len, :] = out.T[:part_len].astype(jnp.bfloat16)
    sent = peak.astype(jnp.bfloat16).astype(jnp.float32)
    totals = totals * jnp.exp2((peak - sent) * scale2)
    high = totals.astype(jnp.bfloat16).astype(jnp.float32)
    kinds = [
        [values[:, at : at + unit] for at in range(0, part_len, unit)]
        for values in (sent, high, totals - high)
    ]
    o_ref[0, part_len:, :] = stat_block(kinds, o_ref.shape[1] - part_len)


def fresh_attention(q_chip, k_window, v_window, token_rows, key_cols, unit, scale2):
    heads, part_len, head_dim = q_chip.shape
    _, _, pad_to = stat_rows_of(part_len, unit)
    own = lambda x: pl.BlockSpec((1,) + x.shape[1:], lambda h: (h, 0, 0))
    fixed = lambda x: pl.BlockSpec(x.shape, lambda h: (0, 0))
    return pl.pallas_call(
        lambda *refs: fresh_kernel(unit, scale2, *refs),
        grid=(heads,),
        in_specs=[own(q_chip), own(k_window), own(v_window), fixed(token_rows), fixed(key_cols)],
        out_specs=pl.BlockSpec((1, part_len + pad_to, head_dim), lambda h: (h, 0, 0)),
        out_shape=jax.ShapeDtypeStruct((heads, part_len + pad_to, head_dim), jnp.bfloat16),
        compiler_params=pltpu.CompilerParams(vmem_limit_bytes=40 * 2**20),
        name="fresh_attention",
    )(q_chip, k_window, v_window, token_rows, key_cols)


def project_kernel(groups, at_ref, *refs):
    att_refs, w_refs = refs[: 2 * groups], refs[2 * groups : -3]
    bias_ref, out_ref, rows_ref = refs[-3:]
    core = at_ref[0]
    wide = rows_ref.shape[2]

    @pl.when(pl.program_id(0) == 0)
    def _():
        for index, ref in enumerate(att_refs):
            rows_ref[index] = jnp.concatenate([ref[h] for h in range(ref.shape[0])], axis=1)

    total = bias_ref[...].reshape(1, -1)
    for s in range(groups):
        for d in range(2):
            feats = pl.ds(pl.multiple_of((core ^ d) * wide, wide), wide)
            total = total + jnp.dot(
                rows_ref[2 * s + d], w_refs[s][0, feats, :], preferred_element_type=jnp.float32
            )
    out_ref[...] = total.astype(jnp.bfloat16).reshape(out_ref.shape)


def project(pieces, weights, bias, core, group_at):
    groups = len(pieces) // 2
    half, tok_dev, head_dim = pieces[0].shape
    blocks, feats, cols = weights.shape
    blocks //= groups
    wide = cols % 128 == 0

    def weight_spec(s):
        return pl.BlockSpec(
            (1, feats, cols),
            lambda j, at: (lax.rem(at[1] + groups - s, groups) * blocks + j, 0, 0),
        )

    if wide:
        out_spec = pl.BlockSpec((tok_dev, cols), lambda j, at: (0, j))
        out_shape = (tok_dev, blocks * cols)
    else:
        out_spec = pl.BlockSpec((1, tok_dev, cols), lambda j, at: (j, 0, 0))
        out_shape = (blocks, tok_dev, cols)
    out = pl.pallas_call(
        lambda *refs: project_kernel(groups, *refs),
        grid_spec=pltpu.PrefetchScalarGridSpec(
            num_scalar_prefetch=1,
            grid=(blocks,),
            in_specs=[pl.BlockSpec(x.shape, lambda j, at: (0, 0, 0)) for x in pieces]
            + [weight_spec(s) for s in range(groups)]
            + [pl.BlockSpec((1, 1, cols), lambda j, at: (j, 0, 0))],
            out_specs=out_spec,
            scratch_shapes=[pltpu.VMEM((2 * groups, tok_dev, half * head_dim), jnp.bfloat16)],
        ),
        out_shape=jax.ShapeDtypeStruct(out_shape, jnp.bfloat16),
        compiler_params=pltpu.CompilerParams(vmem_limit_bytes=40 * 2**20),
        name="project",
    )(
        jnp.stack([core, group_at]),
        *pieces,
        *[weights] * groups,
        bias.reshape(blocks, 1, cols),
    )
    return out if wide else jnp.transpose(out, (1, 0, 2)).reshape(tok_dev, blocks * cols)


def per_device(
    queries,
    keys,
    values,
    key_cache,
    value_cache,
    cache_len,
    page_table,
    append_slots,
    out_weight,
    out_bias,
):
    tok_dev, head_count, head_dim = queries.shape
    requests = cache_len.shape[0]
    max_pages = page_table.shape[1]
    new_pages = append_slots.shape[1]
    span_len = new_pages * PAGE
    slot_count = key_cache.shape[0]
    tokens = requests * span_len
    page_devs = tokens // tok_dev
    scale2 = math.log2(math.e) / math.sqrt(head_dim)
    device_at = lax.axis_index("pages")
    token_ids = device_at * tok_dev + jnp.arange(tok_dev, dtype=jnp.int32)
    request_ids = token_ids // span_len
    request_grid = jnp.arange(requests, dtype=jnp.int32)
    starts = jnp.sum(
        jnp.where(request_ids[:, None] == request_grid[None, :], cache_len[None, :], 0), axis=1
    )
    positions = (starts + token_ids % span_len).astype(jnp.float32)
    rotated_q = rotate(queries.astype(jnp.float32), positions).astype(jnp.bfloat16)
    rotated_k = rotate(keys.astype(jnp.float32), positions).astype(jnp.bfloat16)
    core = device_at % 2
    half = head_count // 2
    chip_len = 2 * tok_dev

    def halves(x):
        return (
            lax.dynamic_slice_in_dim(x, core * half, half, 0),
            lax.dynamic_slice_in_dim(x, (1 - core) * half, half, 0),
        )

    def in_order(mine, got, axis):
        return jnp.where(
            core == 0,
            jnp.concatenate([mine, got], axis=axis),
            jnp.concatenate([got, mine], axis=axis),
        )

    q_own = jnp.transpose(rotated_q, (1, 0, 2))
    q_mine, q_other = halves(q_own)
    q_chip = in_order(q_mine, swap(q_other, 1), 1)
    q_places = gather_lines(q_chip)
    groups = lax.axis_size("heads")
    group_at = lax.axis_index("heads")
    share = page_devs // groups
    moves = [
        (i * page_devs + h * share + j, h * page_devs + i * share + j)
        for i in range(groups)
        for h in range(groups)
        for j in range(share)
    ]
    weight_block = lax.ppermute(out_weight, ("heads", "pages"), moves)
    natural = Layout((0, 1, 2))
    all_k = lax.all_gather(rotated_k, "pages", axis=0, tiled=True)
    all_v = lax.all_gather(values, "pages", axis=0, tiled=True)
    all_k = with_layout_constraint(all_k, natural)
    all_v = with_layout_constraint(all_v, natural)
    weights = lax.all_gather(weight_block, "pages", axis=0, tiled=False)

    my_slots = device_at * slot_count + jnp.arange(slot_count, dtype=jnp.int32)
    chip_slots = jnp.concatenate(
        [my_slots, (device_at ^ 1) * slot_count + jnp.arange(slot_count, dtype=jnp.int32)]
    )
    cached_hit = page_table.reshape(-1)[None, :] == chip_slots[:, None]
    fresh_hit = append_slots.reshape(-1)[None, :] == my_slots[:, None]
    table_at = jnp.arange(requests * max_pages, dtype=jnp.int32)
    shown = (table_at % max_pages) * PAGE < jnp.repeat(cache_len, max_pages)
    is_fresh = jnp.any(fresh_hit, axis=1)
    fresh_index = jnp.sum(
        jnp.where(fresh_hit, jnp.arange(requests * new_pages, dtype=jnp.int32)[None, :], 0), axis=1
    )
    slot_key = requests - jnp.sum(
        jnp.where(cached_hit & shown[None, :], requests - (table_at // max_pages)[None, :], 0),
        axis=1,
    )
    slot_at = jnp.arange(2 * slot_count, dtype=jnp.int32)
    earlier = (slot_key[None, :] < slot_key[:, None]) | (
        (slot_key[None, :] == slot_key[:, None]) & (slot_at[None, :] < slot_at[:, None])
    )
    rank = jnp.sum(earlier.astype(jnp.int32), axis=1)
    order = jnp.sum(jnp.where(rank[None, :] == slot_at[:, None], slot_at[None, :], 0), axis=1)
    slot_starts = jnp.sum((slot_key[None, :] < request_grid[:, None]).astype(jnp.int32), axis=1)
    slot_counts = jnp.sum((slot_key[None, :] == request_grid[:, None]).astype(jnp.int32), axis=1)

    k_mine, k_other = halves(jnp.transpose(key_cache, (2, 0, 1, 3)))
    v_mine, v_other = halves(jnp.transpose(value_cache, (2, 0, 3, 1)))
    k_heads = jnp.concatenate([k_mine, swap(k_other, 1)], axis=1)
    v_heads = jnp.concatenate([v_mine, swap(v_other, 1)], axis=1)

    unit = math.gcd(span_len, tok_dev)
    line = page_devs // 4
    line_at, across = device_at // 4, (device_at // 2) % 2
    outs = cached_attention(
        [q for q, _, _, _ in q_places],
        [jnp.clip(at, 0, line - 1) * 2 + side for _, at, side, _ in q_places],
        [ok for _, _, _, ok in q_places],
        [((line_at + k) % line) * 2 + (across ^ d) for k in range(line) for d in range(2)],
        k_heads,
        v_heads,
        order,
        slot_starts,
        slot_counts,
        span_len,
        unit,
        scale2,
    )
    merged = lambda parts, ok: merge(parts, ok, chip_len, unit, scale2)

    def fresh_part():
        chip_at = device_at // 2
        back = -(-(span_len - math.gcd(span_len, chip_len)) // chip_len)
        window = (back + 1) * chip_len
        window_at = jnp.maximum(chip_at - back, 0) * chip_len

        def by_head(rows):
            rows = lax.dynamic_slice(
                rows, (window_at, core * half, 0), (window, half, head_dim)
            )
            return jnp.transpose(rows, (1, 0, 2))

        chip_tokens = chip_at * chip_len + jnp.arange(chip_len, dtype=jnp.int32)
        token_rows = jnp.stack([chip_tokens, chip_tokens // span_len * span_len])
        key_cols = (window_at + jnp.arange(window, dtype=jnp.int32))[:, None]
        return fresh_attention(
            q_chip, by_head(all_k), by_head(all_v), token_rows, key_cols, unit, scale2
        )

    chip_part = merge_lines(
        [outs[2 * k : 2 * k + 2] for k in range(line)], merged, fresh_part
    )
    rows_of = lambda c: lax.dynamic_slice_in_dim(chip_part[:, :chip_len], c * tok_dev, tok_dev, 1)
    own_rows, other_rows = rows_of(core), rows_of(1 - core)
    pieces = []
    for s in range(groups):
        for d, rows in ((0, own_rows), (1, other_rows)):
            if s or d:
                rows = lax.ppermute(
                    rows,
                    ("heads", "pages"),
                    [
                        (h * page_devs + p, (h + s) % groups * page_devs + (p ^ d))
                        for h in range(groups)
                        for p in range(page_devs)
                    ],
                )
            pieces.append(rows)
    hidden = project(pieces, weights, out_bias, core, group_at)
    page_shape = (requests * new_pages, PAGE, head_count, head_dim)
    key_out, value_out = write_pages(
        key_cache,
        value_cache,
        all_k.reshape(page_shape),
        all_v.reshape(page_shape),
        is_fresh,
        fresh_index,
    )
    return (hidden, key_out, value_out)


def solution(mesh):
    placed = (
        P("pages", "heads", None),
        P("pages", "heads", None),
        P("pages", "heads", None),
        P("pages", None, "heads", None),
        P("pages", None, "heads", None),
        P(),
        P(),
        P(),
        P("heads", "pages"),
        P("heads"),
    )
    return jax.shard_map(
        per_device,
        mesh=mesh,
        in_specs=placed,
        out_specs=(
            P("pages", "heads"),
            P("pages", None, "heads", None),
            P("pages", None, "heads", None),
        ),
        check_vma=False,
    )
```

```python
import functools
import math

import jax
import jax.numpy as jnp
from jax import lax
from jax.experimental import pallas as pl
from jax.experimental.pallas import tpu as pltpu
from jax.sharding import PartitionSpec as P

ROT = 32
PAGE = 128
QTILE = 256

low_score = -(2.0**99)


def rotate(vectors, positions):
    half_rot = ROT // 2
    inv_freq = 10000.0 ** (-2.0 * jnp.arange(half_rot, dtype=jnp.float32) / ROT)
    angles = positions[:, None] * inv_freq[None, :]
    cosine = jnp.cos(angles)[:, None, :]
    sine = jnp.sin(angles)[:, None, :]
    first_half = vectors[..., :half_rot]
    second_half = vectors[..., half_rot:ROT]
    return jnp.concatenate(
        [
            first_half * cosine - second_half * sine,
            second_half * cosine + first_half * sine,
            vectors[..., ROT:],
        ],
        axis=-1,
    )


def stat_rows_of(part_len, unit):
    per_unit = -(-unit // 128)
    units = part_len // unit
    return per_unit, units, -(-3 * units * per_unit // 16) * 16


def stat_rows(row):
    unit = row.shape[1]
    full = -(-unit // 128) * 128
    if full > unit:
        row = jnp.concatenate([row, jnp.zeros((1, full - unit), row.dtype)], axis=1)
    return [row[:, at : at + 128] for at in range(0, full, 128)]


def stat_block(kinds, pad_to):
    rows = [piece for kind in kinds for row in kind for piece in stat_rows(row)]
    rows.append(jnp.zeros((pad_to - len(rows), 128), jnp.float32))
    return jnp.concatenate(rows, axis=0).astype(jnp.bfloat16)


def cached_kernel(unit, stat_unit, span, scale2, places, at_ref, ok_ref, order_ref, start_ref, count_ref,
                  *refs):
    q_refs, (k_ref, v_ref), refs = refs[:places], refs[places : places + 2], refs[places + 2 :]
    o_refs, (q_all, o_all, s_all, q_scr, m_scr, l_scr, acc_scr) = refs[:-7], refs[-7:]
    requests = count_ref.shape[0]
    chips, part_len, _ = q_all.shape
    per_part = part_len // unit
    per_request = span // unit
    per_unit, units, pad_to = stat_rows_of(part_len, stat_unit)

    for index in range(places):

        @pl.when(ok_ref[index] > 0)
        def _(index=index):
            q_all[at_ref[index]] = q_refs[index][0]

    def place(at, per_part):
        return at // per_part, at % per_part

    def one_request(request, _):
        for index in range(per_request):
            part, piece = place(request * per_request + index, per_part)
            row = pl.ds(pl.multiple_of(piece * unit, unit), unit)
            q_scr[index * unit : (index + 1) * unit, :] = q_all[part, row, :]
        first = start_ref[request]
        count = count_ref[request]
        m_scr[...] = jnp.full((1, span), low_score, jnp.float32)
        l_scr[...] = jnp.zeros((1, span), jnp.float32)
        acc_scr[...] = jnp.zeros(acc_scr.shape, jnp.float32)

        def pages(slots):
            k = jnp.concatenate([k_ref[0, s] for s in slots], axis=0)
            v = jnp.concatenate([v_ref[0, s] for s in slots], axis=1)
            for c in range(0, span, QTILE):
                cols = slice(c, c + QTILE)
                scores = lax.dot_general(
                    k, q_scr[cols, :], (((1,), (1,)), ((), ())),
                    preferred_element_type=jnp.float32,
                )
                before = m_scr[:, cols]
                peak = jnp.maximum(before, jnp.max(scores, axis=0, keepdims=True))
                weights = jnp.exp2((scores - peak) * scale2)
                fade = jnp.exp2((before - peak) * scale2)
                m_scr[:, cols] = peak
                l_scr[:, cols] = l_scr[:, cols] * fade + jnp.sum(weights, axis=0, keepdims=True)
                acc_scr[:, cols] = acc_scr[:, cols] * fade + jnp.dot(
                    v, weights.astype(jnp.bfloat16), preferred_element_type=jnp.float32
                )

        def pair(index, _):
            at = first + 2 * index
            pages([order_ref[at], order_ref[at + 1]])
            return 0

        lax.fori_loop(0, count // 2, pair, 0)

        @pl.when(count % 2 == 1)
        def _():
            pages([order_ref[first + count - 1]])

        totals = l_scr[...]
        peaks = m_scr[...]
        out = (acc_scr[...] / jnp.maximum(totals, 1e-30)).T.astype(jnp.bfloat16)
        sent = peaks.astype(jnp.bfloat16).astype(jnp.float32)
        totals = totals * jnp.exp2((peaks - sent) * scale2)
        high = totals.astype(jnp.bfloat16).astype(jnp.float32)
        kinds = [sent, high, totals - high]
        for index in range(per_request):
            part, piece = place(request * per_request + index, per_part)
            row = pl.ds(pl.multiple_of(piece * unit, unit), unit)
            o_all[part, row, :] = out[index * unit : (index + 1) * unit, :]
        for index in range(span // stat_unit):
            part, piece = place(request * (span // stat_unit) + index, units)
            cols = slice(index * stat_unit, (index + 1) * stat_unit)
            for kind, values in enumerate(kinds):
                for r, line in enumerate(stat_rows(values[:, cols])):
                    at = (kind * units + piece) * per_unit + r
                    s_all[part, pl.ds(at, 1), :] = line
        return 0

    lax.fori_loop(0, requests, one_request, 0)
    for index in range(chips):
        part = at_ref[places + index]
        o_refs[index][0, :part_len, :] = o_all[part]
        o_refs[index][0, part_len:, :] = s_all[part].astype(jnp.bfloat16)


def cached_attention(q_places, at, ok, out_at, k_heads, v_heads, order, starts, counts, span,
                     stat_unit, scale2):
    places = len(q_places)
    chips = len(out_at)
    heads, part_len, head_dim = q_places[0].shape
    slots = k_heads.shape[1]
    unit = math.gcd(span, part_len)
    _, _, pad_to = stat_rows_of(part_len, stat_unit)
    own_block = lambda *dims: pl.BlockSpec(
        (1,) + dims, lambda h, *_: (h,) + (0,) * len(dims)
    )
    return pl.pallas_call(
        lambda *refs: cached_kernel(unit, stat_unit, span, scale2, places, *refs),
        grid_spec=pltpu.PrefetchScalarGridSpec(
            num_scalar_prefetch=5,
            grid=(heads,),
            in_specs=[own_block(part_len, head_dim)] * places
            + [own_block(slots, PAGE, head_dim), own_block(slots, head_dim, PAGE)],
            out_specs=[own_block(part_len + pad_to, head_dim)] * chips,
            scratch_shapes=[
                pltpu.VMEM((chips, part_len, head_dim), jnp.bfloat16),
                pltpu.VMEM((chips, part_len, head_dim), jnp.bfloat16),
                pltpu.VMEM((chips, pad_to, 128), jnp.float32),
                pltpu.VMEM((span, head_dim), jnp.bfloat16),
                pltpu.VMEM((1, span), jnp.float32),
                pltpu.VMEM((1, span), jnp.float32),
                pltpu.VMEM((head_dim, span), jnp.float32),
            ],
        ),
        out_shape=[
            jax.ShapeDtypeStruct((heads, part_len + pad_to, head_dim), jnp.bfloat16)
        ] * chips,
        compiler_params=pltpu.CompilerParams(vmem_limit_bytes=40 * 2**20),
        cost_estimate=pl.CostEstimate(
            flops=40 * 10**9, bytes_accessed=20 * 2**20, transcendentals=10**7
        ),
        name="cached_attention",
    )(jnp.stack(at + out_at), jnp.stack(ok), order, starts, counts, *q_places, k_heads, v_heads)


def merge_kernel(unit, part_len, scale2, ok_ref, *refs):
    in_refs, out_ref = refs[:-1], refs[-1]
    heads, _, width = out_ref.shape
    _, units, pad_to = stat_rows_of(part_len, unit)
    oks = [ok_ref[index] > 0 for index in range(len(in_refs))]
    for h in range(heads):
        peaks, totals = [], []
        for ok, ref in zip(oks, in_refs):
            stat = ref[h, part_len:, :].astype(jnp.float32)
            peaks.append(jnp.where(ok, stat[:units], low_score))
            total = stat[units : 2 * units] + stat[2 * units : 3 * units]
            totals.append(jnp.where(ok, total, 0.0))
        top = functools.reduce(jnp.maximum, peaks)
        shares = [t * jnp.exp2((p - top) * scale2) for t, p in zip(totals, peaks)]
        total = functools.reduce(jnp.add, shares)
        inverse = 1.0 / jnp.maximum(total, 1e-30)
        merged = [0.0] * units
        for ref, share in zip(in_refs, shares):
            weight = jnp.concatenate(
                [share * inverse, jnp.zeros((-units % 8, 128), jnp.float32)], axis=0
            ).T
            rows = ref[h, :part_len, :].astype(jnp.float32)
            for u in range(units):
                merged[u] = merged[u] + weight[:unit, u : u + 1] * rows[u * unit : (u + 1) * unit]
        high = total.astype(jnp.bfloat16).astype(jnp.float32)
        stats = [top, high, total - high, jnp.zeros((pad_to - 3 * units, width), jnp.float32)]
        out_ref[h, :part_len, :] = jnp.concatenate(merged, axis=0).astype(jnp.bfloat16)
        out_ref[h, part_len:, :] = jnp.concatenate(stats, axis=0).astype(jnp.bfloat16)


def merge(parts, ok, part_len, unit, scale2):
    heads = parts[0].shape[0]
    step = max(1, heads // 2)
    block = pl.BlockSpec((step,) + parts[0].shape[1:], lambda h, *_: (h, 0, 0))
    return pl.pallas_call(
        lambda *refs: merge_kernel(unit, part_len, scale2, *refs),
        grid_spec=pltpu.PrefetchScalarGridSpec(
            num_scalar_prefetch=1,
            grid=(heads // step,),
            in_specs=[block] * len(parts),
            out_specs=block,
        ),
        out_shape=jax.ShapeDtypeStruct(parts[0].shape, jnp.bfloat16),
        name="merge",
    )(jnp.stack(ok).astype(jnp.int32), *parts)


def page_kernel(seg, at_ref, *refs):
    caches, (k_new, v_new), outs = refs[:2], (refs[2:6], refs[6:10]), refs[10:12]
    held, sems = refs[12:14], refs[14]
    slots, page = caches[0].shape[:2]
    pieces = page // seg
    per_block = k_new[0].shape[1] // seg

    def one_slot(slot, _):
        page_at = at_ref[slot]

        @pl.when(page_at < 0)
        def _():
            for i in range(2):
                pltpu.make_async_copy(caches[i].at[slot], held[i].at[slot], sems.at[i]).start()

        @pl.when(page_at >= 0)
        def _():
            for piece in range(pieces):
                at = page_at * pieces + piece
                device = at // per_block
                rows = pl.ds((at % per_block) * seg, seg)
                for k in range(4):

                    @pl.when(device % 4 == (k ^ at_ref[slots]))
                    def _(k=k, piece=piece, device=device, rows=rows):
                        for i, new in enumerate((k_new[k], v_new[k])):
                            pltpu.make_async_copy(
                                new.at[device // 4, rows],
                                held[i].at[slot, pl.ds(piece * seg, seg)],
                                sems.at[i],
                            ).start()

        return 0

    lax.fori_loop(0, slots, one_slot, 0)
    for i in range(2):
        pltpu.make_async_copy(caches[i], held[i], sems.at[i]).wait()
        pltpu.make_async_copy(held[i], outs[i], sems.at[i]).start()
    for i in range(2):
        pltpu.make_async_copy(held[i], outs[i], sems.at[i]).wait()


def write_pages(key_cache, value_cache, new_keys, new_values, page_at, side):
    seg = math.gcd(PAGE, new_keys[0].shape[1])
    anywhere = pl.BlockSpec(memory_space=pl.ANY)
    return pl.pallas_call(
        lambda *refs: page_kernel(seg, *refs),
        grid_spec=pltpu.PrefetchScalarGridSpec(
            num_scalar_prefetch=1,
            grid=(1,),
            in_specs=[anywhere] * 10,
            out_specs=[anywhere] * 2,
            scratch_shapes=[pltpu.VMEM(key_cache.shape, key_cache.dtype)] * 2
            + [pltpu.SemaphoreType.DMA((2,))],
        ),
        out_shape=[jax.ShapeDtypeStruct(key_cache.shape, key_cache.dtype)] * 2,
        compiler_params=pltpu.CompilerParams(vmem_limit_bytes=40 * 2**20),
        name="write_pages",
    )(jnp.concatenate([page_at, side[None]]), key_cache, value_cache, *new_keys, *new_values)


def swap(x, bit):
    devs = lax.axis_size("pages")
    return lax.ppermute(x, "pages", [(p, p ^ bit) for p in range(devs)])


def shift(x, hop, senders):
    devs = lax.axis_size("pages")
    moves = [(p, p + 4 * hop) for p in range(devs) if p // 4 in senders]
    return lax.ppermute(x, "pages", moves)


def gather_line(x):
    line = lax.axis_size("pages") // 4
    groups = [[g + 4 * i for i in range(line)] for g in range(4)]
    return lax.all_gather(x, "pages", axis=0, tiled=False, axis_index_groups=groups)


def gather_lines(x):
    line = lax.axis_size("pages") // 4
    device_at = lax.axis_index("pages")
    at, across = device_at // 4, (device_at // 2) % 2
    always = jnp.int32(1)
    held = [(x, at, across, always), (swap(x, 2), at, 1 - across, always)]
    up = down = x
    for t in range(1, line):
        up = shift(up, 1, range(t - 1, line - 1))
        down = shift(down, -1, range(1, line - t + 1))
        has_up = (at >= t).astype(jnp.int32)
        has_down = (at + t < line).astype(jnp.int32)
        devs = lax.axis_size("pages")
        cross_up = [(p, p ^ 2) for p in range(devs) if p // 4 >= t]
        cross_down = [(p, p ^ 2) for p in range(devs) if p // 4 + t < line]
        held += [
            (up, at - t, across, has_up),
            (lax.ppermute(up, "pages", cross_up), at - t, 1 - across, has_up),
            (down, at + t, across, has_down),
            (lax.ppermute(down, "pages", cross_down), at + t, 1 - across, has_down),
        ]
    return held


def merge_lines(parts, merged, last):
    line = lax.axis_size("pages") // 4
    at = lax.axis_index("pages") // 4
    turns = []
    for t in range(1, line):
        turns += [k for k in (line - t, t) if k not in turns]
    yes = jnp.int32(1)
    crossed = {k: swap(parts[k][1], 2) for k in turns + [0]}
    shares = {}

    def share(k):
        if k not in shares:
            shares[k] = merged([parts[k][0], crossed[k]], [yes, yes])
        return shares[k]

    up = down = None
    for t in range(1, line):
        up_out, down_out = share(line - t), share(t)
        if up is not None:
            up_out = merged([up_out, up], [yes, (at >= 1) & (at <= t - 1)])
            down_out = merged([down_out, down], [yes, (at <= line - 2) & (at >= line - t)])
        up = shift(up_out, 1, range(0, t))
        down = shift(down_out, -1, range(line - t, line))
    own, extra = last(share(0))
    return merged([own, up, down, extra], [yes, at >= 1, at <= line - 2, yes])


def fresh_kernel(unit, scale2, q_ref, *refs):
    k_refs, v_refs = refs[:-3:2], refs[1:-3:2]
    tok_ref, key_ref, o_ref = refs[-3:]
    k = jnp.concatenate([ref[0] for ref in k_refs], axis=0)
    v = jnp.concatenate([ref[0] for ref in v_refs], axis=0)
    token, first, key = tok_ref[0:1, :], tok_ref[1:2, :], key_ref[:, 0:1]
    scores = lax.dot_general(
        k, q_ref[0], (((1,), (1,)), ((), ())), preferred_element_type=jnp.float32
    )
    visible = (key <= token) & (key >= first)
    scores = jnp.where(visible, scores, low_score)
    peak = jnp.max(scores, axis=0, keepdims=True)
    weights = jnp.where(visible, jnp.exp2((scores - peak) * scale2), 0.0)
    totals = jnp.sum(weights, axis=0, keepdims=True)
    out = lax.dot_general(
        v, weights.astype(jnp.bfloat16), (((0,), (0,)), ((), ())),
        preferred_element_type=jnp.float32,
    )
    out = out / totals
    part_len = out.shape[1]
    pad = -part_len % 128
    out = jnp.concatenate([out, jnp.zeros((out.shape[0], pad), jnp.float32)], axis=1)
    o_ref[0, :part_len, :] = out.T[:part_len].astype(jnp.bfloat16)
    sent = peak.astype(jnp.bfloat16).astype(jnp.float32)
    totals = totals * jnp.exp2((peak - sent) * scale2)
    high = totals.astype(jnp.bfloat16).astype(jnp.float32)
    kinds = [
        [values[:, at : at + unit] for at in range(0, part_len, unit)]
        for values in (sent, high, totals - high)
    ]
    o_ref[0, part_len:, :] = stat_block(kinds, o_ref.shape[1] - part_len)


def fresh_attention(q_chip, k_blocks, v_blocks, token_rows, key_cols, unit, scale2):
    heads, part_len, head_dim = q_chip.shape
    _, _, pad_to = stat_rows_of(part_len, unit)
    own = lambda x: pl.BlockSpec((1,) + x.shape[1:], lambda h: (h, 0, 0))
    fixed = lambda x: pl.BlockSpec(x.shape, lambda h: (0, 0))
    blocks = [x for pair in zip(k_blocks, v_blocks) for x in pair]
    return pl.pallas_call(
        lambda *refs: fresh_kernel(unit, scale2, *refs),
        grid=(heads,),
        in_specs=[own(q_chip)]
        + [own(x) for x in blocks]
        + [fixed(token_rows), fixed(key_cols)],
        out_specs=pl.BlockSpec((1, part_len + pad_to, head_dim), lambda h: (h, 0, 0)),
        out_shape=jax.ShapeDtypeStruct((heads, part_len + pad_to, head_dim), jnp.bfloat16),
        compiler_params=pltpu.CompilerParams(vmem_limit_bytes=40 * 2**20),
        name="fresh_attention",
    )(q_chip, *blocks, token_rows, key_cols)


def project_kernel(groups, at_ref, *refs):
    att_refs, w_refs = refs[: 2 * groups], refs[2 * groups : -3]
    bias_ref, out_ref, rows_ref = refs[-3:]
    core = lax.rem(at_ref[0], 2)
    wide = rows_ref.shape[2]

    @pl.when((pl.program_id(0) == 0) & (pl.program_id(1) == 0))
    def _():
        for index, ref in enumerate(att_refs):
            rows_ref[index] = jnp.concatenate([ref[h] for h in range(ref.shape[0])], axis=1)

    for k in range(4):

        @pl.when(pl.program_id(1) == k)
        def _(k=k):
            total = bias_ref[...].reshape(1, -1)
            for s in range(groups):
                for d in range(2):
                    feats = pl.ds(pl.multiple_of((core ^ d) * wide, wide), wide)
                    total = total + jnp.dot(
                        rows_ref[2 * s + d],
                        w_refs[k * groups + s][0, feats, :],
                        preferred_element_type=jnp.float32,
                    )
            out_ref[...] = total.astype(jnp.bfloat16).reshape(out_ref.shape)


def project(pieces, weights, bias, side, group_at):
    groups = len(pieces) // 2
    half, tok_dev, head_dim = pieces[0].shape
    line, feats, cols = weights[0].shape
    share = line // groups
    blocks = share * 4
    wide = cols % 128 == 0
    place = lambda j, k, at: j * 4 + (k ^ at[0])

    def weight_spec(s):
        return pl.BlockSpec(
            (1, feats, cols),
            lambda j, k, at: (lax.rem(at[1] + groups - s, groups) * share + j, 0, 0),
        )

    if wide:
        out_spec = pl.BlockSpec((tok_dev, cols), lambda j, k, at: (0, place(j, k, at)))
        out_shape = (tok_dev, blocks * cols)
    else:
        out_spec = pl.BlockSpec((1, tok_dev, cols), lambda j, k, at: (place(j, k, at), 0, 0))
        out_shape = (blocks, tok_dev, cols)
    out = pl.pallas_call(
        lambda *refs: project_kernel(groups, *refs),
        grid_spec=pltpu.PrefetchScalarGridSpec(
            num_scalar_prefetch=1,
            grid=(share, 4),
            in_specs=[pl.BlockSpec(x.shape, lambda j, k, at: (0, 0, 0)) for x in pieces]
            + [weight_spec(s) for _ in range(4) for s in range(groups)]
            + [pl.BlockSpec((1, 1, cols), lambda j, k, at: (place(j, k, at), 0, 0))],
            out_specs=out_spec,
            scratch_shapes=[pltpu.VMEM((2 * groups, tok_dev, half * head_dim), jnp.bfloat16)],
        ),
        out_shape=jax.ShapeDtypeStruct(out_shape, jnp.bfloat16),
        compiler_params=pltpu.CompilerParams(vmem_limit_bytes=40 * 2**20),
        name="project",
    )(
        jnp.stack([side, group_at]),
        *pieces,
        *[w for w in weights for _ in range(groups)],
        bias.reshape(blocks, 1, cols),
    )
    return out if wide else jnp.transpose(out, (1, 0, 2)).reshape(tok_dev, blocks * cols)


def per_device(
    queries,
    keys,
    values,
    key_cache,
    value_cache,
    cache_len,
    page_table,
    append_slots,
    out_weight,
    out_bias,
):
    tok_dev, head_count, head_dim = queries.shape
    requests = cache_len.shape[0]
    max_pages = page_table.shape[1]
    new_pages = append_slots.shape[1]
    span_len = new_pages * PAGE
    slot_count = key_cache.shape[0]
    tokens = requests * span_len
    page_devs = tokens // tok_dev
    scale2 = math.log2(math.e) / math.sqrt(head_dim)
    device_at = lax.axis_index("pages")
    token_ids = device_at * tok_dev + jnp.arange(tok_dev, dtype=jnp.int32)
    request_ids = token_ids // span_len
    request_grid = jnp.arange(requests, dtype=jnp.int32)
    starts = jnp.sum(
        jnp.where(request_ids[:, None] == request_grid[None, :], cache_len[None, :], 0), axis=1
    )
    positions = (starts + token_ids % span_len).astype(jnp.float32)
    rotated_q = rotate(queries.astype(jnp.float32), positions).astype(jnp.bfloat16)
    rotated_k = rotate(keys.astype(jnp.float32), positions).astype(jnp.bfloat16)
    core = device_at % 2
    half = head_count // 2
    chip_len = 2 * tok_dev

    def halves(x):
        return (
            lax.dynamic_slice_in_dim(x, core * half, half, 0),
            lax.dynamic_slice_in_dim(x, (1 - core) * half, half, 0),
        )

    def in_order(mine, got, axis):
        return jnp.where(
            core == 0,
            jnp.concatenate([mine, got], axis=axis),
            jnp.concatenate([got, mine], axis=axis),
        )

    q_own = jnp.transpose(rotated_q, (1, 0, 2))
    q_mine, q_other = halves(q_own)
    q_chip = in_order(q_mine, swap(q_other, 1), 1)
    q_places = gather_lines(q_chip)
    groups = lax.axis_size("heads")
    group_at = lax.axis_index("heads")
    share = page_devs // groups
    moves = [
        (i * page_devs + h * share + j, h * page_devs + i * share + j)
        for i in range(groups)
        for h in range(groups)
        for j in range(share)
    ]
    side = device_at % 4
    barrier = lax.optimization_barrier
    line_k = gather_line(rotated_k)
    q_blocks, line_k, values, out_weight = barrier(
        ([q for q, _, _, _ in q_places], line_k, values, out_weight)
    )
    across_k = swap(line_k, 2)
    line_v = gather_line(values)
    line_w = gather_line(lax.ppermute(out_weight, ("heads", "pages"), moves))

    my_slots = device_at * slot_count + jnp.arange(slot_count, dtype=jnp.int32)
    chip_slots = jnp.concatenate(
        [my_slots, (device_at ^ 1) * slot_count + jnp.arange(slot_count, dtype=jnp.int32)]
    )
    cached_hit = page_table.reshape(-1)[None, :] == chip_slots[:, None]
    fresh_hit = append_slots.reshape(-1)[None, :] == my_slots[:, None]
    table_at = jnp.arange(requests * max_pages, dtype=jnp.int32)
    shown = (table_at % max_pages) * PAGE < jnp.repeat(cache_len, max_pages)
    is_fresh = jnp.any(fresh_hit, axis=1)
    fresh_index = jnp.sum(
        jnp.where(fresh_hit, jnp.arange(requests * new_pages, dtype=jnp.int32)[None, :], 0), axis=1
    )
    slot_key = requests - jnp.sum(
        jnp.where(cached_hit & shown[None, :], requests - (table_at // max_pages)[None, :], 0),
        axis=1,
    )
    slot_at = jnp.arange(2 * slot_count, dtype=jnp.int32)
    earlier = (slot_key[None, :] < slot_key[:, None]) | (
        (slot_key[None, :] == slot_key[:, None]) & (slot_at[None, :] < slot_at[:, None])
    )
    rank = jnp.sum(earlier.astype(jnp.int32), axis=1)
    order = jnp.sum(jnp.where(rank[None, :] == slot_at[:, None], slot_at[None, :], 0), axis=1)
    slot_starts = jnp.sum((slot_key[None, :] < request_grid[:, None]).astype(jnp.int32), axis=1)
    slot_counts = jnp.sum((slot_key[None, :] == request_grid[:, None]).astype(jnp.int32), axis=1)

    k_mine, k_other = halves(jnp.transpose(key_cache, (2, 0, 1, 3)))
    v_mine, v_other = halves(jnp.transpose(value_cache, (2, 0, 3, 1)))
    k_heads = jnp.concatenate([k_mine, swap(k_other, 1)], axis=1)
    v_heads = jnp.concatenate([v_mine, swap(v_other, 1)], axis=1)

    unit = math.gcd(span_len, tok_dev)
    line = page_devs // 4
    line_at, across = device_at // 4, (device_at // 2) % 2
    outs = cached_attention(
        q_blocks,
        [jnp.clip(at, 0, line - 1) * 2 + side for _, at, side, _ in q_places],
        [ok for _, _, _, ok in q_places],
        [((line_at + k) % line) * 2 + (across ^ d) for k in range(line) for d in range(2)],
        k_heads,
        v_heads,
        order,
        slot_starts,
        slot_counts,
        span_len,
        unit,
        scale2,
    )
    outs, across_k = barrier((outs, across_k))
    merged = lambda parts, ok: merge(parts, ok, chip_len, unit, scale2)
    later = {}

    def fresh_part(own):
        own, here_v, here_w = barrier((own, line_v, line_w))
        across_v = swap(here_v, 2)
        across_v, here_w = barrier((across_v, here_w))
        across_w = swap(here_w, 2)
        all_k = [line_k, swap(line_k, 1), across_k, swap(across_k, 1)]
        all_v = [here_v, swap(here_v, 1), across_v, swap(across_v, 1)]
        later["k"], later["v"] = all_k, all_v
        later["w"] = [here_w, swap(here_w, 1), across_w, swap(across_w, 1)]
        chip_at = device_at // 2
        back = -(-(span_len - math.gcd(span_len, chip_len)) // chip_len)
        blocks, places = [[], []], []
        for step in range(back, -1, -1):
            chip = chip_at - step
            far = (chip % 2) != across
            for d in range(2):
                places.append(jnp.where(chip < 0, tokens, chip * chip_len) + (core ^ d) * tok_dev)
                for found, arrays in zip(blocks, (all_k, all_v)):
                    at = jnp.maximum(chip, 0) // 2
                    if step == 0:
                        block = lax.dynamic_index_in_dim(arrays[d], at, 0, keepdims=False)
                    else:
                        block = jnp.where(
                            far,
                            lax.dynamic_index_in_dim(arrays[2 + d], at, 0, keepdims=False),
                            lax.dynamic_index_in_dim(arrays[d], at, 0, keepdims=False),
                        )
                    block = lax.dynamic_slice_in_dim(block, core * half, half, 1)
                    found.append(jnp.transpose(block, (1, 0, 2)))
        chip_tokens = chip_at * chip_len + jnp.arange(chip_len, dtype=jnp.int32)
        token_rows = jnp.stack([chip_tokens, chip_tokens // span_len * span_len])
        row = jnp.arange(tok_dev, dtype=jnp.int32)
        key_cols = jnp.concatenate([place + row for place in places])[:, None]
        return own, fresh_attention(q_chip, *blocks, token_rows, key_cols, unit, scale2)

    chip_part = merge_lines(
        [outs[2 * k : 2 * k + 2] for k in range(line)], merged, fresh_part
    )
    rows_of = lambda c: lax.dynamic_slice_in_dim(chip_part[:, :chip_len], c * tok_dev, tok_dev, 1)
    own_rows, other_rows = rows_of(core), rows_of(1 - core)
    pieces = []
    for s in range(groups):
        for d, rows in ((0, own_rows), (1, other_rows)):
            if s or d:
                rows = lax.ppermute(
                    rows,
                    ("heads", "pages"),
                    [
                        (h * page_devs + p, (h + s) % groups * page_devs + (p ^ d))
                        for h in range(groups)
                        for p in range(page_devs)
                    ],
                )
            pieces.append(rows)
    hidden = project(pieces, later["w"], out_bias, side, group_at)
    page_at = jnp.where(is_fresh, fresh_index, -1)
    key_out, value_out = write_pages(
        key_cache, value_cache, later["k"], later["v"], page_at, side
    )
    return (hidden, key_out, value_out)


def solution(mesh):
    placed = (
        P("pages", "heads", None),
        P("pages", "heads", None),
        P("pages", "heads", None),
        P("pages", None, "heads", None),
        P("pages", None, "heads", None),
        P(),
        P(),
        P(),
        P("heads", "pages"),
        P("heads"),
    )
    return jax.shard_map(
        per_device,
        mesh=mesh,
        in_specs=placed,
        out_specs=(
            P("pages", "heads"),
            P("pages", None, "heads", None),
            P("pages", None, "heads", None),
        ),
        check_vma=False,
    )
```

```python
import functools
import math

import jax
import jax.numpy as jnp
from jax import lax
from jax.experimental import pallas as pl
from jax.experimental.layout import Layout, with_layout_constraint
from jax.experimental.pallas import tpu as pltpu
from jax.sharding import PartitionSpec as P

ROT = 32
PAGE = 128
QTILE = 256

low_score = -(2.0**99)


def rotate(vectors, positions):
    half_rot = ROT // 2
    inv_freq = 10000.0 ** (-2.0 * jnp.arange(half_rot, dtype=jnp.float32) / ROT)
    angles = positions[:, None] * inv_freq[None, :]
    cosine = jnp.cos(angles)[:, None, :]
    sine = jnp.sin(angles)[:, None, :]
    first_half = vectors[..., :half_rot]
    second_half = vectors[..., half_rot:ROT]
    return jnp.concatenate(
        [
            first_half * cosine - second_half * sine,
            second_half * cosine + first_half * sine,
            vectors[..., ROT:],
        ],
        axis=-1,
    )


def stat_rows_of(part_len, unit):
    per_unit = -(-unit // 128)
    units = part_len // unit
    return per_unit, units, -(-3 * units * per_unit // 16) * 16


def stat_rows(row):
    unit = row.shape[1]
    full = -(-unit // 128) * 128
    if full > unit:
        row = jnp.concatenate([row, jnp.zeros((1, full - unit), row.dtype)], axis=1)
    return [row[:, at : at + 128] for at in range(0, full, 128)]


def stat_block(kinds, pad_to):
    rows = [piece for kind in kinds for row in kind for piece in stat_rows(row)]
    rows.append(jnp.zeros((pad_to - len(rows), 128), jnp.float32))
    return jnp.concatenate(rows, axis=0).astype(jnp.bfloat16)


def cached_kernel(unit, stat_unit, span, scale2, places, at_ref, ok_ref, order_ref, start_ref, count_ref,
                  *refs):
    q_refs, (k_ref, v_ref), refs = refs[:places], refs[places : places + 2], refs[places + 2 :]
    o_refs, (q_all, o_all, s_all, q_scr, m_scr, l_scr, acc_scr) = refs[:-7], refs[-7:]
    requests = count_ref.shape[0]
    chips, part_len, _ = q_all.shape
    per_part = part_len // unit
    per_request = span // unit
    per_unit, units, pad_to = stat_rows_of(part_len, stat_unit)

    for index in range(places):

        @pl.when(ok_ref[index] > 0)
        def _(index=index):
            q_all[at_ref[index]] = q_refs[index][0]

    def place(at, per_part):
        return at // per_part, at % per_part

    def one_request(request, _):
        for index in range(per_request):
            part, piece = place(request * per_request + index, per_part)
            row = pl.ds(pl.multiple_of(piece * unit, unit), unit)
            q_scr[index * unit : (index + 1) * unit, :] = q_all[part, row, :]
        first = start_ref[request]
        count = count_ref[request]
        m_scr[...] = jnp.full((1, span), low_score, jnp.float32)
        l_scr[...] = jnp.zeros((1, span), jnp.float32)
        acc_scr[...] = jnp.zeros(acc_scr.shape, jnp.float32)

        def pages(slots):
            k = jnp.concatenate([k_ref[0, s] for s in slots], axis=0)
            v = jnp.concatenate([v_ref[0, s] for s in slots], axis=1)
            for c in range(0, span, QTILE):
                cols = slice(c, c + QTILE)
                scores = lax.dot_general(
                    k, q_scr[cols, :], (((1,), (1,)), ((), ())),
                    preferred_element_type=jnp.float32,
                )
                before = m_scr[:, cols]
                peak = jnp.maximum(before, jnp.max(scores, axis=0, keepdims=True))
                weights = jnp.exp2((scores - peak) * scale2)
                fade = jnp.exp2((before - peak) * scale2)
                m_scr[:, cols] = peak
                l_scr[:, cols] = l_scr[:, cols] * fade + jnp.sum(weights, axis=0, keepdims=True)
                acc_scr[:, cols] = acc_scr[:, cols] * fade + jnp.dot(
                    v, weights.astype(jnp.bfloat16), preferred_element_type=jnp.float32
                )

        def pair(index, _):
            at = first + 2 * index
            pages([order_ref[at], order_ref[at + 1]])
            return 0

        lax.fori_loop(0, count // 2, pair, 0)

        @pl.when(count % 2 == 1)
        def _():
            pages([order_ref[first + count - 1]])

        totals = l_scr[...]
        peaks = m_scr[...]
        out = (acc_scr[...] / jnp.maximum(totals, 1e-30)).T.astype(jnp.bfloat16)
        sent = peaks.astype(jnp.bfloat16).astype(jnp.float32)
        totals = totals * jnp.exp2((peaks - sent) * scale2)
        high = totals.astype(jnp.bfloat16).astype(jnp.float32)
        kinds = [sent, high, totals - high]
        for index in range(per_request):
            part, piece = place(request * per_request + index, per_part)
            row = pl.ds(pl.multiple_of(piece * unit, unit), unit)
            o_all[part, row, :] = out[index * unit : (index + 1) * unit, :]
        for index in range(span // stat_unit):
            part, piece = place(request * (span // stat_unit) + index, units)
            cols = slice(index * stat_unit, (index + 1) * stat_unit)
            for kind, values in enumerate(kinds):
                for r, line in enumerate(stat_rows(values[:, cols])):
                    at = (kind * units + piece) * per_unit + r
                    s_all[part, pl.ds(at, 1), :] = line
        return 0

    lax.fori_loop(0, requests, one_request, 0)
    for index in range(chips):
        part = at_ref[places + index]
        o_refs[index][0, :part_len, :] = o_all[part]
        o_refs[index][0, part_len:, :] = s_all[part].astype(jnp.bfloat16)


def cached_attention(q_places, at, ok, out_at, k_heads, v_heads, order, starts, counts, span,
                     stat_unit, scale2):
    places = len(q_places)
    chips = len(out_at)
    heads, part_len, head_dim = q_places[0].shape
    slots = k_heads.shape[1]
    unit = math.gcd(span, part_len)
    _, _, pad_to = stat_rows_of(part_len, stat_unit)
    own_block = lambda *dims: pl.BlockSpec(
        (1,) + dims, lambda h, *_: (h,) + (0,) * len(dims)
    )
    return pl.pallas_call(
        lambda *refs: cached_kernel(unit, stat_unit, span, scale2, places, *refs),
        grid_spec=pltpu.PrefetchScalarGridSpec(
            num_scalar_prefetch=5,
            grid=(heads,),
            in_specs=[own_block(part_len, head_dim)] * places
            + [own_block(slots, PAGE, head_dim), own_block(slots, head_dim, PAGE)],
            out_specs=[own_block(part_len + pad_to, head_dim)] * chips,
            scratch_shapes=[
                pltpu.VMEM((chips, part_len, head_dim), jnp.bfloat16),
                pltpu.VMEM((chips, part_len, head_dim), jnp.bfloat16),
                pltpu.VMEM((chips, pad_to, 128), jnp.float32),
                pltpu.VMEM((span, head_dim), jnp.bfloat16),
                pltpu.VMEM((1, span), jnp.float32),
                pltpu.VMEM((1, span), jnp.float32),
                pltpu.VMEM((head_dim, span), jnp.float32),
            ],
        ),
        out_shape=[
            jax.ShapeDtypeStruct((heads, part_len + pad_to, head_dim), jnp.bfloat16)
        ] * chips,
        compiler_params=pltpu.CompilerParams(vmem_limit_bytes=60 * 2**20),
        cost_estimate=pl.CostEstimate(
            flops=40 * 10**9, bytes_accessed=20 * 2**20, transcendentals=10**7
        ),
        name="cached_attention",
    )(jnp.stack(at + out_at), jnp.stack(ok), order, starts, counts, *q_places, k_heads, v_heads)


def merge_kernel(unit, part_len, scale2, ok_ref, *refs):
    in_refs, out_ref = refs[:-1], refs[-1]
    heads, _, width = out_ref.shape
    _, units, pad_to = stat_rows_of(part_len, unit)
    oks = [ok_ref[index] > 0 for index in range(len(in_refs))]
    for h in range(heads):
        peaks, totals = [], []
        for ok, ref in zip(oks, in_refs):
            stat = ref[h, part_len:, :].astype(jnp.float32)
            peaks.append(jnp.where(ok, stat[:units], low_score))
            total = stat[units : 2 * units] + stat[2 * units : 3 * units]
            totals.append(jnp.where(ok, total, 0.0))
        top = functools.reduce(jnp.maximum, peaks)
        shares = [t * jnp.exp2((p - top) * scale2) for t, p in zip(totals, peaks)]
        total = functools.reduce(jnp.add, shares)
        inverse = 1.0 / jnp.maximum(total, 1e-30)
        merged = [0.0] * units
        for ref, share in zip(in_refs, shares):
            weight = jnp.concatenate(
                [share * inverse, jnp.zeros((-units % 8, 128), jnp.float32)], axis=0
            ).T
            rows = ref[h, :part_len, :].astype(jnp.float32)
            for u in range(units):
                merged[u] = merged[u] + weight[:unit, u : u + 1] * rows[u * unit : (u + 1) * unit]
        high = total.astype(jnp.bfloat16).astype(jnp.float32)
        stats = [top, high, total - high, jnp.zeros((pad_to - 3 * units, width), jnp.float32)]
        out_ref[h, :part_len, :] = jnp.concatenate(merged, axis=0).astype(jnp.bfloat16)
        out_ref[h, part_len:, :] = jnp.concatenate(stats, axis=0).astype(jnp.bfloat16)


def merge(parts, ok, part_len, unit, scale2):
    heads = parts[0].shape[0]
    step = max(1, heads // 2)
    block = pl.BlockSpec((step,) + parts[0].shape[1:], lambda h, *_: (h, 0, 0))
    return pl.pallas_call(
        lambda *refs: merge_kernel(unit, part_len, scale2, *refs),
        grid_spec=pltpu.PrefetchScalarGridSpec(
            num_scalar_prefetch=1,
            grid=(heads // step,),
            in_specs=[block] * len(parts),
            out_specs=block,
        ),
        out_shape=jax.ShapeDtypeStruct(parts[0].shape, jnp.bfloat16),
        name="merge",
    )(jnp.stack(ok).astype(jnp.int32), *parts)


def page_kernel(fresh_ref, index_ref, kc_ref, vc_ref, kn_ref, vn_ref, ko_ref, vo_ref):
    fresh = fresh_ref[pl.program_id(0)] > 0

    @pl.when(fresh)
    def _():
        ko_ref[...] = kn_ref[...]
        vo_ref[...] = vn_ref[...]

    @pl.when(jnp.logical_not(fresh))
    def _():
        ko_ref[...] = kc_ref[...]
        vo_ref[...] = vc_ref[...]


def write_pages(key_cache, value_cache, new_keys, new_values, is_fresh, fresh_index):
    block = (1,) + key_cache.shape[1:]
    own = pl.BlockSpec(block, lambda s, fresh, index: (s, 0, 0, 0))
    new = pl.BlockSpec(block, lambda s, fresh, index: (index[s], 0, 0, 0))
    return pl.pallas_call(
        page_kernel,
        grid_spec=pltpu.PrefetchScalarGridSpec(
            num_scalar_prefetch=2,
            grid=(key_cache.shape[0],),
            in_specs=[own, own, new, new],
            out_specs=[own, own],
        ),
        out_shape=[jax.ShapeDtypeStruct(key_cache.shape, key_cache.dtype)] * 2,
        compiler_params=pltpu.CompilerParams(vmem_limit_bytes=40 * 2**20),
        name="write_pages",
    )(is_fresh.astype(jnp.int32), fresh_index, key_cache, value_cache, new_keys, new_values)


def swap(x, bit):
    devs = lax.axis_size("pages")
    return lax.ppermute(x, "pages", [(p, p ^ bit) for p in range(devs)])


def shift(x, hop, senders):
    devs = lax.axis_size("pages")
    moves = [(p, p + 4 * hop) for p in range(devs) if p // 4 in senders]
    return lax.ppermute(x, "pages", moves)


def gather_lines(x):
    line = lax.axis_size("pages") // 4
    device_at = lax.axis_index("pages")
    at, across = device_at // 4, (device_at // 2) % 2
    always = jnp.int32(1)
    held = [(x, at, across, always), (swap(x, 2), at, 1 - across, always)]
    up = down = x
    for t in range(1, line):
        up = shift(up, 1, range(t - 1, line - 1))
        down = shift(down, -1, range(1, line - t + 1))
        has_up = (at >= t).astype(jnp.int32)
        has_down = (at + t < line).astype(jnp.int32)
        devs = lax.axis_size("pages")
        cross_up = [(p, p ^ 2) for p in range(devs) if p // 4 >= t]
        cross_down = [(p, p ^ 2) for p in range(devs) if p // 4 + t < line]
        held += [
            (up, at - t, across, has_up),
            (lax.ppermute(up, "pages", cross_up), at - t, 1 - across, has_up),
            (down, at + t, across, has_down),
            (lax.ppermute(down, "pages", cross_down), at + t, 1 - across, has_down),
        ]
    return held


def merge_lines(parts, merged, last):
    line = lax.axis_size("pages") // 4
    at = lax.axis_index("pages") // 4
    turns = []
    for t in range(1, line):
        turns += [k for k in (line - t, t) if k not in turns]
    yes = jnp.int32(1)
    crossed = {k: swap(parts[k][1], 2) for k in turns + [0]}
    shares = {}

    def share(k):
        if k not in shares:
            shares[k] = merged([parts[k][0], crossed[k]], [yes, yes])
        return shares[k]

    up = down = None
    for t in range(1, line):
        up_out, down_out = share(line - t), share(t)
        if up is not None:
            up_out = merged([up_out, up], [yes, (at >= 1) & (at <= t - 1)])
            down_out = merged([down_out, down], [yes, (at <= line - 2) & (at >= line - t)])
        up = shift(up_out, 1, range(0, t))
        down = shift(down_out, -1, range(line - t, line))
    return merged([share(0), up, down, last()], [yes, at >= 1, at <= line - 2, yes])


def fresh_kernel(unit, scale2, q_ref, k_ref, v_ref, tok_ref, key_ref, o_ref):
    token, first, key = tok_ref[0:1, :], tok_ref[1:2, :], key_ref[:, 0:1]
    scores = lax.dot_general(
        k_ref[0], q_ref[0], (((1,), (1,)), ((), ())), preferred_element_type=jnp.float32
    )
    visible = (key <= token) & (key >= first)
    scores = jnp.where(visible, scores, low_score)
    peak = jnp.max(scores, axis=0, keepdims=True)
    weights = jnp.where(visible, jnp.exp2((scores - peak) * scale2), 0.0)
    totals = jnp.sum(weights, axis=0, keepdims=True)
    out = lax.dot_general(
        v_ref[0], weights.astype(jnp.bfloat16), (((0,), (0,)), ((), ())),
        preferred_element_type=jnp.float32,
    )
    out = out / totals
    part_len = out.shape[1]
    pad = -part_len % 128
    out = jnp.concatenate([out, jnp.zeros((out.shape[0], pad), jnp.float32)], axis=1)
    o_ref[0, :part_len, :] = out.T[:part_len].astype(jnp.bfloat16)
    sent = peak.astype(jnp.bfloat16).astype(jnp.float32)
    totals = totals * jnp.exp2((peak - sent) * scale2)
    high = totals.astype(jnp.bfloat16).astype(jnp.float32)
    kinds = [
        [values[:, at : at + unit] for at in range(0, part_len, unit)]
        for values in (sent, high, totals - high)
    ]
    o_ref[0, part_len:, :] = stat_block(kinds, o_ref.shape[1] - part_len)


def fresh_attention(q_chip, k_window, v_window, token_rows, key_cols, unit, scale2):
    heads, part_len, head_dim = q_chip.shape
    _, _, pad_to = stat_rows_of(part_len, unit)
    own = lambda x: pl.BlockSpec((1,) + x.shape[1:], lambda h: (h, 0, 0))
    fixed = lambda x: pl.BlockSpec(x.shape, lambda h: (0, 0))
    return pl.pallas_call(
        lambda *refs: fresh_kernel(unit, scale2, *refs),
        grid=(heads,),
        in_specs=[own(q_chip), own(k_window), own(v_window), fixed(token_rows), fixed(key_cols)],
        out_specs=pl.BlockSpec((1, part_len + pad_to, head_dim), lambda h: (h, 0, 0)),
        out_shape=jax.ShapeDtypeStruct((heads, part_len + pad_to, head_dim), jnp.bfloat16),
        compiler_params=pltpu.CompilerParams(vmem_limit_bytes=40 * 2**20),
        name="fresh_attention",
    )(q_chip, k_window, v_window, token_rows, key_cols)


def project_kernel(groups, at_ref, *refs):
    att_refs, w_refs = refs[: 2 * groups], refs[2 * groups : -3]
    bias_ref, out_ref, rows_ref = refs[-3:]
    core = at_ref[0]
    wide = rows_ref.shape[2]

    @pl.when(pl.program_id(0) == 0)
    def _():
        for index, ref in enumerate(att_refs):
            rows_ref[index] = jnp.concatenate([ref[h] for h in range(ref.shape[0])], axis=1)

    total = bias_ref[...].reshape(1, -1)
    for s in range(groups):
        for d in range(2):
            feats = pl.ds(pl.multiple_of((core ^ d) * wide, wide), wide)
            total = total + jnp.dot(
                rows_ref[2 * s + d], w_refs[s][0, feats, :], preferred_element_type=jnp.float32
            )
    out_ref[...] = total.astype(jnp.bfloat16).reshape(out_ref.shape)


def project(pieces, weights, bias, core, group_at):
    groups = len(pieces) // 2
    half, tok_dev, head_dim = pieces[0].shape
    blocks, feats, cols = weights.shape
    blocks //= groups
    wide = cols % 128 == 0

    def weight_spec(s):
        return pl.BlockSpec(
            (1, feats, cols),
            lambda j, at: (lax.rem(at[1] + groups - s, groups) * blocks + j, 0, 0),
        )

    if wide:
        out_spec = pl.BlockSpec((tok_dev, cols), lambda j, at: (0, j))
        out_shape = (tok_dev, blocks * cols)
    else:
        out_spec = pl.BlockSpec((1, tok_dev, cols), lambda j, at: (j, 0, 0))
        out_shape = (blocks, tok_dev, cols)
    out = pl.pallas_call(
        lambda *refs: project_kernel(groups, *refs),
        grid_spec=pltpu.PrefetchScalarGridSpec(
            num_scalar_prefetch=1,
            grid=(blocks,),
            in_specs=[pl.BlockSpec(x.shape, lambda j, at: (0, 0, 0)) for x in pieces]
            + [weight_spec(s) for s in range(groups)]
            + [pl.BlockSpec((1, 1, cols), lambda j, at: (j, 0, 0))],
            out_specs=out_spec,
            scratch_shapes=[pltpu.VMEM((2 * groups, tok_dev, half * head_dim), jnp.bfloat16)],
        ),
        out_shape=jax.ShapeDtypeStruct(out_shape, jnp.bfloat16),
        compiler_params=pltpu.CompilerParams(vmem_limit_bytes=40 * 2**20),
        name="project",
    )(
        jnp.stack([core, group_at]),
        *pieces,
        *[weights] * groups,
        bias.reshape(blocks, 1, cols),
    )
    return out if wide else jnp.transpose(out, (1, 0, 2)).reshape(tok_dev, blocks * cols)


def per_device(
    queries,
    keys,
    values,
    key_cache,
    value_cache,
    cache_len,
    page_table,
    append_slots,
    out_weight,
    out_bias,
):
    tok_dev, head_count, head_dim = queries.shape
    requests = cache_len.shape[0]
    max_pages = page_table.shape[1]
    new_pages = append_slots.shape[1]
    span_len = new_pages * PAGE
    slot_count = key_cache.shape[0]
    tokens = requests * span_len
    page_devs = tokens // tok_dev
    scale2 = math.log2(math.e) / math.sqrt(head_dim)
    device_at = lax.axis_index("pages")
    token_ids = device_at * tok_dev + jnp.arange(tok_dev, dtype=jnp.int32)
    request_ids = token_ids // span_len
    request_grid = jnp.arange(requests, dtype=jnp.int32)
    starts = jnp.sum(
        jnp.where(request_ids[:, None] == request_grid[None, :], cache_len[None, :], 0), axis=1
    )
    positions = (starts + token_ids % span_len).astype(jnp.float32)
    rotated_q = rotate(queries.astype(jnp.float32), positions).astype(jnp.bfloat16)
    rotated_k = rotate(keys.astype(jnp.float32), positions).astype(jnp.bfloat16)
    core = device_at % 2
    half = head_count // 2
    chip_len = 2 * tok_dev

    def halves(x):
        return (
            lax.dynamic_slice_in_dim(x, core * half, half, 0),
            lax.dynamic_slice_in_dim(x, (1 - core) * half, half, 0),
        )

    def in_order(mine, got, axis):
        return jnp.where(
            core == 0,
            jnp.concatenate([mine, got], axis=axis),
            jnp.concatenate([got, mine], axis=axis),
        )

    q_own = jnp.transpose(rotated_q, (1, 0, 2))
    q_mine, q_other = halves(q_own)
    q_chip = in_order(q_mine, swap(q_other, 1), 1)
    q_places = gather_lines(q_chip)
    groups = lax.axis_size("heads")
    group_at = lax.axis_index("heads")
    share = page_devs // groups
    moves = [
        (i * page_devs + h * share + j, h * page_devs + i * share + j)
        for i in range(groups)
        for h in range(groups)
        for j in range(share)
    ]
    q_blocks, out_weight = lax.optimization_barrier(
        ([q for q, _, _, _ in q_places], out_weight)
    )
    weight_block = lax.ppermute(out_weight, ("heads", "pages"), moves)
    natural = Layout((0, 1, 2))
    all_k = lax.all_gather(rotated_k, "pages", axis=0, tiled=True)
    all_v = lax.all_gather(values, "pages", axis=0, tiled=True)
    all_k = with_layout_constraint(all_k, natural)
    all_v = with_layout_constraint(all_v, natural)
    weights = lax.all_gather(weight_block, "pages", axis=0, tiled=False)

    my_slots = device_at * slot_count + jnp.arange(slot_count, dtype=jnp.int32)
    chip_slots = jnp.concatenate(
        [my_slots, (device_at ^ 1) * slot_count + jnp.arange(slot_count, dtype=jnp.int32)]
    )
    cached_hit = page_table.reshape(-1)[None, :] == chip_slots[:, None]
    fresh_hit = append_slots.reshape(-1)[None, :] == my_slots[:, None]
    table_at = jnp.arange(requests * max_pages, dtype=jnp.int32)
    shown = (table_at % max_pages) * PAGE < jnp.repeat(cache_len, max_pages)
    is_fresh = jnp.any(fresh_hit, axis=1)
    fresh_index = jnp.sum(
        jnp.where(fresh_hit, jnp.arange(requests * new_pages, dtype=jnp.int32)[None, :], 0), axis=1
    )
    slot_key = requests - jnp.sum(
        jnp.where(cached_hit & shown[None, :], requests - (table_at // max_pages)[None, :], 0),
        axis=1,
    )
    slot_at = jnp.arange(2 * slot_count, dtype=jnp.int32)
    earlier = (slot_key[None, :] < slot_key[:, None]) | (
        (slot_key[None, :] == slot_key[:, None]) & (slot_at[None, :] < slot_at[:, None])
    )
    rank = jnp.sum(earlier.astype(jnp.int32), axis=1)
    order = jnp.sum(jnp.where(rank[None, :] == slot_at[:, None], slot_at[None, :], 0), axis=1)
    slot_starts = jnp.sum((slot_key[None, :] < request_grid[:, None]).astype(jnp.int32), axis=1)
    slot_counts = jnp.sum((slot_key[None, :] == request_grid[:, None]).astype(jnp.int32), axis=1)

    k_mine, k_other = halves(jnp.transpose(key_cache, (2, 0, 1, 3)))
    v_mine, v_other = halves(jnp.transpose(value_cache, (2, 0, 3, 1)))
    k_heads = jnp.concatenate([k_mine, swap(k_other, 1)], axis=1)
    v_heads = jnp.concatenate([v_mine, swap(v_other, 1)], axis=1)

    unit = math.gcd(span_len, tok_dev)
    line = page_devs // 4
    line_at, across = device_at // 4, (device_at // 2) % 2
    outs = cached_attention(
        q_blocks,
        [jnp.clip(at, 0, line - 1) * 2 + side for _, at, side, _ in q_places],
        [ok for _, _, _, ok in q_places],
        [((line_at + k) % line) * 2 + (across ^ d) for k in range(line) for d in range(2)],
        k_heads,
        v_heads,
        order,
        slot_starts,
        slot_counts,
        span_len,
        unit,
        scale2,
    )
    merged = lambda parts, ok: merge(parts, ok, chip_len, unit, scale2)

    def fresh_part():
        chip_at = device_at // 2
        back = -(-(span_len - math.gcd(span_len, chip_len)) // chip_len)
        window = (back + 1) * chip_len
        window_at = jnp.maximum(chip_at - back, 0) * chip_len

        def by_head(rows):
            rows = lax.dynamic_slice(
                rows, (window_at, core * half, 0), (window, half, head_dim)
            )
            return jnp.transpose(rows, (1, 0, 2))

        chip_tokens = chip_at * chip_len + jnp.arange(chip_len, dtype=jnp.int32)
        token_rows = jnp.stack([chip_tokens, chip_tokens // span_len * span_len])
        key_cols = (window_at + jnp.arange(window, dtype=jnp.int32))[:, None]
        return fresh_attention(
            q_chip, by_head(all_k), by_head(all_v), token_rows, key_cols, unit, scale2
        )

    chip_part = merge_lines(
        [outs[2 * k : 2 * k + 2] for k in range(line)], merged, fresh_part
    )
    rows_of = lambda c: lax.dynamic_slice_in_dim(chip_part[:, :chip_len], c * tok_dev, tok_dev, 1)
    own_rows, other_rows = rows_of(core), rows_of(1 - core)
    pieces = []
    for s in range(groups):
        for d, rows in ((0, own_rows), (1, other_rows)):
            if s or d:
                rows = lax.ppermute(
                    rows,
                    ("heads", "pages"),
                    [
                        (h * page_devs + p, (h + s) % groups * page_devs + (p ^ d))
                        for h in range(groups)
                        for p in range(page_devs)
                    ],
                )
            pieces.append(rows)
    hidden = project(pieces, weights, out_bias, core, group_at)
    page_shape = (requests * new_pages, PAGE, head_count, head_dim)
    key_out, value_out = write_pages(
        key_cache,
        value_cache,
        all_k.reshape(page_shape),
        all_v.reshape(page_shape),
        is_fresh,
        fresh_index,
    )
    return (hidden, key_out, value_out)


def solution(mesh):
    placed = (
        P("pages", "heads", None),
        P("pages", "heads", None),
        P("pages", "heads", None),
        P("pages", None, "heads", None),
        P("pages", None, "heads", None),
        P(),
        P(),
        P(),
        P("heads", "pages"),
        P("heads"),
    )
    return jax.shard_map(
        per_device,
        mesh=mesh,
        in_specs=placed,
        out_specs=(
            P("pages", "heads"),
            P("pages", None, "heads", None),
            P("pages", None, "heads", None),
        ),
        check_vma=False,
    )
```

```python
import functools
import math

import jax
import jax.numpy as jnp
from jax import lax
from jax.experimental import pallas as pl
from jax.experimental.layout import Layout, with_layout_constraint
from jax.experimental.pallas import tpu as pltpu
from jax.sharding import PartitionSpec as P

ROT = 32
PAGE = 128
QTILE = 256

low_score = -(2.0**99)


def rotate(vectors, positions):
    half_rot = ROT // 2
    inv_freq = 10000.0 ** (-2.0 * jnp.arange(half_rot, dtype=jnp.float32) / ROT)
    angles = positions[:, None] * inv_freq[None, :]
    cosine = jnp.cos(angles)[:, None, :]
    sine = jnp.sin(angles)[:, None, :]
    first_half = vectors[..., :half_rot]
    second_half = vectors[..., half_rot:ROT]
    return jnp.concatenate(
        [
            first_half * cosine - second_half * sine,
            second_half * cosine + first_half * sine,
            vectors[..., ROT:],
        ],
        axis=-1,
    )


def stat_rows_of(part_len, unit):
    per_unit = -(-unit // 128)
    units = part_len // unit
    return per_unit, units, -(-3 * units * per_unit // 16) * 16


def stat_rows(row):
    unit = row.shape[1]
    full = -(-unit // 128) * 128
    if full > unit:
        row = jnp.concatenate([row, jnp.zeros((1, full - unit), row.dtype)], axis=1)
    return [row[:, at : at + 128] for at in range(0, full, 128)]


def stat_block(kinds, pad_to):
    rows = [piece for kind in kinds for row in kind for piece in stat_rows(row)]
    rows.append(jnp.zeros((pad_to - len(rows), 128), jnp.float32))
    return jnp.concatenate(rows, axis=0).astype(jnp.bfloat16)


def cached_kernel(unit, stat_unit, span, scale2, places, at_ref, ok_ref, order_ref, start_ref, count_ref,
                  *refs):
    q_refs, (k_ref, v_ref), refs = refs[:places], refs[places : places + 2], refs[places + 2 :]
    o_refs, (q_all, o_all, s_all, q_scr, m_scr, l_scr, acc_scr) = refs[:-7], refs[-7:]
    requests = count_ref.shape[0]
    chips, part_len, _ = q_all.shape
    per_part = part_len // unit
    per_request = span // unit
    per_unit, units, pad_to = stat_rows_of(part_len, stat_unit)

    for index in range(places):

        @pl.when(ok_ref[index] > 0)
        def _(index=index):
            q_all[at_ref[index]] = q_refs[index][0]

    def place(at, per_part):
        return at // per_part, at % per_part

    def one_request(request, _):
        for index in range(per_request):
            part, piece = place(request * per_request + index, per_part)
            row = pl.ds(pl.multiple_of(piece * unit, unit), unit)
            q_scr[index * unit : (index + 1) * unit, :] = q_all[part, row, :]
        first = start_ref[request]
        count = count_ref[request]
        m_scr[...] = jnp.full((1, span), low_score, jnp.float32)
        l_scr[...] = jnp.zeros((1, span), jnp.float32)
        acc_scr[...] = jnp.zeros(acc_scr.shape, jnp.float32)

        def pages(slots):
            k = jnp.concatenate([k_ref[0, s] for s in slots], axis=0)
            v = jnp.concatenate([v_ref[0, s] for s in slots], axis=1)
            for c in range(0, span, QTILE):
                cols = slice(c, c + QTILE)
                scores = lax.dot_general(
                    k, q_scr[cols, :], (((1,), (1,)), ((), ())),
                    preferred_element_type=jnp.float32,
                )
                before = m_scr[:, cols]
                peak = jnp.maximum(before, jnp.max(scores, axis=0, keepdims=True))
                weights = jnp.exp2((scores - peak) * scale2)
                fade = jnp.exp2((before - peak) * scale2)
                m_scr[:, cols] = peak
                l_scr[:, cols] = l_scr[:, cols] * fade + jnp.sum(weights, axis=0, keepdims=True)
                acc_scr[:, cols] = acc_scr[:, cols] * fade + jnp.dot(
                    v, weights.astype(jnp.bfloat16), preferred_element_type=jnp.float32
                )

        def pair(index, _):
            at = first + 2 * index
            pages([order_ref[at], order_ref[at + 1]])
            return 0

        lax.fori_loop(0, count // 2, pair, 0)

        @pl.when(count % 2 == 1)
        def _():
            pages([order_ref[first + count - 1]])

        totals = l_scr[...]
        peaks = m_scr[...]
        out = (acc_scr[...] / jnp.maximum(totals, 1e-30)).T.astype(jnp.bfloat16)
        sent = peaks.astype(jnp.bfloat16).astype(jnp.float32)
        totals = totals * jnp.exp2((peaks - sent) * scale2)
        high = totals.astype(jnp.bfloat16).astype(jnp.float32)
        kinds = [sent, high, totals - high]
        for index in range(per_request):
            part, piece = place(request * per_request + index, per_part)
            row = pl.ds(pl.multiple_of(piece * unit, unit), unit)
            o_all[part, row, :] = out[index * unit : (index + 1) * unit, :]
        for index in range(span // stat_unit):
            part, piece = place(request * (span // stat_unit) + index, units)
            cols = slice(index * stat_unit, (index + 1) * stat_unit)
            for kind, values in enumerate(kinds):
                for r, line in enumerate(stat_rows(values[:, cols])):
                    at = (kind * units + piece) * per_unit + r
                    s_all[part, pl.ds(at, 1), :] = line
        return 0

    lax.fori_loop(0, requests, one_request, 0)
    for index in range(chips):
        part = at_ref[places + index]
        o_refs[index][0, :part_len, :] = o_all[part]
        o_refs[index][0, part_len:, :] = s_all[part].astype(jnp.bfloat16)


def cached_attention(q_places, at, ok, out_at, k_heads, v_heads, order, starts, counts, span,
                     stat_unit, scale2):
    places = len(q_places)
    chips = len(out_at)
    heads, part_len, head_dim = q_places[0].shape
    slots = k_heads.shape[1]
    unit = math.gcd(span, part_len)
    _, _, pad_to = stat_rows_of(part_len, stat_unit)
    own_block = lambda *dims: pl.BlockSpec(
        (1,) + dims, lambda h, *_: (h,) + (0,) * len(dims)
    )
    return pl.pallas_call(
        lambda *refs: cached_kernel(unit, stat_unit, span, scale2, places, *refs),
        grid_spec=pltpu.PrefetchScalarGridSpec(
            num_scalar_prefetch=5,
            grid=(heads,),
            in_specs=[own_block(part_len, head_dim)] * places
            + [own_block(slots, PAGE, head_dim), own_block(slots, head_dim, PAGE)],
            out_specs=[own_block(part_len + pad_to, head_dim)] * chips,
            scratch_shapes=[
                pltpu.VMEM((chips, part_len, head_dim), jnp.bfloat16),
                pltpu.VMEM((chips, part_len, head_dim), jnp.bfloat16),
                pltpu.VMEM((chips, pad_to, 128), jnp.float32),
                pltpu.VMEM((span, head_dim), jnp.bfloat16),
                pltpu.VMEM((1, span), jnp.float32),
                pltpu.VMEM((1, span), jnp.float32),
                pltpu.VMEM((head_dim, span), jnp.float32),
            ],
        ),
        out_shape=[
            jax.ShapeDtypeStruct((heads, part_len + pad_to, head_dim), jnp.bfloat16)
        ] * chips,
        compiler_params=pltpu.CompilerParams(vmem_limit_bytes=60 * 2**20),
        cost_estimate=pl.CostEstimate(
            flops=40 * 10**9, bytes_accessed=20 * 2**20, transcendentals=10**7
        ),
        name="cached_attention",
    )(jnp.stack(at + out_at), jnp.stack(ok), order, starts, counts, *q_places, k_heads, v_heads)


def merge_kernel(unit, part_len, scale2, ok_ref, *refs):
    in_refs, out_ref = refs[:-1], refs[-1]
    heads, _, width = out_ref.shape
    _, units, pad_to = stat_rows_of(part_len, unit)
    oks = [ok_ref[index] > 0 for index in range(len(in_refs))]
    for h in range(heads):
        peaks, totals = [], []
        for ok, ref in zip(oks, in_refs):
            stat = ref[h, part_len:, :].astype(jnp.float32)
            peaks.append(jnp.where(ok, stat[:units], low_score))
            total = stat[units : 2 * units] + stat[2 * units : 3 * units]
            totals.append(jnp.where(ok, total, 0.0))
        top = functools.reduce(jnp.maximum, peaks)
        shares = [t * jnp.exp2((p - top) * scale2) for t, p in zip(totals, peaks)]
        total = functools.reduce(jnp.add, shares)
        inverse = 1.0 / jnp.maximum(total, 1e-30)
        merged = [0.0] * units
        for ref, share in zip(in_refs, shares):
            weight = jnp.concatenate(
                [share * inverse, jnp.zeros((-units % 8, 128), jnp.float32)], axis=0
            ).T
            rows = ref[h, :part_len, :].astype(jnp.float32)
            for u in range(units):
                merged[u] = merged[u] + weight[:unit, u : u + 1] * rows[u * unit : (u + 1) * unit]
        high = total.astype(jnp.bfloat16).astype(jnp.float32)
        stats = [top, high, total - high, jnp.zeros((pad_to - 3 * units, width), jnp.float32)]
        out_ref[h, :part_len, :] = jnp.concatenate(merged, axis=0).astype(jnp.bfloat16)
        out_ref[h, part_len:, :] = jnp.concatenate(stats, axis=0).astype(jnp.bfloat16)


def merge(parts, ok, part_len, unit, scale2):
    heads = parts[0].shape[0]
    step = max(1, heads // 2)
    block = pl.BlockSpec((step,) + parts[0].shape[1:], lambda h, *_: (h, 0, 0))
    return pl.pallas_call(
        lambda *refs: merge_kernel(unit, part_len, scale2, *refs),
        grid_spec=pltpu.PrefetchScalarGridSpec(
            num_scalar_prefetch=1,
            grid=(heads // step,),
            in_specs=[block] * len(parts),
            out_specs=block,
        ),
        out_shape=jax.ShapeDtypeStruct(parts[0].shape, jnp.bfloat16),
        name="merge",
    )(jnp.stack(ok).astype(jnp.int32), *parts)


def page_kernel(fresh_ref, index_ref, kc_ref, vc_ref, kn_ref, vn_ref, ko_ref, vo_ref):
    fresh = fresh_ref[pl.program_id(0)] > 0

    @pl.when(fresh)
    def _():
        ko_ref[...] = kn_ref[...]
        vo_ref[...] = vn_ref[...]

    @pl.when(jnp.logical_not(fresh))
    def _():
        ko_ref[...] = kc_ref[...]
        vo_ref[...] = vc_ref[...]


def write_pages(key_cache, value_cache, new_keys, new_values, is_fresh, fresh_index):
    block = (1,) + key_cache.shape[1:]
    own = pl.BlockSpec(block, lambda s, fresh, index: (s, 0, 0, 0))
    new = pl.BlockSpec(block, lambda s, fresh, index: (index[s], 0, 0, 0))
    return pl.pallas_call(
        page_kernel,
        grid_spec=pltpu.PrefetchScalarGridSpec(
            num_scalar_prefetch=2,
            grid=(key_cache.shape[0],),
            in_specs=[own, own, new, new],
            out_specs=[own, own],
        ),
        out_shape=[jax.ShapeDtypeStruct(key_cache.shape, key_cache.dtype)] * 2,
        compiler_params=pltpu.CompilerParams(vmem_limit_bytes=40 * 2**20),
        name="write_pages",
    )(is_fresh.astype(jnp.int32), fresh_index, key_cache, value_cache, new_keys, new_values)


def swap(x, bit):
    devs = lax.axis_size("pages")
    return lax.ppermute(x, "pages", [(p, p ^ bit) for p in range(devs)])


def shift(x, hop, senders):
    devs = lax.axis_size("pages")
    moves = [(p, p + 4 * hop) for p in range(devs) if p // 4 in senders]
    return lax.ppermute(x, "pages", moves)


def gather_lines(x):
    line = lax.axis_size("pages") // 4
    device_at = lax.axis_index("pages")
    at, across = device_at // 4, (device_at // 2) % 2
    always = jnp.int32(1)
    held = [(x, at, across, always), (swap(x, 2), at, 1 - across, always)]
    up = down = x
    for t in range(1, line):
        up = shift(up, 1, range(t - 1, line - 1))
        down = shift(down, -1, range(1, line - t + 1))
        has_up = (at >= t).astype(jnp.int32)
        has_down = (at + t < line).astype(jnp.int32)
        devs = lax.axis_size("pages")
        cross_up = [(p, p ^ 2) for p in range(devs) if p // 4 >= t]
        cross_down = [(p, p ^ 2) for p in range(devs) if p // 4 + t < line]
        held += [
            (up, at - t, across, has_up),
            (lax.ppermute(up, "pages", cross_up), at - t, 1 - across, has_up),
            (down, at + t, across, has_down),
            (lax.ppermute(down, "pages", cross_down), at + t, 1 - across, has_down),
        ]
    return held


def merge_lines(parts, merged, last):
    line = lax.axis_size("pages") // 4
    at = lax.axis_index("pages") // 4
    turns = []
    for t in range(1, line):
        turns += [k for k in (line - t, t) if k not in turns]
    yes = jnp.int32(1)
    crossed = {k: swap(parts[k][1], 2) for k in turns + [0]}
    shares = {}

    def share(k):
        if k not in shares:
            shares[k] = merged([parts[k][0], crossed[k]], [yes, yes])
        return shares[k]

    up = down = None
    for t in range(1, line):
        up_out, down_out = share(line - t), share(t)
        if up is not None:
            up_out = merged([up_out, up], [yes, (at >= 1) & (at <= t - 1)])
            down_out = merged([down_out, down], [yes, (at <= line - 2) & (at >= line - t)])
        up = shift(up_out, 1, range(0, t))
        down = shift(down_out, -1, range(line - t, line))
    return merged([share(0), up, down, last()], [yes, at >= 1, at <= line - 2, yes])


def fresh_kernel(unit, scale2, q_ref, k_ref, v_ref, tok_ref, key_ref, o_ref):
    token, first, key = tok_ref[0:1, :], tok_ref[1:2, :], key_ref[:, 0:1]
    scores = lax.dot_general(
        k_ref[0], q_ref[0], (((1,), (1,)), ((), ())), preferred_element_type=jnp.float32
    )
    visible = (key <= token) & (key >= first)
    scores = jnp.where(visible, scores, low_score)
    peak = jnp.max(scores, axis=0, keepdims=True)
    weights = jnp.where(visible, jnp.exp2((scores - peak) * scale2), 0.0)
    totals = jnp.sum(weights, axis=0, keepdims=True)
    out = lax.dot_general(
        v_ref[0], weights.astype(jnp.bfloat16), (((0,), (0,)), ((), ())),
        preferred_element_type=jnp.float32,
    )
    out = out / totals
    part_len = out.shape[1]
    pad = -part_len % 128
    out = jnp.concatenate([out, jnp.zeros((out.shape[0], pad), jnp.float32)], axis=1)
    o_ref[0, :part_len, :] = out.T[:part_len].astype(jnp.bfloat16)
    sent = peak.astype(jnp.bfloat16).astype(jnp.float32)
    totals = totals * jnp.exp2((peak - sent) * scale2)
    high = totals.astype(jnp.bfloat16).astype(jnp.float32)
    kinds = [
        [values[:, at : at + unit] for at in range(0, part_len, unit)]
        for values in (sent, high, totals - high)
    ]
    o_ref[0, part_len:, :] = stat_block(kinds, o_ref.shape[1] - part_len)


def fresh_attention(q_chip, k_window, v_window, token_rows, key_cols, unit, scale2):
    heads, part_len, head_dim = q_chip.shape
    _, _, pad_to = stat_rows_of(part_len, unit)
    own = lambda x: pl.BlockSpec((1,) + x.shape[1:], lambda h: (h, 0, 0))
    fixed = lambda x: pl.BlockSpec(x.shape, lambda h: (0, 0))
    return pl.pallas_call(
        lambda *refs: fresh_kernel(unit, scale2, *refs),
        grid=(heads,),
        in_specs=[own(q_chip), own(k_window), own(v_window), fixed(token_rows), fixed(key_cols)],
        out_specs=pl.BlockSpec((1, part_len + pad_to, head_dim), lambda h: (h, 0, 0)),
        out_shape=jax.ShapeDtypeStruct((heads, part_len + pad_to, head_dim), jnp.bfloat16),
        compiler_params=pltpu.CompilerParams(vmem_limit_bytes=40 * 2**20),
        name="fresh_attention",
    )(q_chip, k_window, v_window, token_rows, key_cols)


def project_kernel(groups, at_ref, *refs):
    att_refs, w_refs = refs[: 2 * groups], refs[2 * groups : -3]
    bias_ref, out_ref, rows_ref = refs[-3:]
    core = at_ref[0]
    wide = rows_ref.shape[2]

    @pl.when(pl.program_id(0) == 0)
    def _():
        for index, ref in enumerate(att_refs):
            rows_ref[index] = jnp.concatenate([ref[h] for h in range(ref.shape[0])], axis=1)

    total = bias_ref[...].reshape(1, -1)
    for s in range(groups):
        for d in range(2):
            feats = pl.ds(pl.multiple_of((core ^ d) * wide, wide), wide)
            total = total + jnp.dot(
                rows_ref[2 * s + d], w_refs[s][0, feats, :], preferred_element_type=jnp.float32
            )
    out_ref[...] = total.astype(jnp.bfloat16).reshape(out_ref.shape)


def project(pieces, weights, bias, core, group_at):
    groups = len(pieces) // 2
    half, tok_dev, head_dim = pieces[0].shape
    blocks, feats, cols = weights.shape
    blocks //= groups
    wide = cols % 128 == 0

    def weight_spec(s):
        return pl.BlockSpec(
            (1, feats, cols),
            lambda j, at: (lax.rem(at[1] + groups - s, groups) * blocks + j, 0, 0),
        )

    if wide:
        out_spec = pl.BlockSpec((tok_dev, cols), lambda j, at: (0, j))
        out_shape = (tok_dev, blocks * cols)
    else:
        out_spec = pl.BlockSpec((1, tok_dev, cols), lambda j, at: (j, 0, 0))
        out_shape = (blocks, tok_dev, cols)
    out = pl.pallas_call(
        lambda *refs: project_kernel(groups, *refs),
        grid_spec=pltpu.PrefetchScalarGridSpec(
            num_scalar_prefetch=1,
            grid=(blocks,),
            in_specs=[pl.BlockSpec(x.shape, lambda j, at: (0, 0, 0)) for x in pieces]
            + [weight_spec(s) for s in range(groups)]
            + [pl.BlockSpec((1, 1, cols), lambda j, at: (j, 0, 0))],
            out_specs=out_spec,
            scratch_shapes=[pltpu.VMEM((2 * groups, tok_dev, half * head_dim), jnp.bfloat16)],
        ),
        out_shape=jax.ShapeDtypeStruct(out_shape, jnp.bfloat16),
        compiler_params=pltpu.CompilerParams(vmem_limit_bytes=40 * 2**20),
        name="project",
    )(
        jnp.stack([core, group_at]),
        *pieces,
        *[weights] * groups,
        bias.reshape(blocks, 1, cols),
    )
    return out if wide else jnp.transpose(out, (1, 0, 2)).reshape(tok_dev, blocks * cols)


def per_device(
    queries,
    keys,
    values,
    key_cache,
    value_cache,
    cache_len,
    page_table,
    append_slots,
    out_weight,
    out_bias,
):
    tok_dev, head_count, head_dim = queries.shape
    requests = cache_len.shape[0]
    max_pages = page_table.shape[1]
    new_pages = append_slots.shape[1]
    span_len = new_pages * PAGE
    slot_count = key_cache.shape[0]
    tokens = requests * span_len
    page_devs = tokens // tok_dev
    scale2 = math.log2(math.e) / math.sqrt(head_dim)
    device_at = lax.axis_index("pages")
    token_ids = device_at * tok_dev + jnp.arange(tok_dev, dtype=jnp.int32)
    request_ids = token_ids // span_len
    request_grid = jnp.arange(requests, dtype=jnp.int32)
    starts = jnp.sum(
        jnp.where(request_ids[:, None] == request_grid[None, :], cache_len[None, :], 0), axis=1
    )
    positions = (starts + token_ids % span_len).astype(jnp.float32)
    rotated_q = rotate(queries.astype(jnp.float32), positions).astype(jnp.bfloat16)
    rotated_k = rotate(keys.astype(jnp.float32), positions).astype(jnp.bfloat16)
    core = device_at % 2
    half = head_count // 2
    chip_len = 2 * tok_dev

    def halves(x):
        return (
            lax.dynamic_slice_in_dim(x, core * half, half, 0),
            lax.dynamic_slice_in_dim(x, (1 - core) * half, half, 0),
        )

    def in_order(mine, got, axis):
        return jnp.where(
            core == 0,
            jnp.concatenate([mine, got], axis=axis),
            jnp.concatenate([got, mine], axis=axis),
        )

    q_own = jnp.transpose(rotated_q, (1, 0, 2))
    q_mine, q_other = halves(q_own)
    q_chip = in_order(q_mine, swap(q_other, 1), 1)
    q_places = gather_lines(q_chip)
    groups = lax.axis_size("heads")
    group_at = lax.axis_index("heads")
    share = page_devs // groups
    q_list = [q for q, _, _, _ in q_places]
    own_share = device_at // share

    def to_owner(block):
        found = block
        for s in range(1, groups):
            moved = lax.ppermute(block, "heads", [(i, (i + s) % groups) for i in range(groups)])
            moved, _ = lax.optimization_barrier((moved, q_list))
            moved = lax.ppermute(
                moved,
                "pages",
                [(p, (p - s * share) % page_devs) for p in range(page_devs)],
            )
            found = jnp.where(own_share == (group_at - s) % groups, moved, found)
        return found

    weight_block = to_owner(out_weight)
    natural = Layout((0, 1, 2))
    all_k = lax.all_gather(rotated_k, "pages", axis=0, tiled=True)
    all_v = lax.all_gather(values, "pages", axis=0, tiled=True)
    all_k = with_layout_constraint(all_k, natural)
    all_v = with_layout_constraint(all_v, natural)
    weights = lax.all_gather(weight_block, "pages", axis=0, tiled=False)

    my_slots = device_at * slot_count + jnp.arange(slot_count, dtype=jnp.int32)
    chip_slots = jnp.concatenate(
        [my_slots, (device_at ^ 1) * slot_count + jnp.arange(slot_count, dtype=jnp.int32)]
    )
    cached_hit = page_table.reshape(-1)[None, :] == chip_slots[:, None]
    fresh_hit = append_slots.reshape(-1)[None, :] == my_slots[:, None]
    table_at = jnp.arange(requests * max_pages, dtype=jnp.int32)
    shown = (table_at % max_pages) * PAGE < jnp.repeat(cache_len, max_pages)
    is_fresh = jnp.any(fresh_hit, axis=1)
    fresh_index = jnp.sum(
        jnp.where(fresh_hit, jnp.arange(requests * new_pages, dtype=jnp.int32)[None, :], 0), axis=1
    )
    slot_key = requests - jnp.sum(
        jnp.where(cached_hit & shown[None, :], requests - (table_at // max_pages)[None, :], 0),
        axis=1,
    )
    slot_at = jnp.arange(2 * slot_count, dtype=jnp.int32)
    earlier = (slot_key[None, :] < slot_key[:, None]) | (
        (slot_key[None, :] == slot_key[:, None]) & (slot_at[None, :] < slot_at[:, None])
    )
    rank = jnp.sum(earlier.astype(jnp.int32), axis=1)
    order = jnp.sum(jnp.where(rank[None, :] == slot_at[:, None], slot_at[None, :], 0), axis=1)
    slot_starts = jnp.sum((slot_key[None, :] < request_grid[:, None]).astype(jnp.int32), axis=1)
    slot_counts = jnp.sum((slot_key[None, :] == request_grid[:, None]).astype(jnp.int32), axis=1)

    k_mine, k_other = halves(jnp.transpose(key_cache, (2, 0, 1, 3)))
    v_mine, v_other = halves(jnp.transpose(value_cache, (2, 0, 3, 1)))
    k_heads = jnp.concatenate([k_mine, swap(k_other, 1)], axis=1)
    v_heads = jnp.concatenate([v_mine, swap(v_other, 1)], axis=1)

    q_list, k_heads, v_heads = lax.optimization_barrier((q_list, k_heads, v_heads))
    unit = math.gcd(span_len, tok_dev)
    line = page_devs // 4
    line_at, across = device_at // 4, (device_at // 2) % 2
    outs = cached_attention(
        q_list,
        [jnp.clip(at, 0, line - 1) * 2 + side for _, at, side, _ in q_places],
        [ok for _, _, _, ok in q_places],
        [((line_at + k) % line) * 2 + (across ^ d) for k in range(line) for d in range(2)],
        k_heads,
        v_heads,
        order,
        slot_starts,
        slot_counts,
        span_len,
        unit,
        scale2,
    )
    merged = lambda parts, ok: merge(parts, ok, chip_len, unit, scale2)

    def fresh_part():
        chip_at = device_at // 2
        back = -(-(span_len - math.gcd(span_len, chip_len)) // chip_len)
        window = (back + 1) * chip_len
        window_at = jnp.maximum(chip_at - back, 0) * chip_len

        def by_head(rows):
            rows = lax.dynamic_slice(
                rows, (window_at, core * half, 0), (window, half, head_dim)
            )
            return jnp.transpose(rows, (1, 0, 2))

        chip_tokens = chip_at * chip_len + jnp.arange(chip_len, dtype=jnp.int32)
        token_rows = jnp.stack([chip_tokens, chip_tokens // span_len * span_len])
        key_cols = (window_at + jnp.arange(window, dtype=jnp.int32))[:, None]
        return fresh_attention(
            q_chip, by_head(all_k), by_head(all_v), token_rows, key_cols, unit, scale2
        )

    chip_part = merge_lines(
        [outs[2 * k : 2 * k + 2] for k in range(line)], merged, fresh_part
    )
    rows_of = lambda c: lax.dynamic_slice_in_dim(chip_part[:, :chip_len], c * tok_dev, tok_dev, 1)
    own_rows, other_rows = rows_of(core), rows_of(1 - core)
    pieces = []
    for s in range(groups):
        for d, rows in ((0, own_rows), (1, other_rows)):
            if s or d:
                rows = lax.ppermute(
                    rows,
                    ("heads", "pages"),
                    [
                        (h * page_devs + p, (h + s) % groups * page_devs + (p ^ d))
                        for h in range(groups)
                        for p in range(page_devs)
                    ],
                )
            pieces.append(rows)
    hidden = project(pieces, weights, out_bias, core, group_at)
    page_shape = (requests * new_pages, PAGE, head_count, head_dim)
    key_out, value_out = write_pages(
        key_cache,
        value_cache,
        all_k.reshape(page_shape),
        all_v.reshape(page_shape),
        is_fresh,
        fresh_index,
    )
    return (hidden, key_out, value_out)


def solution(mesh):
    placed = (
        P("pages", "heads", None),
        P("pages", "heads", None),
        P("pages", "heads", None),
        P("pages", None, "heads", None),
        P("pages", None, "heads", None),
        P(),
        P(),
        P(),
        P("heads", "pages"),
        P("heads"),
    )
    return jax.shard_map(
        per_device,
        mesh=mesh,
        in_specs=placed,
        out_specs=(
            P("pages", "heads"),
            P("pages", None, "heads", None),
            P("pages", None, "heads", None),
        ),
        check_vma=False,
    )
```

```python
import functools
import math

import jax
import jax.numpy as jnp
from jax import lax
from jax.experimental import pallas as pl
from jax.experimental.layout import Layout, with_layout_constraint
from jax.experimental.pallas import tpu as pltpu
from jax.sharding import PartitionSpec as P

ROT = 32
PAGE = 128
QTILE = 256

low_score = -(2.0**99)


def rotate(vectors, positions):
    half_rot = ROT // 2
    inv_freq = 10000.0 ** (-2.0 * jnp.arange(half_rot, dtype=jnp.float32) / ROT)
    angles = positions[:, None] * inv_freq[None, :]
    cosine = jnp.cos(angles)[:, None, :]
    sine = jnp.sin(angles)[:, None, :]
    first_half = vectors[..., :half_rot]
    second_half = vectors[..., half_rot:ROT]
    return jnp.concatenate(
        [
            first_half * cosine - second_half * sine,
            second_half * cosine + first_half * sine,
            vectors[..., ROT:],
        ],
        axis=-1,
    )


def stat_rows_of(part_len, unit):
    per_unit = -(-unit // 128)
    units = part_len // unit
    return per_unit, units, -(-3 * units * per_unit // 16) * 16


def stat_rows(row):
    unit = row.shape[1]
    full = -(-unit // 128) * 128
    if full > unit:
        row = jnp.concatenate([row, jnp.zeros((1, full - unit), row.dtype)], axis=1)
    return [row[:, at : at + 128] for at in range(0, full, 128)]


def stat_block(kinds, pad_to):
    rows = [piece for kind in kinds for row in kind for piece in stat_rows(row)]
    rows.append(jnp.zeros((pad_to - len(rows), 128), jnp.float32))
    return jnp.concatenate(rows, axis=0).astype(jnp.bfloat16)


def cached_kernel(unit, stat_unit, span, scale2, places, at_ref, ok_ref, order_ref, start_ref, count_ref,
                  *refs):
    q_refs, (k_ref, v_ref), refs = refs[:places], refs[places : places + 2], refs[places + 2 :]
    o_refs, (q_all, o_all, s_all, q_scr, m_scr, l_scr, acc_scr) = refs[:-7], refs[-7:]
    requests = count_ref.shape[0]
    chips, part_len, _ = q_all.shape
    per_part = part_len // unit
    per_request = span // unit
    per_unit, units, pad_to = stat_rows_of(part_len, stat_unit)

    for index in range(places):

        @pl.when(ok_ref[index] > 0)
        def _(index=index):
            q_all[at_ref[index]] = q_refs[index][0]

    def place(at, per_part):
        return at // per_part, at % per_part

    def one_request(request, _):
        for index in range(per_request):
            part, piece = place(request * per_request + index, per_part)
            row = pl.ds(pl.multiple_of(piece * unit, unit), unit)
            q_scr[index * unit : (index + 1) * unit, :] = q_all[part, row, :]
        first = start_ref[request]
        count = count_ref[request]
        m_scr[...] = jnp.full((1, span), low_score, jnp.float32)
        l_scr[...] = jnp.zeros((1, span), jnp.float32)
        acc_scr[...] = jnp.zeros(acc_scr.shape, jnp.float32)

        def pages(slots):
            k = jnp.concatenate([k_ref[0, s] for s in slots], axis=0)
            v = jnp.concatenate([v_ref[0, s] for s in slots], axis=1)
            for c in range(0, span, QTILE):
                cols = slice(c, c + QTILE)
                scores = lax.dot_general(
                    k, q_scr[cols, :], (((1,), (1,)), ((), ())),
                    preferred_element_type=jnp.float32,
                )
                before = m_scr[:, cols]
                peak = jnp.maximum(before, jnp.max(scores, axis=0, keepdims=True))
                weights = jnp.exp2((scores - peak) * scale2)
                fade = jnp.exp2((before - peak) * scale2)
                m_scr[:, cols] = peak
                l_scr[:, cols] = l_scr[:, cols] * fade + jnp.sum(weights, axis=0, keepdims=True)
                acc_scr[:, cols] = acc_scr[:, cols] * fade + jnp.dot(
                    v, weights.astype(jnp.bfloat16), preferred_element_type=jnp.float32
                )

        def pair(index, _):
            at = first + 2 * index
            pages([order_ref[at], order_ref[at + 1]])
            return 0

        lax.fori_loop(0, count // 2, pair, 0)

        @pl.when(count % 2 == 1)
        def _():
            pages([order_ref[first + count - 1]])

        totals = l_scr[...]
        peaks = m_scr[...]
        out = (acc_scr[...] / jnp.maximum(totals, 1e-30)).T.astype(jnp.bfloat16)
        sent = peaks.astype(jnp.bfloat16).astype(jnp.float32)
        totals = totals * jnp.exp2((peaks - sent) * scale2)
        high = totals.astype(jnp.bfloat16).astype(jnp.float32)
        kinds = [sent, high, totals - high]
        for index in range(per_request):
            part, piece = place(request * per_request + index, per_part)
            row = pl.ds(pl.multiple_of(piece * unit, unit), unit)
            o_all[part, row, :] = out[index * unit : (index + 1) * unit, :]
        for index in range(span // stat_unit):
            part, piece = place(request * (span // stat_unit) + index, units)
            cols = slice(index * stat_unit, (index + 1) * stat_unit)
            for kind, values in enumerate(kinds):
                for r, line in enumerate(stat_rows(values[:, cols])):
                    at = (kind * units + piece) * per_unit + r
                    s_all[part, pl.ds(at, 1), :] = line
        return 0

    lax.fori_loop(0, requests, one_request, 0)
    for index in range(chips):
        part = at_ref[places + index]
        o_refs[index][0, :part_len, :] = o_all[part]
        o_refs[index][0, part_len:, :] = s_all[part].astype(jnp.bfloat16)


def cached_attention(q_places, at, ok, out_at, k_heads, v_heads, order, starts, counts, span,
                     stat_unit, scale2):
    places = len(q_places)
    chips = len(out_at)
    heads, part_len, head_dim = q_places[0].shape
    slots = k_heads.shape[1]
    unit = math.gcd(span, part_len)
    _, _, pad_to = stat_rows_of(part_len, stat_unit)
    own_block = lambda *dims: pl.BlockSpec(
        (1,) + dims, lambda h, *_: (h,) + (0,) * len(dims)
    )
    return pl.pallas_call(
        lambda *refs: cached_kernel(unit, stat_unit, span, scale2, places, *refs),
        grid_spec=pltpu.PrefetchScalarGridSpec(
            num_scalar_prefetch=5,
            grid=(heads,),
            in_specs=[own_block(part_len, head_dim)] * places
            + [own_block(slots, PAGE, head_dim), own_block(slots, head_dim, PAGE)],
            out_specs=[own_block(part_len + pad_to, head_dim)] * chips,
            scratch_shapes=[
                pltpu.VMEM((chips, part_len, head_dim), jnp.bfloat16),
                pltpu.VMEM((chips, part_len, head_dim), jnp.bfloat16),
                pltpu.VMEM((chips, pad_to, 128), jnp.float32),
                pltpu.VMEM((span, head_dim), jnp.bfloat16),
                pltpu.VMEM((1, span), jnp.float32),
                pltpu.VMEM((1, span), jnp.float32),
                pltpu.VMEM((head_dim, span), jnp.float32),
            ],
        ),
        out_shape=[
            jax.ShapeDtypeStruct((heads, part_len + pad_to, head_dim), jnp.bfloat16)
        ] * chips,
        compiler_params=pltpu.CompilerParams(vmem_limit_bytes=60 * 2**20),
        cost_estimate=pl.CostEstimate(
            flops=40 * 10**9, bytes_accessed=20 * 2**20, transcendentals=10**7
        ),
        name="cached_attention",
    )(jnp.stack(at + out_at), jnp.stack(ok), order, starts, counts, *q_places, k_heads, v_heads)


def merge_kernel(unit, part_len, scale2, ok_ref, *refs):
    in_refs, out_ref = refs[:-1], refs[-1]
    heads, _, width = out_ref.shape
    _, units, pad_to = stat_rows_of(part_len, unit)
    oks = [ok_ref[index] > 0 for index in range(len(in_refs))]
    for h in range(heads):
        peaks, totals = [], []
        for ok, ref in zip(oks, in_refs):
            stat = ref[h, part_len:, :].astype(jnp.float32)
            peaks.append(jnp.where(ok, stat[:units], low_score))
            total = stat[units : 2 * units] + stat[2 * units : 3 * units]
            totals.append(jnp.where(ok, total, 0.0))
        top = functools.reduce(jnp.maximum, peaks)
        shares = [t * jnp.exp2((p - top) * scale2) for t, p in zip(totals, peaks)]
        total = functools.reduce(jnp.add, shares)
        inverse = 1.0 / jnp.maximum(total, 1e-30)
        merged = [0.0] * units
        for ref, share in zip(in_refs, shares):
            weight = jnp.concatenate(
                [share * inverse, jnp.zeros((-units % 8, 128), jnp.float32)], axis=0
            ).T
            rows = ref[h, :part_len, :].astype(jnp.float32)
            for u in range(units):
                merged[u] = merged[u] + weight[:unit, u : u + 1] * rows[u * unit : (u + 1) * unit]
        high = total.astype(jnp.bfloat16).astype(jnp.float32)
        stats = [top, high, total - high, jnp.zeros((pad_to - 3 * units, width), jnp.float32)]
        out_ref[h, :part_len, :] = jnp.concatenate(merged, axis=0).astype(jnp.bfloat16)
        out_ref[h, part_len:, :] = jnp.concatenate(stats, axis=0).astype(jnp.bfloat16)


def merge(parts, ok, part_len, unit, scale2):
    heads = parts[0].shape[0]
    step = max(1, heads // 2)
    block = pl.BlockSpec((step,) + parts[0].shape[1:], lambda h, *_: (h, 0, 0))
    return pl.pallas_call(
        lambda *refs: merge_kernel(unit, part_len, scale2, *refs),
        grid_spec=pltpu.PrefetchScalarGridSpec(
            num_scalar_prefetch=1,
            grid=(heads // step,),
            in_specs=[block] * len(parts),
            out_specs=block,
        ),
        out_shape=jax.ShapeDtypeStruct(parts[0].shape, jnp.bfloat16),
        name="merge",
    )(jnp.stack(ok).astype(jnp.int32), *parts)


def page_kernel(fresh_ref, index_ref, kc_ref, vc_ref, kn_ref, vn_ref, ko_ref, vo_ref):
    fresh = fresh_ref[pl.program_id(0)] > 0

    @pl.when(fresh)
    def _():
        ko_ref[...] = kn_ref[...]
        vo_ref[...] = vn_ref[...]

    @pl.when(jnp.logical_not(fresh))
    def _():
        ko_ref[...] = kc_ref[...]
        vo_ref[...] = vc_ref[...]


def write_pages(key_cache, value_cache, new_keys, new_values, is_fresh, fresh_index):
    block = (1,) + key_cache.shape[1:]
    own = pl.BlockSpec(block, lambda s, fresh, index: (s, 0, 0, 0))
    new = pl.BlockSpec(block, lambda s, fresh, index: (index[s], 0, 0, 0))
    return pl.pallas_call(
        page_kernel,
        grid_spec=pltpu.PrefetchScalarGridSpec(
            num_scalar_prefetch=2,
            grid=(key_cache.shape[0],),
            in_specs=[own, own, new, new],
            out_specs=[own, own],
        ),
        out_shape=[jax.ShapeDtypeStruct(key_cache.shape, key_cache.dtype)] * 2,
        compiler_params=pltpu.CompilerParams(vmem_limit_bytes=40 * 2**20),
        name="write_pages",
    )(is_fresh.astype(jnp.int32), fresh_index, key_cache, value_cache, new_keys, new_values)


def swap(x, bit):
    devs = lax.axis_size("pages")
    return lax.ppermute(x, "pages", [(p, p ^ bit) for p in range(devs)])


def shift(x, hop, senders):
    devs = lax.axis_size("pages")
    moves = [(p, p + 4 * hop) for p in range(devs) if p // 4 in senders]
    return lax.ppermute(x, "pages", moves)


def gather_lines(x):
    line = lax.axis_size("pages") // 4
    device_at = lax.axis_index("pages")
    at, across = device_at // 4, (device_at // 2) % 2
    always = jnp.int32(1)
    held = [(x, at, across, always), (swap(x, 2), at, 1 - across, always)]
    up = down = x
    for t in range(1, line):
        up = shift(up, 1, range(t - 1, line - 1))
        down = shift(down, -1, range(1, line - t + 1))
        has_up = (at >= t).astype(jnp.int32)
        has_down = (at + t < line).astype(jnp.int32)
        devs = lax.axis_size("pages")
        cross_up = [(p, p ^ 2) for p in range(devs) if p // 4 >= t]
        cross_down = [(p, p ^ 2) for p in range(devs) if p // 4 + t < line]
        held += [
            (up, at - t, across, has_up),
            (lax.ppermute(up, "pages", cross_up), at - t, 1 - across, has_up),
            (down, at + t, across, has_down),
            (lax.ppermute(down, "pages", cross_down), at + t, 1 - across, has_down),
        ]
    return held


def merge_lines(parts, merged, last):
    line = lax.axis_size("pages") // 4
    at = lax.axis_index("pages") // 4
    turns = []
    for t in range(1, line):
        turns += [k for k in (line - t, t) if k not in turns]
    yes = jnp.int32(1)
    crossed = {k: swap(parts[k][1], 2) for k in turns + [0]}
    shares = {}

    def share(k):
        if k not in shares:
            shares[k] = merged([parts[k][0], crossed[k]], [yes, yes])
        return shares[k]

    up = down = None
    for t in range(1, line):
        up_out, down_out = share(line - t), share(t)
        if up is not None:
            up_out = merged([up_out, up], [yes, (at >= 1) & (at <= t - 1)])
            down_out = merged([down_out, down], [yes, (at <= line - 2) & (at >= line - t)])
        up = shift(up_out, 1, range(0, t))
        down = shift(down_out, -1, range(line - t, line))
    return merged([share(0), up, down, last()], [yes, at >= 1, at <= line - 2, yes])


def fresh_kernel(unit, scale2, q_ref, k_ref, v_ref, tok_ref, key_ref, o_ref):
    token, first, key = tok_ref[0:1, :], tok_ref[1:2, :], key_ref[:, 0:1]
    scores = lax.dot_general(
        k_ref[0], q_ref[0], (((1,), (1,)), ((), ())), preferred_element_type=jnp.float32
    )
    visible = (key <= token) & (key >= first)
    scores = jnp.where(visible, scores, low_score)
    peak = jnp.max(scores, axis=0, keepdims=True)
    weights = jnp.where(visible, jnp.exp2((scores - peak) * scale2), 0.0)
    totals = jnp.sum(weights, axis=0, keepdims=True)
    out = lax.dot_general(
        v_ref[0], weights.astype(jnp.bfloat16), (((0,), (0,)), ((), ())),
        preferred_element_type=jnp.float32,
    )
    out = out / totals
    part_len = out.shape[1]
    pad = -part_len % 128
    out = jnp.concatenate([out, jnp.zeros((out.shape[0], pad), jnp.float32)], axis=1)
    o_ref[0, :part_len, :] = out.T[:part_len].astype(jnp.bfloat16)
    sent = peak.astype(jnp.bfloat16).astype(jnp.float32)
    totals = totals * jnp.exp2((peak - sent) * scale2)
    high = totals.astype(jnp.bfloat16).astype(jnp.float32)
    kinds = [
        [values[:, at : at + unit] for at in range(0, part_len, unit)]
        for values in (sent, high, totals - high)
    ]
    o_ref[0, part_len:, :] = stat_block(kinds, o_ref.shape[1] - part_len)


def fresh_attention(q_chip, k_window, v_window, token_rows, key_cols, unit, scale2):
    heads, part_len, head_dim = q_chip.shape
    _, _, pad_to = stat_rows_of(part_len, unit)
    own = lambda x: pl.BlockSpec((1,) + x.shape[1:], lambda h: (h, 0, 0))
    fixed = lambda x: pl.BlockSpec(x.shape, lambda h: (0, 0))
    return pl.pallas_call(
        lambda *refs: fresh_kernel(unit, scale2, *refs),
        grid=(heads,),
        in_specs=[own(q_chip), own(k_window), own(v_window), fixed(token_rows), fixed(key_cols)],
        out_specs=pl.BlockSpec((1, part_len + pad_to, head_dim), lambda h: (h, 0, 0)),
        out_shape=jax.ShapeDtypeStruct((heads, part_len + pad_to, head_dim), jnp.bfloat16),
        compiler_params=pltpu.CompilerParams(vmem_limit_bytes=40 * 2**20),
        name="fresh_attention",
    )(q_chip, k_window, v_window, token_rows, key_cols)


def project_kernel(groups, at_ref, *refs):
    att_refs, w_refs = refs[: 2 * groups], refs[2 * groups : -3]
    bias_ref, out_ref, rows_ref = refs[-3:]
    core = at_ref[0]
    wide = rows_ref.shape[2]

    @pl.when(pl.program_id(0) == 0)
    def _():
        for index, ref in enumerate(att_refs):
            rows_ref[index] = jnp.concatenate([ref[h] for h in range(ref.shape[0])], axis=1)

    total = bias_ref[...].reshape(1, -1)
    for s in range(groups):
        for d in range(2):
            feats = pl.ds(pl.multiple_of((core ^ d) * wide, wide), wide)
            total = total + jnp.dot(
                rows_ref[2 * s + d], w_refs[s][0, feats, :], preferred_element_type=jnp.float32
            )
    out_ref[...] = total.astype(jnp.bfloat16).reshape(out_ref.shape)


def project(pieces, weights, bias, core, group_at):
    groups = len(pieces) // 2
    half, tok_dev, head_dim = pieces[0].shape
    blocks, feats, cols = weights.shape
    blocks //= groups
    wide = cols % 128 == 0

    def weight_spec(s):
        return pl.BlockSpec(
            (1, feats, cols),
            lambda j, at: (lax.rem(at[1] + groups - s, groups) * blocks + j, 0, 0),
        )

    if wide:
        out_spec = pl.BlockSpec((tok_dev, cols), lambda j, at: (0, j))
        out_shape = (tok_dev, blocks * cols)
    else:
        out_spec = pl.BlockSpec((1, tok_dev, cols), lambda j, at: (j, 0, 0))
        out_shape = (blocks, tok_dev, cols)
    out = pl.pallas_call(
        lambda *refs: project_kernel(groups, *refs),
        grid_spec=pltpu.PrefetchScalarGridSpec(
            num_scalar_prefetch=1,
            grid=(blocks,),
            in_specs=[pl.BlockSpec(x.shape, lambda j, at: (0, 0, 0)) for x in pieces]
            + [weight_spec(s) for s in range(groups)]
            + [pl.BlockSpec((1, 1, cols), lambda j, at: (j, 0, 0))],
            out_specs=out_spec,
            scratch_shapes=[pltpu.VMEM((2 * groups, tok_dev, half * head_dim), jnp.bfloat16)],
        ),
        out_shape=jax.ShapeDtypeStruct(out_shape, jnp.bfloat16),
        compiler_params=pltpu.CompilerParams(vmem_limit_bytes=40 * 2**20),
        name="project",
    )(
        jnp.stack([core, group_at]),
        *pieces,
        *[weights] * groups,
        bias.reshape(blocks, 1, cols),
    )
    return out if wide else jnp.transpose(out, (1, 0, 2)).reshape(tok_dev, blocks * cols)


def per_device(
    queries,
    keys,
    values,
    key_cache,
    value_cache,
    cache_len,
    page_table,
    append_slots,
    out_weight,
    out_bias,
):
    tok_dev, head_count, head_dim = queries.shape
    requests = cache_len.shape[0]
    max_pages = page_table.shape[1]
    new_pages = append_slots.shape[1]
    span_len = new_pages * PAGE
    slot_count = key_cache.shape[0]
    tokens = requests * span_len
    page_devs = tokens // tok_dev
    scale2 = math.log2(math.e) / math.sqrt(head_dim)
    device_at = lax.axis_index("pages")
    token_ids = device_at * tok_dev + jnp.arange(tok_dev, dtype=jnp.int32)
    request_ids = token_ids // span_len
    request_grid = jnp.arange(requests, dtype=jnp.int32)
    starts = jnp.sum(
        jnp.where(request_ids[:, None] == request_grid[None, :], cache_len[None, :], 0), axis=1
    )
    positions = (starts + token_ids % span_len).astype(jnp.float32)
    rotated_q = rotate(queries.astype(jnp.float32), positions).astype(jnp.bfloat16)
    rotated_k = rotate(keys.astype(jnp.float32), positions).astype(jnp.bfloat16)
    core = device_at % 2
    half = head_count // 2
    chip_len = 2 * tok_dev

    def halves(x):
        return (
            lax.dynamic_slice_in_dim(x, core * half, half, 0),
            lax.dynamic_slice_in_dim(x, (1 - core) * half, half, 0),
        )

    def in_order(mine, got, axis):
        return jnp.where(
            core == 0,
            jnp.concatenate([mine, got], axis=axis),
            jnp.concatenate([got, mine], axis=axis),
        )

    q_own = jnp.transpose(rotated_q, (1, 0, 2))
    q_mine, q_other = halves(q_own)
    q_chip = in_order(q_mine, swap(q_other, 1), 1)
    q_places = gather_lines(q_chip)
    groups = lax.axis_size("heads")
    group_at = lax.axis_index("heads")
    share = page_devs // groups
    q_list = [q for q, _, _, _ in q_places]
    own_share = device_at // share

    def to_owner(block):
        found = block
        for s in range(1, groups):
            moved = lax.ppermute(block, "heads", [(i, (i + s) % groups) for i in range(groups)])
            moved = lax.ppermute(
                moved,
                "pages",
                [(p, (p - s * share) % page_devs) for p in range(page_devs)],
            )
            found = jnp.where(own_share == (group_at - s) % groups, moved, found)
        return found

    weight_block = to_owner(out_weight)
    natural = Layout((0, 1, 2))
    all_k = lax.all_gather(rotated_k, "pages", axis=0, tiled=True)
    all_v = lax.all_gather(values, "pages", axis=0, tiled=True)
    all_k = with_layout_constraint(all_k, natural)
    all_v = with_layout_constraint(all_v, natural)
    weights = lax.all_gather(weight_block, "pages", axis=0, tiled=False)

    my_slots = device_at * slot_count + jnp.arange(slot_count, dtype=jnp.int32)
    chip_slots = jnp.concatenate(
        [my_slots, (device_at ^ 1) * slot_count + jnp.arange(slot_count, dtype=jnp.int32)]
    )
    cached_hit = page_table.reshape(-1)[None, :] == chip_slots[:, None]
    fresh_hit = append_slots.reshape(-1)[None, :] == my_slots[:, None]
    table_at = jnp.arange(requests * max_pages, dtype=jnp.int32)
    shown = (table_at % max_pages) * PAGE < jnp.repeat(cache_len, max_pages)
    is_fresh = jnp.any(fresh_hit, axis=1)
    fresh_index = jnp.sum(
        jnp.where(fresh_hit, jnp.arange(requests * new_pages, dtype=jnp.int32)[None, :], 0), axis=1
    )
    slot_key = requests - jnp.sum(
        jnp.where(cached_hit & shown[None, :], requests - (table_at // max_pages)[None, :], 0),
        axis=1,
    )
    slot_at = jnp.arange(2 * slot_count, dtype=jnp.int32)
    earlier = (slot_key[None, :] < slot_key[:, None]) | (
        (slot_key[None, :] == slot_key[:, None]) & (slot_at[None, :] < slot_at[:, None])
    )
    rank = jnp.sum(earlier.astype(jnp.int32), axis=1)
    order = jnp.sum(jnp.where(rank[None, :] == slot_at[:, None], slot_at[None, :], 0), axis=1)
    slot_starts = jnp.sum((slot_key[None, :] < request_grid[:, None]).astype(jnp.int32), axis=1)
    slot_counts = jnp.sum((slot_key[None, :] == request_grid[:, None]).astype(jnp.int32), axis=1)

    k_mine, k_other = halves(jnp.transpose(key_cache, (2, 0, 1, 3)))
    v_mine, v_other = halves(jnp.transpose(value_cache, (2, 0, 3, 1)))
    k_heads = jnp.concatenate([k_mine, swap(k_other, 1)], axis=1)
    v_heads = jnp.concatenate([v_mine, swap(v_other, 1)], axis=1)

    unit = math.gcd(span_len, tok_dev)
    line = page_devs // 4
    line_at, across = device_at // 4, (device_at // 2) % 2
    outs = cached_attention(
        q_list,
        [jnp.clip(at, 0, line - 1) * 2 + side for _, at, side, _ in q_places],
        [ok for _, _, _, ok in q_places],
        [((line_at + k) % line) * 2 + (across ^ d) for k in range(line) for d in range(2)],
        k_heads,
        v_heads,
        order,
        slot_starts,
        slot_counts,
        span_len,
        unit,
        scale2,
    )
    merged = lambda parts, ok: merge(parts, ok, chip_len, unit, scale2)

    def fresh_part():
        chip_at = device_at // 2
        back = -(-(span_len - math.gcd(span_len, chip_len)) // chip_len)
        window = (back + 1) * chip_len
        window_at = jnp.maximum(chip_at - back, 0) * chip_len

        def by_head(rows):
            rows = lax.dynamic_slice(
                rows, (window_at, core * half, 0), (window, half, head_dim)
            )
            return jnp.transpose(rows, (1, 0, 2))

        chip_tokens = chip_at * chip_len + jnp.arange(chip_len, dtype=jnp.int32)
        token_rows = jnp.stack([chip_tokens, chip_tokens // span_len * span_len])
        key_cols = (window_at + jnp.arange(window, dtype=jnp.int32))[:, None]
        return fresh_attention(
            q_chip, by_head(all_k), by_head(all_v), token_rows, key_cols, unit, scale2
        )

    chip_part = merge_lines(
        [outs[2 * k : 2 * k + 2] for k in range(line)], merged, fresh_part
    )
    rows_of = lambda c: lax.dynamic_slice_in_dim(chip_part[:, :chip_len], c * tok_dev, tok_dev, 1)
    own_rows, other_rows = rows_of(core), rows_of(1 - core)
    pieces = []
    for s in range(groups):
        for d, rows in ((0, own_rows), (1, other_rows)):
            if s or d:
                rows = lax.ppermute(
                    rows,
                    ("heads", "pages"),
                    [
                        (h * page_devs + p, (h + s) % groups * page_devs + (p ^ d))
                        for h in range(groups)
                        for p in range(page_devs)
                    ],
                )
            pieces.append(rows)
    hidden = project(pieces, weights, out_bias, core, group_at)
    page_shape = (requests * new_pages, PAGE, head_count, head_dim)
    key_out, value_out = write_pages(
        key_cache,
        value_cache,
        all_k.reshape(page_shape),
        all_v.reshape(page_shape),
        is_fresh,
        fresh_index,
    )
    return (hidden, key_out, value_out)


def solution(mesh):
    placed = (
        P("pages", "heads", None),
        P("pages", "heads", None),
        P("pages", "heads", None),
        P("pages", None, "heads", None),
        P("pages", None, "heads", None),
        P(),
        P(),
        P(),
        P("heads", "pages"),
        P("heads"),
    )
    return jax.shard_map(
        per_device,
        mesh=mesh,
        in_specs=placed,
        out_specs=(
            P("pages", "heads"),
            P("pages", None, "heads", None),
            P("pages", None, "heads", None),
        ),
        check_vma=False,
    )
```

```python
import functools
import math

import jax
import jax.numpy as jnp
from jax import lax
from jax.experimental import pallas as pl
from jax.experimental.layout import Layout, with_layout_constraint
from jax.experimental.pallas import tpu as pltpu
from jax.sharding import PartitionSpec as P

ROT = 32
PAGE = 128
QTILE = 256

low_score = -(2.0**99)


def rotate(vectors, positions):
    half_rot = ROT // 2
    inv_freq = 10000.0 ** (-2.0 * jnp.arange(half_rot, dtype=jnp.float32) / ROT)
    angles = positions[:, None] * inv_freq[None, :]
    cosine = jnp.cos(angles)[:, None, :]
    sine = jnp.sin(angles)[:, None, :]
    first_half = vectors[..., :half_rot]
    second_half = vectors[..., half_rot:ROT]
    return jnp.concatenate(
        [
            first_half * cosine - second_half * sine,
            second_half * cosine + first_half * sine,
            vectors[..., ROT:],
        ],
        axis=-1,
    )


def stat_rows_of(part_len, unit):
    per_unit = -(-unit // 128)
    units = part_len // unit
    return per_unit, units, -(-3 * units * per_unit // 16) * 16


def stat_rows(row):
    unit = row.shape[1]
    full = -(-unit // 128) * 128
    if full > unit:
        row = jnp.concatenate([row, jnp.zeros((1, full - unit), row.dtype)], axis=1)
    return [row[:, at : at + 128] for at in range(0, full, 128)]


def stat_block(kinds, pad_to):
    rows = [piece for kind in kinds for row in kind for piece in stat_rows(row)]
    rows.append(jnp.zeros((pad_to - len(rows), 128), jnp.float32))
    return jnp.concatenate(rows, axis=0).astype(jnp.bfloat16)


def cached_kernel(unit, stat_unit, span, scale2, places, at_ref, ok_ref, order_ref, start_ref, count_ref,
                  *refs):
    q_refs, (k_ref, v_ref), refs = refs[:places], refs[places : places + 2], refs[places + 2 :]
    o_refs, (q_all, o_all, s_all, q_scr, m_scr, l_scr, acc_scr) = refs[:-7], refs[-7:]
    requests = count_ref.shape[0]
    chips, part_len, _ = q_all.shape
    per_part = part_len // unit
    per_request = span // unit
    per_unit, units, pad_to = stat_rows_of(part_len, stat_unit)

    for index in range(places):

        @pl.when(ok_ref[index] > 0)
        def _(index=index):
            q_all[at_ref[index]] = q_refs[index][0]

    def place(at, per_part):
        return at // per_part, at % per_part

    def one_request(request, _):
        for index in range(per_request):
            part, piece = place(request * per_request + index, per_part)
            row = pl.ds(pl.multiple_of(piece * unit, unit), unit)
            q_scr[index * unit : (index + 1) * unit, :] = q_all[part, row, :]
        first = start_ref[request]
        count = count_ref[request]
        m_scr[...] = jnp.full((1, span), low_score, jnp.float32)
        l_scr[...] = jnp.zeros((1, span), jnp.float32)
        acc_scr[...] = jnp.zeros(acc_scr.shape, jnp.float32)

        def pages(slots):
            k = jnp.concatenate([k_ref[0, s] for s in slots], axis=0)
            v = jnp.concatenate([v_ref[0, s] for s in slots], axis=1)
            for c in range(0, span, QTILE):
                cols = slice(c, c + QTILE)
                scores = lax.dot_general(
                    k, q_scr[cols, :], (((1,), (1,)), ((), ())),
                    preferred_element_type=jnp.float32,
                )
                before = m_scr[:, cols]
                peak = jnp.maximum(before, jnp.max(scores, axis=0, keepdims=True))
                weights = jnp.exp2((scores - peak) * scale2)
                fade = jnp.exp2((before - peak) * scale2)
                m_scr[:, cols] = peak
                l_scr[:, cols] = l_scr[:, cols] * fade + jnp.sum(weights, axis=0, keepdims=True)
                acc_scr[:, cols] = acc_scr[:, cols] * fade + jnp.dot(
                    v, weights.astype(jnp.bfloat16), preferred_element_type=jnp.float32
                )

        def pair(index, _):
            at = first + 2 * index
            pages([order_ref[at], order_ref[at + 1]])
            return 0

        lax.fori_loop(0, count // 2, pair, 0)

        @pl.when(count % 2 == 1)
        def _():
            pages([order_ref[first + count - 1]])

        totals = l_scr[...]
        peaks = m_scr[...]
        out = (acc_scr[...] / jnp.maximum(totals, 1e-30)).T.astype(jnp.bfloat16)
        sent = peaks.astype(jnp.bfloat16).astype(jnp.float32)
        totals = totals * jnp.exp2((peaks - sent) * scale2)
        high = totals.astype(jnp.bfloat16).astype(jnp.float32)
        kinds = [sent, high, totals - high]
        for index in range(per_request):
            part, piece = place(request * per_request + index, per_part)
            row = pl.ds(pl.multiple_of(piece * unit, unit), unit)
            o_all[part, row, :] = out[index * unit : (index + 1) * unit, :]
        for index in range(span // stat_unit):
            part, piece = place(request * (span // stat_unit) + index, units)
            cols = slice(index * stat_unit, (index + 1) * stat_unit)
            for kind, values in enumerate(kinds):
                for r, line in enumerate(stat_rows(values[:, cols])):
                    at = (kind * units + piece) * per_unit + r
                    s_all[part, pl.ds(at, 1), :] = line
        return 0

    lax.fori_loop(0, requests, one_request, 0)
    for index in range(chips):
        part = at_ref[places + index]
        o_refs[index][0, :part_len, :] = o_all[part]
        o_refs[index][0, part_len:, :] = s_all[part].astype(jnp.bfloat16)


def cached_attention(q_places, at, ok, out_at, k_heads, v_heads, order, starts, counts, span,
                     stat_unit, scale2):
    places = len(q_places)
    chips = len(out_at)
    heads, part_len, head_dim = q_places[0].shape
    slots = k_heads.shape[1]
    unit = math.gcd(span, part_len)
    _, _, pad_to = stat_rows_of(part_len, stat_unit)
    own_block = lambda *dims: pl.BlockSpec(
        (1,) + dims, lambda h, *_: (h,) + (0,) * len(dims)
    )
    return pl.pallas_call(
        lambda *refs: cached_kernel(unit, stat_unit, span, scale2, places, *refs),
        grid_spec=pltpu.PrefetchScalarGridSpec(
            num_scalar_prefetch=5,
            grid=(heads,),
            in_specs=[own_block(part_len, head_dim)] * places
            + [own_block(slots, PAGE, head_dim), own_block(slots, head_dim, PAGE)],
            out_specs=[own_block(part_len + pad_to, head_dim)] * chips,
            scratch_shapes=[
                pltpu.VMEM((chips, part_len, head_dim), jnp.bfloat16),
                pltpu.VMEM((chips, part_len, head_dim), jnp.bfloat16),
                pltpu.VMEM((chips, pad_to, 128), jnp.float32),
                pltpu.VMEM((span, head_dim), jnp.bfloat16),
                pltpu.VMEM((1, span), jnp.float32),
                pltpu.VMEM((1, span), jnp.float32),
                pltpu.VMEM((head_dim, span), jnp.float32),
            ],
        ),
        out_shape=[
            jax.ShapeDtypeStruct((heads, part_len + pad_to, head_dim), jnp.bfloat16)
        ] * chips,
        compiler_params=pltpu.CompilerParams(vmem_limit_bytes=60 * 2**20),
        cost_estimate=pl.CostEstimate(
            flops=40 * 10**9, bytes_accessed=20 * 2**20, transcendentals=10**7
        ),
        name="cached_attention",
    )(jnp.stack(at + out_at), jnp.stack(ok), order, starts, counts, *q_places, k_heads, v_heads)


def merge_kernel(unit, part_len, scale2, ok_ref, *refs):
    in_refs, out_ref = refs[:-1], refs[-1]
    heads, _, width = out_ref.shape
    _, units, pad_to = stat_rows_of(part_len, unit)
    oks = [ok_ref[index] > 0 for index in range(len(in_refs))]
    for h in range(heads):
        peaks, totals = [], []
        for ok, ref in zip(oks, in_refs):
            stat = ref[h, part_len:, :].astype(jnp.float32)
            peaks.append(jnp.where(ok, stat[:units], low_score))
            total = stat[units : 2 * units] + stat[2 * units : 3 * units]
            totals.append(jnp.where(ok, total, 0.0))
        top = functools.reduce(jnp.maximum, peaks)
        shares = [t * jnp.exp2((p - top) * scale2) for t, p in zip(totals, peaks)]
        total = functools.reduce(jnp.add, shares)
        inverse = 1.0 / jnp.maximum(total, 1e-30)
        merged = [0.0] * units
        for ref, share in zip(in_refs, shares):
            weight = jnp.concatenate(
                [share * inverse, jnp.zeros((-units % 8, 128), jnp.float32)], axis=0
            ).T
            rows = ref[h, :part_len, :].astype(jnp.float32)
            for u in range(units):
                merged[u] = merged[u] + weight[:unit, u : u + 1] * rows[u * unit : (u + 1) * unit]
        high = total.astype(jnp.bfloat16).astype(jnp.float32)
        stats = [top, high, total - high, jnp.zeros((pad_to - 3 * units, width), jnp.float32)]
        out_ref[h, :part_len, :] = jnp.concatenate(merged, axis=0).astype(jnp.bfloat16)
        out_ref[h, part_len:, :] = jnp.concatenate(stats, axis=0).astype(jnp.bfloat16)


def merge(parts, ok, part_len, unit, scale2):
    heads = parts[0].shape[0]
    step = max(1, heads // 2)
    block = pl.BlockSpec((step,) + parts[0].shape[1:], lambda h, *_: (h, 0, 0))
    return pl.pallas_call(
        lambda *refs: merge_kernel(unit, part_len, scale2, *refs),
        grid_spec=pltpu.PrefetchScalarGridSpec(
            num_scalar_prefetch=1,
            grid=(heads // step,),
            in_specs=[block] * len(parts),
            out_specs=block,
        ),
        out_shape=jax.ShapeDtypeStruct(parts[0].shape, jnp.bfloat16),
        name="merge",
    )(jnp.stack(ok).astype(jnp.int32), *parts)


def page_kernel(fresh_ref, index_ref, kc_ref, vc_ref, kn_ref, vn_ref, ko_ref, vo_ref):
    fresh = fresh_ref[pl.program_id(0)] > 0

    @pl.when(fresh)
    def _():
        ko_ref[...] = kn_ref[...]
        vo_ref[...] = vn_ref[...]

    @pl.when(jnp.logical_not(fresh))
    def _():
        ko_ref[...] = kc_ref[...]
        vo_ref[...] = vc_ref[...]


def write_pages(key_cache, value_cache, new_keys, new_values, is_fresh, fresh_index):
    block = (1,) + key_cache.shape[1:]
    own = pl.BlockSpec(block, lambda s, fresh, index: (s, 0, 0, 0))
    new = pl.BlockSpec(block, lambda s, fresh, index: (index[s], 0, 0, 0))
    return pl.pallas_call(
        page_kernel,
        grid_spec=pltpu.PrefetchScalarGridSpec(
            num_scalar_prefetch=2,
            grid=(key_cache.shape[0],),
            in_specs=[own, own, new, new],
            out_specs=[own, own],
        ),
        out_shape=[jax.ShapeDtypeStruct(key_cache.shape, key_cache.dtype)] * 2,
        compiler_params=pltpu.CompilerParams(vmem_limit_bytes=40 * 2**20),
        name="write_pages",
    )(is_fresh.astype(jnp.int32), fresh_index, key_cache, value_cache, new_keys, new_values)


def swap(x, bit):
    devs = lax.axis_size("pages")
    return lax.ppermute(x, "pages", [(p, p ^ bit) for p in range(devs)])


def shift(x, hop, senders):
    devs = lax.axis_size("pages")
    moves = [(p, p + 4 * hop) for p in range(devs) if p // 4 in senders]
    return lax.ppermute(x, "pages", moves)


def gather_lines(x):
    line = lax.axis_size("pages") // 4
    device_at = lax.axis_index("pages")
    at, across = device_at // 4, (device_at // 2) % 2
    always = jnp.int32(1)
    held = [(x, at, across, always), (swap(x, 2), at, 1 - across, always)]
    up = down = x
    for t in range(1, line):
        up = shift(up, 1, range(t - 1, line - 1))
        down = shift(down, -1, range(1, line - t + 1))
        has_up = (at >= t).astype(jnp.int32)
        has_down = (at + t < line).astype(jnp.int32)
        devs = lax.axis_size("pages")
        cross_up = [(p, p ^ 2) for p in range(devs) if p // 4 >= t]
        cross_down = [(p, p ^ 2) for p in range(devs) if p // 4 + t < line]
        held += [
            (up, at - t, across, has_up),
            (lax.ppermute(up, "pages", cross_up), at - t, 1 - across, has_up),
            (down, at + t, across, has_down),
            (lax.ppermute(down, "pages", cross_down), at + t, 1 - across, has_down),
        ]
    return held


def merge_lines(parts, merged, last):
    line = lax.axis_size("pages") // 4
    at = lax.axis_index("pages") // 4
    turns = []
    for t in range(1, line):
        turns += [k for k in (line - t, t) if k not in turns]
    yes = jnp.int32(1)
    crossed = {k: swap(parts[k][1], 2) for k in turns + [0]}
    shares = {}

    def share(k):
        if k not in shares:
            shares[k] = merged([parts[k][0], crossed[k]], [yes, yes])
        return shares[k]

    up = down = None
    for t in range(1, line):
        up_out, down_out = share(line - t), share(t)
        if up is not None:
            up_out = merged([up_out, up], [yes, (at >= 1) & (at <= t - 1)])
            down_out = merged([down_out, down], [yes, (at <= line - 2) & (at >= line - t)])
        up = shift(up_out, 1, range(0, t))
        down = shift(down_out, -1, range(line - t, line))
    return merged([share(0), up, down, last()], [yes, at >= 1, at <= line - 2, yes])


def fresh_kernel(unit, scale2, q_ref, k_ref, v_ref, tok_ref, key_ref, o_ref):
    token, first, key = tok_ref[0:1, :], tok_ref[1:2, :], key_ref[:, 0:1]
    scores = lax.dot_general(
        k_ref[0], q_ref[0], (((1,), (1,)), ((), ())), preferred_element_type=jnp.float32
    )
    visible = (key <= token) & (key >= first)
    scores = jnp.where(visible, scores, low_score)
    peak = jnp.max(scores, axis=0, keepdims=True)
    weights = jnp.where(visible, jnp.exp2((scores - peak) * scale2), 0.0)
    totals = jnp.sum(weights, axis=0, keepdims=True)
    out = lax.dot_general(
        v_ref[0], weights.astype(jnp.bfloat16), (((0,), (0,)), ((), ())),
        preferred_element_type=jnp.float32,
    )
    out = out / totals
    part_len = out.shape[1]
    pad = -part_len % 128
    out = jnp.concatenate([out, jnp.zeros((out.shape[0], pad), jnp.float32)], axis=1)
    o_ref[0, :part_len, :] = out.T[:part_len].astype(jnp.bfloat16)
    sent = peak.astype(jnp.bfloat16).astype(jnp.float32)
    totals = totals * jnp.exp2((peak - sent) * scale2)
    high = totals.astype(jnp.bfloat16).astype(jnp.float32)
    kinds = [
        [values[:, at : at + unit] for at in range(0, part_len, unit)]
        for values in (sent, high, totals - high)
    ]
    o_ref[0, part_len:, :] = stat_block(kinds, o_ref.shape[1] - part_len)


def fresh_attention(q_chip, k_window, v_window, token_rows, key_cols, unit, scale2):
    heads, part_len, head_dim = q_chip.shape
    _, _, pad_to = stat_rows_of(part_len, unit)
    own = lambda x: pl.BlockSpec((1,) + x.shape[1:], lambda h: (h, 0, 0))
    fixed = lambda x: pl.BlockSpec(x.shape, lambda h: (0, 0))
    return pl.pallas_call(
        lambda *refs: fresh_kernel(unit, scale2, *refs),
        grid=(heads,),
        in_specs=[own(q_chip), own(k_window), own(v_window), fixed(token_rows), fixed(key_cols)],
        out_specs=pl.BlockSpec((1, part_len + pad_to, head_dim), lambda h: (h, 0, 0)),
        out_shape=jax.ShapeDtypeStruct((heads, part_len + pad_to, head_dim), jnp.bfloat16),
        compiler_params=pltpu.CompilerParams(vmem_limit_bytes=40 * 2**20),
        name="fresh_attention",
    )(q_chip, k_window, v_window, token_rows, key_cols)


def project_kernel(at_ref, mine_ref, other_ref, w_ref, out_ref, rows_ref):
    core = at_ref[0]
    wide = rows_ref.shape[2]

    @pl.when(pl.program_id(0) == 0)
    def _():
        for index, ref in enumerate((mine_ref, other_ref)):
            rows_ref[index] = jnp.concatenate([ref[h] for h in range(ref.shape[0])], axis=1)

    total = 0.0
    for d in range(2):
        feats = pl.ds(pl.multiple_of((core ^ d) * wide, wide), wide)
        total = total + jnp.dot(
            rows_ref[d], w_ref[0, feats, :], preferred_element_type=jnp.float32
        )
    out_ref[...] = total.astype(out_ref.dtype).reshape(out_ref.shape)


def project(mine, other, weights, core, owner, groups, dtype):
    half, tok_dev, head_dim = mine.shape
    blocks, feats, cols = weights.shape
    blocks //= groups
    wide = cols % 128 == 0
    if wide:
        out_spec = pl.BlockSpec((tok_dev, cols), lambda j, at: (0, j))
        out_shape = (tok_dev, blocks * cols)
    else:
        out_spec = pl.BlockSpec((1, tok_dev, cols), lambda j, at: (j, 0, 0))
        out_shape = (blocks, tok_dev, cols)
    rows_spec = pl.BlockSpec(mine.shape, lambda j, at: (0, 0, 0))
    out = pl.pallas_call(
        project_kernel,
        grid_spec=pltpu.PrefetchScalarGridSpec(
            num_scalar_prefetch=1,
            grid=(blocks,),
            in_specs=[
                rows_spec,
                rows_spec,
                pl.BlockSpec((1, feats, cols), lambda j, at: (at[1] * blocks + j, 0, 0)),
            ],
            out_specs=out_spec,
            scratch_shapes=[pltpu.VMEM((2, tok_dev, half * head_dim), jnp.bfloat16)],
        ),
        out_shape=jax.ShapeDtypeStruct(out_shape, dtype),
        compiler_params=pltpu.CompilerParams(vmem_limit_bytes=40 * 2**20),
        name="project",
    )(jnp.stack([core, owner]), mine, other, weights)
    return out if wide else jnp.transpose(out, (1, 0, 2)).reshape(tok_dev, blocks * cols)


def per_device(
    queries,
    keys,
    values,
    key_cache,
    value_cache,
    cache_len,
    page_table,
    append_slots,
    out_weight,
    out_bias,
):
    tok_dev, head_count, head_dim = queries.shape
    requests = cache_len.shape[0]
    max_pages = page_table.shape[1]
    new_pages = append_slots.shape[1]
    span_len = new_pages * PAGE
    slot_count = key_cache.shape[0]
    tokens = requests * span_len
    page_devs = tokens // tok_dev
    scale2 = math.log2(math.e) / math.sqrt(head_dim)
    device_at = lax.axis_index("pages")
    token_ids = device_at * tok_dev + jnp.arange(tok_dev, dtype=jnp.int32)
    request_ids = token_ids // span_len
    request_grid = jnp.arange(requests, dtype=jnp.int32)
    starts = jnp.sum(
        jnp.where(request_ids[:, None] == request_grid[None, :], cache_len[None, :], 0), axis=1
    )
    positions = (starts + token_ids % span_len).astype(jnp.float32)
    rotated_q = rotate(queries.astype(jnp.float32), positions).astype(jnp.bfloat16)
    rotated_k = rotate(keys.astype(jnp.float32), positions).astype(jnp.bfloat16)
    core = device_at % 2
    half = head_count // 2
    chip_len = 2 * tok_dev

    def halves(x):
        return (
            lax.dynamic_slice_in_dim(x, core * half, half, 0),
            lax.dynamic_slice_in_dim(x, (1 - core) * half, half, 0),
        )

    def in_order(mine, got, axis):
        return jnp.where(
            core == 0,
            jnp.concatenate([mine, got], axis=axis),
            jnp.concatenate([got, mine], axis=axis),
        )

    q_own = jnp.transpose(rotated_q, (1, 0, 2))
    q_mine, q_other = halves(q_own)
    q_chip = in_order(q_mine, swap(q_other, 1), 1)
    q_places = gather_lines(q_chip)
    groups = lax.axis_size("heads")
    group_at = lax.axis_index("heads")
    q_list = [q for q, _, _, _ in q_places]
    natural = Layout((0, 1, 2))
    all_k = lax.all_gather(rotated_k, "pages", axis=0, tiled=True)
    all_v = lax.all_gather(values, "pages", axis=0, tiled=True)
    all_k = with_layout_constraint(all_k, natural)
    all_v = with_layout_constraint(all_v, natural)
    weights = lax.all_gather(out_weight, "pages", axis=0, tiled=False)

    my_slots = device_at * slot_count + jnp.arange(slot_count, dtype=jnp.int32)
    chip_slots = jnp.concatenate(
        [my_slots, (device_at ^ 1) * slot_count + jnp.arange(slot_count, dtype=jnp.int32)]
    )
    cached_hit = page_table.reshape(-1)[None, :] == chip_slots[:, None]
    fresh_hit = append_slots.reshape(-1)[None, :] == my_slots[:, None]
    table_at = jnp.arange(requests * max_pages, dtype=jnp.int32)
    shown = (table_at % max_pages) * PAGE < jnp.repeat(cache_len, max_pages)
    is_fresh = jnp.any(fresh_hit, axis=1)
    fresh_index = jnp.sum(
        jnp.where(fresh_hit, jnp.arange(requests * new_pages, dtype=jnp.int32)[None, :], 0), axis=1
    )
    slot_key = requests - jnp.sum(
        jnp.where(cached_hit & shown[None, :], requests - (table_at // max_pages)[None, :], 0),
        axis=1,
    )
    slot_at = jnp.arange(2 * slot_count, dtype=jnp.int32)
    earlier = (slot_key[None, :] < slot_key[:, None]) | (
        (slot_key[None, :] == slot_key[:, None]) & (slot_at[None, :] < slot_at[:, None])
    )
    rank = jnp.sum(earlier.astype(jnp.int32), axis=1)
    order = jnp.sum(jnp.where(rank[None, :] == slot_at[:, None], slot_at[None, :], 0), axis=1)
    slot_starts = jnp.sum((slot_key[None, :] < request_grid[:, None]).astype(jnp.int32), axis=1)
    slot_counts = jnp.sum((slot_key[None, :] == request_grid[:, None]).astype(jnp.int32), axis=1)

    k_mine, k_other = halves(jnp.transpose(key_cache, (2, 0, 1, 3)))
    v_mine, v_other = halves(jnp.transpose(value_cache, (2, 0, 3, 1)))
    k_heads = jnp.concatenate([k_mine, swap(k_other, 1)], axis=1)
    v_heads = jnp.concatenate([v_mine, swap(v_other, 1)], axis=1)

    unit = math.gcd(span_len, tok_dev)
    line = page_devs // 4
    line_at, across = device_at // 4, (device_at // 2) % 2
    outs = cached_attention(
        q_list,
        [jnp.clip(at, 0, line - 1) * 2 + side for _, at, side, _ in q_places],
        [ok for _, _, _, ok in q_places],
        [((line_at + k) % line) * 2 + (across ^ d) for k in range(line) for d in range(2)],
        k_heads,
        v_heads,
        order,
        slot_starts,
        slot_counts,
        span_len,
        unit,
        scale2,
    )
    merged = lambda parts, ok: merge(parts, ok, chip_len, unit, scale2)

    def fresh_part():
        chip_at = device_at // 2
        back = -(-(span_len - math.gcd(span_len, chip_len)) // chip_len)
        window = (back + 1) * chip_len
        window_at = jnp.maximum(chip_at - back, 0) * chip_len

        def by_head(rows):
            rows = lax.dynamic_slice(
                rows, (window_at, core * half, 0), (window, half, head_dim)
            )
            return jnp.transpose(rows, (1, 0, 2))

        chip_tokens = chip_at * chip_len + jnp.arange(chip_len, dtype=jnp.int32)
        token_rows = jnp.stack([chip_tokens, chip_tokens // span_len * span_len])
        key_cols = (window_at + jnp.arange(window, dtype=jnp.int32))[:, None]
        return fresh_attention(
            q_chip, by_head(all_k), by_head(all_v), token_rows, key_cols, unit, scale2
        )

    chip_part = merge_lines(
        [outs[2 * k : 2 * k + 2] for k in range(line)], merged, fresh_part
    )
    rows_of = lambda c: lax.dynamic_slice_in_dim(chip_part[:, :chip_len], c * tok_dev, tok_dev, 1)
    own_rows, got_rows = rows_of(core), swap(rows_of(1 - core), 1)
    total = out_bias[None, :]
    for s in range(groups - 1, -1, -1):
        owner = (group_at + s) % groups
        part = project(
            own_rows, got_rows, weights, core, owner, groups, jnp.bfloat16 if s else jnp.float32
        )
        if s:
            part = lax.ppermute(part, "heads", [(h, (h + s) % groups) for h in range(groups)])
        total = total + part.astype(jnp.float32)
    hidden = total.astype(jnp.bfloat16)
    page_shape = (requests * new_pages, PAGE, head_count, head_dim)
    key_out, value_out = write_pages(
        key_cache,
        value_cache,
        all_k.reshape(page_shape),
        all_v.reshape(page_shape),
        is_fresh,
        fresh_index,
    )
    return (hidden, key_out, value_out)


def solution(mesh):
    placed = (
        P("pages", "heads", None),
        P("pages", "heads", None),
        P("pages", "heads", None),
        P("pages", None, "heads", None),
        P("pages", None, "heads", None),
        P(),
        P(),
        P(),
        P("heads", "pages"),
        P("heads"),
    )
    return jax.shard_map(
        per_device,
        mesh=mesh,
        in_specs=placed,
        out_specs=(
            P("pages", "heads"),
            P("pages", None, "heads", None),
            P("pages", None, "heads", None),
        ),
        check_vma=False,
    )
```

```python
import functools
import math

import jax
import jax.numpy as jnp
from jax import lax
from jax.experimental import pallas as pl
from jax.experimental.layout import Layout, with_layout_constraint
from jax.experimental.pallas import tpu as pltpu
from jax.sharding import PartitionSpec as P

ROT = 32
PAGE = 128
QTILE = 256

low_score = -(2.0**99)


def rotate(vectors, positions):
    half_rot = ROT // 2
    inv_freq = 10000.0 ** (-2.0 * jnp.arange(half_rot, dtype=jnp.float32) / ROT)
    angles = positions[:, None] * inv_freq[None, :]
    cosine = jnp.cos(angles)[:, None, :]
    sine = jnp.sin(angles)[:, None, :]
    first_half = vectors[..., :half_rot]
    second_half = vectors[..., half_rot:ROT]
    return jnp.concatenate(
        [
            first_half * cosine - second_half * sine,
            second_half * cosine + first_half * sine,
            vectors[..., ROT:],
        ],
        axis=-1,
    )


def stat_rows_of(part_len, unit):
    per_unit = -(-unit // 128)
    units = part_len // unit
    return per_unit, units, -(-3 * units * per_unit // 16) * 16


def stat_rows(row):
    unit = row.shape[1]
    full = -(-unit // 128) * 128
    if full > unit:
        row = jnp.concatenate([row, jnp.zeros((1, full - unit), row.dtype)], axis=1)
    return [row[:, at : at + 128] for at in range(0, full, 128)]


def stat_block(kinds, pad_to):
    rows = [piece for kind in kinds for row in kind for piece in stat_rows(row)]
    rows.append(jnp.zeros((pad_to - len(rows), 128), jnp.float32))
    return jnp.concatenate(rows, axis=0).astype(jnp.bfloat16)


def cached_kernel(unit, stat_unit, span, scale2, places, at_ref, ok_ref, order_ref, start_ref, count_ref,
                  *refs):
    q_refs, (k_ref, v_ref), refs = refs[:places], refs[places : places + 2], refs[places + 2 :]
    o_refs, (q_all, o_all, s_all, q_scr, m_scr, l_scr, acc_scr) = refs[:-7], refs[-7:]
    requests = count_ref.shape[0]
    chips, part_len, _ = q_all.shape
    per_part = part_len // unit
    per_request = span // unit
    per_unit, units, pad_to = stat_rows_of(part_len, stat_unit)

    for index in range(places):

        @pl.when(ok_ref[index] > 0)
        def _(index=index):
            q_all[at_ref[index]] = q_refs[index][0]

    def place(at, per_part):
        return at // per_part, at % per_part

    def one_request(request, _):
        for index in range(per_request):
            part, piece = place(request * per_request + index, per_part)
            row = pl.ds(pl.multiple_of(piece * unit, unit), unit)
            q_scr[index * unit : (index + 1) * unit, :] = q_all[part, row, :]
        first = start_ref[request]
        count = count_ref[request]
        m_scr[...] = jnp.full((1, span), low_score, jnp.float32)
        l_scr[...] = jnp.zeros((1, span), jnp.float32)
        acc_scr[...] = jnp.zeros(acc_scr.shape, jnp.float32)

        def pages(slots):
            k = jnp.concatenate([k_ref[0, s] for s in slots], axis=0)
            v = jnp.concatenate([v_ref[0, s] for s in slots], axis=1)
            for c in range(0, span, QTILE):
                cols = slice(c, c + QTILE)
                scores = lax.dot_general(
                    k, q_scr[cols, :], (((1,), (1,)), ((), ())),
                    preferred_element_type=jnp.float32,
                )
                before = m_scr[:, cols]
                peak = jnp.maximum(before, jnp.max(scores, axis=0, keepdims=True))
                weights = jnp.exp2((scores - peak) * scale2)
                fade = jnp.exp2((before - peak) * scale2)
                m_scr[:, cols] = peak
                l_scr[:, cols] = l_scr[:, cols] * fade + jnp.sum(weights, axis=0, keepdims=True)
                acc_scr[:, cols] = acc_scr[:, cols] * fade + jnp.dot(
                    v, weights.astype(jnp.bfloat16), preferred_element_type=jnp.float32
                )

        def pair(index, _):
            at = first + 2 * index
            pages([order_ref[at], order_ref[at + 1]])
            return 0

        lax.fori_loop(0, count // 2, pair, 0)

        @pl.when(count % 2 == 1)
        def _():
            pages([order_ref[first + count - 1]])

        totals = l_scr[...]
        peaks = m_scr[...]
        out = (acc_scr[...] / jnp.maximum(totals, 1e-30)).T.astype(jnp.bfloat16)
        sent = peaks.astype(jnp.bfloat16).astype(jnp.float32)
        totals = totals * jnp.exp2((peaks - sent) * scale2)
        high = totals.astype(jnp.bfloat16).astype(jnp.float32)
        kinds = [sent, high, totals - high]
        for index in range(per_request):
            part, piece = place(request * per_request + index, per_part)
            row = pl.ds(pl.multiple_of(piece * unit, unit), unit)
            o_all[part, row, :] = out[index * unit : (index + 1) * unit, :]
        for index in range(span // stat_unit):
            part, piece = place(request * (span // stat_unit) + index, units)
            cols = slice(index * stat_unit, (index + 1) * stat_unit)
            for kind, values in enumerate(kinds):
                for r, line in enumerate(stat_rows(values[:, cols])):
                    at = (kind * units + piece) * per_unit + r
                    s_all[part, pl.ds(at, 1), :] = line
        return 0

    lax.fori_loop(0, requests, one_request, 0)
    for index in range(chips):
        part = at_ref[places + index]
        o_refs[index][0, :part_len, :] = o_all[part]
        o_refs[index][0, part_len:, :] = s_all[part].astype(jnp.bfloat16)


def cached_attention(q_places, at, ok, out_at, k_heads, v_heads, order, starts, counts, span,
                     stat_unit, scale2):
    places = len(q_places)
    chips = len(out_at)
    heads, part_len, head_dim = q_places[0].shape
    slots = k_heads.shape[1]
    unit = math.gcd(span, part_len)
    _, _, pad_to = stat_rows_of(part_len, stat_unit)
    own_block = lambda *dims: pl.BlockSpec(
        (1,) + dims, lambda h, *_: (h,) + (0,) * len(dims)
    )
    return pl.pallas_call(
        lambda *refs: cached_kernel(unit, stat_unit, span, scale2, places, *refs),
        grid_spec=pltpu.PrefetchScalarGridSpec(
            num_scalar_prefetch=5,
            grid=(heads,),
            in_specs=[own_block(part_len, head_dim)] * places
            + [own_block(slots, PAGE, head_dim), own_block(slots, head_dim, PAGE)],
            out_specs=[own_block(part_len + pad_to, head_dim)] * chips,
            scratch_shapes=[
                pltpu.VMEM((chips, part_len, head_dim), jnp.bfloat16),
                pltpu.VMEM((chips, part_len, head_dim), jnp.bfloat16),
                pltpu.VMEM((chips, pad_to, 128), jnp.float32),
                pltpu.VMEM((span, head_dim), jnp.bfloat16),
                pltpu.VMEM((1, span), jnp.float32),
                pltpu.VMEM((1, span), jnp.float32),
                pltpu.VMEM((head_dim, span), jnp.float32),
            ],
        ),
        out_shape=[
            jax.ShapeDtypeStruct((heads, part_len + pad_to, head_dim), jnp.bfloat16)
        ] * chips,
        compiler_params=pltpu.CompilerParams(vmem_limit_bytes=60 * 2**20),
        cost_estimate=pl.CostEstimate(
            flops=40 * 10**9, bytes_accessed=20 * 2**20, transcendentals=10**7
        ),
        name="cached_attention",
    )(jnp.stack(at + out_at), jnp.stack(ok), order, starts, counts, *q_places, k_heads, v_heads)


def merge_kernel(unit, part_len, scale2, ok_ref, *refs):
    in_refs, out_ref = refs[:-1], refs[-1]
    heads, _, width = out_ref.shape
    _, units, pad_to = stat_rows_of(part_len, unit)
    oks = [ok_ref[index] > 0 for index in range(len(in_refs))]
    for h in range(heads):
        peaks, totals = [], []
        for ok, ref in zip(oks, in_refs):
            stat = ref[h, part_len:, :].astype(jnp.float32)
            peaks.append(jnp.where(ok, stat[:units], low_score))
            total = stat[units : 2 * units] + stat[2 * units : 3 * units]
            totals.append(jnp.where(ok, total, 0.0))
        top = functools.reduce(jnp.maximum, peaks)
        shares = [t * jnp.exp2((p - top) * scale2) for t, p in zip(totals, peaks)]
        total = functools.reduce(jnp.add, shares)
        inverse = 1.0 / jnp.maximum(total, 1e-30)
        merged = [0.0] * units
        for ref, share in zip(in_refs, shares):
            weight = jnp.concatenate(
                [share * inverse, jnp.zeros((-units % 8, 128), jnp.float32)], axis=0
            ).T
            rows = ref[h, :part_len, :].astype(jnp.float32)
            for u in range(units):
                merged[u] = merged[u] + weight[:unit, u : u + 1] * rows[u * unit : (u + 1) * unit]
        high = total.astype(jnp.bfloat16).astype(jnp.float32)
        stats = [top, high, total - high, jnp.zeros((pad_to - 3 * units, width), jnp.float32)]
        out_ref[h, :part_len, :] = jnp.concatenate(merged, axis=0).astype(jnp.bfloat16)
        out_ref[h, part_len:, :] = jnp.concatenate(stats, axis=0).astype(jnp.bfloat16)


def merge(parts, ok, part_len, unit, scale2):
    heads = parts[0].shape[0]
    step = max(1, heads // 2)
    block = pl.BlockSpec((step,) + parts[0].shape[1:], lambda h, *_: (h, 0, 0))
    return pl.pallas_call(
        lambda *refs: merge_kernel(unit, part_len, scale2, *refs),
        grid_spec=pltpu.PrefetchScalarGridSpec(
            num_scalar_prefetch=1,
            grid=(heads // step,),
            in_specs=[block] * len(parts),
            out_specs=block,
        ),
        out_shape=jax.ShapeDtypeStruct(parts[0].shape, jnp.bfloat16),
        name="merge",
    )(jnp.stack(ok).astype(jnp.int32), *parts)


def page_kernel(fresh_ref, index_ref, kc_ref, vc_ref, kn_ref, vn_ref, ko_ref, vo_ref):
    fresh = fresh_ref[pl.program_id(0)] > 0

    @pl.when(fresh)
    def _():
        ko_ref[...] = kn_ref[...]
        vo_ref[...] = vn_ref[...]

    @pl.when(jnp.logical_not(fresh))
    def _():
        ko_ref[...] = kc_ref[...]
        vo_ref[...] = vc_ref[...]


def write_pages(key_cache, value_cache, new_keys, new_values, is_fresh, fresh_index):
    block = (1,) + key_cache.shape[1:]
    own = pl.BlockSpec(block, lambda s, fresh, index: (s, 0, 0, 0))
    new = pl.BlockSpec(block, lambda s, fresh, index: (index[s], 0, 0, 0))
    return pl.pallas_call(
        page_kernel,
        grid_spec=pltpu.PrefetchScalarGridSpec(
            num_scalar_prefetch=2,
            grid=(key_cache.shape[0],),
            in_specs=[own, own, new, new],
            out_specs=[own, own],
        ),
        out_shape=[jax.ShapeDtypeStruct(key_cache.shape, key_cache.dtype)] * 2,
        compiler_params=pltpu.CompilerParams(vmem_limit_bytes=40 * 2**20),
        name="write_pages",
    )(is_fresh.astype(jnp.int32), fresh_index, key_cache, value_cache, new_keys, new_values)


def swap(x, bit):
    devs = lax.axis_size("pages")
    return lax.ppermute(x, "pages", [(p, p ^ bit) for p in range(devs)])


def shift(x, hop, senders):
    devs = lax.axis_size("pages")
    moves = [(p, p + 4 * hop) for p in range(devs) if p // 4 in senders]
    return lax.ppermute(x, "pages", moves)


def cross_arrivals(up, down, t):
    devs = lax.axis_size("pages")
    line = devs // 4
    cross_up = [(p, p ^ 2) for p in range(devs) if p // 4 >= t]
    cross_down = [(p, p ^ 2) for p in range(devs) if p // 4 + t < line]
    return lax.ppermute(up, "pages", cross_up), lax.ppermute(down, "pages", cross_down)


def gather_lines(x):
    line = lax.axis_size("pages") // 4
    device_at = lax.axis_index("pages")
    at, across = device_at // 4, (device_at // 2) % 2
    always = jnp.int32(1)
    held = [(x, at, across, always), (swap(x, 2), at, 1 - across, always)]
    up = down = x
    for t in range(1, line):
        up = shift(up, 1, range(t - 1, line - 1))
        down = shift(down, -1, range(1, line - t + 1))
        has_up = (at >= t).astype(jnp.int32)
        has_down = (at + t < line).astype(jnp.int32)
        crossed_up, crossed_down = cross_arrivals(up, down, t)
        held += [
            (up, at - t, across, has_up),
            (crossed_up, at - t, 1 - across, has_up),
            (down, at + t, across, has_down),
            (crossed_down, at + t, 1 - across, has_down),
        ]
    return held


def merge_lines(parts, merged, beside, last):
    line = lax.axis_size("pages") // 4
    at = lax.axis_index("pages") // 4
    turns = []
    for t in range(1, line):
        turns += [k for k in (line - t, t) if k not in turns]
    yes = jnp.int32(1)
    crossed = {k: swap(parts[k][1], 2) for k in turns + [0]}
    shares = {}

    def share(k):
        if k not in shares:
            shares[k] = merged([parts[k][0], crossed[k]], [yes, yes])
        return shares[k]

    up = down = None
    for t in range(1, line):
        up_out, down_out = share(line - t), share(t)
        if up is not None:
            up_out = merged([up_out, up], [yes, (at >= 1) & (at <= t - 1)])
            down_out = merged([down_out, down], [yes, (at <= line - 2) & (at >= line - t)])
        up_out, down_out = beside(t, (up_out, down_out))
        up = shift(up_out, 1, range(0, t))
        down = shift(down_out, -1, range(line - t, line))
    return merged([share(0), up, down, last()], [yes, at >= 1, at <= line - 2, yes])


def fresh_kernel(unit, scale2, q_ref, k_ref, v_ref, tok_ref, key_ref, o_ref):
    token, first, key = tok_ref[0:1, :], tok_ref[1:2, :], key_ref[:, 0:1]
    scores = lax.dot_general(
        k_ref[0], q_ref[0], (((1,), (1,)), ((), ())), preferred_element_type=jnp.float32
    )
    visible = (key <= token) & (key >= first)
    scores = jnp.where(visible, scores, low_score)
    peak = jnp.max(scores, axis=0, keepdims=True)
    weights = jnp.where(visible, jnp.exp2((scores - peak) * scale2), 0.0)
    totals = jnp.sum(weights, axis=0, keepdims=True)
    out = lax.dot_general(
        v_ref[0], weights.astype(jnp.bfloat16), (((0,), (0,)), ((), ())),
        preferred_element_type=jnp.float32,
    )
    out = out / totals
    part_len = out.shape[1]
    pad = -part_len % 128
    out = jnp.concatenate([out, jnp.zeros((out.shape[0], pad), jnp.float32)], axis=1)
    o_ref[0, :part_len, :] = out.T[:part_len].astype(jnp.bfloat16)
    sent = peak.astype(jnp.bfloat16).astype(jnp.float32)
    totals = totals * jnp.exp2((peak - sent) * scale2)
    high = totals.astype(jnp.bfloat16).astype(jnp.float32)
    kinds = [
        [values[:, at : at + unit] for at in range(0, part_len, unit)]
        for values in (sent, high, totals - high)
    ]
    o_ref[0, part_len:, :] = stat_block(kinds, o_ref.shape[1] - part_len)


def fresh_attention(q_chip, k_window, v_window, token_rows, key_cols, unit, scale2):
    heads, part_len, head_dim = q_chip.shape
    _, _, pad_to = stat_rows_of(part_len, unit)
    own = lambda x: pl.BlockSpec((1,) + x.shape[1:], lambda h: (h, 0, 0))
    fixed = lambda x: pl.BlockSpec(x.shape, lambda h: (0, 0))
    return pl.pallas_call(
        lambda *refs: fresh_kernel(unit, scale2, *refs),
        grid=(heads,),
        in_specs=[own(q_chip), own(k_window), own(v_window), fixed(token_rows), fixed(key_cols)],
        out_specs=pl.BlockSpec((1, part_len + pad_to, head_dim), lambda h: (h, 0, 0)),
        out_shape=jax.ShapeDtypeStruct((heads, part_len + pad_to, head_dim), jnp.bfloat16),
        compiler_params=pltpu.CompilerParams(vmem_limit_bytes=40 * 2**20),
        name="fresh_attention",
    )(q_chip, k_window, v_window, token_rows, key_cols)


def project_kernel(at_ref, mine_ref, other_ref, w_mine_ref, w_other_ref, out_ref, rows_ref):
    core = at_ref[0]
    wide = rows_ref.shape[2]

    @pl.when(pl.program_id(0) == 0)
    def _():
        for index, ref in enumerate((mine_ref, other_ref)):
            rows_ref[index] = jnp.concatenate([ref[h] for h in range(ref.shape[0])], axis=1)

    parts = []
    for w_ref in (w_mine_ref, w_other_ref):
        total = 0.0
        for d in range(2):
            feats = pl.ds(pl.multiple_of((core ^ d) * wide, wide), wide)
            total = total + jnp.dot(
                rows_ref[d], w_ref[0, feats, :], preferred_element_type=jnp.float32
            )
        parts.append(total)
    out = jnp.where(
        core == 0, jnp.concatenate(parts, axis=1), jnp.concatenate(parts[::-1], axis=1)
    )
    out_ref[...] = out.astype(out_ref.dtype)


def project(mine, other, weights, core, line_at, across, owner, groups, dtype):
    half, tok_dev, head_dim = mine.shape
    chips, feats, cols = weights[0].shape
    line = chips // 2
    blocks = chips // groups

    def place(j, at):
        there = at[3] * (line // groups) + j // 2
        return (2 * lax.rem(at[1] + line - there, line) + ((j % 2) ^ at[2]), 0, 0)

    rows_spec = pl.BlockSpec(mine.shape, lambda j, at: (0, 0, 0))
    return pl.pallas_call(
        project_kernel,
        grid_spec=pltpu.PrefetchScalarGridSpec(
            num_scalar_prefetch=1,
            grid=(blocks,),
            in_specs=[rows_spec, rows_spec] + [pl.BlockSpec((1, feats, cols), place)] * 2,
            out_specs=pl.BlockSpec((tok_dev, 2 * cols), lambda j, at: (0, j)),
            scratch_shapes=[pltpu.VMEM((2, tok_dev, half * head_dim), jnp.bfloat16)],
        ),
        out_shape=jax.ShapeDtypeStruct((tok_dev, blocks * 2 * cols), dtype),
        compiler_params=pltpu.CompilerParams(vmem_limit_bytes=60 * 2**20),
        name="project",
    )(jnp.stack([core, line_at, across, owner]), mine, other, *weights)


def per_device(
    queries,
    keys,
    values,
    key_cache,
    value_cache,
    cache_len,
    page_table,
    append_slots,
    out_weight,
    out_bias,
):
    tok_dev, head_count, head_dim = queries.shape
    requests = cache_len.shape[0]
    max_pages = page_table.shape[1]
    new_pages = append_slots.shape[1]
    span_len = new_pages * PAGE
    slot_count = key_cache.shape[0]
    tokens = requests * span_len
    page_devs = tokens // tok_dev
    scale2 = math.log2(math.e) / math.sqrt(head_dim)
    device_at = lax.axis_index("pages")
    token_ids = device_at * tok_dev + jnp.arange(tok_dev, dtype=jnp.int32)
    request_ids = token_ids // span_len
    request_grid = jnp.arange(requests, dtype=jnp.int32)
    starts = jnp.sum(
        jnp.where(request_ids[:, None] == request_grid[None, :], cache_len[None, :], 0), axis=1
    )
    positions = (starts + token_ids % span_len).astype(jnp.float32)
    rotated_q = rotate(queries.astype(jnp.float32), positions).astype(jnp.bfloat16)
    rotated_k = rotate(keys.astype(jnp.float32), positions).astype(jnp.bfloat16)
    core = device_at % 2
    half = head_count // 2
    chip_len = 2 * tok_dev

    def halves(x):
        return (
            lax.dynamic_slice_in_dim(x, core * half, half, 0),
            lax.dynamic_slice_in_dim(x, (1 - core) * half, half, 0),
        )

    def in_order(mine, got, axis):
        return jnp.where(
            core == 0,
            jnp.concatenate([mine, got], axis=axis),
            jnp.concatenate([got, mine], axis=axis),
        )

    q_own = jnp.transpose(rotated_q, (1, 0, 2))
    q_mine, q_other = halves(q_own)
    q_chip = in_order(q_mine, swap(q_other, 1), 1)
    q_places = gather_lines(q_chip)
    groups = lax.axis_size("heads")
    group_at = lax.axis_index("heads")
    q_list = [q for q, _, _, _ in q_places]
    natural = Layout((0, 1, 2))
    all_k = lax.all_gather(rotated_k, "pages", axis=0, tiled=True)
    all_v = lax.all_gather(values, "pages", axis=0, tiled=True)
    all_k = with_layout_constraint(all_k, natural)
    all_v = with_layout_constraint(all_v, natural)
    barrier = lax.optimization_barrier
    line = page_devs // 4
    q_list, w_own = barrier((q_list, out_weight))
    w_up, w_down = {1: shift(w_own, 1, range(line - 1))}, {1: shift(w_own, -1, range(1, line))}
    w_cross = {0: swap(w_own, 2)}

    my_slots = device_at * slot_count + jnp.arange(slot_count, dtype=jnp.int32)
    chip_slots = jnp.concatenate(
        [my_slots, (device_at ^ 1) * slot_count + jnp.arange(slot_count, dtype=jnp.int32)]
    )
    cached_hit = page_table.reshape(-1)[None, :] == chip_slots[:, None]
    fresh_hit = append_slots.reshape(-1)[None, :] == my_slots[:, None]
    table_at = jnp.arange(requests * max_pages, dtype=jnp.int32)
    shown = (table_at % max_pages) * PAGE < jnp.repeat(cache_len, max_pages)
    is_fresh = jnp.any(fresh_hit, axis=1)
    fresh_index = jnp.sum(
        jnp.where(fresh_hit, jnp.arange(requests * new_pages, dtype=jnp.int32)[None, :], 0), axis=1
    )
    slot_key = requests - jnp.sum(
        jnp.where(cached_hit & shown[None, :], requests - (table_at // max_pages)[None, :], 0),
        axis=1,
    )
    slot_at = jnp.arange(2 * slot_count, dtype=jnp.int32)
    earlier = (slot_key[None, :] < slot_key[:, None]) | (
        (slot_key[None, :] == slot_key[:, None]) & (slot_at[None, :] < slot_at[:, None])
    )
    rank = jnp.sum(earlier.astype(jnp.int32), axis=1)
    order = jnp.sum(jnp.where(rank[None, :] == slot_at[:, None], slot_at[None, :], 0), axis=1)
    slot_starts = jnp.sum((slot_key[None, :] < request_grid[:, None]).astype(jnp.int32), axis=1)
    slot_counts = jnp.sum((slot_key[None, :] == request_grid[:, None]).astype(jnp.int32), axis=1)

    k_mine, k_other = halves(jnp.transpose(key_cache, (2, 0, 1, 3)))
    v_mine, v_other = halves(jnp.transpose(value_cache, (2, 0, 3, 1)))
    k_heads = jnp.concatenate([k_mine, swap(k_other, 1)], axis=1)
    v_heads = jnp.concatenate([v_mine, swap(v_other, 1)], axis=1)

    unit = math.gcd(span_len, tok_dev)
    line_at, across = device_at // 4, (device_at // 2) % 2
    outs = cached_attention(
        q_list,
        [jnp.clip(at, 0, line - 1) * 2 + side for _, at, side, _ in q_places],
        [ok for _, _, _, ok in q_places],
        [((line_at + k) % line) * 2 + (across ^ d) for k in range(line) for d in range(2)],
        k_heads,
        v_heads,
        order,
        slot_starts,
        slot_counts,
        span_len,
        unit,
        scale2,
    )
    outs, w_up[1], w_down[1], w_cross[0] = barrier((outs, w_up[1], w_down[1], w_cross[0]))
    merged = lambda parts, ok: merge(parts, ok, chip_len, unit, scale2)

    def beside(t, sent):
        if t + 1 < line:
            up = shift(w_up[t], 1, range(t, line - 1))
            down = shift(w_down[t], -1, range(1, line - t))
            sent, w_up[t + 1], w_down[t + 1] = barrier((sent, up, down))
        if t > 1:
            sent, w_cross[t - 1] = barrier((sent, w_cross[t - 1]))
        w_cross[t] = cross_arrivals(w_up[t], w_down[t], t)
        return sent

    def fresh_part():
        chip_at = device_at // 2
        back = -(-(span_len - math.gcd(span_len, chip_len)) // chip_len)
        window = (back + 1) * chip_len
        window_at = jnp.maximum(chip_at - back, 0) * chip_len

        def by_head(rows):
            rows = lax.dynamic_slice(
                rows, (window_at, core * half, 0), (window, half, head_dim)
            )
            return jnp.transpose(rows, (1, 0, 2))

        chip_tokens = chip_at * chip_len + jnp.arange(chip_len, dtype=jnp.int32)
        token_rows = jnp.stack([chip_tokens, chip_tokens // span_len * span_len])
        key_cols = (window_at + jnp.arange(window, dtype=jnp.int32))[:, None]
        return fresh_attention(
            q_chip, by_head(all_k), by_head(all_v), token_rows, key_cols, unit, scale2
        )

    chip_part = merge_lines(
        [outs[2 * k : 2 * k + 2] for k in range(line)], merged, beside, fresh_part
    )
    rows_of = lambda c: lax.dynamic_slice_in_dim(chip_part[:, :chip_len], c * tok_dev, tok_dev, 1)
    own_rows, got_rows = rows_of(core), swap(rows_of(1 - core), 1)
    found = [w_own, w_cross[0]]
    for k in range(1, line):
        for pick in (lambda t: (w_up[t], w_down[t]), lambda t: w_cross[t]):
            found.append(jnp.where(line_at >= k, pick(k)[0], pick(line - k)[1]))
    w_mine = jnp.stack(found)
    weights = [w_mine, swap(w_mine, 1)]
    total = out_bias[None, :]
    for s in range(groups - 1, -1, -1):
        owner = (group_at + s) % groups
        part = project(
            own_rows,
            got_rows,
            weights,
            core,
            line_at,
            across,
            owner,
            groups,
            jnp.bfloat16 if s else jnp.float32,
        )
        if s:
            part = lax.ppermute(part, "heads", [(h, (h + s) % groups) for h in range(groups)])
        total = total + part.astype(jnp.float32)
    hidden = total.astype(jnp.bfloat16)
    page_shape = (requests * new_pages, PAGE, head_count, head_dim)
    key_out, value_out = write_pages(
        key_cache,
        value_cache,
        all_k.reshape(page_shape),
        all_v.reshape(page_shape),
        is_fresh,
        fresh_index,
    )
    return (hidden, key_out, value_out)


def solution(mesh):
    placed = (
        P("pages", "heads", None),
        P("pages", "heads", None),
        P("pages", "heads", None),
        P("pages", None, "heads", None),
        P("pages", None, "heads", None),
        P(),
        P(),
        P(),
        P("heads", "pages"),
        P("heads"),
    )
    return jax.shard_map(
        per_device,
        mesh=mesh,
        in_specs=placed,
        out_specs=(
            P("pages", "heads"),
            P("pages", None, "heads", None),
            P("pages", None, "heads", None),
        ),
        check_vma=False,
    )
```

```python
import functools
import math

import jax
import jax.numpy as jnp
from jax import lax
from jax.experimental import pallas as pl
from jax.experimental.layout import Layout, with_layout_constraint
from jax.experimental.pallas import tpu as pltpu
from jax.sharding import PartitionSpec as P

ROT = 32
PAGE = 128
QTILE = 256

low_score = -(2.0**99)


def rotate(vectors, positions):
    half_rot = ROT // 2
    inv_freq = 10000.0 ** (-2.0 * jnp.arange(half_rot, dtype=jnp.float32) / ROT)
    angles = positions[:, None] * inv_freq[None, :]
    cosine = jnp.cos(angles)[:, None, :]
    sine = jnp.sin(angles)[:, None, :]
    first_half = vectors[..., :half_rot]
    second_half = vectors[..., half_rot:ROT]
    return jnp.concatenate(
        [
            first_half * cosine - second_half * sine,
            second_half * cosine + first_half * sine,
            vectors[..., ROT:],
        ],
        axis=-1,
    )


def stat_rows_of(part_len, unit):
    per_unit = -(-unit // 128)
    units = part_len // unit
    return per_unit, units, -(-3 * units * per_unit // 16) * 16


def stat_rows(row):
    unit = row.shape[1]
    full = -(-unit // 128) * 128
    if full > unit:
        row = jnp.concatenate([row, jnp.zeros((1, full - unit), row.dtype)], axis=1)
    return [row[:, at : at + 128] for at in range(0, full, 128)]


def stat_block(kinds, pad_to):
    rows = [piece for kind in kinds for row in kind for piece in stat_rows(row)]
    rows.append(jnp.zeros((pad_to - len(rows), 128), jnp.float32))
    return jnp.concatenate(rows, axis=0).astype(jnp.bfloat16)


def cached_kernel(unit, stat_unit, span, scale2, places, at_ref, ok_ref, order_ref, start_ref, count_ref,
                  *refs):
    q_refs, (k_ref, v_ref), refs = refs[:places], refs[places : places + 2], refs[places + 2 :]
    o_refs, (q_all, o_all, s_all, q_scr, m_scr, l_scr, acc_scr) = refs[:-7], refs[-7:]
    requests = count_ref.shape[0]
    chips, part_len, _ = q_all.shape
    per_part = part_len // unit
    per_request = span // unit
    per_unit, units, pad_to = stat_rows_of(part_len, stat_unit)

    for index in range(places):

        @pl.when(ok_ref[index] > 0)
        def _(index=index):
            q_all[at_ref[index]] = q_refs[index][0]

    def place(at, per_part):
        return at // per_part, at % per_part

    def one_request(request, _):
        for index in range(per_request):
            part, piece = place(request * per_request + index, per_part)
            row = pl.ds(pl.multiple_of(piece * unit, unit), unit)
            q_scr[index * unit : (index + 1) * unit, :] = q_all[part, row, :]
        first = start_ref[request]
        count = count_ref[request]
        m_scr[...] = jnp.full((1, span), low_score, jnp.float32)
        l_scr[...] = jnp.zeros((1, span), jnp.float32)
        acc_scr[...] = jnp.zeros(acc_scr.shape, jnp.float32)

        def pages(slots):
            k = jnp.concatenate([k_ref[0, s] for s in slots], axis=0)
            v = jnp.concatenate([v_ref[0, s] for s in slots], axis=1)
            for c in range(0, span, QTILE):
                cols = slice(c, c + QTILE)
                scores = lax.dot_general(
                    k, q_scr[cols, :], (((1,), (1,)), ((), ())),
                    preferred_element_type=jnp.float32,
                )
                before = m_scr[:, cols]
                peak = jnp.maximum(before, jnp.max(scores, axis=0, keepdims=True))
                weights = jnp.exp2((scores - peak) * scale2)
                fade = jnp.exp2((before - peak) * scale2)
                m_scr[:, cols] = peak
                l_scr[:, cols] = l_scr[:, cols] * fade + jnp.sum(weights, axis=0, keepdims=True)
                acc_scr[:, cols] = acc_scr[:, cols] * fade + jnp.dot(
                    v, weights.astype(jnp.bfloat16), preferred_element_type=jnp.float32
                )

        def pair(index, _):
            at = first + 2 * index
            pages([order_ref[at], order_ref[at + 1]])
            return 0

        lax.fori_loop(0, count // 2, pair, 0)

        @pl.when(count % 2 == 1)
        def _():
            pages([order_ref[first + count - 1]])

        totals = l_scr[...]
        peaks = m_scr[...]
        out = (acc_scr[...] / jnp.maximum(totals, 1e-30)).T.astype(jnp.bfloat16)
        sent = peaks.astype(jnp.bfloat16).astype(jnp.float32)
        totals = totals * jnp.exp2((peaks - sent) * scale2)
        high = totals.astype(jnp.bfloat16).astype(jnp.float32)
        kinds = [sent, high, totals - high]
        for index in range(per_request):
            part, piece = place(request * per_request + index, per_part)
            row = pl.ds(pl.multiple_of(piece * unit, unit), unit)
            o_all[part, row, :] = out[index * unit : (index + 1) * unit, :]
        for index in range(span // stat_unit):
            part, piece = place(request * (span // stat_unit) + index, units)
            cols = slice(index * stat_unit, (index + 1) * stat_unit)
            for kind, values in enumerate(kinds):
                for r, line in enumerate(stat_rows(values[:, cols])):
                    at = (kind * units + piece) * per_unit + r
                    s_all[part, pl.ds(at, 1), :] = line
        return 0

    lax.fori_loop(0, requests, one_request, 0)
    for index in range(chips):
        part = at_ref[places + index]
        o_refs[index][0, :part_len, :] = o_all[part]
        o_refs[index][0, part_len:, :] = s_all[part].astype(jnp.bfloat16)


def cached_attention(q_places, at, ok, out_at, k_heads, v_heads, order, starts, counts, span,
                     stat_unit, scale2):
    places = len(q_places)
    chips = len(out_at)
    heads, part_len, head_dim = q_places[0].shape
    slots = k_heads.shape[1]
    unit = math.gcd(span, part_len)
    _, _, pad_to = stat_rows_of(part_len, stat_unit)
    own_block = lambda *dims: pl.BlockSpec(
        (1,) + dims, lambda h, *_: (h,) + (0,) * len(dims)
    )
    return pl.pallas_call(
        lambda *refs: cached_kernel(unit, stat_unit, span, scale2, places, *refs),
        grid_spec=pltpu.PrefetchScalarGridSpec(
            num_scalar_prefetch=5,
            grid=(heads,),
            in_specs=[own_block(part_len, head_dim)] * places
            + [own_block(slots, PAGE, head_dim), own_block(slots, head_dim, PAGE)],
            out_specs=[own_block(part_len + pad_to, head_dim)] * chips,
            scratch_shapes=[
                pltpu.VMEM((chips, part_len, head_dim), jnp.bfloat16),
                pltpu.VMEM((chips, part_len, head_dim), jnp.bfloat16),
                pltpu.VMEM((chips, pad_to, 128), jnp.float32),
                pltpu.VMEM((span, head_dim), jnp.bfloat16),
                pltpu.VMEM((1, span), jnp.float32),
                pltpu.VMEM((1, span), jnp.float32),
                pltpu.VMEM((head_dim, span), jnp.float32),
            ],
        ),
        out_shape=[
            jax.ShapeDtypeStruct((heads, part_len + pad_to, head_dim), jnp.bfloat16)
        ] * chips,
        compiler_params=pltpu.CompilerParams(vmem_limit_bytes=60 * 2**20),
        cost_estimate=pl.CostEstimate(
            flops=40 * 10**9, bytes_accessed=20 * 2**20, transcendentals=10**7
        ),
        name="cached_attention",
    )(jnp.stack(at + out_at), jnp.stack(ok), order, starts, counts, *q_places, k_heads, v_heads)


def merge_kernel(unit, part_len, scale2, ok_ref, *refs):
    in_refs, out_ref = refs[:-1], refs[-1]
    heads, _, width = out_ref.shape
    _, units, pad_to = stat_rows_of(part_len, unit)
    oks = [ok_ref[index] > 0 for index in range(len(in_refs))]
    for h in range(heads):
        peaks, totals = [], []
        for ok, ref in zip(oks, in_refs):
            stat = ref[h, part_len:, :].astype(jnp.float32)
            peaks.append(jnp.where(ok, stat[:units], low_score))
            total = stat[units : 2 * units] + stat[2 * units : 3 * units]
            totals.append(jnp.where(ok, total, 0.0))
        top = functools.reduce(jnp.maximum, peaks)
        shares = [t * jnp.exp2((p - top) * scale2) for t, p in zip(totals, peaks)]
        total = functools.reduce(jnp.add, shares)
        inverse = 1.0 / jnp.maximum(total, 1e-30)
        merged = [0.0] * units
        for ref, share in zip(in_refs, shares):
            weight = jnp.concatenate(
                [share * inverse, jnp.zeros((-units % 8, 128), jnp.float32)], axis=0
            ).T
            rows = ref[h, :part_len, :].astype(jnp.float32)
            for u in range(units):
                merged[u] = merged[u] + weight[:unit, u : u + 1] * rows[u * unit : (u + 1) * unit]
        high = total.astype(jnp.bfloat16).astype(jnp.float32)
        stats = [top, high, total - high, jnp.zeros((pad_to - 3 * units, width), jnp.float32)]
        out_ref[h, :part_len, :] = jnp.concatenate(merged, axis=0).astype(jnp.bfloat16)
        out_ref[h, part_len:, :] = jnp.concatenate(stats, axis=0).astype(jnp.bfloat16)


def merge(parts, ok, part_len, unit, scale2):
    heads = parts[0].shape[0]
    step = max(1, heads // 2)
    block = pl.BlockSpec((step,) + parts[0].shape[1:], lambda h, *_: (h, 0, 0))
    return pl.pallas_call(
        lambda *refs: merge_kernel(unit, part_len, scale2, *refs),
        grid_spec=pltpu.PrefetchScalarGridSpec(
            num_scalar_prefetch=1,
            grid=(heads // step,),
            in_specs=[block] * len(parts),
            out_specs=block,
        ),
        out_shape=jax.ShapeDtypeStruct(parts[0].shape, jnp.bfloat16),
        name="merge",
    )(jnp.stack(ok).astype(jnp.int32), *parts)


def page_kernel(fresh_ref, index_ref, kc_ref, vc_ref, kn_ref, vn_ref, ko_ref, vo_ref):
    fresh = fresh_ref[pl.program_id(0)] > 0

    @pl.when(fresh)
    def _():
        ko_ref[...] = kn_ref[...]
        vo_ref[...] = vn_ref[...]

    @pl.when(jnp.logical_not(fresh))
    def _():
        ko_ref[...] = kc_ref[...]
        vo_ref[...] = vc_ref[...]


def write_pages(key_cache, value_cache, new_keys, new_values, is_fresh, fresh_index):
    block = (1,) + key_cache.shape[1:]
    own = pl.BlockSpec(block, lambda s, fresh, index: (s, 0, 0, 0))
    new = pl.BlockSpec(block, lambda s, fresh, index: (index[s], 0, 0, 0))
    return pl.pallas_call(
        page_kernel,
        grid_spec=pltpu.PrefetchScalarGridSpec(
            num_scalar_prefetch=2,
            grid=(key_cache.shape[0],),
            in_specs=[own, own, new, new],
            out_specs=[own, own],
        ),
        out_shape=[jax.ShapeDtypeStruct(key_cache.shape, key_cache.dtype)] * 2,
        compiler_params=pltpu.CompilerParams(vmem_limit_bytes=40 * 2**20),
        name="write_pages",
    )(is_fresh.astype(jnp.int32), fresh_index, key_cache, value_cache, new_keys, new_values)


def swap(x, bit):
    devs = lax.axis_size("pages")
    return lax.ppermute(x, "pages", [(p, p ^ bit) for p in range(devs)])


def shift(x, hop, senders):
    devs = lax.axis_size("pages")
    moves = [(p, p + 4 * hop) for p in range(devs) if p // 4 in senders]
    return lax.ppermute(x, "pages", moves)


def gather_line(x):
    line = lax.axis_size("pages") // 4
    groups = [[g + 4 * i for i in range(line)] for g in range(4)]
    return lax.all_gather(x, "pages", axis=0, tiled=False, axis_index_groups=groups)


def gather_lines(x):
    line = lax.axis_size("pages") // 4
    device_at = lax.axis_index("pages")
    at, across = device_at // 4, (device_at // 2) % 2
    always = jnp.int32(1)
    held = [(x, at, across, always), (swap(x, 2), at, 1 - across, always)]
    up = down = x
    for t in range(1, line):
        up = shift(up, 1, range(t - 1, line - 1))
        down = shift(down, -1, range(1, line - t + 1))
        has_up = (at >= t).astype(jnp.int32)
        has_down = (at + t < line).astype(jnp.int32)
        devs = lax.axis_size("pages")
        cross_up = [(p, p ^ 2) for p in range(devs) if p // 4 >= t]
        cross_down = [(p, p ^ 2) for p in range(devs) if p // 4 + t < line]
        held += [
            (up, at - t, across, has_up),
            (lax.ppermute(up, "pages", cross_up), at - t, 1 - across, has_up),
            (down, at + t, across, has_down),
            (lax.ppermute(down, "pages", cross_down), at + t, 1 - across, has_down),
        ]
    return held


def merge_lines(parts, merged, last):
    line = lax.axis_size("pages") // 4
    at = lax.axis_index("pages") // 4
    turns = []
    for t in range(1, line):
        turns += [k for k in (line - t, t) if k not in turns]
    yes = jnp.int32(1)
    crossed = {k: swap(parts[k][1], 2) for k in turns + [0]}
    shares = {}

    def share(k):
        if k not in shares:
            shares[k] = merged([parts[k][0], crossed[k]], [yes, yes])
        return shares[k]

    up = down = None
    for t in range(1, line):
        up_out, down_out = share(line - t), share(t)
        if up is not None:
            up_out = merged([up_out, up], [yes, (at >= 1) & (at <= t - 1)])
            down_out = merged([down_out, down], [yes, (at <= line - 2) & (at >= line - t)])
        up = shift(up_out, 1, range(0, t))
        down = shift(down_out, -1, range(line - t, line))
    return merged([share(0), up, down, last()], [yes, at >= 1, at <= line - 2, yes])


def fresh_kernel(unit, scale2, q_ref, k_ref, v_ref, tok_ref, key_ref, o_ref):
    token, first, key = tok_ref[0:1, :], tok_ref[1:2, :], key_ref[:, 0:1]
    scores = lax.dot_general(
        k_ref[0], q_ref[0], (((1,), (1,)), ((), ())), preferred_element_type=jnp.float32
    )
    visible = (key <= token) & (key >= first)
    scores = jnp.where(visible, scores, low_score)
    peak = jnp.max(scores, axis=0, keepdims=True)
    weights = jnp.where(visible, jnp.exp2((scores - peak) * scale2), 0.0)
    totals = jnp.sum(weights, axis=0, keepdims=True)
    out = lax.dot_general(
        v_ref[0], weights.astype(jnp.bfloat16), (((0,), (0,)), ((), ())),
        preferred_element_type=jnp.float32,
    )
    out = out / totals
    part_len = out.shape[1]
    pad = -part_len % 128
    out = jnp.concatenate([out, jnp.zeros((out.shape[0], pad), jnp.float32)], axis=1)
    o_ref[0, :part_len, :] = out.T[:part_len].astype(jnp.bfloat16)
    sent = peak.astype(jnp.bfloat16).astype(jnp.float32)
    totals = totals * jnp.exp2((peak - sent) * scale2)
    high = totals.astype(jnp.bfloat16).astype(jnp.float32)
    kinds = [
        [values[:, at : at + unit] for at in range(0, part_len, unit)]
        for values in (sent, high, totals - high)
    ]
    o_ref[0, part_len:, :] = stat_block(kinds, o_ref.shape[1] - part_len)


def fresh_attention(q_chip, k_window, v_window, token_rows, key_cols, unit, scale2):
    heads, part_len, head_dim = q_chip.shape
    _, _, pad_to = stat_rows_of(part_len, unit)
    own = lambda x: pl.BlockSpec((1,) + x.shape[1:], lambda h: (h, 0, 0))
    fixed = lambda x: pl.BlockSpec(x.shape, lambda h: (0, 0))
    return pl.pallas_call(
        lambda *refs: fresh_kernel(unit, scale2, *refs),
        grid=(heads,),
        in_specs=[own(q_chip), own(k_window), own(v_window), fixed(token_rows), fixed(key_cols)],
        out_specs=pl.BlockSpec((1, part_len + pad_to, head_dim), lambda h: (h, 0, 0)),
        out_shape=jax.ShapeDtypeStruct((heads, part_len + pad_to, head_dim), jnp.bfloat16),
        compiler_params=pltpu.CompilerParams(vmem_limit_bytes=40 * 2**20),
        name="fresh_attention",
    )(q_chip, k_window, v_window, token_rows, key_cols)


def project_kernel(at_ref, mine_ref, other_ref, *refs):
    w_refs, (out_ref, rows_ref) = refs[:4], refs[4:]
    core = at_ref[0]
    wide = rows_ref.shape[2]

    @pl.when((pl.program_id(0) == 0) & (pl.program_id(1) == 0))
    def _():
        for index, ref in enumerate((mine_ref, other_ref)):
            rows_ref[index] = jnp.concatenate([ref[h] for h in range(ref.shape[0])], axis=1)

    for there in range(2):

        @pl.when(pl.program_id(0) == there)
        def _(there=there):
            parts = []
            for w_ref in w_refs[2 * there : 2 * there + 2]:
                total = 0.0
                for d in range(2):
                    feats = pl.ds(pl.multiple_of((core ^ d) * wide, wide), wide)
                    total = total + jnp.dot(
                        rows_ref[d], w_ref[0, feats, :], preferred_element_type=jnp.float32
                    )
                parts.append(total)
            out = jnp.where(
                core == 0, jnp.concatenate(parts, axis=1), jnp.concatenate(parts[::-1], axis=1)
            )
            out_ref[...] = out.astype(out_ref.dtype)


def project(mine, other, weights, core, across, owner, groups, dtype):
    half, tok_dev, head_dim = mine.shape
    line, feats, cols = weights[0].shape
    share = line // groups
    rows_spec = pl.BlockSpec(mine.shape, lambda y, z, at: (0, 0, 0))

    def weight_spec(there):
        def place(y, z, at):
            here = (y == there).astype(jnp.int32)
            return (at[2] * share + here * z + (1 - here) * (1 - there) * (share - 1), 0, 0)

        return pl.BlockSpec((1, feats, cols), place)

    return pl.pallas_call(
        project_kernel,
        grid_spec=pltpu.PrefetchScalarGridSpec(
            num_scalar_prefetch=1,
            grid=(2, share),
            in_specs=[rows_spec, rows_spec] + [weight_spec(t) for t in (0, 0, 1, 1)],
            out_specs=pl.BlockSpec((tok_dev, 2 * cols), lambda y, z, at: (0, 2 * z + (y ^ at[1]))),
            scratch_shapes=[pltpu.VMEM((2, tok_dev, half * head_dim), jnp.bfloat16)],
        ),
        out_shape=jax.ShapeDtypeStruct((tok_dev, 4 * share * cols), dtype),
        compiler_params=pltpu.CompilerParams(vmem_limit_bytes=60 * 2**20),
        name="project",
    )(jnp.stack([core, across, owner]), mine, other, *weights)


def per_device(
    queries,
    keys,
    values,
    key_cache,
    value_cache,
    cache_len,
    page_table,
    append_slots,
    out_weight,
    out_bias,
):
    tok_dev, head_count, head_dim = queries.shape
    requests = cache_len.shape[0]
    max_pages = page_table.shape[1]
    new_pages = append_slots.shape[1]
    span_len = new_pages * PAGE
    slot_count = key_cache.shape[0]
    tokens = requests * span_len
    page_devs = tokens // tok_dev
    scale2 = math.log2(math.e) / math.sqrt(head_dim)
    device_at = lax.axis_index("pages")
    token_ids = device_at * tok_dev + jnp.arange(tok_dev, dtype=jnp.int32)
    request_ids = token_ids // span_len
    request_grid = jnp.arange(requests, dtype=jnp.int32)
    starts = jnp.sum(
        jnp.where(request_ids[:, None] == request_grid[None, :], cache_len[None, :], 0), axis=1
    )
    positions = (starts + token_ids % span_len).astype(jnp.float32)
    rotated_q = rotate(queries.astype(jnp.float32), positions).astype(jnp.bfloat16)
    rotated_k = rotate(keys.astype(jnp.float32), positions).astype(jnp.bfloat16)
    core = device_at % 2
    half = head_count // 2
    chip_len = 2 * tok_dev

    def halves(x):
        return (
            lax.dynamic_slice_in_dim(x, core * half, half, 0),
            lax.dynamic_slice_in_dim(x, (1 - core) * half, half, 0),
        )

    def in_order(mine, got, axis):
        return jnp.where(
            core == 0,
            jnp.concatenate([mine, got], axis=axis),
            jnp.concatenate([got, mine], axis=axis),
        )

    q_own = jnp.transpose(rotated_q, (1, 0, 2))
    q_mine, q_other = halves(q_own)
    q_chip = in_order(q_mine, swap(q_other, 1), 1)
    q_places = gather_lines(q_chip)
    groups = lax.axis_size("heads")
    group_at = lax.axis_index("heads")
    q_list = [q for q, _, _, _ in q_places]
    natural = Layout((0, 1, 2))
    all_k = lax.all_gather(rotated_k, "pages", axis=0, tiled=True)
    all_v = lax.all_gather(values, "pages", axis=0, tiled=True)
    all_k = with_layout_constraint(all_k, natural)
    all_v = with_layout_constraint(all_v, natural)
    barrier = lax.optimization_barrier
    q_list, line_w = barrier((q_list, gather_line(out_weight)))
    across_w = swap(line_w, 2)

    my_slots = device_at * slot_count + jnp.arange(slot_count, dtype=jnp.int32)
    chip_slots = jnp.concatenate(
        [my_slots, (device_at ^ 1) * slot_count + jnp.arange(slot_count, dtype=jnp.int32)]
    )
    cached_hit = page_table.reshape(-1)[None, :] == chip_slots[:, None]
    fresh_hit = append_slots.reshape(-1)[None, :] == my_slots[:, None]
    table_at = jnp.arange(requests * max_pages, dtype=jnp.int32)
    shown = (table_at % max_pages) * PAGE < jnp.repeat(cache_len, max_pages)
    is_fresh = jnp.any(fresh_hit, axis=1)
    fresh_index = jnp.sum(
        jnp.where(fresh_hit, jnp.arange(requests * new_pages, dtype=jnp.int32)[None, :], 0), axis=1
    )
    slot_key = requests - jnp.sum(
        jnp.where(cached_hit & shown[None, :], requests - (table_at // max_pages)[None, :], 0),
        axis=1,
    )
    slot_at = jnp.arange(2 * slot_count, dtype=jnp.int32)
    earlier = (slot_key[None, :] < slot_key[:, None]) | (
        (slot_key[None, :] == slot_key[:, None]) & (slot_at[None, :] < slot_at[:, None])
    )
    rank = jnp.sum(earlier.astype(jnp.int32), axis=1)
    order = jnp.sum(jnp.where(rank[None, :] == slot_at[:, None], slot_at[None, :], 0), axis=1)
    slot_starts = jnp.sum((slot_key[None, :] < request_grid[:, None]).astype(jnp.int32), axis=1)
    slot_counts = jnp.sum((slot_key[None, :] == request_grid[:, None]).astype(jnp.int32), axis=1)

    k_mine, k_other = halves(jnp.transpose(key_cache, (2, 0, 1, 3)))
    v_mine, v_other = halves(jnp.transpose(value_cache, (2, 0, 3, 1)))
    k_heads = jnp.concatenate([k_mine, swap(k_other, 1)], axis=1)
    v_heads = jnp.concatenate([v_mine, swap(v_other, 1)], axis=1)

    unit = math.gcd(span_len, tok_dev)
    line = page_devs // 4
    line_at, across = device_at // 4, (device_at // 2) % 2
    outs = cached_attention(
        q_list,
        [jnp.clip(at, 0, line - 1) * 2 + side for _, at, side, _ in q_places],
        [ok for _, _, _, ok in q_places],
        [((line_at + k) % line) * 2 + (across ^ d) for k in range(line) for d in range(2)],
        k_heads,
        v_heads,
        order,
        slot_starts,
        slot_counts,
        span_len,
        unit,
        scale2,
    )
    outs, across_w = barrier((outs, across_w))
    merged = lambda parts, ok: merge(parts, ok, chip_len, unit, scale2)

    def fresh_part():
        chip_at = device_at // 2
        back = -(-(span_len - math.gcd(span_len, chip_len)) // chip_len)
        window = (back + 1) * chip_len
        window_at = jnp.maximum(chip_at - back, 0) * chip_len

        def by_head(rows):
            rows = lax.dynamic_slice(
                rows, (window_at, core * half, 0), (window, half, head_dim)
            )
            return jnp.transpose(rows, (1, 0, 2))

        chip_tokens = chip_at * chip_len + jnp.arange(chip_len, dtype=jnp.int32)
        token_rows = jnp.stack([chip_tokens, chip_tokens // span_len * span_len])
        key_cols = (window_at + jnp.arange(window, dtype=jnp.int32))[:, None]
        return fresh_attention(
            q_chip, by_head(all_k), by_head(all_v), token_rows, key_cols, unit, scale2
        )

    chip_part = merge_lines(
        [outs[2 * k : 2 * k + 2] for k in range(line)], merged, fresh_part
    )
    rows_of = lambda c: lax.dynamic_slice_in_dim(chip_part[:, :chip_len], c * tok_dev, tok_dev, 1)
    own_rows, got_rows = rows_of(core), swap(rows_of(1 - core), 1)
    weights = [line_w, swap(line_w, 1), across_w, swap(across_w, 1)]
    total = out_bias[None, :]
    for s in range(groups - 1, -1, -1):
        owner = (group_at + s) % groups
        part = project(
            own_rows,
            got_rows,
            weights,
            core,
            across,
            owner,
            groups,
            jnp.bfloat16 if s else jnp.float32,
        )
        if s:
            part = lax.ppermute(part, "heads", [(h, (h + s) % groups) for h in range(groups)])
        total = total + part.astype(jnp.float32)
    hidden = total.astype(jnp.bfloat16)
    page_shape = (requests * new_pages, PAGE, head_count, head_dim)
    key_out, value_out = write_pages(
        key_cache,
        value_cache,
        all_k.reshape(page_shape),
        all_v.reshape(page_shape),
        is_fresh,
        fresh_index,
    )
    return (hidden, key_out, value_out)


def solution(mesh):
    placed = (
        P("pages", "heads", None),
        P("pages", "heads", None),
        P("pages", "heads", None),
        P("pages", None, "heads", None),
        P("pages", None, "heads", None),
        P(),
        P(),
        P(),
        P("heads", "pages"),
        P("heads"),
    )
    return jax.shard_map(
        per_device,
        mesh=mesh,
        in_specs=placed,
        out_specs=(
            P("pages", "heads"),
            P("pages", None, "heads", None),
            P("pages", None, "heads", None),
        ),
        check_vma=False,
    )
```

```python
import functools
import math

import jax
import jax.numpy as jnp
from jax import lax
from jax.experimental import pallas as pl
from jax.experimental.layout import Layout, with_layout_constraint
from jax.experimental.pallas import tpu as pltpu
from jax.sharding import PartitionSpec as P

ROT = 32
PAGE = 128
QTILE = 256

low_score = -(2.0**99)


def rotate(vectors, positions):
    half_rot = ROT // 2
    inv_freq = 10000.0 ** (-2.0 * jnp.arange(half_rot, dtype=jnp.float32) / ROT)
    angles = positions[:, None] * inv_freq[None, :]
    cosine = jnp.cos(angles)[:, None, :]
    sine = jnp.sin(angles)[:, None, :]
    first_half = vectors[..., :half_rot]
    second_half = vectors[..., half_rot:ROT]
    return jnp.concatenate(
        [
            first_half * cosine - second_half * sine,
            second_half * cosine + first_half * sine,
            vectors[..., ROT:],
        ],
        axis=-1,
    )


def stat_rows_of(part_len, unit):
    per_unit = -(-unit // 128)
    units = part_len // unit
    return per_unit, units, -(-3 * units * per_unit // 16) * 16


def stat_rows(row):
    unit = row.shape[1]
    full = -(-unit // 128) * 128
    if full > unit:
        row = jnp.concatenate([row, jnp.zeros((1, full - unit), row.dtype)], axis=1)
    return [row[:, at : at + 128] for at in range(0, full, 128)]


def stat_block(kinds, pad_to):
    rows = [piece for kind in kinds for row in kind for piece in stat_rows(row)]
    rows.append(jnp.zeros((pad_to - len(rows), 128), jnp.float32))
    return jnp.concatenate(rows, axis=0).astype(jnp.bfloat16)


def cached_kernel(unit, stat_unit, span, scale2, places, at_ref, ok_ref, order_ref, start_ref, count_ref,
                  *refs):
    q_refs, (k_ref, v_ref), refs = refs[:places], refs[places : places + 2], refs[places + 2 :]
    o_refs, (q_all, o_all, s_all, q_scr, m_scr, l_scr, acc_scr) = refs[:-7], refs[-7:]
    requests = count_ref.shape[0]
    chips, part_len, _ = q_all.shape
    per_part = part_len // unit
    per_request = span // unit
    per_unit, units, pad_to = stat_rows_of(part_len, stat_unit)

    for index in range(places):

        @pl.when(ok_ref[index] > 0)
        def _(index=index):
            q_all[at_ref[index]] = q_refs[index][0]

    def place(at, per_part):
        return at // per_part, at % per_part

    def one_request(request, _):
        for index in range(per_request):
            part, piece = place(request * per_request + index, per_part)
            row = pl.ds(pl.multiple_of(piece * unit, unit), unit)
            q_scr[index * unit : (index + 1) * unit, :] = q_all[part, row, :]
        first = start_ref[request]
        count = count_ref[request]
        m_scr[...] = jnp.full((1, span), low_score, jnp.float32)
        l_scr[...] = jnp.zeros((1, span), jnp.float32)
        acc_scr[...] = jnp.zeros(acc_scr.shape, jnp.float32)

        def pages(slots):
            k = jnp.concatenate([k_ref[0, s] for s in slots], axis=0)
            v = jnp.concatenate([v_ref[0, s] for s in slots], axis=1)
            for c in range(0, span, QTILE):
                cols = slice(c, c + QTILE)
                scores = lax.dot_general(
                    k, q_scr[cols, :], (((1,), (1,)), ((), ())),
                    preferred_element_type=jnp.float32,
                )
                before = m_scr[:, cols]
                peak = jnp.maximum(before, jnp.max(scores, axis=0, keepdims=True))
                weights = jnp.exp2((scores - peak) * scale2)
                fade = jnp.exp2((before - peak) * scale2)
                m_scr[:, cols] = peak
                l_scr[:, cols] = l_scr[:, cols] * fade + jnp.sum(weights, axis=0, keepdims=True)
                acc_scr[:, cols] = acc_scr[:, cols] * fade + jnp.dot(
                    v, weights.astype(jnp.bfloat16), preferred_element_type=jnp.float32
                )

        def four(index, _):
            pages([order_ref[first + 4 * index + i] for i in range(4)])
            return 0

        lax.fori_loop(0, count // 4, four, 0)
        for many in (2, 1):

            @pl.when((count // many) % 2 == 1)
            def _(many=many):
                at = first + count // (2 * many) * (2 * many)
                pages([order_ref[at + i] for i in range(many)])

        totals = l_scr[...]
        peaks = m_scr[...]
        out = (acc_scr[...] / jnp.maximum(totals, 1e-30)).T.astype(jnp.bfloat16)
        sent = peaks.astype(jnp.bfloat16).astype(jnp.float32)
        totals = totals * jnp.exp2((peaks - sent) * scale2)
        high = totals.astype(jnp.bfloat16).astype(jnp.float32)
        kinds = [sent, high, totals - high]
        for index in range(per_request):
            part, piece = place(request * per_request + index, per_part)
            row = pl.ds(pl.multiple_of(piece * unit, unit), unit)
            o_all[part, row, :] = out[index * unit : (index + 1) * unit, :]
        for index in range(span // stat_unit):
            part, piece = place(request * (span // stat_unit) + index, units)
            cols = slice(index * stat_unit, (index + 1) * stat_unit)
            for kind, values in enumerate(kinds):
                for r, line in enumerate(stat_rows(values[:, cols])):
                    at = (kind * units + piece) * per_unit + r
                    s_all[part, pl.ds(at, 1), :] = line
        return 0

    lax.fori_loop(0, requests, one_request, 0)
    for index in range(chips):
        part = at_ref[places + index]
        o_refs[index][0, :part_len, :] = o_all[part]
        o_refs[index][0, part_len:, :] = s_all[part].astype(jnp.bfloat16)


def cached_attention(q_places, at, ok, out_at, k_heads, v_heads, order, starts, counts, span,
                     stat_unit, scale2):
    places = len(q_places)
    chips = len(out_at)
    heads, part_len, head_dim = q_places[0].shape
    slots = k_heads.shape[1]
    unit = math.gcd(span, part_len)
    _, _, pad_to = stat_rows_of(part_len, stat_unit)
    own_block = lambda *dims: pl.BlockSpec(
        (1,) + dims, lambda h, *_: (h,) + (0,) * len(dims)
    )
    return pl.pallas_call(
        lambda *refs: cached_kernel(unit, stat_unit, span, scale2, places, *refs),
        grid_spec=pltpu.PrefetchScalarGridSpec(
            num_scalar_prefetch=5,
            grid=(heads,),
            in_specs=[own_block(part_len, head_dim)] * places
            + [own_block(slots, PAGE, head_dim), own_block(slots, head_dim, PAGE)],
            out_specs=[own_block(part_len + pad_to, head_dim)] * chips,
            scratch_shapes=[
                pltpu.VMEM((chips, part_len, head_dim), jnp.bfloat16),
                pltpu.VMEM((chips, part_len, head_dim), jnp.bfloat16),
                pltpu.VMEM((chips, pad_to, 128), jnp.float32),
                pltpu.VMEM((span, head_dim), jnp.bfloat16),
                pltpu.VMEM((1, span), jnp.float32),
                pltpu.VMEM((1, span), jnp.float32),
                pltpu.VMEM((head_dim, span), jnp.float32),
            ],
        ),
        out_shape=[
            jax.ShapeDtypeStruct((heads, part_len + pad_to, head_dim), jnp.bfloat16)
        ] * chips,
        compiler_params=pltpu.CompilerParams(vmem_limit_bytes=60 * 2**20),
        cost_estimate=pl.CostEstimate(
            flops=40 * 10**9, bytes_accessed=20 * 2**20, transcendentals=10**7
        ),
        name="cached_attention",
    )(jnp.stack(at + out_at), jnp.stack(ok), order, starts, counts, *q_places, k_heads, v_heads)


def merge_kernel(unit, part_len, scale2, ok_ref, *refs):
    in_refs, out_ref = refs[:-1], refs[-1]
    heads, _, width = out_ref.shape
    _, units, pad_to = stat_rows_of(part_len, unit)
    oks = [ok_ref[index] > 0 for index in range(len(in_refs))]
    for h in range(heads):
        peaks, totals = [], []
        for ok, ref in zip(oks, in_refs):
            stat = ref[h, part_len:, :].astype(jnp.float32)
            peaks.append(jnp.where(ok, stat[:units], low_score))
            total = stat[units : 2 * units] + stat[2 * units : 3 * units]
            totals.append(jnp.where(ok, total, 0.0))
        top = functools.reduce(jnp.maximum, peaks)
        shares = [t * jnp.exp2((p - top) * scale2) for t, p in zip(totals, peaks)]
        total = functools.reduce(jnp.add, shares)
        inverse = 1.0 / jnp.maximum(total, 1e-30)
        merged = [0.0] * units
        for ref, share in zip(in_refs, shares):
            weight = jnp.concatenate(
                [share * inverse, jnp.zeros((-units % 8, 128), jnp.float32)], axis=0
            ).T
            rows = ref[h, :part_len, :].astype(jnp.float32)
            for u in range(units):
                merged[u] = merged[u] + weight[:unit, u : u + 1] * rows[u * unit : (u + 1) * unit]
        high = total.astype(jnp.bfloat16).astype(jnp.float32)
        stats = [top, high, total - high, jnp.zeros((pad_to - 3 * units, width), jnp.float32)]
        out_ref[h, :part_len, :] = jnp.concatenate(merged, axis=0).astype(jnp.bfloat16)
        out_ref[h, part_len:, :] = jnp.concatenate(stats, axis=0).astype(jnp.bfloat16)


def merge(parts, ok, part_len, unit, scale2):
    heads = parts[0].shape[0]
    step = max(1, heads // 2)
    block = pl.BlockSpec((step,) + parts[0].shape[1:], lambda h, *_: (h, 0, 0))
    return pl.pallas_call(
        lambda *refs: merge_kernel(unit, part_len, scale2, *refs),
        grid_spec=pltpu.PrefetchScalarGridSpec(
            num_scalar_prefetch=1,
            grid=(heads // step,),
            in_specs=[block] * len(parts),
            out_specs=block,
        ),
        out_shape=jax.ShapeDtypeStruct(parts[0].shape, jnp.bfloat16),
        name="merge",
    )(jnp.stack(ok).astype(jnp.int32), *parts)


def page_kernel(fresh_ref, index_ref, kc_ref, vc_ref, kn_ref, vn_ref, ko_ref, vo_ref):
    fresh = fresh_ref[pl.program_id(0)] > 0

    @pl.when(fresh)
    def _():
        ko_ref[...] = kn_ref[...]
        vo_ref[...] = vn_ref[...]

    @pl.when(jnp.logical_not(fresh))
    def _():
        ko_ref[...] = kc_ref[...]
        vo_ref[...] = vc_ref[...]


def write_pages(key_cache, value_cache, new_keys, new_values, is_fresh, fresh_index):
    block = (1,) + key_cache.shape[1:]
    own = pl.BlockSpec(block, lambda s, fresh, index: (s, 0, 0, 0))
    new = pl.BlockSpec(block, lambda s, fresh, index: (index[s], 0, 0, 0))
    return pl.pallas_call(
        page_kernel,
        grid_spec=pltpu.PrefetchScalarGridSpec(
            num_scalar_prefetch=2,
            grid=(key_cache.shape[0],),
            in_specs=[own, own, new, new],
            out_specs=[own, own],
        ),
        out_shape=[jax.ShapeDtypeStruct(key_cache.shape, key_cache.dtype)] * 2,
        compiler_params=pltpu.CompilerParams(vmem_limit_bytes=40 * 2**20),
        name="write_pages",
    )(is_fresh.astype(jnp.int32), fresh_index, key_cache, value_cache, new_keys, new_values)


def swap(x, bit):
    devs = lax.axis_size("pages")
    return lax.ppermute(x, "pages", [(p, p ^ bit) for p in range(devs)])


def shift(x, hop, senders):
    devs = lax.axis_size("pages")
    moves = [(p, p + 4 * hop) for p in range(devs) if p // 4 in senders]
    return lax.ppermute(x, "pages", moves)


def gather_lines(x):
    line = lax.axis_size("pages") // 4
    device_at = lax.axis_index("pages")
    at, across = device_at // 4, (device_at // 2) % 2
    always = jnp.int32(1)
    held = [(x, at, across, always), (swap(x, 2), at, 1 - across, always)]
    up = down = x
    for t in range(1, line):
        up = shift(up, 1, range(t - 1, line - 1))
        down = shift(down, -1, range(1, line - t + 1))
        has_up = (at >= t).astype(jnp.int32)
        has_down = (at + t < line).astype(jnp.int32)
        devs = lax.axis_size("pages")
        cross_up = [(p, p ^ 2) for p in range(devs) if p // 4 >= t]
        cross_down = [(p, p ^ 2) for p in range(devs) if p // 4 + t < line]
        held += [
            (up, at - t, across, has_up),
            (lax.ppermute(up, "pages", cross_up), at - t, 1 - across, has_up),
            (down, at + t, across, has_down),
            (lax.ppermute(down, "pages", cross_down), at + t, 1 - across, has_down),
        ]
    return held


def merge_lines(parts, merged, last):
    line = lax.axis_size("pages") // 4
    at = lax.axis_index("pages") // 4
    turns = []
    for t in range(1, line):
        turns += [k for k in (line - t, t) if k not in turns]
    yes = jnp.int32(1)
    crossed = {k: swap(parts[k][1], 2) for k in turns + [0]}
    shares = {}

    def share(k):
        if k not in shares:
            shares[k] = merged([parts[k][0], crossed[k]], [yes, yes])
        return shares[k]

    up = down = None
    for t in range(1, line):
        up_out, down_out = share(line - t), share(t)
        if up is not None:
            up_out = merged([up_out, up], [yes, (at >= 1) & (at <= t - 1)])
            down_out = merged([down_out, down], [yes, (at <= line - 2) & (at >= line - t)])
        up = shift(up_out, 1, range(0, t))
        down = shift(down_out, -1, range(line - t, line))
    return merged([share(0), up, down, last()], [yes, at >= 1, at <= line - 2, yes])


def fresh_kernel(unit, scale2, q_ref, k_ref, v_ref, tok_ref, key_ref, o_ref):
    token, first, key = tok_ref[0:1, :], tok_ref[1:2, :], key_ref[:, 0:1]
    scores = lax.dot_general(
        k_ref[0], q_ref[0], (((1,), (1,)), ((), ())), preferred_element_type=jnp.float32
    )
    visible = (key <= token) & (key >= first)
    scores = jnp.where(visible, scores, low_score)
    peak = jnp.max(scores, axis=0, keepdims=True)
    weights = jnp.where(visible, jnp.exp2((scores - peak) * scale2), 0.0)
    totals = jnp.sum(weights, axis=0, keepdims=True)
    out = lax.dot_general(
        v_ref[0], weights.astype(jnp.bfloat16), (((0,), (0,)), ((), ())),
        preferred_element_type=jnp.float32,
    )
    out = out / totals
    part_len = out.shape[1]
    pad = -part_len % 128
    out = jnp.concatenate([out, jnp.zeros((out.shape[0], pad), jnp.float32)], axis=1)
    o_ref[0, :part_len, :] = out.T[:part_len].astype(jnp.bfloat16)
    sent = peak.astype(jnp.bfloat16).astype(jnp.float32)
    totals = totals * jnp.exp2((peak - sent) * scale2)
    high = totals.astype(jnp.bfloat16).astype(jnp.float32)
    kinds = [
        [values[:, at : at + unit] for at in range(0, part_len, unit)]
        for values in (sent, high, totals - high)
    ]
    o_ref[0, part_len:, :] = stat_block(kinds, o_ref.shape[1] - part_len)


def fresh_attention(q_chip, k_window, v_window, token_rows, key_cols, unit, scale2):
    heads, part_len, head_dim = q_chip.shape
    _, _, pad_to = stat_rows_of(part_len, unit)
    own = lambda x: pl.BlockSpec((1,) + x.shape[1:], lambda h: (h, 0, 0))
    fixed = lambda x: pl.BlockSpec(x.shape, lambda h: (0, 0))
    return pl.pallas_call(
        lambda *refs: fresh_kernel(unit, scale2, *refs),
        grid=(heads,),
        in_specs=[own(q_chip), own(k_window), own(v_window), fixed(token_rows), fixed(key_cols)],
        out_specs=pl.BlockSpec((1, part_len + pad_to, head_dim), lambda h: (h, 0, 0)),
        out_shape=jax.ShapeDtypeStruct((heads, part_len + pad_to, head_dim), jnp.bfloat16),
        compiler_params=pltpu.CompilerParams(vmem_limit_bytes=40 * 2**20),
        name="fresh_attention",
    )(q_chip, k_window, v_window, token_rows, key_cols)


def project_kernel(at_ref, mine_ref, other_ref, w_ref, out_ref, rows_ref):
    core = at_ref[0]
    wide = rows_ref.shape[2]

    @pl.when(pl.program_id(0) == 0)
    def _():
        for index, ref in enumerate((mine_ref, other_ref)):
            rows_ref[index] = jnp.concatenate([ref[h] for h in range(ref.shape[0])], axis=1)

    total = 0.0
    for d in range(2):
        feats = pl.ds(pl.multiple_of((core ^ d) * wide, wide), wide)
        total = total + jnp.dot(
            rows_ref[d], w_ref[0, feats, :], preferred_element_type=jnp.float32
        )
    out_ref[...] = total.astype(out_ref.dtype).reshape(out_ref.shape)


def project(mine, other, weights, core, owner, groups, dtype):
    half, tok_dev, head_dim = mine.shape
    blocks, feats, cols = weights.shape
    blocks //= groups
    wide = cols % 128 == 0
    if wide:
        out_spec = pl.BlockSpec((tok_dev, cols), lambda j, at: (0, j))
        out_shape = (tok_dev, blocks * cols)
    else:
        out_spec = pl.BlockSpec((1, tok_dev, cols), lambda j, at: (j, 0, 0))
        out_shape = (blocks, tok_dev, cols)
    rows_spec = pl.BlockSpec(mine.shape, lambda j, at: (0, 0, 0))
    out = pl.pallas_call(
        project_kernel,
        grid_spec=pltpu.PrefetchScalarGridSpec(
            num_scalar_prefetch=1,
            grid=(blocks,),
            in_specs=[
                rows_spec,
                rows_spec,
                pl.BlockSpec((1, feats, cols), lambda j, at: (at[1] * blocks + j, 0, 0)),
            ],
            out_specs=out_spec,
            scratch_shapes=[pltpu.VMEM((2, tok_dev, half * head_dim), jnp.bfloat16)],
        ),
        out_shape=jax.ShapeDtypeStruct(out_shape, dtype),
        compiler_params=pltpu.CompilerParams(vmem_limit_bytes=60 * 2**20),
        name="project",
    )(jnp.stack([core, owner]), mine, other, weights)
    return out if wide else jnp.transpose(out, (1, 0, 2)).reshape(tok_dev, blocks * cols)


def per_device(
    queries,
    keys,
    values,
    key_cache,
    value_cache,
    cache_len,
    page_table,
    append_slots,
    out_weight,
    out_bias,
):
    tok_dev, head_count, head_dim = queries.shape
    requests = cache_len.shape[0]
    max_pages = page_table.shape[1]
    new_pages = append_slots.shape[1]
    span_len = new_pages * PAGE
    slot_count = key_cache.shape[0]
    tokens = requests * span_len
    page_devs = tokens // tok_dev
    scale2 = math.log2(math.e) / math.sqrt(head_dim)
    device_at = lax.axis_index("pages")
    token_ids = device_at * tok_dev + jnp.arange(tok_dev, dtype=jnp.int32)
    request_ids = token_ids // span_len
    request_grid = jnp.arange(requests, dtype=jnp.int32)
    starts = jnp.sum(
        jnp.where(request_ids[:, None] == request_grid[None, :], cache_len[None, :], 0), axis=1
    )
    positions = (starts + token_ids % span_len).astype(jnp.float32)
    rotated_q = rotate(queries.astype(jnp.float32), positions).astype(jnp.bfloat16)
    rotated_k = rotate(keys.astype(jnp.float32), positions).astype(jnp.bfloat16)
    core = device_at % 2
    half = head_count // 2
    chip_len = 2 * tok_dev

    def halves(x):
        return (
            lax.dynamic_slice_in_dim(x, core * half, half, 0),
            lax.dynamic_slice_in_dim(x, (1 - core) * half, half, 0),
        )

    def in_order(mine, got, axis):
        return jnp.where(
            core == 0,
            jnp.concatenate([mine, got], axis=axis),
            jnp.concatenate([got, mine], axis=axis),
        )

    q_own = jnp.transpose(rotated_q, (1, 0, 2))
    q_mine, q_other = halves(q_own)
    q_chip = in_order(q_mine, swap(q_other, 1), 1)
    q_places = gather_lines(q_chip)
    groups = lax.axis_size("heads")
    group_at = lax.axis_index("heads")
    q_list = [q for q, _, _, _ in q_places]
    natural = Layout((0, 1, 2))
    late_k, late_v, _ = lax.optimization_barrier((rotated_k, values, q_list[2]))
    all_k = lax.all_gather(late_k, "pages", axis=0, tiled=True)
    all_v = lax.all_gather(late_v, "pages", axis=0, tiled=True)
    all_k = with_layout_constraint(all_k, natural)
    all_v = with_layout_constraint(all_v, natural)
    weights = lax.all_gather(out_weight, "pages", axis=0, tiled=False)
    own_kv = jnp.stack([jnp.transpose(rotated_k, (1, 0, 2)), jnp.transpose(values, (1, 0, 2))], 1)
    kv_mine, kv_other = halves(own_kv)
    kv_chip = in_order(kv_mine, swap(kv_other, 1), 2)
    back = -(-(span_len - math.gcd(span_len, chip_len)) // chip_len)
    barrier = lax.optimization_barrier
    q_list, weights, kv_chip = barrier((q_list, weights, kv_chip))
    kv_back = [
        lax.ppermute(kv_chip, "pages", [(p, p + 2 * b) for p in range(page_devs - 2 * b)])
        for b in range(back, 0, -1)
    ]

    my_slots = device_at * slot_count + jnp.arange(slot_count, dtype=jnp.int32)
    chip_slots = jnp.concatenate(
        [my_slots, (device_at ^ 1) * slot_count + jnp.arange(slot_count, dtype=jnp.int32)]
    )
    cached_hit = page_table.reshape(-1)[None, :] == chip_slots[:, None]
    fresh_hit = append_slots.reshape(-1)[None, :] == my_slots[:, None]
    table_at = jnp.arange(requests * max_pages, dtype=jnp.int32)
    shown = (table_at % max_pages) * PAGE < jnp.repeat(cache_len, max_pages)
    is_fresh = jnp.any(fresh_hit, axis=1)
    fresh_index = jnp.sum(
        jnp.where(fresh_hit, jnp.arange(requests * new_pages, dtype=jnp.int32)[None, :], 0), axis=1
    )
    slot_key = requests - jnp.sum(
        jnp.where(cached_hit & shown[None, :], requests - (table_at // max_pages)[None, :], 0),
        axis=1,
    )
    slot_at = jnp.arange(2 * slot_count, dtype=jnp.int32)
    earlier = (slot_key[None, :] < slot_key[:, None]) | (
        (slot_key[None, :] == slot_key[:, None]) & (slot_at[None, :] < slot_at[:, None])
    )
    rank = jnp.sum(earlier.astype(jnp.int32), axis=1)
    order = jnp.sum(jnp.where(rank[None, :] == slot_at[:, None], slot_at[None, :], 0), axis=1)
    slot_starts = jnp.sum((slot_key[None, :] < request_grid[:, None]).astype(jnp.int32), axis=1)
    slot_counts = jnp.sum((slot_key[None, :] == request_grid[:, None]).astype(jnp.int32), axis=1)

    k_mine, k_other = halves(jnp.transpose(key_cache, (2, 0, 1, 3)))
    v_mine, v_other = halves(jnp.transpose(value_cache, (2, 0, 3, 1)))
    k_heads = jnp.concatenate([k_mine, swap(k_other, 1)], axis=1)
    v_heads = jnp.concatenate([v_mine, swap(v_other, 1)], axis=1)

    unit = math.gcd(span_len, tok_dev)
    line = page_devs // 4
    line_at, across = device_at // 4, (device_at // 2) % 2
    outs = cached_attention(
        q_list,
        [jnp.clip(at, 0, line - 1) * 2 + side for _, at, side, _ in q_places],
        [ok for _, _, _, ok in q_places],
        [((line_at + k) % line) * 2 + (across ^ d) for k in range(line) for d in range(2)],
        k_heads,
        v_heads,
        order,
        slot_starts,
        slot_counts,
        span_len,
        unit,
        scale2,
    )
    outs, kv_back = barrier((outs, kv_back))
    merged = lambda parts, ok: merge(parts, ok, chip_len, unit, scale2)

    def fresh_part():
        chip_at = device_at // 2
        window = jnp.concatenate(kv_back + [kv_chip], axis=2)
        chip_tokens = chip_at * chip_len + jnp.arange(chip_len, dtype=jnp.int32)
        token_rows = jnp.stack([chip_tokens, chip_tokens // span_len * span_len])
        keys_at = (chip_at - back) * chip_len
        keys_at = keys_at + jnp.arange((back + 1) * chip_len, dtype=jnp.int32)
        key_cols = jnp.where(keys_at < 0, tokens, keys_at)[:, None]
        return fresh_attention(
            q_chip, window[:, 0], window[:, 1], token_rows, key_cols, unit, scale2
        )

    chip_part = merge_lines(
        [outs[2 * k : 2 * k + 2] for k in range(line)], merged, fresh_part
    )
    rows_of = lambda c: lax.dynamic_slice_in_dim(chip_part[:, :chip_len], c * tok_dev, tok_dev, 1)
    own_rows, got_rows = rows_of(core), swap(rows_of(1 - core), 1)
    total = out_bias[None, :]
    for s in range(groups - 1, -1, -1):
        owner = (group_at + s) % groups
        part = project(
            own_rows, got_rows, weights, core, owner, groups, jnp.bfloat16 if s else jnp.float32
        )
        if s:
            part = lax.ppermute(part, "heads", [(h, (h + s) % groups) for h in range(groups)])
        total = total + part.astype(jnp.float32)
    hidden = total.astype(jnp.bfloat16)
    page_shape = (requests * new_pages, PAGE, head_count, head_dim)
    key_out, value_out = write_pages(
        key_cache,
        value_cache,
        all_k.reshape(page_shape),
        all_v.reshape(page_shape),
        is_fresh,
        fresh_index,
    )
    return (hidden, key_out, value_out)


def solution(mesh):
    placed = (
        P("pages", "heads", None),
        P("pages", "heads", None),
        P("pages", "heads", None),
        P("pages", None, "heads", None),
        P("pages", None, "heads", None),
        P(),
        P(),
        P(),
        P("heads", "pages"),
        P("heads"),
    )
    return jax.shard_map(
        per_device,
        mesh=mesh,
        in_specs=placed,
        out_specs=(
            P("pages", "heads"),
            P("pages", None, "heads", None),
            P("pages", None, "heads", None),
        ),
        check_vma=False,
    )
```

```python
import functools
import math

import jax
import jax.numpy as jnp
from jax import lax
from jax.experimental import pallas as pl
from jax.experimental.layout import Layout, with_layout_constraint
from jax.experimental.pallas import tpu as pltpu
from jax.sharding import PartitionSpec as P

ROT = 32
PAGE = 128
QTILE = 256

low_score = -(2.0**99)


def rotate(vectors, positions):
    half_rot = ROT // 2
    inv_freq = 10000.0 ** (-2.0 * jnp.arange(half_rot, dtype=jnp.float32) / ROT)
    angles = positions[:, None] * inv_freq[None, :]
    cosine = jnp.cos(angles)[:, None, :]
    sine = jnp.sin(angles)[:, None, :]
    first_half = vectors[..., :half_rot]
    second_half = vectors[..., half_rot:ROT]
    return jnp.concatenate(
        [
            first_half * cosine - second_half * sine,
            second_half * cosine + first_half * sine,
            vectors[..., ROT:],
        ],
        axis=-1,
    )


def stat_rows_of(part_len, unit):
    per_unit = -(-unit // 128)
    units = part_len // unit
    return per_unit, units, -(-3 * units * per_unit // 16) * 16


def stat_rows(row):
    unit = row.shape[1]
    full = -(-unit // 128) * 128
    if full > unit:
        row = jnp.concatenate([row, jnp.zeros((1, full - unit), row.dtype)], axis=1)
    return [row[:, at : at + 128] for at in range(0, full, 128)]


def stat_block(kinds, pad_to):
    rows = [piece for kind in kinds for row in kind for piece in stat_rows(row)]
    rows.append(jnp.zeros((pad_to - len(rows), 128), jnp.float32))
    return jnp.concatenate(rows, axis=0).astype(jnp.bfloat16)


def cached_kernel(unit, stat_unit, span, scale2, places, at_ref, ok_ref, order_ref, start_ref, count_ref,
                  *refs):
    q_refs, (k_ref, v_ref), refs = refs[:places], refs[places : places + 2], refs[places + 2 :]
    o_refs, (q_all, o_all, s_all, q_scr, m_scr, l_scr, acc_scr) = refs[:-7], refs[-7:]
    requests = count_ref.shape[0]
    chips, part_len, _ = q_all.shape
    per_part = part_len // unit
    per_request = span // unit
    per_unit, units, pad_to = stat_rows_of(part_len, stat_unit)

    for index in range(places):

        @pl.when(ok_ref[index] > 0)
        def _(index=index):
            q_all[at_ref[index]] = q_refs[index][0]

    def place(at, per_part):
        return at // per_part, at % per_part

    def one_request(request, _):
        for index in range(per_request):
            part, piece = place(request * per_request + index, per_part)
            row = pl.ds(pl.multiple_of(piece * unit, unit), unit)
            q_scr[index * unit : (index + 1) * unit, :] = q_all[part, row, :]
        first = start_ref[request]
        count = count_ref[request]
        m_scr[...] = jnp.full((1, span), low_score, jnp.float32)
        l_scr[...] = jnp.zeros((1, span), jnp.float32)
        acc_scr[...] = jnp.zeros(acc_scr.shape, jnp.float32)

        def pages(slots):
            k = jnp.concatenate([k_ref[0, s] for s in slots], axis=0)
            v = jnp.concatenate([v_ref[0, s] for s in slots], axis=1)
            for c in range(0, span, QTILE):
                cols = slice(c, c + QTILE)
                scores = lax.dot_general(
                    k, q_scr[cols, :], (((1,), (1,)), ((), ())),
                    preferred_element_type=jnp.float32,
                )
                before = m_scr[:, cols]
                peak = jnp.maximum(before, jnp.max(scores, axis=0, keepdims=True))
                weights = jnp.exp2((scores - peak) * scale2)
                fade = jnp.exp2((before - peak) * scale2)
                m_scr[:, cols] = peak
                l_scr[:, cols] = l_scr[:, cols] * fade + jnp.sum(weights, axis=0, keepdims=True)
                acc_scr[:, cols] = acc_scr[:, cols] * fade + jnp.dot(
                    v, weights.astype(jnp.bfloat16), preferred_element_type=jnp.float32
                )

        def pair(index, _):
            at = first + 2 * index
            pages([order_ref[at], order_ref[at + 1]])
            return 0

        lax.fori_loop(0, count // 2, pair, 0)

        @pl.when(count % 2 == 1)
        def _():
            pages([order_ref[first + count - 1]])

        totals = l_scr[...]
        peaks = m_scr[...]
        out = (acc_scr[...] / jnp.maximum(totals, 1e-30)).T.astype(jnp.bfloat16)
        sent = peaks.astype(jnp.bfloat16).astype(jnp.float32)
        totals = totals * jnp.exp2((peaks - sent) * scale2)
        high = totals.astype(jnp.bfloat16).astype(jnp.float32)
        kinds = [sent, high, totals - high]
        for index in range(per_request):
            part, piece = place(request * per_request + index, per_part)
            row = pl.ds(pl.multiple_of(piece * unit, unit), unit)
            o_all[part, row, :] = out[index * unit : (index + 1) * unit, :]
        for index in range(span // stat_unit):
            part, piece = place(request * (span // stat_unit) + index, units)
            cols = slice(index * stat_unit, (index + 1) * stat_unit)
            for kind, values in enumerate(kinds):
                for r, line in enumerate(stat_rows(values[:, cols])):
                    at = (kind * units + piece) * per_unit + r
                    s_all[part, pl.ds(at, 1), :] = line
        return 0

    lax.fori_loop(0, requests, one_request, 0)
    for index in range(chips):
        part = at_ref[places + index]
        o_refs[index][0, :part_len, :] = o_all[part]
        o_refs[index][0, part_len:, :] = s_all[part].astype(jnp.bfloat16)


def cached_attention(q_places, at, ok, out_at, k_heads, v_heads, order, starts, counts, span,
                     stat_unit, scale2):
    places = len(q_places)
    chips = len(out_at)
    heads, part_len, head_dim = q_places[0].shape
    slots = k_heads.shape[1]
    unit = math.gcd(span, part_len)
    _, _, pad_to = stat_rows_of(part_len, stat_unit)
    own_block = lambda *dims: pl.BlockSpec(
        (1,) + dims, lambda h, *_: (h,) + (0,) * len(dims)
    )
    return pl.pallas_call(
        lambda *refs: cached_kernel(unit, stat_unit, span, scale2, places, *refs),
        grid_spec=pltpu.PrefetchScalarGridSpec(
            num_scalar_prefetch=5,
            grid=(heads,),
            in_specs=[own_block(part_len, head_dim)] * places
            + [own_block(slots, PAGE, head_dim), own_block(slots, head_dim, PAGE)],
            out_specs=[own_block(part_len + pad_to, head_dim)] * chips,
            scratch_shapes=[
                pltpu.VMEM((chips, part_len, head_dim), jnp.bfloat16),
                pltpu.VMEM((chips, part_len, head_dim), jnp.bfloat16),
                pltpu.VMEM((chips, pad_to, 128), jnp.float32),
                pltpu.VMEM((span, head_dim), jnp.bfloat16),
                pltpu.VMEM((1, span), jnp.float32),
                pltpu.VMEM((1, span), jnp.float32),
                pltpu.VMEM((head_dim, span), jnp.float32),
            ],
        ),
        out_shape=[
            jax.ShapeDtypeStruct((heads, part_len + pad_to, head_dim), jnp.bfloat16)
        ] * chips,
        compiler_params=pltpu.CompilerParams(vmem_limit_bytes=60 * 2**20),
        cost_estimate=pl.CostEstimate(
            flops=40 * 10**9, bytes_accessed=20 * 2**20, transcendentals=10**7
        ),
        name="cached_attention",
    )(jnp.stack(at + out_at), jnp.stack(ok), order, starts, counts, *q_places, k_heads, v_heads)


def merge_kernel(unit, part_len, scale2, ok_ref, *refs):
    in_refs, out_ref = refs[:-1], refs[-1]
    heads, _, width = out_ref.shape
    _, units, pad_to = stat_rows_of(part_len, unit)
    oks = [ok_ref[index] > 0 for index in range(len(in_refs))]
    for h in range(heads):
        peaks, totals = [], []
        for ok, ref in zip(oks, in_refs):
            stat = ref[h, part_len:, :].astype(jnp.float32)
            peaks.append(jnp.where(ok, stat[:units], low_score))
            total = stat[units : 2 * units] + stat[2 * units : 3 * units]
            totals.append(jnp.where(ok, total, 0.0))
        top = functools.reduce(jnp.maximum, peaks)
        shares = [t * jnp.exp2((p - top) * scale2) for t, p in zip(totals, peaks)]
        total = functools.reduce(jnp.add, shares)
        inverse = 1.0 / jnp.maximum(total, 1e-30)
        merged = [0.0] * units
        for ref, share in zip(in_refs, shares):
            weight = jnp.concatenate(
                [share * inverse, jnp.zeros((-units % 8, 128), jnp.float32)], axis=0
            ).T
            rows = ref[h, :part_len, :].astype(jnp.float32)
            for u in range(units):
                merged[u] = merged[u] + weight[:unit, u : u + 1] * rows[u * unit : (u + 1) * unit]
        high = total.astype(jnp.bfloat16).astype(jnp.float32)
        stats = [top, high, total - high, jnp.zeros((pad_to - 3 * units, width), jnp.float32)]
        out_ref[h, :part_len, :] = jnp.concatenate(merged, axis=0).astype(jnp.bfloat16)
        out_ref[h, part_len:, :] = jnp.concatenate(stats, axis=0).astype(jnp.bfloat16)


def merge(parts, ok, part_len, unit, scale2):
    heads = parts[0].shape[0]
    step = max(1, heads // 2)
    block = pl.BlockSpec((step,) + parts[0].shape[1:], lambda h, *_: (h, 0, 0))
    return pl.pallas_call(
        lambda *refs: merge_kernel(unit, part_len, scale2, *refs),
        grid_spec=pltpu.PrefetchScalarGridSpec(
            num_scalar_prefetch=1,
            grid=(heads // step,),
            in_specs=[block] * len(parts),
            out_specs=block,
        ),
        out_shape=jax.ShapeDtypeStruct(parts[0].shape, jnp.bfloat16),
        name="merge",
    )(jnp.stack(ok).astype(jnp.int32), *parts)


def page_kernel(fresh_ref, index_ref, kc_ref, vc_ref, kn_ref, vn_ref, ko_ref, vo_ref):
    fresh = fresh_ref[pl.program_id(0)] > 0

    @pl.when(fresh)
    def _():
        ko_ref[...] = kn_ref[...]
        vo_ref[...] = vn_ref[...]

    @pl.when(jnp.logical_not(fresh))
    def _():
        ko_ref[...] = kc_ref[...]
        vo_ref[...] = vc_ref[...]


def write_pages(key_cache, value_cache, new_keys, new_values, is_fresh, fresh_index):
    block = (1,) + key_cache.shape[1:]
    own = pl.BlockSpec(block, lambda s, fresh, index: (s, 0, 0, 0))
    new = pl.BlockSpec(block, lambda s, fresh, index: (index[s], 0, 0, 0))
    return pl.pallas_call(
        page_kernel,
        grid_spec=pltpu.PrefetchScalarGridSpec(
            num_scalar_prefetch=2,
            grid=(key_cache.shape[0],),
            in_specs=[own, own, new, new],
            out_specs=[own, own],
        ),
        out_shape=[jax.ShapeDtypeStruct(key_cache.shape, key_cache.dtype)] * 2,
        compiler_params=pltpu.CompilerParams(vmem_limit_bytes=40 * 2**20),
        name="write_pages",
    )(is_fresh.astype(jnp.int32), fresh_index, key_cache, value_cache, new_keys, new_values)


def swap(x, bit):
    devs = lax.axis_size("pages")
    return lax.ppermute(x, "pages", [(p, p ^ bit) for p in range(devs)])


def shift(x, hop, senders):
    devs = lax.axis_size("pages")
    moves = [(p, p + 4 * hop) for p in range(devs) if p // 4 in senders]
    return lax.ppermute(x, "pages", moves)


def gather_lines(x):
    line = lax.axis_size("pages") // 4
    device_at = lax.axis_index("pages")
    at, across = device_at // 4, (device_at // 2) % 2
    always = jnp.int32(1)
    held = [(x, at, across, always), (swap(x, 2), at, 1 - across, always)]
    up = down = x
    for t in range(1, line):
        up = shift(up, 1, range(t - 1, line - 1))
        down = shift(down, -1, range(1, line - t + 1))
        has_up = (at >= t).astype(jnp.int32)
        has_down = (at + t < line).astype(jnp.int32)
        devs = lax.axis_size("pages")
        cross_up = [(p, p ^ 2) for p in range(devs) if p // 4 >= t]
        cross_down = [(p, p ^ 2) for p in range(devs) if p // 4 + t < line]
        held += [
            (up, at - t, across, has_up),
            (lax.ppermute(up, "pages", cross_up), at - t, 1 - across, has_up),
            (down, at + t, across, has_down),
            (lax.ppermute(down, "pages", cross_down), at + t, 1 - across, has_down),
        ]
    return held


def merge_lines(parts, merged, last):
    line = lax.axis_size("pages") // 4
    at = lax.axis_index("pages") // 4
    turns = []
    for t in range(1, line):
        turns += [k for k in (line - t, t) if k not in turns]
    yes = jnp.int32(1)
    crossed = {k: swap(parts[k][1], 2) for k in turns + [0]}
    shares = {}

    def share(k):
        if k not in shares:
            shares[k] = merged([parts[k][0], crossed[k]], [yes, yes])
        return shares[k]

    up = down = None
    for t in range(1, line):
        up_out, down_out = share(line - t), share(t)
        if up is not None:
            up_out = merged([up_out, up], [yes, (at >= 1) & (at <= t - 1)])
            down_out = merged([down_out, down], [yes, (at <= line - 2) & (at >= line - t)])
        up = shift(up_out, 1, range(0, t))
        down = shift(down_out, -1, range(line - t, line))
    return merged([share(0), up, down, last()], [yes, at >= 1, at <= line - 2, yes])


def fresh_kernel(unit, scale2, q_ref, k_ref, v_ref, tok_ref, key_ref, o_ref):
    token, first, key = tok_ref[0:1, :], tok_ref[1:2, :], key_ref[:, 0:1]
    scores = lax.dot_general(
        k_ref[0], q_ref[0], (((1,), (1,)), ((), ())), preferred_element_type=jnp.float32
    )
    visible = (key <= token) & (key >= first)
    scores = jnp.where(visible, scores, low_score)
    peak = jnp.max(scores, axis=0, keepdims=True)
    weights = jnp.where(visible, jnp.exp2((scores - peak) * scale2), 0.0)
    totals = jnp.sum(weights, axis=0, keepdims=True)
    out = lax.dot_general(
        v_ref[0], weights.astype(jnp.bfloat16), (((0,), (0,)), ((), ())),
        preferred_element_type=jnp.float32,
    )
    out = out / totals
    part_len = out.shape[1]
    pad = -part_len % 128
    out = jnp.concatenate([out, jnp.zeros((out.shape[0], pad), jnp.float32)], axis=1)
    o_ref[0, :part_len, :] = out.T[:part_len].astype(jnp.bfloat16)
    sent = peak.astype(jnp.bfloat16).astype(jnp.float32)
    totals = totals * jnp.exp2((peak - sent) * scale2)
    high = totals.astype(jnp.bfloat16).astype(jnp.float32)
    kinds = [
        [values[:, at : at + unit] for at in range(0, part_len, unit)]
        for values in (sent, high, totals - high)
    ]
    o_ref[0, part_len:, :] = stat_block(kinds, o_ref.shape[1] - part_len)


def fresh_attention(q_chip, k_window, v_window, token_rows, key_cols, unit, scale2):
    heads, part_len, head_dim = q_chip.shape
    _, _, pad_to = stat_rows_of(part_len, unit)
    own = lambda x: pl.BlockSpec((1,) + x.shape[1:], lambda h: (h, 0, 0))
    fixed = lambda x: pl.BlockSpec(x.shape, lambda h: (0, 0))
    return pl.pallas_call(
        lambda *refs: fresh_kernel(unit, scale2, *refs),
        grid=(heads,),
        in_specs=[own(q_chip), own(k_window), own(v_window), fixed(token_rows), fixed(key_cols)],
        out_specs=pl.BlockSpec((1, part_len + pad_to, head_dim), lambda h: (h, 0, 0)),
        out_shape=jax.ShapeDtypeStruct((heads, part_len + pad_to, head_dim), jnp.bfloat16),
        compiler_params=pltpu.CompilerParams(vmem_limit_bytes=40 * 2**20),
        name="fresh_attention",
    )(q_chip, k_window, v_window, token_rows, key_cols)


def project_kernel(at_ref, mine_ref, other_ref, w_ref, out_ref, rows_ref):
    core = at_ref[0]
    wide = rows_ref.shape[2]

    @pl.when(pl.program_id(0) == 0)
    def _():
        for index, ref in enumerate((mine_ref, other_ref)):
            rows_ref[index] = jnp.concatenate([ref[h] for h in range(ref.shape[0])], axis=1)

    total = 0.0
    for d in range(2):
        feats = pl.ds(pl.multiple_of((core ^ d) * wide, wide), wide)
        total = total + jnp.dot(
            rows_ref[d], w_ref[0, feats, :], preferred_element_type=jnp.float32
        )
    out_ref[...] = total.astype(out_ref.dtype).reshape(out_ref.shape)


def project(mine, other, weights, core, first, blocks, dtype):
    half, tok_dev, head_dim = mine.shape
    _, feats, cols = weights.shape
    wide = cols % 128 == 0
    if wide:
        out_spec = pl.BlockSpec((tok_dev, cols), lambda j, at: (0, j))
        out_shape = (tok_dev, blocks * cols)
    else:
        out_spec = pl.BlockSpec((1, tok_dev, cols), lambda j, at: (j, 0, 0))
        out_shape = (blocks, tok_dev, cols)
    rows_spec = pl.BlockSpec(mine.shape, lambda j, at: (0, 0, 0))
    out = pl.pallas_call(
        project_kernel,
        grid_spec=pltpu.PrefetchScalarGridSpec(
            num_scalar_prefetch=1,
            grid=(blocks,),
            in_specs=[
                rows_spec,
                rows_spec,
                pl.BlockSpec((1, feats, cols), lambda j, at: (at[1] + j, 0, 0)),
            ],
            out_specs=out_spec,
            scratch_shapes=[pltpu.VMEM((2, tok_dev, half * head_dim), jnp.bfloat16)],
        ),
        out_shape=jax.ShapeDtypeStruct(out_shape, dtype),
        compiler_params=pltpu.CompilerParams(vmem_limit_bytes=40 * 2**20),
        name="project",
    )(jnp.stack([core, first]), mine, other, weights)
    return out if wide else jnp.transpose(out, (1, 0, 2)).reshape(tok_dev, blocks * cols)


def per_device(
    queries,
    keys,
    values,
    key_cache,
    value_cache,
    cache_len,
    page_table,
    append_slots,
    out_weight,
    out_bias,
):
    tok_dev, head_count, head_dim = queries.shape
    requests = cache_len.shape[0]
    max_pages = page_table.shape[1]
    new_pages = append_slots.shape[1]
    span_len = new_pages * PAGE
    slot_count = key_cache.shape[0]
    tokens = requests * span_len
    page_devs = tokens // tok_dev
    scale2 = math.log2(math.e) / math.sqrt(head_dim)
    device_at = lax.axis_index("pages")
    token_ids = device_at * tok_dev + jnp.arange(tok_dev, dtype=jnp.int32)
    request_ids = token_ids // span_len
    request_grid = jnp.arange(requests, dtype=jnp.int32)
    starts = jnp.sum(
        jnp.where(request_ids[:, None] == request_grid[None, :], cache_len[None, :], 0), axis=1
    )
    positions = (starts + token_ids % span_len).astype(jnp.float32)
    rotated_q = rotate(queries.astype(jnp.float32), positions).astype(jnp.bfloat16)
    core = device_at % 2
    half = head_count // 2
    chip_len = 2 * tok_dev

    def halves(x):
        return (
            lax.dynamic_slice_in_dim(x, core * half, half, 0),
            lax.dynamic_slice_in_dim(x, (1 - core) * half, half, 0),
        )

    def in_order(mine, got, axis):
        return jnp.where(
            core == 0,
            jnp.concatenate([mine, got], axis=axis),
            jnp.concatenate([got, mine], axis=axis),
        )

    q_own = jnp.transpose(rotated_q, (1, 0, 2))
    q_mine, q_other = halves(q_own)
    q_chip = in_order(q_mine, swap(q_other, 1), 1)
    groups = lax.axis_size("heads")
    group_at = lax.axis_index("heads")
    natural = Layout((0, 1, 2))
    q_chip, late_k, late_weight = lax.optimization_barrier((q_chip, keys, out_weight))
    q_places = gather_lines(q_chip)
    rotated_k = rotate(late_k.astype(jnp.float32), positions).astype(jnp.bfloat16)
    all_k = lax.all_gather(rotated_k, "pages", axis=0, tiled=True)
    all_v = lax.all_gather(values, "pages", axis=0, tiled=True)
    all_k = with_layout_constraint(all_k, natural)
    all_v = with_layout_constraint(all_v, natural)
    weights = lax.all_gather(late_weight, "pages", axis=0, tiled=False)

    my_slots = device_at * slot_count + jnp.arange(slot_count, dtype=jnp.int32)
    chip_slots = jnp.concatenate(
        [my_slots, (device_at ^ 1) * slot_count + jnp.arange(slot_count, dtype=jnp.int32)]
    )
    cached_hit = page_table.reshape(-1)[None, :] == chip_slots[:, None]
    fresh_hit = append_slots.reshape(-1)[None, :] == my_slots[:, None]
    table_at = jnp.arange(requests * max_pages, dtype=jnp.int32)
    shown = (table_at % max_pages) * PAGE < jnp.repeat(cache_len, max_pages)
    is_fresh = jnp.any(fresh_hit, axis=1)
    fresh_index = jnp.sum(
        jnp.where(fresh_hit, jnp.arange(requests * new_pages, dtype=jnp.int32)[None, :], 0), axis=1
    )
    slot_key = requests - jnp.sum(
        jnp.where(cached_hit & shown[None, :], requests - (table_at // max_pages)[None, :], 0),
        axis=1,
    )
    slot_at = jnp.arange(2 * slot_count, dtype=jnp.int32)
    earlier = (slot_key[None, :] < slot_key[:, None]) | (
        (slot_key[None, :] == slot_key[:, None]) & (slot_at[None, :] < slot_at[:, None])
    )
    rank = jnp.sum(earlier.astype(jnp.int32), axis=1)
    order = jnp.sum(jnp.where(rank[None, :] == slot_at[:, None], slot_at[None, :], 0), axis=1)
    slot_starts = jnp.sum((slot_key[None, :] < request_grid[:, None]).astype(jnp.int32), axis=1)
    slot_counts = jnp.sum((slot_key[None, :] == request_grid[:, None]).astype(jnp.int32), axis=1)

    k_mine, k_other = halves(jnp.transpose(key_cache, (2, 0, 1, 3)))
    v_mine, v_other = halves(jnp.transpose(value_cache, (2, 0, 3, 1)))
    k_heads = jnp.concatenate([k_mine, swap(k_other, 1)], axis=1)
    v_heads = jnp.concatenate([v_mine, swap(v_other, 1)], axis=1)

    unit = math.gcd(span_len, tok_dev)
    line = page_devs // 4
    line_at, across = device_at // 4, (device_at // 2) % 2
    outs = cached_attention(
        [q for q, _, _, _ in q_places],
        [jnp.clip(at, 0, line - 1) * 2 + side for _, at, side, _ in q_places],
        [ok for _, _, _, ok in q_places],
        [((line_at + k) % line) * 2 + (across ^ d) for k in range(line) for d in range(2)],
        k_heads,
        v_heads,
        order,
        slot_starts,
        slot_counts,
        span_len,
        unit,
        scale2,
    )
    merged = lambda parts, ok: merge(parts, ok, chip_len, unit, scale2)

    def fresh_part():
        chip_at = device_at // 2
        back = -(-(span_len - math.gcd(span_len, chip_len)) // chip_len)
        window = (back + 1) * chip_len
        window_at = jnp.maximum(chip_at - back, 0) * chip_len

        def by_head(rows):
            rows = lax.dynamic_slice(
                rows, (window_at, core * half, 0), (window, half, head_dim)
            )
            return jnp.transpose(rows, (1, 0, 2))

        chip_tokens = chip_at * chip_len + jnp.arange(chip_len, dtype=jnp.int32)
        token_rows = jnp.stack([chip_tokens, chip_tokens // span_len * span_len])
        key_cols = (window_at + jnp.arange(window, dtype=jnp.int32))[:, None]
        return fresh_attention(
            q_chip, by_head(all_k), by_head(all_v), token_rows, key_cols, unit, scale2
        )

    chip_part = merge_lines(
        [outs[2 * k : 2 * k + 2] for k in range(line)], merged, fresh_part
    )
    rows_of = lambda c: lax.dynamic_slice_in_dim(chip_part[:, :chip_len], c * tok_dev, tok_dev, 1)
    own_rows, got_rows = rows_of(core), swap(rows_of(1 - core), 1)
    blocks = page_devs // groups
    pieces = 2
    sent = []
    for s in range(groups - 1, 0, -1):
        for piece in range(pieces):
            part = project(
                own_rows,
                got_rows,
                weights,
                core,
                (group_at + s) % groups * blocks + piece * (blocks // pieces),
                blocks // pieces,
                jnp.bfloat16,
            )
            moves = [(h, (h + s) % groups) for h in range(groups)]
            sent.append(lax.ppermute(part, "heads", moves))
    total = project(
        own_rows, got_rows, weights, core, group_at * blocks, blocks, jnp.float32
    ) + out_bias[None, :]
    for at in range(0, len(sent), pieces):
        total = total + jnp.concatenate(sent[at : at + pieces], axis=1).astype(jnp.float32)
    hidden = total.astype(jnp.bfloat16)
    page_shape = (requests * new_pages, PAGE, head_count, head_dim)
    key_out, value_out = write_pages(
        key_cache,
        value_cache,
        all_k.reshape(page_shape),
        all_v.reshape(page_shape),
        is_fresh,
        fresh_index,
    )
    return (hidden, key_out, value_out)


def solution(mesh):
    placed = (
        P("pages", "heads", None),
        P("pages", "heads", None),
        P("pages", "heads", None),
        P("pages", None, "heads", None),
        P("pages", None, "heads", None),
        P(),
        P(),
        P(),
        P("heads", "pages"),
        P("heads"),
    )
    return jax.shard_map(
        per_device,
        mesh=mesh,
        in_specs=placed,
        out_specs=(
            P("pages", "heads"),
            P("pages", None, "heads", None),
            P("pages", None, "heads", None),
        ),
        check_vma=False,
    )
```

```python
import functools
import math

import jax
import jax.numpy as jnp
from jax import lax
from jax.experimental import pallas as pl
from jax.experimental.layout import Layout, with_layout_constraint
from jax.experimental.pallas import tpu as pltpu
from jax.sharding import PartitionSpec as P

ROT = 32
PAGE = 128
QTILE = 256

low_score = -(2.0**99)


def rotate(vectors, positions):
    half_rot = ROT // 2
    inv_freq = 10000.0 ** (-2.0 * jnp.arange(half_rot, dtype=jnp.float32) / ROT)
    angles = positions[:, None] * inv_freq[None, :]
    cosine = jnp.cos(angles)[:, None, :]
    sine = jnp.sin(angles)[:, None, :]
    first_half = vectors[..., :half_rot]
    second_half = vectors[..., half_rot:ROT]
    return jnp.concatenate(
        [
            first_half * cosine - second_half * sine,
            second_half * cosine + first_half * sine,
            vectors[..., ROT:],
        ],
        axis=-1,
    )


def stat_rows_of(part_len, unit):
    per_unit = -(-unit // 128)
    units = part_len // unit
    return per_unit, units, -(-3 * units * per_unit // 16) * 16


def stat_rows(row):
    unit = row.shape[1]
    full = -(-unit // 128) * 128
    if full > unit:
        row = jnp.concatenate([row, jnp.zeros((1, full - unit), row.dtype)], axis=1)
    return [row[:, at : at + 128] for at in range(0, full, 128)]


def stat_block(kinds, pad_to):
    rows = [piece for kind in kinds for row in kind for piece in stat_rows(row)]
    rows.append(jnp.zeros((pad_to - len(rows), 128), jnp.float32))
    return jnp.concatenate(rows, axis=0).astype(jnp.bfloat16)


def cached_kernel(unit, stat_unit, span, scale2, places, at_ref, ok_ref, order_ref, start_ref, count_ref,
                  *refs):
    q_refs, (k_ref, v_ref), refs = refs[:places], refs[places : places + 2], refs[places + 2 :]
    o_refs, (q_all, o_all, s_all, q_scr, m_scr, l_scr, acc_scr) = refs[:-7], refs[-7:]
    requests = count_ref.shape[0]
    chips, part_len, _ = q_all.shape
    per_part = part_len // unit
    per_request = span // unit
    per_unit, units, pad_to = stat_rows_of(part_len, stat_unit)

    for index in range(places):

        @pl.when(ok_ref[index] > 0)
        def _(index=index):
            q_all[at_ref[index]] = q_refs[index][0]

    def place(at, per_part):
        return at // per_part, at % per_part

    def one_request(request, _):
        for index in range(per_request):
            part, piece = place(request * per_request + index, per_part)
            row = pl.ds(pl.multiple_of(piece * unit, unit), unit)
            q_scr[index * unit : (index + 1) * unit, :] = q_all[part, row, :]
        first = start_ref[request]
        count = count_ref[request]
        m_scr[...] = jnp.full((1, span), low_score, jnp.float32)
        l_scr[...] = jnp.zeros((1, span), jnp.float32)
        acc_scr[...] = jnp.zeros(acc_scr.shape, jnp.float32)

        def pages(slots):
            k = jnp.concatenate([k_ref[0, s] for s in slots], axis=0)
            v = jnp.concatenate([v_ref[0, s] for s in slots], axis=1)
            for c in range(0, span, QTILE):
                cols = slice(c, c + QTILE)
                scores = lax.dot_general(
                    k, q_scr[cols, :], (((1,), (1,)), ((), ())),
                    preferred_element_type=jnp.float32,
                )
                before = m_scr[:, cols]
                peak = jnp.maximum(before, jnp.max(scores, axis=0, keepdims=True))
                weights = jnp.exp2((scores - peak) * scale2)
                fade = jnp.exp2((before - peak) * scale2)
                m_scr[:, cols] = peak
                l_scr[:, cols] = l_scr[:, cols] * fade + jnp.sum(weights, axis=0, keepdims=True)
                acc_scr[:, cols] = acc_scr[:, cols] * fade + jnp.dot(
                    v, weights.astype(jnp.bfloat16), preferred_element_type=jnp.float32
                )

        def pair(index, _):
            at = first + 2 * index
            pages([order_ref[at], order_ref[at + 1]])
            return 0

        lax.fori_loop(0, count // 2, pair, 0)

        @pl.when(count % 2 == 1)
        def _():
            pages([order_ref[first + count - 1]])

        totals = l_scr[...]
        peaks = m_scr[...]
        out = (acc_scr[...] / jnp.maximum(totals, 1e-30)).T.astype(jnp.bfloat16)
        sent = peaks.astype(jnp.bfloat16).astype(jnp.float32)
        totals = totals * jnp.exp2((peaks - sent) * scale2)
        high = totals.astype(jnp.bfloat16).astype(jnp.float32)
        kinds = [sent, high, totals - high]
        for index in range(per_request):
            part, piece = place(request * per_request + index, per_part)
            row = pl.ds(pl.multiple_of(piece * unit, unit), unit)
            o_all[part, row, :] = out[index * unit : (index + 1) * unit, :]
        for index in range(span // stat_unit):
            part, piece = place(request * (span // stat_unit) + index, units)
            cols = slice(index * stat_unit, (index + 1) * stat_unit)
            for kind, values in enumerate(kinds):
                for r, line in enumerate(stat_rows(values[:, cols])):
                    at = (kind * units + piece) * per_unit + r
                    s_all[part, pl.ds(at, 1), :] = line
        return 0

    lax.fori_loop(0, requests, one_request, 0)
    for index in range(chips):
        part = at_ref[places + index]
        o_refs[index][0, :part_len, :] = o_all[part]
        o_refs[index][0, part_len:, :] = s_all[part].astype(jnp.bfloat16)


def cached_attention(first, heads, q_places, at, ok, out_at, k_heads, v_heads, order, starts,
                     counts, span, stat_unit, scale2):
    places = len(q_places)
    chips = len(out_at)
    _, part_len, head_dim = q_places[0].shape
    slots = k_heads.shape[1]
    unit = math.gcd(span, part_len)
    _, _, pad_to = stat_rows_of(part_len, stat_unit)
    own_block = lambda *dims: pl.BlockSpec(
        (1,) + dims, lambda h, *_: (first + h,) + (0,) * len(dims)
    )
    out_block = pl.BlockSpec((1, part_len + pad_to, head_dim), lambda h, *_: (h, 0, 0))
    return pl.pallas_call(
        lambda *refs: cached_kernel(unit, stat_unit, span, scale2, places, *refs),
        grid_spec=pltpu.PrefetchScalarGridSpec(
            num_scalar_prefetch=5,
            grid=(heads,),
            in_specs=[own_block(part_len, head_dim)] * places
            + [own_block(slots, PAGE, head_dim), own_block(slots, head_dim, PAGE)],
            out_specs=[out_block] * chips,
            scratch_shapes=[
                pltpu.VMEM((chips, part_len, head_dim), jnp.bfloat16),
                pltpu.VMEM((chips, part_len, head_dim), jnp.bfloat16),
                pltpu.VMEM((chips, pad_to, 128), jnp.float32),
                pltpu.VMEM((span, head_dim), jnp.bfloat16),
                pltpu.VMEM((1, span), jnp.float32),
                pltpu.VMEM((1, span), jnp.float32),
                pltpu.VMEM((head_dim, span), jnp.float32),
            ],
        ),
        out_shape=[
            jax.ShapeDtypeStruct((heads, part_len + pad_to, head_dim), jnp.bfloat16)
        ] * chips,
        compiler_params=pltpu.CompilerParams(vmem_limit_bytes=60 * 2**20),
        cost_estimate=pl.CostEstimate(
            flops=20 * 10**9, bytes_accessed=10 * 2**20, transcendentals=10**7
        ),
        name="cached_attention",
    )(jnp.stack(at + out_at), jnp.stack(ok), order, starts, counts, *q_places, k_heads, v_heads)


def merge_kernel(unit, part_len, scale2, ok_ref, *refs):
    in_refs, out_ref = refs[:-1], refs[-1]
    heads, _, width = out_ref.shape
    _, units, pad_to = stat_rows_of(part_len, unit)
    oks = [ok_ref[index] > 0 for index in range(len(in_refs))]
    for h in range(heads):
        peaks, totals = [], []
        for ok, ref in zip(oks, in_refs):
            stat = ref[h, part_len:, :].astype(jnp.float32)
            peaks.append(jnp.where(ok, stat[:units], low_score))
            total = stat[units : 2 * units] + stat[2 * units : 3 * units]
            totals.append(jnp.where(ok, total, 0.0))
        top = functools.reduce(jnp.maximum, peaks)
        shares = [t * jnp.exp2((p - top) * scale2) for t, p in zip(totals, peaks)]
        total = functools.reduce(jnp.add, shares)
        inverse = 1.0 / jnp.maximum(total, 1e-30)
        merged = [0.0] * units
        for ref, share in zip(in_refs, shares):
            weight = jnp.concatenate(
                [share * inverse, jnp.zeros((-units % 8, 128), jnp.float32)], axis=0
            ).T
            rows = ref[h, :part_len, :].astype(jnp.float32)
            for u in range(units):
                merged[u] = merged[u] + weight[:unit, u : u + 1] * rows[u * unit : (u + 1) * unit]
        high = total.astype(jnp.bfloat16).astype(jnp.float32)
        stats = [top, high, total - high, jnp.zeros((pad_to - 3 * units, width), jnp.float32)]
        out_ref[h, :part_len, :] = jnp.concatenate(merged, axis=0).astype(jnp.bfloat16)
        out_ref[h, part_len:, :] = jnp.concatenate(stats, axis=0).astype(jnp.bfloat16)


def merge(parts, ok, part_len, unit, scale2):
    heads = parts[0].shape[0]
    step = max(1, heads // 2)
    block = pl.BlockSpec((step,) + parts[0].shape[1:], lambda h, *_: (h, 0, 0))
    return pl.pallas_call(
        lambda *refs: merge_kernel(unit, part_len, scale2, *refs),
        grid_spec=pltpu.PrefetchScalarGridSpec(
            num_scalar_prefetch=1,
            grid=(heads // step,),
            in_specs=[block] * len(parts),
            out_specs=block,
        ),
        out_shape=jax.ShapeDtypeStruct(parts[0].shape, jnp.bfloat16),
        name="merge",
    )(jnp.stack(ok).astype(jnp.int32), *parts)


def merge_two(halves, part_len, unit, scale2):
    heads, rows, width = halves[0][0].shape
    whole = pl.BlockSpec((heads, rows, width), lambda h, *_: (0, 0, 0))

    def kernel(ok_ref, *refs):
        for half in range(2):

            @pl.when(pl.program_id(0) == half)
            def _(half=half):
                merge_kernel(
                    unit, part_len, scale2, ok_ref, refs[2 * half], refs[2 * half + 1], refs[4]
                )

    return pl.pallas_call(
        kernel,
        grid_spec=pltpu.PrefetchScalarGridSpec(
            num_scalar_prefetch=1,
            grid=(2,),
            in_specs=[whole] * 4,
            out_specs=pl.BlockSpec((heads, rows, width), lambda h, *_: (h, 0, 0)),
        ),
        out_shape=jax.ShapeDtypeStruct((2 * heads, rows, width), jnp.bfloat16),
        name="merge_two",
    )(jnp.ones((2,), jnp.int32), *halves[0], *halves[1])


def page_kernel(fresh_ref, index_ref, kc_ref, vc_ref, kn_ref, vn_ref, ko_ref, vo_ref):
    fresh = fresh_ref[pl.program_id(0)] > 0

    @pl.when(fresh)
    def _():
        ko_ref[...] = kn_ref[...]
        vo_ref[...] = vn_ref[...]

    @pl.when(jnp.logical_not(fresh))
    def _():
        ko_ref[...] = kc_ref[...]
        vo_ref[...] = vc_ref[...]


def write_pages(key_cache, value_cache, new_keys, new_values, is_fresh, fresh_index):
    block = (1,) + key_cache.shape[1:]
    own = pl.BlockSpec(block, lambda s, fresh, index: (s, 0, 0, 0))
    new = pl.BlockSpec(block, lambda s, fresh, index: (index[s], 0, 0, 0))
    return pl.pallas_call(
        page_kernel,
        grid_spec=pltpu.PrefetchScalarGridSpec(
            num_scalar_prefetch=2,
            grid=(key_cache.shape[0],),
            in_specs=[own, own, new, new],
            out_specs=[own, own],
        ),
        out_shape=[jax.ShapeDtypeStruct(key_cache.shape, key_cache.dtype)] * 2,
        compiler_params=pltpu.CompilerParams(vmem_limit_bytes=40 * 2**20),
        name="write_pages",
    )(is_fresh.astype(jnp.int32), fresh_index, key_cache, value_cache, new_keys, new_values)


def swap(x, bit):
    devs = lax.axis_size("pages")
    return lax.ppermute(x, "pages", [(p, p ^ bit) for p in range(devs)])


def shift(x, hop, senders):
    devs = lax.axis_size("pages")
    moves = [(p, p + 4 * hop) for p in range(devs) if p // 4 in senders]
    return lax.ppermute(x, "pages", moves)


def gather_lines(x):
    line = lax.axis_size("pages") // 4
    device_at = lax.axis_index("pages")
    at, across = device_at // 4, (device_at // 2) % 2
    always = jnp.int32(1)
    held = [(x, at, across, always), (swap(x, 2), at, 1 - across, always)]
    up = down = x
    for t in range(1, line):
        up = shift(up, 1, range(t - 1, line - 1))
        down = shift(down, -1, range(1, line - t + 1))
        has_up = (at >= t).astype(jnp.int32)
        has_down = (at + t < line).astype(jnp.int32)
        devs = lax.axis_size("pages")
        cross_up = [(p, p ^ 2) for p in range(devs) if p // 4 >= t]
        cross_down = [(p, p ^ 2) for p in range(devs) if p // 4 + t < line]
        held += [
            (up, at - t, across, has_up),
            (lax.ppermute(up, "pages", cross_up), at - t, 1 - across, has_up),
            (down, at + t, across, has_down),
            (lax.ppermute(down, "pages", cross_down), at + t, 1 - across, has_down),
        ]
    return held


def merge_lines(parts, merged, merged_two, last):
    line = lax.axis_size("pages") // 4
    at = lax.axis_index("pages") // 4
    turns = []
    for t in range(1, line):
        turns += [k for k in (line - t, t) if k not in turns]
    yes = jnp.int32(1)
    crossed = {k: [swap(x, 2) for x in parts[k][1]] for k in turns + [0]}
    shares = {}

    def share(k):
        if k not in shares:
            shares[k] = merged_two(list(zip(parts[k][0], crossed[k])))
        return shares[k]

    up = down = None
    for t in range(1, line):
        up_out, down_out = share(line - t), share(t)
        if up is not None:
            up_out = merged([up_out, up], [yes, (at >= 1) & (at <= t - 1)])
            down_out = merged([down_out, down], [yes, (at <= line - 2) & (at >= line - t)])
        up = shift(up_out, 1, range(0, t))
        down = shift(down_out, -1, range(line - t, line))
    return merged([share(0), up, down, last([crossed[k] for k in turns])], [yes, at >= 1, at <= line - 2, yes])


def fresh_kernel(unit, scale2, q_ref, k_ref, v_ref, tok_ref, key_ref, o_ref):
    token, first, key = tok_ref[0:1, :], tok_ref[1:2, :], key_ref[:, 0:1]
    scores = lax.dot_general(
        k_ref[0], q_ref[0], (((1,), (1,)), ((), ())), preferred_element_type=jnp.float32
    )
    visible = (key <= token) & (key >= first)
    scores = jnp.where(visible, scores, low_score)
    peak = jnp.max(scores, axis=0, keepdims=True)
    weights = jnp.where(visible, jnp.exp2((scores - peak) * scale2), 0.0)
    totals = jnp.sum(weights, axis=0, keepdims=True)
    out = lax.dot_general(
        v_ref[0], weights.astype(jnp.bfloat16), (((0,), (0,)), ((), ())),
        preferred_element_type=jnp.float32,
    )
    out = out / totals
    part_len = out.shape[1]
    pad = -part_len % 128
    out = jnp.concatenate([out, jnp.zeros((out.shape[0], pad), jnp.float32)], axis=1)
    o_ref[0, :part_len, :] = out.T[:part_len].astype(jnp.bfloat16)
    sent = peak.astype(jnp.bfloat16).astype(jnp.float32)
    totals = totals * jnp.exp2((peak - sent) * scale2)
    high = totals.astype(jnp.bfloat16).astype(jnp.float32)
    kinds = [
        [values[:, at : at + unit] for at in range(0, part_len, unit)]
        for values in (sent, high, totals - high)
    ]
    o_ref[0, part_len:, :] = stat_block(kinds, o_ref.shape[1] - part_len)


def fresh_attention(q_chip, k_window, v_window, token_rows, key_cols, unit, scale2):
    heads, part_len, head_dim = q_chip.shape
    _, _, pad_to = stat_rows_of(part_len, unit)
    own = lambda x: pl.BlockSpec((1,) + x.shape[1:], lambda h: (h, 0, 0))
    fixed = lambda x: pl.BlockSpec(x.shape, lambda h: (0, 0))
    return pl.pallas_call(
        lambda *refs: fresh_kernel(unit, scale2, *refs),
        grid=(heads,),
        in_specs=[own(q_chip), own(k_window), own(v_window), fixed(token_rows), fixed(key_cols)],
        out_specs=pl.BlockSpec((1, part_len + pad_to, head_dim), lambda h: (h, 0, 0)),
        out_shape=jax.ShapeDtypeStruct((heads, part_len + pad_to, head_dim), jnp.bfloat16),
        compiler_params=pltpu.CompilerParams(vmem_limit_bytes=40 * 2**20),
        name="fresh_attention",
    )(q_chip, k_window, v_window, token_rows, key_cols)


def project_kernel(at_ref, mine_ref, other_ref, w_ref, out_ref, rows_ref):
    core = at_ref[0]
    wide = rows_ref.shape[2]

    @pl.when(pl.program_id(0) == 0)
    def _():
        for index, ref in enumerate((mine_ref, other_ref)):
            rows_ref[index] = jnp.concatenate([ref[h] for h in range(ref.shape[0])], axis=1)

    total = 0.0
    for d in range(2):
        feats = pl.ds(pl.multiple_of((core ^ d) * wide, wide), wide)
        total = total + jnp.dot(
            rows_ref[d], w_ref[0, feats, :], preferred_element_type=jnp.float32
        )
    out_ref[...] = total.astype(out_ref.dtype).reshape(out_ref.shape)


def project(mine, other, weights, core, first, blocks, dtype):
    half, tok_dev, head_dim = mine.shape
    _, feats, cols = weights.shape
    wide = cols % 128 == 0
    if wide:
        out_spec = pl.BlockSpec((tok_dev, cols), lambda j, at: (0, j))
        out_shape = (tok_dev, blocks * cols)
    else:
        out_spec = pl.BlockSpec((1, tok_dev, cols), lambda j, at: (j, 0, 0))
        out_shape = (blocks, tok_dev, cols)
    rows_spec = pl.BlockSpec(mine.shape, lambda j, at: (0, 0, 0))
    out = pl.pallas_call(
        project_kernel,
        grid_spec=pltpu.PrefetchScalarGridSpec(
            num_scalar_prefetch=1,
            grid=(blocks,),
            in_specs=[
                rows_spec,
                rows_spec,
                pl.BlockSpec((1, feats, cols), lambda j, at: (at[1] + j, 0, 0)),
            ],
            out_specs=out_spec,
            scratch_shapes=[pltpu.VMEM((2, tok_dev, half * head_dim), jnp.bfloat16)],
        ),
        out_shape=jax.ShapeDtypeStruct(out_shape, dtype),
        compiler_params=pltpu.CompilerParams(vmem_limit_bytes=40 * 2**20),
        name="project",
    )(jnp.stack([core, first]), mine, other, weights)
    return out if wide else jnp.transpose(out, (1, 0, 2)).reshape(tok_dev, blocks * cols)


def per_device(
    queries,
    keys,
    values,
    key_cache,
    value_cache,
    cache_len,
    page_table,
    append_slots,
    out_weight,
    out_bias,
):
    tok_dev, head_count, head_dim = queries.shape
    requests = cache_len.shape[0]
    max_pages = page_table.shape[1]
    new_pages = append_slots.shape[1]
    span_len = new_pages * PAGE
    slot_count = key_cache.shape[0]
    tokens = requests * span_len
    page_devs = tokens // tok_dev
    scale2 = math.log2(math.e) / math.sqrt(head_dim)
    device_at = lax.axis_index("pages")
    token_ids = device_at * tok_dev + jnp.arange(tok_dev, dtype=jnp.int32)
    request_ids = token_ids // span_len
    request_grid = jnp.arange(requests, dtype=jnp.int32)
    starts = jnp.sum(
        jnp.where(request_ids[:, None] == request_grid[None, :], cache_len[None, :], 0), axis=1
    )
    positions = (starts + token_ids % span_len).astype(jnp.float32)
    rotated_q = rotate(queries.astype(jnp.float32), positions).astype(jnp.bfloat16)
    core = device_at % 2
    half = head_count // 2
    chip_len = 2 * tok_dev

    def halves(x):
        return (
            lax.dynamic_slice_in_dim(x, core * half, half, 0),
            lax.dynamic_slice_in_dim(x, (1 - core) * half, half, 0),
        )

    def in_order(mine, got, axis):
        return jnp.where(
            core == 0,
            jnp.concatenate([mine, got], axis=axis),
            jnp.concatenate([got, mine], axis=axis),
        )

    q_own = jnp.transpose(rotated_q, (1, 0, 2))
    q_mine, q_other = halves(q_own)
    q_chip = in_order(q_mine, swap(q_other, 1), 1)
    groups = lax.axis_size("heads")
    group_at = lax.axis_index("heads")
    natural = Layout((0, 1, 2))
    q_chip, late_k, late_v = lax.optimization_barrier((q_chip, keys, values))
    q_places = gather_lines(q_chip)
    rotated_k = rotate(late_k.astype(jnp.float32), positions).astype(jnp.bfloat16)
    all_k = lax.all_gather(rotated_k, "pages", axis=0, tiled=True)
    all_v = lax.all_gather(late_v, "pages", axis=0, tiled=True)
    all_k = with_layout_constraint(all_k, natural)
    all_v = with_layout_constraint(all_v, natural)
    weights = lax.all_gather(out_weight, "pages", axis=0, tiled=False)

    my_slots = device_at * slot_count + jnp.arange(slot_count, dtype=jnp.int32)
    chip_slots = jnp.concatenate(
        [my_slots, (device_at ^ 1) * slot_count + jnp.arange(slot_count, dtype=jnp.int32)]
    )
    cached_hit = page_table.reshape(-1)[None, :] == chip_slots[:, None]
    fresh_hit = append_slots.reshape(-1)[None, :] == my_slots[:, None]
    table_at = jnp.arange(requests * max_pages, dtype=jnp.int32)
    shown = (table_at % max_pages) * PAGE < jnp.repeat(cache_len, max_pages)
    is_fresh = jnp.any(fresh_hit, axis=1)
    fresh_index = jnp.sum(
        jnp.where(fresh_hit, jnp.arange(requests * new_pages, dtype=jnp.int32)[None, :], 0), axis=1
    )
    slot_key = requests - jnp.sum(
        jnp.where(cached_hit & shown[None, :], requests - (table_at // max_pages)[None, :], 0),
        axis=1,
    )
    slot_at = jnp.arange(2 * slot_count, dtype=jnp.int32)
    earlier = (slot_key[None, :] < slot_key[:, None]) | (
        (slot_key[None, :] == slot_key[:, None]) & (slot_at[None, :] < slot_at[:, None])
    )
    rank = jnp.sum(earlier.astype(jnp.int32), axis=1)
    order = jnp.sum(jnp.where(rank[None, :] == slot_at[:, None], slot_at[None, :], 0), axis=1)
    slot_starts = jnp.sum((slot_key[None, :] < request_grid[:, None]).astype(jnp.int32), axis=1)
    slot_counts = jnp.sum((slot_key[None, :] == request_grid[:, None]).astype(jnp.int32), axis=1)

    k_mine, k_other = halves(jnp.transpose(key_cache, (2, 0, 1, 3)))
    v_mine, v_other = halves(jnp.transpose(value_cache, (2, 0, 3, 1)))
    k_heads = jnp.concatenate([k_mine, swap(k_other, 1)], axis=1)
    v_heads = jnp.concatenate([v_mine, swap(v_other, 1)], axis=1)

    unit = math.gcd(span_len, tok_dev)
    line = page_devs // 4
    line_at, across = device_at // 4, (device_at // 2) % 2
    outs = [
        cached_attention(
            first,
            half // 2,
            [q for q, _, _, _ in q_places],
            [jnp.clip(at, 0, line - 1) * 2 + side for _, at, side, _ in q_places],
            [ok for _, _, _, ok in q_places],
            [((line_at + k) % line) * 2 + (across ^ d) for k in range(line) for d in range(2)],
            k_heads,
            v_heads,
            order,
            slot_starts,
            slot_counts,
            span_len,
            unit,
            scale2,
        )
        for first in (0, half // 2)
    ]
    merged = lambda parts, ok: merge(parts, ok, chip_len, unit, scale2)

    merged_two = lambda halves: merge_two(halves, chip_len, unit, scale2)

    def fresh_part(after):
        back = -(-(span_len - math.gcd(span_len, chip_len)) // chip_len)
        own_kv = jnp.stack(
            [jnp.transpose(rotated_k, (1, 0, 2)), jnp.transpose(late_v, (1, 0, 2))], 1
        )
        kv_mine, kv_other = halves(own_kv)
        kv_chip = in_order(kv_mine, swap(kv_other, 1), 2)
        kv_chip, _ = lax.optimization_barrier((kv_chip, after))
        kv_back = [
            lax.ppermute(kv_chip, "pages", [(p, p + 2 * b) for p in range(page_devs - 2 * b)])
            for b in range(back, 0, -1)
        ]
        chip_at = device_at // 2
        window = jnp.concatenate(kv_back + [kv_chip], axis=2)
        chip_tokens = chip_at * chip_len + jnp.arange(chip_len, dtype=jnp.int32)
        token_rows = jnp.stack([chip_tokens, chip_tokens // span_len * span_len])
        keys_at = (chip_at - back) * chip_len
        keys_at = keys_at + jnp.arange((back + 1) * chip_len, dtype=jnp.int32)
        key_cols = jnp.where(keys_at < 0, tokens, keys_at)[:, None]
        return fresh_attention(
            q_chip, window[:, 0], window[:, 1], token_rows, key_cols, unit, scale2
        )

    parts = [[[out[2 * k + d] for out in outs] for d in range(2)] for k in range(line)]
    chip_part = merge_lines(parts, merged, merged_two, fresh_part)
    rows_of = lambda c: lax.dynamic_slice_in_dim(chip_part[:, :chip_len], c * tok_dev, tok_dev, 1)
    own_rows, got_rows = rows_of(core), swap(rows_of(1 - core), 1)
    blocks = page_devs // groups
    pieces = 2
    sent = []
    for s in range(groups - 1, 0, -1):
        for piece in range(pieces):
            part = project(
                own_rows,
                got_rows,
                weights,
                core,
                (group_at + s) % groups * blocks + piece * (blocks // pieces),
                blocks // pieces,
                jnp.bfloat16,
            )
            moves = [(h, (h + s) % groups) for h in range(groups)]
            sent.append(lax.ppermute(part, "heads", moves))
    total = project(
        own_rows, got_rows, weights, core, group_at * blocks, blocks, jnp.float32
    ) + out_bias[None, :]
    for at in range(0, len(sent), pieces):
        total = total + jnp.concatenate(sent[at : at + pieces], axis=1).astype(jnp.float32)
    hidden = total.astype(jnp.bfloat16)
    page_shape = (requests * new_pages, PAGE, head_count, head_dim)
    key_out, value_out = write_pages(
        key_cache,
        value_cache,
        all_k.reshape(page_shape),
        all_v.reshape(page_shape),
        is_fresh,
        fresh_index,
    )
    return (hidden, key_out, value_out)


def solution(mesh):
    placed = (
        P("pages", "heads", None),
        P("pages", "heads", None),
        P("pages", "heads", None),
        P("pages", None, "heads", None),
        P("pages", None, "heads", None),
        P(),
        P(),
        P(),
        P("heads", "pages"),
        P("heads"),
    )
    return jax.shard_map(
        per_device,
        mesh=mesh,
        in_specs=placed,
        out_specs=(
            P("pages", "heads"),
            P("pages", None, "heads", None),
            P("pages", None, "heads", None),
        ),
        check_vma=False,
    )
```

```python
import functools
import math

import jax
import jax.numpy as jnp
from jax import lax
from jax.experimental import pallas as pl
from jax.experimental.layout import Layout, with_layout_constraint
from jax.experimental.pallas import tpu as pltpu
from jax.sharding import PartitionSpec as P

ROT = 32
PAGE = 128
QTILE = 256

low_score = -(2.0**99)


def rotate(vectors, positions):
    half_rot = ROT // 2
    inv_freq = 10000.0 ** (-2.0 * jnp.arange(half_rot, dtype=jnp.float32) / ROT)
    angles = positions[:, None] * inv_freq[None, :]
    cosine = jnp.cos(angles)[:, None, :]
    sine = jnp.sin(angles)[:, None, :]
    first_half = vectors[..., :half_rot]
    second_half = vectors[..., half_rot:ROT]
    return jnp.concatenate(
        [
            first_half * cosine - second_half * sine,
            second_half * cosine + first_half * sine,
            vectors[..., ROT:],
        ],
        axis=-1,
    )


def stat_rows_of(part_len, unit):
    per_unit = -(-unit // 128)
    units = part_len // unit
    return per_unit, units, -(-3 * units * per_unit // 16) * 16


def stat_rows(row):
    unit = row.shape[1]
    full = -(-unit // 128) * 128
    if full > unit:
        row = jnp.concatenate([row, jnp.zeros((1, full - unit), row.dtype)], axis=1)
    return [row[:, at : at + 128] for at in range(0, full, 128)]


def stat_block(kinds, pad_to):
    rows = [piece for kind in kinds for row in kind for piece in stat_rows(row)]
    rows.append(jnp.zeros((pad_to - len(rows), 128), jnp.float32))
    return jnp.concatenate(rows, axis=0).astype(jnp.bfloat16)


def cached_kernel(unit, stat_unit, span, scale2, places, at_ref, ok_ref, order_ref, start_ref, count_ref,
                  *refs):
    q_refs, (k_ref, v_ref), refs = refs[:places], refs[places : places + 2], refs[places + 2 :]
    o_refs, (q_all, o_all, s_all, q_scr, m_scr, l_scr, acc_scr) = refs[:-7], refs[-7:]
    requests = count_ref.shape[0]
    chips, part_len, _ = q_all.shape
    per_part = part_len // unit
    per_request = span // unit
    per_unit, units, pad_to = stat_rows_of(part_len, stat_unit)

    for index in range(places):

        @pl.when(ok_ref[index] > 0)
        def _(index=index):
            q_all[at_ref[index]] = q_refs[index][0]

    def place(at, per_part):
        return at // per_part, at % per_part

    def one_request(request, _):
        for index in range(per_request):
            part, piece = place(request * per_request + index, per_part)
            row = pl.ds(pl.multiple_of(piece * unit, unit), unit)
            q_scr[index * unit : (index + 1) * unit, :] = q_all[part, row, :]
        first = start_ref[request]
        count = count_ref[request]
        m_scr[...] = jnp.full((1, span), low_score, jnp.float32)
        l_scr[...] = jnp.zeros((1, span), jnp.float32)
        acc_scr[...] = jnp.zeros(acc_scr.shape, jnp.float32)

        def pages(slots):
            k = jnp.concatenate([k_ref[0, s] for s in slots], axis=0)
            v = jnp.concatenate([v_ref[0, s] for s in slots], axis=1)
            for c in range(0, span, QTILE):
                cols = slice(c, c + QTILE)
                scores = lax.dot_general(
                    k, q_scr[cols, :], (((1,), (1,)), ((), ())),
                    preferred_element_type=jnp.float32,
                )
                before = m_scr[:, cols]
                peak = jnp.maximum(before, jnp.max(scores, axis=0, keepdims=True))
                weights = jnp.exp2((scores - peak) * scale2)
                fade = jnp.exp2((before - peak) * scale2)
                m_scr[:, cols] = peak
                l_scr[:, cols] = l_scr[:, cols] * fade + jnp.sum(weights, axis=0, keepdims=True)
                acc_scr[:, cols] = acc_scr[:, cols] * fade + jnp.dot(
                    v, weights.astype(jnp.bfloat16), preferred_element_type=jnp.float32
                )

        def pair(index, _):
            at = first + 2 * index
            pages([order_ref[at], order_ref[at + 1]])
            return 0

        lax.fori_loop(0, count // 2, pair, 0)

        @pl.when(count % 2 == 1)
        def _():
            pages([order_ref[first + count - 1]])

        totals = l_scr[...]
        peaks = m_scr[...]
        out = (acc_scr[...] / jnp.maximum(totals, 1e-30)).T.astype(jnp.bfloat16)
        sent = peaks.astype(jnp.bfloat16).astype(jnp.float32)
        totals = totals * jnp.exp2((peaks - sent) * scale2)
        high = totals.astype(jnp.bfloat16).astype(jnp.float32)
        kinds = [sent, high, totals - high]
        for index in range(per_request):
            part, piece = place(request * per_request + index, per_part)
            row = pl.ds(pl.multiple_of(piece * unit, unit), unit)
            o_all[part, row, :] = out[index * unit : (index + 1) * unit, :]
        for index in range(span // stat_unit):
            part, piece = place(request * (span // stat_unit) + index, units)
            cols = slice(index * stat_unit, (index + 1) * stat_unit)
            for kind, values in enumerate(kinds):
                for r, line in enumerate(stat_rows(values[:, cols])):
                    at = (kind * units + piece) * per_unit + r
                    s_all[part, pl.ds(at, 1), :] = line
        return 0

    lax.fori_loop(0, requests, one_request, 0)
    for index in range(chips):
        part = at_ref[places + index]
        o_refs[index][0, :part_len, :] = o_all[part]
        o_refs[index][0, part_len:, :] = s_all[part].astype(jnp.bfloat16)


def cached_attention(first, heads, q_places, at, ok, out_at, k_heads, v_heads, order, starts,
                     counts, span, stat_unit, scale2):
    places = len(q_places)
    chips = len(out_at)
    _, part_len, head_dim = q_places[0].shape
    slots = k_heads.shape[1]
    unit = math.gcd(span, part_len)
    _, _, pad_to = stat_rows_of(part_len, stat_unit)
    own_block = lambda *dims: pl.BlockSpec(
        (1,) + dims, lambda h, *_: (first + h,) + (0,) * len(dims)
    )
    out_block = pl.BlockSpec((1, part_len + pad_to, head_dim), lambda h, *_: (h, 0, 0))
    return pl.pallas_call(
        lambda *refs: cached_kernel(unit, stat_unit, span, scale2, places, *refs),
        grid_spec=pltpu.PrefetchScalarGridSpec(
            num_scalar_prefetch=5,
            grid=(heads,),
            in_specs=[own_block(part_len, head_dim)] * places
            + [own_block(slots, PAGE, head_dim), own_block(slots, head_dim, PAGE)],
            out_specs=[out_block] * chips,
            scratch_shapes=[
                pltpu.VMEM((chips, part_len, head_dim), jnp.bfloat16),
                pltpu.VMEM((chips, part_len, head_dim), jnp.bfloat16),
                pltpu.VMEM((chips, pad_to, 128), jnp.float32),
                pltpu.VMEM((span, head_dim), jnp.bfloat16),
                pltpu.VMEM((1, span), jnp.float32),
                pltpu.VMEM((1, span), jnp.float32),
                pltpu.VMEM((head_dim, span), jnp.float32),
            ],
        ),
        out_shape=[
            jax.ShapeDtypeStruct((heads, part_len + pad_to, head_dim), jnp.bfloat16)
        ] * chips,
        compiler_params=pltpu.CompilerParams(vmem_limit_bytes=60 * 2**20),
        cost_estimate=pl.CostEstimate(
            flops=20 * 10**9, bytes_accessed=10 * 2**20, transcendentals=10**7
        ),
        name="cached_attention",
    )(jnp.stack(at + out_at), jnp.stack(ok), order, starts, counts, *q_places, k_heads, v_heads)


def merge_kernel(unit, part_len, scale2, ok_ref, *refs):
    in_refs, out_ref = refs[:-1], refs[-1]
    heads, _, width = out_ref.shape
    _, units, pad_to = stat_rows_of(part_len, unit)
    oks = [ok_ref[index] > 0 for index in range(len(in_refs))]
    for h in range(heads):
        peaks, totals = [], []
        for ok, ref in zip(oks, in_refs):
            stat = ref[h, part_len:, :].astype(jnp.float32)
            peaks.append(jnp.where(ok, stat[:units], low_score))
            total = stat[units : 2 * units] + stat[2 * units : 3 * units]
            totals.append(jnp.where(ok, total, 0.0))
        top = functools.reduce(jnp.maximum, peaks)
        shares = [t * jnp.exp2((p - top) * scale2) for t, p in zip(totals, peaks)]
        total = functools.reduce(jnp.add, shares)
        inverse = 1.0 / jnp.maximum(total, 1e-30)
        merged = [0.0] * units
        for ref, share in zip(in_refs, shares):
            weight = jnp.concatenate(
                [share * inverse, jnp.zeros((-units % 8, 128), jnp.float32)], axis=0
            ).T
            rows = ref[h, :part_len, :].astype(jnp.float32)
            for u in range(units):
                merged[u] = merged[u] + weight[:unit, u : u + 1] * rows[u * unit : (u + 1) * unit]
        high = total.astype(jnp.bfloat16).astype(jnp.float32)
        stats = [top, high, total - high, jnp.zeros((pad_to - 3 * units, width), jnp.float32)]
        out_ref[h, :part_len, :] = jnp.concatenate(merged, axis=0).astype(jnp.bfloat16)
        out_ref[h, part_len:, :] = jnp.concatenate(stats, axis=0).astype(jnp.bfloat16)


def merge(parts, ok, part_len, unit, scale2):
    heads = parts[0].shape[0]
    step = max(1, heads // 2)
    block = pl.BlockSpec((step,) + parts[0].shape[1:], lambda h, *_: (h, 0, 0))
    return pl.pallas_call(
        lambda *refs: merge_kernel(unit, part_len, scale2, *refs),
        grid_spec=pltpu.PrefetchScalarGridSpec(
            num_scalar_prefetch=1,
            grid=(heads // step,),
            in_specs=[block] * len(parts),
            out_specs=block,
        ),
        out_shape=jax.ShapeDtypeStruct(parts[0].shape, jnp.bfloat16),
        name="merge",
    )(jnp.stack(ok).astype(jnp.int32), *parts)


def merge_two(halves, part_len, unit, scale2):
    heads, rows, width = halves[0][0].shape
    whole = pl.BlockSpec((heads, rows, width), lambda h, *_: (0, 0, 0))

    def kernel(ok_ref, *refs):
        for half in range(2):

            @pl.when(pl.program_id(0) == half)
            def _(half=half):
                merge_kernel(
                    unit, part_len, scale2, ok_ref, refs[2 * half], refs[2 * half + 1], refs[4]
                )

    return pl.pallas_call(
        kernel,
        grid_spec=pltpu.PrefetchScalarGridSpec(
            num_scalar_prefetch=1,
            grid=(2,),
            in_specs=[whole] * 4,
            out_specs=pl.BlockSpec((heads, rows, width), lambda h, *_: (h, 0, 0)),
        ),
        out_shape=jax.ShapeDtypeStruct((2 * heads, rows, width), jnp.bfloat16),
        name="merge_two",
    )(jnp.ones((2,), jnp.int32), *halves[0], *halves[1])


def page_kernel(fresh_ref, index_ref, kc_ref, vc_ref, kn_ref, vn_ref, ko_ref, vo_ref):
    fresh = fresh_ref[pl.program_id(0)] > 0

    @pl.when(fresh)
    def _():
        ko_ref[...] = kn_ref[...]
        vo_ref[...] = vn_ref[...]

    @pl.when(jnp.logical_not(fresh))
    def _():
        ko_ref[...] = kc_ref[...]
        vo_ref[...] = vc_ref[...]


def write_pages(key_cache, value_cache, new_keys, new_values, is_fresh, fresh_index):
    block = (1,) + key_cache.shape[1:]
    own = pl.BlockSpec(block, lambda s, fresh, index: (s, 0, 0, 0))
    new = pl.BlockSpec(block, lambda s, fresh, index: (index[s], 0, 0, 0))
    return pl.pallas_call(
        page_kernel,
        grid_spec=pltpu.PrefetchScalarGridSpec(
            num_scalar_prefetch=2,
            grid=(key_cache.shape[0],),
            in_specs=[own, own, new, new],
            out_specs=[own, own],
        ),
        out_shape=[jax.ShapeDtypeStruct(key_cache.shape, key_cache.dtype)] * 2,
        compiler_params=pltpu.CompilerParams(vmem_limit_bytes=40 * 2**20),
        name="write_pages",
    )(is_fresh.astype(jnp.int32), fresh_index, key_cache, value_cache, new_keys, new_values)


def swap(x, bit):
    devs = lax.axis_size("pages")
    return lax.ppermute(x, "pages", [(p, p ^ bit) for p in range(devs)])


def shift(x, hop, senders):
    devs = lax.axis_size("pages")
    moves = [(p, p + 4 * hop) for p in range(devs) if p // 4 in senders]
    return lax.ppermute(x, "pages", moves)


def gather_lines(x):
    line = lax.axis_size("pages") // 4
    device_at = lax.axis_index("pages")
    at, across = device_at // 4, (device_at // 2) % 2
    always = jnp.int32(1)
    held = [(x, at, across, always), (swap(x, 2), at, 1 - across, always)]
    up = down = x
    for t in range(1, line):
        up = shift(up, 1, range(t - 1, line - 1))
        down = shift(down, -1, range(1, line - t + 1))
        has_up = (at >= t).astype(jnp.int32)
        has_down = (at + t < line).astype(jnp.int32)
        devs = lax.axis_size("pages")
        cross_up = [(p, p ^ 2) for p in range(devs) if p // 4 >= t]
        cross_down = [(p, p ^ 2) for p in range(devs) if p // 4 + t < line]
        held += [
            (up, at - t, across, has_up),
            (lax.ppermute(up, "pages", cross_up), at - t, 1 - across, has_up),
            (down, at + t, across, has_down),
            (lax.ppermute(down, "pages", cross_down), at + t, 1 - across, has_down),
        ]
    return held


def merge_lines(parts, merged, merged_two, last):
    line = lax.axis_size("pages") // 4
    at = lax.axis_index("pages") // 4
    turns = []
    for t in range(1, line):
        turns += [k for k in (line - t, t) if k not in turns]
    yes = jnp.int32(1)
    crossed = {k: [swap(x, 2) for x in parts[k][1]] for k in turns + [0]}
    shares = {}

    def share(k):
        if k not in shares:
            shares[k] = merged_two(list(zip(parts[k][0], crossed[k])))
        return shares[k]

    up = down = None
    for t in range(1, line):
        up_out, down_out = share(line - t), share(t)
        if up is not None:
            up_out = merged([up_out, up], [yes, (at >= 1) & (at <= t - 1)])
            down_out = merged([down_out, down], [yes, (at <= line - 2) & (at >= line - t)])
        up = shift(up_out, 1, range(0, t))
        down = shift(down_out, -1, range(line - t, line))
    return merged([share(0), up, down, last([crossed[k] for k in turns + [0]])], [yes, at >= 1, at <= line - 2, yes])


def fresh_kernel(unit, scale2, q_ref, k_ref, v_ref, tok_ref, key_ref, o_ref):
    token, first, key = tok_ref[0:1, :], tok_ref[1:2, :], key_ref[:, 0:1]
    scores = lax.dot_general(
        k_ref[0], q_ref[0], (((1,), (1,)), ((), ())), preferred_element_type=jnp.float32
    )
    visible = (key <= token) & (key >= first)
    scores = jnp.where(visible, scores, low_score)
    peak = jnp.max(scores, axis=0, keepdims=True)
    weights = jnp.where(visible, jnp.exp2((scores - peak) * scale2), 0.0)
    totals = jnp.sum(weights, axis=0, keepdims=True)
    out = lax.dot_general(
        v_ref[0], weights.astype(jnp.bfloat16), (((0,), (0,)), ((), ())),
        preferred_element_type=jnp.float32,
    )
    out = out / totals
    part_len = out.shape[1]
    pad = -part_len % 128
    out = jnp.concatenate([out, jnp.zeros((out.shape[0], pad), jnp.float32)], axis=1)
    o_ref[0, :part_len, :] = out.T[:part_len].astype(jnp.bfloat16)
    sent = peak.astype(jnp.bfloat16).astype(jnp.float32)
    totals = totals * jnp.exp2((peak - sent) * scale2)
    high = totals.astype(jnp.bfloat16).astype(jnp.float32)
    kinds = [
        [values[:, at : at + unit] for at in range(0, part_len, unit)]
        for values in (sent, high, totals - high)
    ]
    o_ref[0, part_len:, :] = stat_block(kinds, o_ref.shape[1] - part_len)


def fresh_attention(q_chip, k_window, v_window, token_rows, key_cols, unit, scale2):
    heads, part_len, head_dim = q_chip.shape
    _, _, pad_to = stat_rows_of(part_len, unit)
    own = lambda x: pl.BlockSpec((1,) + x.shape[1:], lambda h: (h, 0, 0))
    fixed = lambda x: pl.BlockSpec(x.shape, lambda h: (0, 0))
    return pl.pallas_call(
        lambda *refs: fresh_kernel(unit, scale2, *refs),
        grid=(heads,),
        in_specs=[own(q_chip), own(k_window), own(v_window), fixed(token_rows), fixed(key_cols)],
        out_specs=pl.BlockSpec((1, part_len + pad_to, head_dim), lambda h: (h, 0, 0)),
        out_shape=jax.ShapeDtypeStruct((heads, part_len + pad_to, head_dim), jnp.bfloat16),
        compiler_params=pltpu.CompilerParams(vmem_limit_bytes=40 * 2**20),
        name="fresh_attention",
    )(q_chip, k_window, v_window, token_rows, key_cols)


def project_kernel(at_ref, mine_ref, other_ref, w_ref, out_ref, rows_ref):
    core = at_ref[0]
    wide = rows_ref.shape[2]

    @pl.when(pl.program_id(0) == 0)
    def _():
        for index, ref in enumerate((mine_ref, other_ref)):
            rows_ref[index] = jnp.concatenate([ref[h] for h in range(ref.shape[0])], axis=1)

    total = 0.0
    for d in range(2):
        feats = pl.ds(pl.multiple_of((core ^ d) * wide, wide), wide)
        total = total + jnp.dot(
            rows_ref[d], w_ref[0, feats, :], preferred_element_type=jnp.float32
        )
    out_ref[...] = total.astype(out_ref.dtype).reshape(out_ref.shape)


def project(mine, other, weights, core, first, blocks, dtype):
    half, tok_dev, head_dim = mine.shape
    _, feats, cols = weights.shape
    wide = cols % 128 == 0
    if wide:
        out_spec = pl.BlockSpec((tok_dev, cols), lambda j, at: (0, j))
        out_shape = (tok_dev, blocks * cols)
    else:
        out_spec = pl.BlockSpec((1, tok_dev, cols), lambda j, at: (j, 0, 0))
        out_shape = (blocks, tok_dev, cols)
    rows_spec = pl.BlockSpec(mine.shape, lambda j, at: (0, 0, 0))
    out = pl.pallas_call(
        project_kernel,
        grid_spec=pltpu.PrefetchScalarGridSpec(
            num_scalar_prefetch=1,
            grid=(blocks,),
            in_specs=[
                rows_spec,
                rows_spec,
                pl.BlockSpec((1, feats, cols), lambda j, at: (at[1] + j, 0, 0)),
            ],
            out_specs=out_spec,
            scratch_shapes=[pltpu.VMEM((2, tok_dev, half * head_dim), jnp.bfloat16)],
        ),
        out_shape=jax.ShapeDtypeStruct(out_shape, dtype),
        compiler_params=pltpu.CompilerParams(vmem_limit_bytes=40 * 2**20),
        name="project",
    )(jnp.stack([core, first]), mine, other, weights)
    return out if wide else jnp.transpose(out, (1, 0, 2)).reshape(tok_dev, blocks * cols)


def per_device(
    queries,
    keys,
    values,
    key_cache,
    value_cache,
    cache_len,
    page_table,
    append_slots,
    out_weight,
    out_bias,
):
    tok_dev, head_count, head_dim = queries.shape
    requests = cache_len.shape[0]
    max_pages = page_table.shape[1]
    new_pages = append_slots.shape[1]
    span_len = new_pages * PAGE
    slot_count = key_cache.shape[0]
    tokens = requests * span_len
    page_devs = tokens // tok_dev
    scale2 = math.log2(math.e) / math.sqrt(head_dim)
    device_at = lax.axis_index("pages")
    token_ids = device_at * tok_dev + jnp.arange(tok_dev, dtype=jnp.int32)
    request_ids = token_ids // span_len
    request_grid = jnp.arange(requests, dtype=jnp.int32)
    starts = jnp.sum(
        jnp.where(request_ids[:, None] == request_grid[None, :], cache_len[None, :], 0), axis=1
    )
    positions = (starts + token_ids % span_len).astype(jnp.float32)
    rotated_q = rotate(queries.astype(jnp.float32), positions).astype(jnp.bfloat16)
    core = device_at % 2
    half = head_count // 2
    chip_len = 2 * tok_dev

    def halves(x):
        return (
            lax.dynamic_slice_in_dim(x, core * half, half, 0),
            lax.dynamic_slice_in_dim(x, (1 - core) * half, half, 0),
        )

    def in_order(mine, got, axis):
        return jnp.where(
            core == 0,
            jnp.concatenate([mine, got], axis=axis),
            jnp.concatenate([got, mine], axis=axis),
        )

    q_own = jnp.transpose(rotated_q, (1, 0, 2))
    q_mine, q_other = halves(q_own)
    q_chip = in_order(q_mine, swap(q_other, 1), 1)
    groups = lax.axis_size("heads")
    group_at = lax.axis_index("heads")
    natural = Layout((0, 1, 2))
    q_chip, late_k, late_v = lax.optimization_barrier((q_chip, keys, values))
    q_places = gather_lines(q_chip)
    rotated_k = rotate(late_k.astype(jnp.float32), positions).astype(jnp.bfloat16)
    all_k = lax.all_gather(rotated_k, "pages", axis=0, tiled=True)
    all_v = lax.all_gather(late_v, "pages", axis=0, tiled=True)
    all_k = with_layout_constraint(all_k, natural)
    all_v = with_layout_constraint(all_v, natural)
    weights = lax.all_gather(out_weight, "pages", axis=0, tiled=False)

    my_slots = device_at * slot_count + jnp.arange(slot_count, dtype=jnp.int32)
    chip_slots = jnp.concatenate(
        [my_slots, (device_at ^ 1) * slot_count + jnp.arange(slot_count, dtype=jnp.int32)]
    )
    cached_hit = page_table.reshape(-1)[None, :] == chip_slots[:, None]
    fresh_hit = append_slots.reshape(-1)[None, :] == my_slots[:, None]
    table_at = jnp.arange(requests * max_pages, dtype=jnp.int32)
    shown = (table_at % max_pages) * PAGE < jnp.repeat(cache_len, max_pages)
    is_fresh = jnp.any(fresh_hit, axis=1)
    fresh_index = jnp.sum(
        jnp.where(fresh_hit, jnp.arange(requests * new_pages, dtype=jnp.int32)[None, :], 0), axis=1
    )
    slot_key = requests - jnp.sum(
        jnp.where(cached_hit & shown[None, :], requests - (table_at // max_pages)[None, :], 0),
        axis=1,
    )
    slot_at = jnp.arange(2 * slot_count, dtype=jnp.int32)
    earlier = (slot_key[None, :] < slot_key[:, None]) | (
        (slot_key[None, :] == slot_key[:, None]) & (slot_at[None, :] < slot_at[:, None])
    )
    rank = jnp.sum(earlier.astype(jnp.int32), axis=1)
    order = jnp.sum(jnp.where(rank[None, :] == slot_at[:, None], slot_at[None, :], 0), axis=1)
    slot_starts = jnp.sum((slot_key[None, :] < request_grid[:, None]).astype(jnp.int32), axis=1)
    slot_counts = jnp.sum((slot_key[None, :] == request_grid[:, None]).astype(jnp.int32), axis=1)

    k_mine, k_other = halves(jnp.transpose(key_cache, (2, 0, 1, 3)))
    v_mine, v_other = halves(jnp.transpose(value_cache, (2, 0, 3, 1)))
    k_heads = jnp.concatenate([k_mine, swap(k_other, 1)], axis=1)
    v_heads = jnp.concatenate([v_mine, swap(v_other, 1)], axis=1)

    unit = math.gcd(span_len, tok_dev)
    line = page_devs // 4
    line_at, across = device_at // 4, (device_at // 2) % 2
    outs = [
        cached_attention(
            first,
            half // 2,
            [q for q, _, _, _ in q_places],
            [jnp.clip(at, 0, line - 1) * 2 + side for _, at, side, _ in q_places],
            [ok for _, _, _, ok in q_places],
            [((line_at + k) % line) * 2 + (across ^ d) for k in range(line) for d in range(2)],
            k_heads,
            v_heads,
            order,
            slot_starts,
            slot_counts,
            span_len,
            unit,
            scale2,
        )
        for first in (0, half // 2)
    ]
    merged = lambda parts, ok: merge(parts, ok, chip_len, unit, scale2)

    merged_two = lambda halves: merge_two(halves, chip_len, unit, scale2)

    def fresh_part(after):
        back = -(-(span_len - math.gcd(span_len, chip_len)) // chip_len)
        own_kv = jnp.stack(
            [jnp.transpose(rotated_k, (1, 0, 2)), jnp.transpose(late_v, (1, 0, 2))], 1
        )
        kv_mine, kv_other = halves(own_kv)
        kv_chip = in_order(kv_mine, swap(kv_other, 1), 2)
        kv_chip, _ = lax.optimization_barrier((kv_chip, after))
        kv_back = [
            lax.ppermute(kv_chip, "pages", [(p, p + 2 * b) for p in range(page_devs - 2 * b)])
            for b in range(back, 0, -1)
        ]
        chip_at = device_at // 2
        window = jnp.concatenate(kv_back + [kv_chip], axis=2)
        chip_tokens = chip_at * chip_len + jnp.arange(chip_len, dtype=jnp.int32)
        token_rows = jnp.stack([chip_tokens, chip_tokens // span_len * span_len])
        keys_at = (chip_at - back) * chip_len
        keys_at = keys_at + jnp.arange((back + 1) * chip_len, dtype=jnp.int32)
        key_cols = jnp.where(keys_at < 0, tokens, keys_at)[:, None]
        return fresh_attention(
            q_chip, window[:, 0], window[:, 1], token_rows, key_cols, unit, scale2
        )

    parts = [[[out[2 * k + d] for out in outs] for d in range(2)] for k in range(line)]
    chip_part = merge_lines(parts, merged, merged_two, fresh_part)
    rows_of = lambda c: lax.dynamic_slice_in_dim(chip_part[:, :chip_len], c * tok_dev, tok_dev, 1)
    own_rows, got_rows = rows_of(core), swap(rows_of(1 - core), 1)
    blocks = page_devs // groups
    pieces = 2
    sent = []
    for s in range(groups - 1, 0, -1):
        for piece in range(pieces):
            part = project(
                own_rows,
                got_rows,
                weights,
                core,
                (group_at + s) % groups * blocks + piece * (blocks // pieces),
                blocks // pieces,
                jnp.bfloat16,
            )
            moves = [(h, (h + s) % groups) for h in range(groups)]
            sent.append(lax.ppermute(part, "heads", moves))
    total = project(
        own_rows, got_rows, weights, core, group_at * blocks, blocks, jnp.float32
    ) + out_bias[None, :]
    for at in range(0, len(sent), pieces):
        total = total + jnp.concatenate(sent[at : at + pieces], axis=1).astype(jnp.float32)
    hidden = total.astype(jnp.bfloat16)
    page_shape = (requests * new_pages, PAGE, head_count, head_dim)
    key_out, value_out = write_pages(
        key_cache,
        value_cache,
        all_k.reshape(page_shape),
        all_v.reshape(page_shape),
        is_fresh,
        fresh_index,
    )
    return (hidden, key_out, value_out)


def solution(mesh):
    placed = (
        P("pages", "heads", None),
        P("pages", "heads", None),
        P("pages", "heads", None),
        P("pages", None, "heads", None),
        P("pages", None, "heads", None),
        P(),
        P(),
        P(),
        P("heads", "pages"),
        P("heads"),
    )
    return jax.shard_map(
        per_device,
        mesh=mesh,
        in_specs=placed,
        out_specs=(
            P("pages", "heads"),
            P("pages", None, "heads", None),
            P("pages", None, "heads", None),
        ),
        check_vma=False,
    )
```
